32 devices in a mesh: seq: 8 (over z, x), fsdp: 4 (over y, core).
Axes of the slice: x: 2, y: 2, z: 4, core: 2. Of those that a mesh axis runs over, the one named last changes fastest.
Arguments:
- tokens: bfloat16 [4096, 1536], P(('seq', 'fsdp')), may hold values from -6 to 6
- cotangent: bfloat16 [4096, 1536], P(('seq', 'fsdp')), may hold values from -6 to 6
- lengths: int32 [7], replicated, may hold values from 1 to 3585, 4096 in all
- attn_gain: bfloat16 [1536], P(('seq', 'fsdp')), may hold values from 0.5 to 1.5
- q_weight: bfloat16 [1536, 1536], P(('seq', 'fsdp')), may hold values from -0.15625 to 0.15625
- q_bias: bfloat16 [1536], P(('seq', 'fsdp')), may hold values from -3 to 3
- k_weight: bfloat16 [1536, 256], P(('seq', 'fsdp')), may hold values from -0.15625 to 0.15625
- k_bias: bfloat16 [256], P(('seq', 'fsdp')), may hold values from -3 to 3
- v_weight: bfloat16 [1536, 256], P(('seq', 'fsdp')), may hold values from -0.15625 to 0.15625
- v_bias: bfloat16 [256], P(('seq', 'fsdp')), may hold values from -3 to 3
- o_weight: bfloat16 [1536, 1536], P(('seq', 'fsdp')), may hold values from -1.25 to 1.25
- mlp_gain: bfloat16 [1536], P(('seq', 'fsdp')), may hold values from 0.5 to 1.5
- gate_weight: bfloat16 [1536, 8960], P(('seq', 'fsdp')), may hold values from -0.15625 to 0.15625
- up_weight: bfloat16 [1536, 8960], P(('seq', 'fsdp')), may hold values from -0.15625 to 0.15625
- down_weight: bfloat16 [8960, 1536], P(('seq', 'fsdp')), may hold values from -0.0625 to 0.0625
Outputs:
- layer_out: bfloat16 [4096, 1536], P(('seq', 'fsdp'))
- input_grad: float32 [4096, 1536], P(('seq', 'fsdp'))
- attn_gain_grad: float32 [1536], P(('seq', 'fsdp'))
- q_weight_grad: float32 [1536, 1536], P(('seq', 'fsdp'))
- q_bias_grad: float32 [1536], P(('seq', 'fsdp'))
- k_weight_grad: float32 [1536, 256], P(('seq', 'fsdp'))
- k_bias_grad: float32 [256], P(('seq', 'fsdp'))
- v_weight_grad: float32 [1536, 256], P(('seq', 'fsdp'))
- v_bias_grad: float32 [256], P(('seq', 'fsdp'))
- o_weight_grad: float32 [1536, 1536], P(('seq', 'fsdp'))
- mlp_gain_grad: float32 [1536], P(('seq', 'fsdp'))
- gate_weight_grad: float32 [1536, 8960], P(('seq', 'fsdp'))
- up_weight_grad: float32 [1536, 8960], P(('seq', 'fsdp'))
- down_weight_grad: float32 [8960, 1536], P(('seq', 'fsdp'))
The draws below stay inside these ranges and needn't reach their ends.
Inputs may be any that keep to these rules, and one draw needn't show every extreme that they name: The lengths of the 7 packed sequences in order; they sum to 4096 and the longest has exactly 3585 tokens.
All inputs are finite; a program needn't handle non-finite values.
Results may differ from the reference program's by a relative error of at most 0.02.
Values may be sent and summed in bfloat16 or wider, within the bound.
A program may use at most 896 MiB of HBM per device.

```python
import math
import jax
import jax.numpy as jnp
import numpy as np
from jax import lax

D = 1536
HEADS = 12
KV_HEADS = 2
HEAD_DIM = 128
FF = 8960
SEGS = 7
QW = 1536
KW = 256
TOKENS = 4096
LONGEST = 3585


def levels(rng, dims, cuts, smallest, high):
    gain, own = 1.0, jax.random.fold_in(rng, 6)
    for dim, shards_of in cuts:
        steps = jnp.exp(jax.random.uniform(jax.random.fold_in(own, dim), (shards_of,), jnp.float32, smallest / len(cuts), high / len(cuts)))
        gain = gain * jnp.repeat(steps, dims[dim] // shards_of).reshape([-1 if axis == dim else 1 for axis in range(len(dims))])
    return gain


def profile(count, total, bound, slope):
    loads = [(1 << 20) // math.isqrt(grade ** slope) + 1 for grade in range(2, count + 1)]
    surplus, holding = total - bound - (count - 1), [1] * (count - 1)
    while surplus > 0:
        movable = [i for i in range(count - 1) if holding[i] < bound]
        whole, remaining = sum([loads[i] for i in movable]), surplus
        for i in movable:
            more = min(bound - holding[i], max(1, remaining * loads[i] // whole), surplus)
            holding[i] = holding[i] + more
            surplus = surplus - more
    return np.array([bound] + holding)


def uneven(stream_key, count, total, most, slope):
    if count == 2:
        one = jax.random.randint(stream_key, (), max(1, total - most), min(most, total - 1) + 1)
        return jnp.stack([one, total - one])
    sizes = jnp.asarray(profile(count, total, most, slope), jnp.int32)
    pairs = (count - 1) // 2
    donor, receiver = sizes[1:1 + 2 * pairs:2], sizes[2:2 + 2 * pairs:2]
    room = jnp.minimum(donor - 1, most - receiver)
    moved = jax.random.randint(jax.random.fold_in(stream_key, 1), (pairs,), 0, 1 << 20) % (room + 1)
    sizes = sizes.at[1:1 + 2 * pairs:2].set(donor - moved).at[2:2 + 2 * pairs:2].set(receiver + moved)
    return sizes[jax.random.permutation(jax.random.fold_in(stream_key, 2), count)]


def gaussian(rng, shape, spread, limit, split=(), held_as=jnp.bfloat16):
    level = levels(rng, shape, split, -0.22, 0.18) if split else 1.0
    values = jax.random.normal(rng, shape, jnp.float32) * spread * level
    return jnp.minimum(jnp.maximum(values, -limit), limit).astype(held_as)


def setup_inputs(seed: int = 0) -> dict:
    seeds = jax.random.split(jax.random.key(seed), 16)
    return {
        "tokens": gaussian(seeds[0], (TOKENS, D), 1.0, 6.0, ((0, 32),)),
        "cotangent": gaussian(seeds[1], (TOKENS, D), 1.0, 6.0, ((0, 32),)),
        "lengths": uneven(seeds[2], SEGS, TOKENS, LONGEST, 2).astype(jnp.int32),
        "attn_gain": jnp.clip(1.0 + 0.1 * jax.random.normal(seeds[3], (D,), jnp.float32), 0.5, 1.5).astype(jnp.bfloat16),
        "q_weight": gaussian(seeds[4], (D, QW), D ** -0.5, 0.15625, ((0, 32),)),
        "q_bias": gaussian(seeds[5], (QW,), 0.5, 3.0, ((0, 32),)),
        "k_weight": gaussian(seeds[6], (D, KW), D ** -0.5, 0.15625, ((0, 32),)),
        "k_bias": gaussian(seeds[7], (KW,), 0.5, 3.0, ((0, 32),)),
        "v_weight": gaussian(seeds[8], (D, KW), D ** -0.5, 0.15625, ((0, 32),)),
        "v_bias": gaussian(seeds[9], (KW,), 0.5, 3.0, ((0, 32),)),
        "o_weight": gaussian(seeds[10], (QW, D), (QW // 64) ** -0.5, 1.25, ((0, 32),)),
        "mlp_gain": jnp.clip(1.0 + 0.1 * jax.random.normal(seeds[11], (D,), jnp.float32), 0.5, 1.5).astype(jnp.bfloat16),
        "gate_weight": gaussian(seeds[12], (D, FF), D ** -0.5, 0.15625, ((0, 32),)),
        "up_weight": gaussian(seeds[13], (D, FF), D ** -0.5, 0.15625, ((0, 32),)),
        "down_weight": gaussian(seeds[14], (FF, D), FF ** -0.5, 0.0625, ((0, 32),)),
    }


EPSILON = 1e-06
ROPE_BASE = 10000.0
HIGHEST = lax.Precision.HIGHEST

@jax.custom_vjp
def low(v):
    return lax.optimization_barrier(v.astype(jnp.bfloat16)).astype(jnp.float32)

@jax.custom_vjp
def low_back(v):
    return v

def low_keep(v):
    return (low(v), None)

def low_pass(kept, grad):
    return (grad,)

def back_keep(v):
    return (v, None)

def back_low(kept, grad):
    return (low(grad),)
low.defvjp(low_keep, low_pass)
low_back.defvjp(back_keep, back_low)

def segment_of(positions, lengths):
    seg_ends = jnp.cumsum(lengths).astype(jnp.int32)
    seg_starts = (seg_ends - lengths).astype(jnp.int32)
    inside = (positions[:, None] >= seg_starts[None, :]) & (positions[:, None] < seg_ends[None, :])
    labels = jnp.arange(lengths.shape[0], dtype=jnp.int32)
    segment = lax.optimization_barrier(jnp.sum(jnp.where(inside, labels[None, :], 0), axis=1)).astype(jnp.int32)
    seg_begin = lax.optimization_barrier(jnp.sum(jnp.where(inside, seg_starts[None, :], 0), axis=1)).astype(jnp.int32)
    return (segment, (positions - seg_begin).astype(jnp.int32), seg_begin)

def rope_tables(places, head_size):
    half_size = head_size // 2
    frequency = ROPE_BASE ** (-2.0 * jnp.arange(half_size, dtype=jnp.float32) / head_size)
    angles = places.astype(jnp.float32)[:, None] * frequency[None, :]
    return (jnp.cos(angles), jnp.sin(angles))

def rotate(vector, cosine, sine_table):
    half_size = vector.shape[-1] // 2
    front_half = vector[..., :half_size]
    back_half = vector[..., half_size:]
    cosine = cosine[:, None, :]
    sine_table = sine_table[:, None, :]
    return jnp.concatenate([front_half * cosine - back_half * sine_table, back_half * cosine + front_half * sine_table], axis=-1)

def rms_norm(vector, gain_row):
    return vector * lax.rsqrt(lax.optimization_barrier(jnp.mean(vector * vector, axis=-1, keepdims=True)) + EPSILON) * gain_row

def matmul(left, right):
    return jnp.dot(left, right, preferred_element_type=jnp.float32, precision=HIGHEST)

def attention(queries, keys, values, segment):
    total_rows = queries.shape[0]
    block_rows = math.gcd(total_rows, 256)
    key_positions = jnp.arange(total_rows, dtype=jnp.int32)
    score_scale = HEAD_DIM ** (-0.5)

    def one_block(number):
        first_row = (number * block_rows).astype(jnp.int32)
        query_rows = lax.dynamic_slice_in_dim(queries, first_row, block_rows, 0)
        query_segment = lax.dynamic_slice_in_dim(segment, first_row, block_rows, 0)
        query_positions = first_row + jnp.arange(block_rows, dtype=jnp.int32)
        raw_scores = jnp.einsum('tgjd,kgd->gjtk', query_rows, keys, precision=HIGHEST)
        scores = low_back(raw_scores * score_scale)
        visible = (query_segment[:, None] == segment[None, :]) & (query_positions[:, None] >= key_positions[None, :])
        scores = jnp.where(visible, scores, -jnp.inf)
        attn_probs = low(jax.nn.softmax(scores, axis=-1))
        return jnp.einsum('gjtk,kgd->tgjd', attn_probs, values, precision=HIGHEST)
    blocks_out = lax.map(jax.checkpoint(one_block), jnp.arange(total_rows // block_rows, dtype=jnp.int32))
    return blocks_out.reshape(total_rows, queries.shape[1], queries.shape[2], queries.shape[3])

def layer(inputs, gain_one, w_query, b_query, w_key, b_key, w_value, b_value, w_out, gain_two, w_gate, w_up, w_down, segment, places):
    total_rows = inputs.shape[0]
    group_size = HEADS // KV_HEADS
    cosine, sine_table = rope_tables(places, HEAD_DIM)
    hidden_one = low(rms_norm(inputs, gain_one))
    query_lin = low_back(matmul(hidden_one, w_query) + b_query)
    key_lin = low_back(matmul(hidden_one, w_key) + b_key)
    value_lin = low_back(matmul(hidden_one, w_value) + b_value)
    queries = low(rotate(query_lin.reshape(total_rows, HEADS, HEAD_DIM), cosine, sine_table))
    keys = low(rotate(key_lin.reshape(total_rows, KV_HEADS, HEAD_DIM), cosine, sine_table))
    values = low(value_lin.reshape(total_rows, KV_HEADS, HEAD_DIM))
    mixed = attention(queries.reshape(total_rows, KV_HEADS, group_size, HEAD_DIM), keys, values, segment)
    mixed = low(low_back(mixed.reshape(total_rows, HEADS * HEAD_DIM)))
    middle = inputs + low_back(matmul(mixed, w_out))
    hidden_two = low(rms_norm(middle, gain_two))
    gate_act = low_back(matmul(hidden_two, w_gate))
    up_act = low_back(matmul(hidden_two, w_up))
    activated = low(jax.nn.silu(gate_act) * up_act)
    return middle + low_back(matmul(activated, w_down))

def reference(tokens, cotangent, lengths, attn_gain, q_weight, q_bias, k_weight, k_bias, v_weight, v_bias, o_weight, mlp_gain, gate_weight, up_weight, down_weight):
    positions = jnp.arange(TOKENS, dtype=jnp.int32)
    segment, places, seg_begin = segment_of(positions, lengths)
    params = [array.astype(jnp.float32) for array in (tokens, attn_gain, q_weight, q_bias, k_weight, k_bias, v_weight, v_bias, o_weight, mlp_gain, gate_weight, up_weight, down_weight)]

    def forward(*values_in):
        return layer(*values_in, segment, places)
    result, pullback = jax.vjp(forward, *params)
    gradients = pullback(cotangent.astype(jnp.float32))
    return (result.astype(jnp.bfloat16), gradients[0], gradients[1], gradients[2], gradients[3], gradients[4], gradients[5], gradients[6], gradients[7], gradients[8], gradients[9], gradients[10], gradients[11], gradients[12])
```

```python
import functools

import jax
import jax.numpy as jnp
from jax import lax
from jax.experimental import pallas as pl
from jax.experimental.pallas import tpu as pltpu
from jax.sharding import PartitionSpec as P

HEADS = 12
KV_HEADS = 2
HEAD_DIM = 128
GROUP = HEADS // KV_HEADS
EPSILON = 1e-06
ROPE_BASE = 10000.0
LOG2E = 1.4426950408889634
AXES = ("seq", "fsdp")
VMEM_LIMIT = 56 << 20
F32 = jnp.float32
BF16 = jnp.bfloat16
DMA = pltpu.SemaphoreType.DMA


class Place:
    def __init__(self, depth):
        self.depth = depth
        self.s = lax.axis_index("seq")
        self.f = lax.axis_index("fsdp")
        self.z = lax.div(self.s, 2)
        self.x = lax.rem(self.s, 2)
        self.y = lax.div(self.f, 2)
        self.c = lax.rem(self.f, 2)
        self.up = self.z + 1 < depth
        self.down = self.z > 0

    def flip_x(self):
        return (self.s + 1 - 2 * self.x, self.f)

    def flip_y(self):
        return (self.s, self.f + 2 - 4 * self.y)

    def flip_c(self):
        return (self.s, self.f + 1 - 2 * self.c)

    def z_up(self):
        return (self.s + 2, self.f)

    def z_down(self):
        return (self.s - 2, self.f)

    def first(self):
        return (
            self.s + (1 - self.c) * (1 - 2 * self.x),
            self.f + self.c * (2 - 4 * self.y),
        )

    def second(self):
        return (
            self.s + self.c * (1 - 2 * self.x),
            self.f + (1 - self.c) * (2 - 4 * self.y),
        )

    def corner(self, i, j):
        over_x = i * (1 - self.c) + j * self.c
        over_y = j * (1 - self.c) + i * self.c
        return (self.x + over_x * (1 - 2 * self.x), self.y + over_y * (1 - 2 * self.y))

    def wave(self, k):
        if k == 0:
            return [(self.z, None)]
        return [(self.z - k, self.z - k >= 0), (self.z + k, self.z + k < self.depth)]


def guard(condition, body):
    if condition is None:
        body()
    else:
        pl.when(condition)(body)


def greet(place, others=()):
    barrier = pltpu.get_barrier_semaphore()
    partners = [place.flip_x(), place.flip_y(), place.flip_c(), *others]
    for partner in partners:
        pl.semaphore_signal(barrier, inc=1, device_id=partner, device_id_type=pl.DeviceIdType.MESH)

    def tell_up():
        pl.semaphore_signal(
            barrier, inc=1, device_id=place.z_up(), device_id_type=pl.DeviceIdType.MESH
        )

    def tell_down():
        pl.semaphore_signal(
            barrier, inc=1, device_id=place.z_down(), device_id_type=pl.DeviceIdType.MESH
        )

    pl.when(place.up)(tell_up)
    pl.when(place.down)(tell_down)
    pl.semaphore_wait(
        barrier, len(partners) + place.up.astype(jnp.int32) + place.down.astype(jnp.int32)
    )


def remote(src, dst, send_sem, recv_sem, device):
    return pltpu.make_async_remote_copy(
        src_ref=src,
        dst_ref=dst,
        send_sem=send_sem,
        recv_sem=recv_sem,
        device_id=device,
        device_id_type=pl.DeviceIdType.MESH,
    )


def add_into(target, term, rows):
    step = 16 if rows % 16 == 0 else rows

    def body(number, carry):
        at = pl.ds(pl.multiple_of(number * step, step), step)
        target[at, :] = (target[at, :].astype(F32) + term[at, :].astype(F32)).astype(BF16)
        return carry

    lax.fori_loop(0, rows // step, body, 0)


class Gather:
    def __init__(self, place, wide, own, out, sems):
        self.place, self.wide, self.own, self.out, self.sems = place, wide, own, out, sems
        self.sent = []

    @staticmethod
    def semaphores(depth, wide):
        base = [DMA((1,)), DMA((2 * depth,)), DMA((depth,)), DMA((depth,)), DMA((depth,))]
        if wide:
            base += [DMA((2 * depth,)), DMA((2 * depth,)), DMA((4 * depth,)), DMA((4 * depth,))]
        return base

    def at(self, zi, i, j):
        place = self.place
        if self.wide:
            x, y = place.corner(i, j)
            return self.out.at[zi, x, y, place.c]
        return self.out.at[zi, place.x + i * (1 - 2 * place.x)]

    def send(self, src, dst, send_sem, recv_sem, device, condition):
        copy = remote(src, dst, send_sem, recv_sem, device)
        guard(condition, copy.start)
        self.sent.append((copy, condition))

    def local(self):
        copy = pltpu.make_async_copy(
            self.own, self.at(self.place.z, 0, 0), self.sems[0].at[0]
        )
        return copy

    def arrive(self, k):
        place, depth = self.place, self.place.depth
        z_send, z_recv, a_send, a_recv = self.sems[1:5]
        across = place.first() if self.wide else place.flip_x()
        for side, (zi, ok) in enumerate(place.wave(k)):
            block = self.at(zi, 0, 0)
            source = self.own if k == 0 else block
            if k > 0:
                landed = remote(block, block, z_send.at[0], z_recv.at[zi], place.z_up())
                guard(ok, landed.wait_recv)
            both = lambda a, b: a if b is None else jnp.logical_and(a, b)
            if k == 0 or side == 0:
                self.send(
                    source, block, z_send.at[k], z_recv.at[zi], place.z_up(), both(place.up, ok)
                )
            if k == 0 or side == 1:
                self.send(
                    source,
                    block,
                    z_send.at[depth + k],
                    z_recv.at[zi],
                    place.z_down(),
                    both(place.down, ok),
                )
            self.send(source, block, a_send.at[zi], a_recv.at[zi], across, ok)
            if self.wide:
                b_send, b_recv = self.sems[5:7]
                self.send(
                    source, block, b_send.at[2 * zi], b_recv.at[2 * zi], place.second(), ok
                )

    def across(self, k):
        place = self.place
        a_send, a_recv = self.sems[3:5]
        for zi, ok in place.wave(k):
            block = self.at(zi, 1, 0)
            landed = remote(block, block, a_send.at[0], a_recv.at[zi], place.first())
            guard(ok, landed.wait_recv)
            if self.wide:
                b_send, b_recv = self.sems[5:7]
                self.send(
                    block, block, b_send.at[2 * zi + 1], b_recv.at[2 * zi + 1], place.second(), ok
                )

    def hand(self, k):
        place = self.place
        b_send, b_recv, c_send, c_recv = self.sems[5:9]
        for zi, ok in place.wave(k):
            for i in range(2):
                block = self.at(zi, i, 1)
                landed = remote(block, block, b_send.at[0], b_recv.at[2 * zi + i], place.second())
                guard(ok, landed.wait_recv)
            for x in range(2):
                for y in range(2):
                    block = self.out.at[zi, x, y, place.c]
                    slot = 4 * zi + 2 * x + y
                    self.send(
                        block, block, c_send.at[slot], c_recv.at[slot], place.flip_c(), ok
                    )

    def take(self, k):
        place = self.place
        c_send, c_recv = self.sems[7:9]
        for zi, ok in place.wave(k):
            for x in range(2):
                for y in range(2):
                    block = self.out.at[zi, x, y, 1 - place.c]
                    slot = 4 * zi + 2 * x + y
                    landed = remote(block, block, c_send.at[0], c_recv.at[slot], place.flip_c())
                    guard(ok, landed.wait_recv)

    def settle(self):
        for copy, condition in self.sent:
            guard(condition, copy.wait_send)


def drive_gathers(place, gathers):
    depth = place.depth
    locals_ = [gather.local() for gather in gathers]
    for copy in locals_:
        copy.start()
    for step in range(depth + 3):
        for gather in gathers:
            if step < depth:
                gather.arrive(step)
        if step == 0:
            for copy in locals_:
                copy.wait()
        for gather in gathers:
            if 0 <= step - 1 < depth:
                gather.across(step - 1)
        for gather in gathers:
            if gather.wide and 0 <= step - 2 < depth:
                gather.hand(step - 2)
        for gather in gathers:
            if gather.wide and 0 <= step - 3 < depth:
                gather.take(step - 3)
    for gather in gathers:
        gather.settle()


def gather_shape(depth, wide, own):
    lead = (depth, 2, 2, 2) if wide else (depth, 2)
    return jax.ShapeDtypeStruct(lead + own.shape, own.dtype)


def call_gathers(depth, collective_id, wides, owns):
    def kernel(*refs):
        count = len(owns)
        place = Place(depth)
        greet(place)
        gathers, used = [], 2 * count
        for number, wide in enumerate(wides):
            need = len(Gather.semaphores(depth, wide))
            gathers.append(
                Gather(place, wide, refs[number], refs[count + number], refs[used : used + need])
            )
            used += need
        drive_gathers(place, gathers)

    scratch = []
    for wide in wides:
        scratch += Gather.semaphores(depth, wide)
    return pl.pallas_call(
        kernel,
        out_shape=[gather_shape(depth, wide, own) for wide, own in zip(wides, owns)],
        in_specs=[pl.BlockSpec(memory_space=pl.ANY)] * len(owns),
        out_specs=[pl.BlockSpec(memory_space=pl.ANY)] * len(owns),
        scratch_shapes=scratch,
        compiler_params=pltpu.CompilerParams(
            collective_id=collective_id, has_side_effects=True, vmem_limit_bytes=VMEM_LIMIT
        ),
    )(*owns)


def start_kernel(depth, *refs):
    (pack, cot, wide_in, down_in, pack_out, cot_out, wide_out, down_out), sems = refs[:8], refs[8:]
    place = Place(depth)
    count = 2 * depth
    partners = []
    for offset in range(1, count):
        partners.append((lax.rem(place.s + offset, count), place.f))
    greet(place, partners)
    first = len(Gather.semaphores(depth, True))
    second = first + len(Gather.semaphores(depth, False))
    gathers = [
        Gather(place, True, pack, pack_out, sems[:first]),
        Gather(place, False, cot, cot_out, sems[first:second]),
    ]
    local_sem, e_send, e_recv, y_send, y_recv, c_send, c_recv, d_sem, d_send, d_recv = sems[second:]
    sent = []

    def send(src, dst, send_sem, recv_sem, device):
        copy = remote(src, dst, send_sem, recv_sem, device)
        copy.start()
        sent.append(copy)

    locals_ = [gather.local() for gather in gathers]
    locals_.append(
        pltpu.make_async_copy(
            wide_in.at[:, place.s], wide_out.at[:, place.s, place.f], local_sem.at[0]
        )
    )
    locals_.append(pltpu.make_async_copy(down_in, down_out.at[place.f], d_sem.at[0]))
    for copy in locals_:
        copy.start()

    y_f = place.f + 2 - 4 * place.y
    c_f = place.f + 1 - 2 * place.c
    yc_f = y_f + 1 - 2 * place.c

    def exchange(offset):
        to = lax.rem(place.s + offset, count)
        send(
            wide_in.at[:, to],
            wide_out.at[:, place.s, place.f],
            e_send.at[offset],
            e_recv.at[offset],
            (to, place.f),
        )

    def onward(offset):
        origin = lax.rem(place.s + count - offset, count)
        block = wide_out.at[:, origin, place.f]
        if offset > 0:
            remote(block, block, e_send.at[0], e_recv.at[offset], place.flip_y()).wait_recv()
        send(block, block, y_send.at[offset], y_recv.at[offset], place.flip_y())
        send(block, block, c_send.at[2 * offset], c_recv.at[2 * offset], place.flip_c())

    def sideways(offset):
        origin = lax.rem(place.s + count - offset, count)
        block = wide_out.at[:, origin, y_f]
        remote(block, block, y_send.at[0], y_recv.at[offset], place.flip_y()).wait_recv()
        send(block, block, c_send.at[2 * offset + 1], c_recv.at[2 * offset + 1], place.flip_c())

    def last(offset):
        origin = lax.rem(place.s + count - offset, count)
        for slot, owner in ((2 * offset, c_f), (2 * offset + 1, yc_f)):
            block = wide_out.at[:, origin, owner]
            remote(block, block, c_send.at[0], c_recv.at[slot], place.flip_c()).wait_recv()

    for gather in gathers:
        gather.arrive(0)
    send(down_in, down_out.at[place.f], d_send.at[0], d_recv.at[0], place.flip_y())
    send(down_in, down_out.at[place.f], d_send.at[1], d_recv.at[1], place.flip_c())
    for offset in range(1, count):
        exchange(offset)
    for copy in locals_:
        copy.wait()
    onward(0)
    total = depth + 3
    for step in range(1, total):
        for gather in gathers:
            if step < depth:
                gather.arrive(step)
        for gather in gathers:
            if 0 <= step - 1 < depth:
                gather.across(step - 1)
        for gather in gathers:
            if gather.wide and 0 <= step - 2 < depth:
                gather.hand(step - 2)
        for gather in gathers:
            if gather.wide and 0 <= step - 3 < depth:
                gather.take(step - 3)
    block = down_out.at[y_f]
    remote(block, block, d_send.at[0], d_recv.at[0], place.flip_y()).wait_recv()
    send(block, block, d_send.at[2], d_recv.at[2], place.flip_c())
    for offset in range(1, count):
        onward(offset)
        sideways(offset - 1)
    sideways(count - 1)
    for offset in range(count):
        last(offset)
    for slot, owner in ((1, c_f), (2, yc_f)):
        block = down_out.at[owner]
        remote(block, block, d_send.at[0], d_recv.at[slot], place.flip_c()).wait_recv()
    for gather in gathers:
        gather.settle()
    for copy in sent:
        copy.wait_send()


def call_start(depth, collective_id, pack, cot, wide, down):
    count = 2 * depth
    _, _, rows, columns = wide.shape
    scratch = Gather.semaphores(depth, True) + Gather.semaphores(depth, False)
    scratch += [DMA((1,)), DMA((count,)), DMA((count,)), DMA((count,)), DMA((count,))]
    scratch += [DMA((2 * count,)), DMA((2 * count,)), DMA((1,)), DMA((3,)), DMA((3,))]
    return pl.pallas_call(
        functools.partial(start_kernel, depth),
        out_shape=[
            gather_shape(depth, True, pack),
            gather_shape(depth, False, cot),
            jax.ShapeDtypeStruct((2, count, 4, rows, columns), BF16),
            jax.ShapeDtypeStruct((4,) + down.shape, BF16),
        ],
        in_specs=[pl.BlockSpec(memory_space=pl.ANY)] * 4,
        out_specs=[pl.BlockSpec(memory_space=pl.ANY)] * 4,
        scratch_shapes=scratch,
        compiler_params=pltpu.CompilerParams(
            collective_id=collective_id, has_side_effects=True, vmem_limit_bytes=VMEM_LIMIT
        ),
    )(pack, cot, wide, down)


class Reduce:
    def __init__(self, place, wide, rows, own, out, buffers, sems):
        self.place, self.wide, self.rows = place, wide, rows
        self.own, self.out, self.buffers, self.sems = own, out, buffers, sems
        self.sent = []

    @staticmethod
    def scratch(depth, wide, block):
        buffers = [
            pltpu.VMEM((depth,) + block, BF16),
            pltpu.VMEM((depth + 1,) + block, BF16),
        ]
        sems = [DMA((depth,)), DMA((depth,)), DMA((2 * depth,)), DMA((2 * depth,))]
        if wide:
            buffers += [
                pltpu.VMEM((depth, 2, 2) + block, BF16),
                pltpu.VMEM((depth, 2) + block, BF16),
            ]
            sems += [DMA((4 * depth,)), DMA((4 * depth,)), DMA((2 * depth,)), DMA((2 * depth,))]
        return buffers, sems

    def send(self, src, dst, send_sem, recv_sem, device, condition):
        copy = remote(src, dst, send_sem, recv_sem, device)
        guard(condition, copy.start)
        self.sent.append((copy, condition))

    def cores(self, k):
        place = self.place
        c_send, c_recv = self.sems[4:6]
        got = self.buffers[2]
        for zi, ok in place.wave(k):
            for x in range(2):
                for y in range(2):
                    slot = 4 * zi + 2 * x + y
                    self.send(
                        self.own.at[zi, x, y, 1 - place.c],
                        got.at[zi, x, y],
                        c_send.at[slot],
                        c_recv.at[slot],
                        place.flip_c(),
                        ok,
                    )

    def over_second(self, k):
        place = self.place
        c_send, c_recv, b_send, b_recv = self.sems[4:8]
        got, next_ = self.buffers[2:4]
        for zi, ok in place.wave(k):

            def body(zi=zi):
                for j in (1, 0):
                    for i in (1, 0):
                        x, y = place.corner(i, j)
                        block = got.at[zi, x, y]
                        slot = 4 * zi + 2 * x + y
                        remote(
                            block, block, c_send.at[0], c_recv.at[slot], place.flip_c()
                        ).wait_recv()
                        add_into(block, self.own.at[zi, x, y, place.c], self.rows)
                        if j == 1:
                            remote(
                                block,
                                next_.at[zi, i],
                                b_send.at[2 * zi + i],
                                b_recv.at[2 * zi + i],
                                place.second(),
                            ).start()

            guard(ok, body)
            for i in (1, 0):
                x, y = place.corner(i, 1)
                copy = remote(
                    got.at[zi, x, y],
                    next_.at[zi, i],
                    b_send.at[2 * zi + i],
                    b_recv.at[2 * zi + i],
                    place.second(),
                )
                self.sent.append((copy, ok))

    def over_first(self, k):
        place = self.place
        a_send, a_recv = self.sems[0:2]
        got = self.buffers[0]
        for zi, ok in place.wave(k):
            if self.wide:
                b_send, b_recv = self.sems[6:8]
                before, held = self.buffers[2:4]

                def body(zi=zi):
                    for i in (1, 0):
                        block = held.at[zi, i]
                        x, y = place.corner(i, 0)
                        remote(
                            block, block, b_send.at[0], b_recv.at[2 * zi + i], place.second()
                        ).wait_recv()
                        add_into(block, before.at[zi, x, y], self.rows)
                        if i == 1:
                            remote(
                                block, got.at[zi], a_send.at[zi], a_recv.at[zi], place.first()
                            ).start()

                guard(ok, body)
                copy = remote(
                    held.at[zi, 1], got.at[zi], a_send.at[zi], a_recv.at[zi], place.first()
                )
                self.sent.append((copy, ok))
            else:
                self.send(
                    self.own.at[zi, 1 - place.x],
                    got.at[zi],
                    a_send.at[zi],
                    a_recv.at[zi],
                    place.flip_x(),
                    ok,
                )

    def along(self, k):
        place, depth = self.place, self.place.depth
        a_send, a_recv, z_send, z_recv = self.sems[0:4]
        held, line = self.buffers[0:2]
        for side, (zi, ok) in enumerate(place.wave(k)):
            block = held.at[zi]

            def body(zi=zi, side=side, block=block):
                remote(block, block, a_send.at[0], a_recv.at[zi], place.first()).wait_recv()
                if self.wide:
                    add_into(block, self.buffers[3].at[zi, 0], self.rows)
                else:
                    add_into(block, self.own.at[zi, place.x], self.rows)

                def more(direction):
                    slot = direction * depth + zi
                    term = line.at[depth if k == 0 and direction == 1 else zi]
                    remote(term, term, z_send.at[0], z_recv.at[slot], place.z_up()).wait_recv()
                    add_into(block, term, self.rows)

                def pass_on(direction, to):
                    slot = direction * depth + zi
                    there = line.at[depth if k == 1 and direction == 1 else zi]
                    remote(block, there, z_send.at[slot], z_recv.at[slot], to).start()

                if k == 0:
                    pl.when(place.down)(functools.partial(more, 0))
                    pl.when(place.up)(functools.partial(more, 1))
                elif side == 0:
                    pl.when(place.up)(functools.partial(more, 1))
                    pass_on(1, place.z_down())
                else:
                    pl.when(place.down)(functools.partial(more, 0))
                    pass_on(0, place.z_up())

            guard(ok, body)
            if k > 0:
                direction = 1 - side
                slot = direction * depth + zi
                to = place.z_up() if side == 1 else place.z_down()
                there = line.at[depth if k == 1 and direction == 1 else zi]
                copy = remote(block, there, z_send.at[slot], z_recv.at[slot], to)
                self.sent.append((copy, ok))

    def finish(self):
        self.out[...] = self.buffers[0][self.place.z].astype(self.out.dtype)

    def settle(self):
        for copy, condition in self.sent:
            guard(condition, copy.wait_send)


def drive_reduces(place, reduces):
    depth = place.depth
    order = list(range(depth - 1, -1, -1))
    for reduce in reduces:
        for k in order:
            reduce.cores(k) if reduce.wide else reduce.over_first(k)
    for step in range(depth + 2):
        for reduce in reduces:
            if not reduce.wide:
                if step < depth:
                    reduce.along(order[step])
                continue
            if step < depth:
                reduce.over_second(order[step])
            if 0 <= step - 1 < depth:
                reduce.over_first(order[step - 1])
            if 0 <= step - 2 < depth:
                reduce.along(order[step - 2])
    for reduce in reduces:
        reduce.finish()
    for reduce in reduces:
        reduce.settle()


def call_reduces(depth, collective_id, wides, owns):
    count = len(owns)
    blocks = [own.shape[-2:] for own in owns]
    parts = [Reduce.scratch(depth, wide, block) for wide, block in zip(wides, blocks)]
    scratch = []
    for buffers, sems in parts:
        scratch += buffers + sems

    def kernel(*refs):
        place = Place(depth)
        greet(place)
        reduces, used = [], 2 * count
        for number, (buffers, sems) in enumerate(parts):
            middle, end = used + len(buffers), used + len(buffers) + len(sems)
            reduces.append(
                Reduce(
                    place,
                    wides[number],
                    blocks[number][0],
                    refs[number],
                    refs[count + number],
                    refs[used:middle],
                    refs[middle:end],
                )
            )
            used = end
        drive_reduces(place, reduces)

    return pl.pallas_call(
        kernel,
        out_shape=[jax.ShapeDtypeStruct(block, F32) for block in blocks],
        in_specs=[pl.BlockSpec(memory_space=pltpu.VMEM)] * count,
        out_specs=[pl.BlockSpec(memory_space=pltpu.VMEM)] * count,
        scratch_shapes=scratch,
        compiler_params=pltpu.CompilerParams(
            collective_id=collective_id, has_side_effects=True, vmem_limit_bytes=VMEM_LIMIT
        ),
    )(*owns)


def end_kernel(depth, shapes, *refs):
    pack, wide, down, pack_out, wide_out, down_out = refs[:6]
    block, wide_block, down_block = shapes
    buffers, sems = Reduce.scratch(depth, True, block)
    used = 6 + len(buffers)
    place = Place(depth)
    count = 2 * depth
    partners = []
    for offset in range(1, count):
        partners.append((lax.rem(place.s + offset, count), place.f))
    greet(place, partners)
    reduce = Reduce(
        place, True, block[0], pack, pack_out, refs[6:used], refs[used : used + len(sems)]
    )
    used += len(sems)
    w_core, w_y, d_core, d_y = refs[used : used + 4]
    wc_send, wc_recv, wy_send, wy_recv, e_send, e_recv, e_sem = refs[used + 4 : used + 11]
    dc_send, dc_recv, dy_send, dy_recv = refs[used + 11 :]
    sent = []
    wide_rows, down_rows = wide_block[1], down_block[0]

    def send(src, dst, send_sem, recv_sem, device):
        copy = remote(src, dst, send_sem, recv_sem, device)
        copy.start()
        sent.append(copy)

    def landed(ref, recv_sem):
        remote(ref, ref, e_send.at[0], recv_sem, place.flip_c()).wait_recv()

    mine_y, other_y = place.y, 1 - place.y
    offsets = list(range(1, count)) + [0]
    for y in range(2):
        side = other_y if y == 0 else mine_y
        send(
            down.at[2 * side + 1 - place.c],
            d_core.at[side],
            dc_send.at[side],
            dc_recv.at[side],
            place.flip_c(),
        )
    for offset in offsets:
        to = lax.rem(place.s + offset, count)
        for y in range(2):
            send(
                wide.at[:, to, 2 * y + 1 - place.c],
                w_core.at[y, offset],
                wc_send.at[2 * offset + y],
                wc_recv.at[2 * offset + y],
                place.flip_c(),
            )
    order = list(range(depth - 1, -1, -1))
    for k in order:
        reduce.cores(k)

    def wide_add(target, term):
        for part in range(2):
            add_into(target.at[part], term.at[part], wide_rows)

    def wide_cores(offset):
        to = lax.rem(place.s + offset, count)
        for side in (other_y, mine_y):
            landed(w_core.at[side, offset], wc_recv.at[2 * offset + side])
            wide_add(w_core.at[side, offset], wide.at[:, to, 2 * side + place.c])
            if side is other_y:
                send(
                    w_core.at[side, offset],
                    w_y.at[offset],
                    wy_send.at[offset],
                    wy_recv.at[offset],
                    place.flip_y(),
                )

    def wide_across(offset):
        landed(w_y.at[offset], wy_recv.at[offset])
        wide_add(w_y.at[offset], w_core.at[mine_y, offset])
        to = lax.rem(place.s + offset, count)
        if offset > 0:
            send(
                w_y.at[offset],
                wide_out.at[place.s],
                e_send.at[offset],
                e_recv.at[offset],
                (to, place.f),
            )
        else:
            pltpu.make_async_copy(w_y.at[0], wide_out.at[place.s], e_sem.at[0]).start()

    for offset in offsets[: count // 2]:
        wide_cores(offset)
    for step in range(depth):
        reduce.over_second(order[step])
        if step >= 1:
            reduce.over_first(order[step - 1])
        if step == 0:
            for offset in offsets[count // 2 :]:
                wide_cores(offset)
            for side in (other_y, mine_y):
                landed(d_core.at[side], dc_recv.at[side])
                add_into(d_core.at[side], down.at[2 * side + place.c], down_rows)
                if side is other_y:
                    send(d_core.at[side], d_y.at[0], dy_send.at[0], dy_recv.at[0], place.flip_y())
        for offset in offsets[step * count // depth : (step + 1) * count // depth]:
            wide_across(offset)
        if step >= 2:
            reduce.along(order[step - 2])
    reduce.over_first(order[depth - 1])
    for step in range(max(depth - 2, 0), depth):
        reduce.along(order[step])
    reduce.finish()
    landed(d_y.at[0], dy_recv.at[0])
    down_out[...] = d_y[0].astype(F32) + d_core[mine_y].astype(F32)
    for offset in range(1, count):
        origin = lax.rem(place.s + count - offset, count)
        landed(wide_out.at[origin], e_recv.at[offset])
    pltpu.make_async_copy(w_y.at[0], wide_out.at[place.s], e_sem.at[0]).wait()
    reduce.settle()
    for copy in sent:
        copy.wait_send()


def call_end(depth, collective_id, pack, wide, down):
    count = 2 * depth
    block = pack.shape[-2:]
    wide_block = (2,) + wide.shape[-2:]
    down_block = down.shape[-2:]
    buffers, sems = Reduce.scratch(depth, True, block)
    scratch = buffers + sems
    scratch += [
        pltpu.VMEM((2, count) + wide_block, BF16),
        pltpu.VMEM((count,) + wide_block, BF16),
        pltpu.VMEM((2,) + down_block, BF16),
        pltpu.VMEM((1,) + down_block, BF16),
    ]
    scratch += [DMA((2 * count,)), DMA((2 * count,)), DMA((count,)), DMA((count,))]
    scratch += [DMA((count,)), DMA((count,)), DMA((1,))]
    scratch += [DMA((2,)), DMA((2,)), DMA((1,)), DMA((1,))]
    vmem = pl.BlockSpec(memory_space=pltpu.VMEM)
    return pl.pallas_call(
        functools.partial(end_kernel, depth, (block, wide_block, down_block)),
        out_shape=[
            jax.ShapeDtypeStruct(block, F32),
            jax.ShapeDtypeStruct((count,) + wide_block, BF16),
            jax.ShapeDtypeStruct(down_block, F32),
        ],
        in_specs=[vmem] * 3,
        out_specs=[vmem, vmem, vmem],
        scratch_shapes=scratch,
        compiler_params=pltpu.CompilerParams(
            collective_id=collective_id, has_side_effects=True, vmem_limit_bytes=VMEM_LIMIT
        ),
    )(pack, wide, down)


def forward_kernel(span, info, begin, query, key, value, mixed, lse, m_acc, l_acc, o_acc):
    rows = begin.shape[0]
    first_row, low, high = info[0], info[1], info[2]
    scale = HEAD_DIM ** (-0.5) * LOG2E
    m_acc[...] = jnp.full_like(m_acc, -1e30)
    l_acc[...] = jnp.zeros_like(l_acc)
    o_acc[...] = jnp.zeros_like(o_acc)
    places = first_row + lax.broadcasted_iota(jnp.int32, (rows, span), 0)
    offsets = lax.broadcasted_iota(jnp.int32, (rows, span), 1)

    def step(number, carry):
        base = pl.multiple_of(number * span, span)
        keys_at = base + offsets
        visible = jnp.logical_and(keys_at >= begin[...], keys_at <= places)
        for g in range(KV_HEADS):
            lanes = slice(g * HEAD_DIM, (g + 1) * HEAD_DIM)
            scores = lax.dot_general(
                query[g],
                key[pl.ds(base, span), lanes],
                (((1,), (1,)), ((), ())),
                preferred_element_type=F32,
            )
            scores = scores.reshape(GROUP, rows, span) * scale
            scores = jnp.where(visible[None], scores, -1e30).reshape(GROUP * rows, span)
            old = m_acc[g]
            new = jnp.maximum(old, jnp.max(scores, axis=-1, keepdims=True))
            weights = jnp.exp2(scores - new[:, :1])
            weights = jnp.where(
                visible[None], weights.reshape(GROUP, rows, span), 0.0
            ).reshape(GROUP * rows, span)
            fade = jnp.exp2(old - new)
            l_acc[g] = l_acc[g] * fade + jnp.sum(weights, axis=-1, keepdims=True)
            o_acc[g] = o_acc[g] * fade + jnp.dot(
                weights.astype(BF16),
                value[pl.ds(base, span), lanes],
                preferred_element_type=F32,
            )
            m_acc[g] = new
        return carry

    lax.fori_loop(low, high, step, 0)
    for g in range(KV_HEADS):
        mixed[g] = o_acc[g] / l_acc[g]
        lse[g] = m_acc[g] + jnp.log2(l_acc[g])


def call_forward(span, info, begin, query, key, value):
    stacked = query.shape[1]
    vmem = pl.BlockSpec(memory_space=pltpu.VMEM)
    return pl.pallas_call(
        functools.partial(forward_kernel, span),
        out_shape=[
            jax.ShapeDtypeStruct((KV_HEADS, stacked, HEAD_DIM), F32),
            jax.ShapeDtypeStruct((KV_HEADS, stacked, HEAD_DIM), F32),
        ],
        in_specs=[pl.BlockSpec(memory_space=pltpu.SMEM)] + [vmem] * 4,
        out_specs=[vmem, vmem],
        scratch_shapes=[pltpu.VMEM((KV_HEADS, stacked, HEAD_DIM), F32)] * 3,
        compiler_params=pltpu.CompilerParams(vmem_limit_bytes=VMEM_LIMIT),
    )(info, begin, query, key, value)


def backward_kernel(
    span, info, begin, query, key, value, mixed, lse, grad, dquery, dkeys, delta
):
    rows = begin.shape[0]
    first_row, low, high = info[0], info[1], info[2]
    scale = HEAD_DIM ** (-0.5) * LOG2E
    dquery[...] = jnp.zeros_like(dquery)
    width = KV_HEADS * HEAD_DIM
    for g in range(KV_HEADS):
        delta[g] = jnp.broadcast_to(
            jnp.sum(grad[g].astype(F32) * mixed[g], axis=-1, keepdims=True), delta.shape[1:]
        )
    places = first_row + lax.broadcasted_iota(jnp.int32, (rows, span), 0)
    offsets = lax.broadcasted_iota(jnp.int32, (rows, span), 1)

    def clear(number, carry):
        base = pl.multiple_of(number * span, span)
        dkeys[pl.ds(base, span), :] = jnp.zeros((span, dkeys.shape[1]), BF16)
        return carry

    lax.fori_loop(0, low, clear, 0)
    lax.fori_loop(high, dkeys.shape[0] // span, clear, 0)

    def step(number, carry):
        base = pl.multiple_of(number * span, span)
        keys_at = base + offsets
        visible = jnp.logical_and(keys_at >= begin[...], keys_at <= places)
        for g in range(KV_HEADS):
            lanes = slice(g * HEAD_DIM, (g + 1) * HEAD_DIM)
            key_rows = key[pl.ds(base, span), lanes]
            value_rows = value[pl.ds(base, span), lanes]
            scores = lax.dot_general(
                query[g], key_rows, (((1,), (1,)), ((), ())), preferred_element_type=F32
            )
            dprobs = lax.dot_general(
                grad[g], value_rows, (((1,), (1,)), ((), ())), preferred_element_type=F32
            )
            probs = jnp.exp2(scores * scale - lse[g][:, :1])
            probs = jnp.where(
                visible[None], probs.reshape(GROUP, rows, span), 0.0
            ).reshape(GROUP * rows, span)
            dscores = (probs * (dprobs - delta[g][:, :1])).astype(BF16)
            dquery[g] += jnp.dot(dscores, key_rows, preferred_element_type=F32)
            dkeys[pl.ds(base, span), lanes] = lax.dot_general(
                dscores, query[g], (((0,), (0,)), ((), ())), preferred_element_type=F32
            ).astype(BF16)
            dkeys[
                pl.ds(base, span), width + g * HEAD_DIM : width + (g + 1) * HEAD_DIM
            ] = lax.dot_general(
                probs.astype(BF16),
                grad[g],
                (((0,), (0,)), ((), ())),
                preferred_element_type=F32,
            ).astype(BF16)
        return carry

    lax.fori_loop(low, high, step, 0)


def call_backward(span, info, begin, query, key, value, mixed, lse, grad):
    stacked = query.shape[1]
    vmem = pl.BlockSpec(memory_space=pltpu.VMEM)
    return pl.pallas_call(
        functools.partial(backward_kernel, span),
        out_shape=[
            jax.ShapeDtypeStruct((KV_HEADS, stacked, HEAD_DIM), F32),
            jax.ShapeDtypeStruct((key.shape[0], 2 * key.shape[1]), BF16),
        ],
        in_specs=[pl.BlockSpec(memory_space=pltpu.SMEM)] + [vmem] * 7,
        out_specs=[vmem, vmem],
        scratch_shapes=[pltpu.VMEM((KV_HEADS, stacked, HEAD_DIM), F32)],
        compiler_params=pltpu.CompilerParams(vmem_limit_bytes=VMEM_LIMIT),
    )(info, begin, query, key, value, mixed, lse, grad)


def begin_of(positions, lengths):
    ends = jnp.cumsum(lengths)
    starts = ends - lengths
    inside = (positions[:, None] >= starts[None, :]) & (positions[:, None] < ends[None, :])
    return jnp.sum(jnp.where(inside, starts[None, :], 0), axis=1)


def rope_tables(places, head_size):
    half_size = head_size // 2
    frequency = ROPE_BASE ** (-2.0 * jnp.arange(half_size, dtype=F32) / head_size)
    angles = places.astype(F32)[:, None] * frequency[None, :]
    return (jnp.cos(angles), jnp.sin(angles))


def rotate(vector, cosine, sine_table, direction):
    half_size = vector.shape[-1] // 2
    front_half = vector[..., :half_size]
    back_half = vector[..., half_size:]
    cosine = cosine[:, None, :]
    sine_table = direction * sine_table[:, None, :]
    return jnp.concatenate(
        [
            front_half * cosine - back_half * sine_table,
            back_half * cosine + front_half * sine_table,
        ],
        axis=-1,
    )


def norm_back(grad_normed, normed, inverse, gain_row):
    scaled = grad_normed * gain_row
    return inverse * (scaled - normed * jnp.mean(scaled * normed, axis=-1, keepdims=True))


def dot(left, right):
    return jnp.dot(left, right, preferred_element_type=F32)


def dot_t(left, right):
    return lax.dot_general(left, right, (((1,), (1,)), ((), ())), preferred_element_type=F32)


def t_dot(left, right):
    return lax.dot_general(left, right, (((0,), (0,)), ((), ())), preferred_element_type=F32)


def column(vector, rows):
    return jnp.pad(vector, (0, rows - vector.shape[0]))[:, None]


def shards(
    tokens,
    cotangent,
    lengths,
    attn_gain,
    q_weight,
    q_bias,
    k_weight,
    k_bias,
    v_weight,
    v_bias,
    o_weight,
    mlp_gain,
    gate_weight,
    up_weight,
    down_weight,
):
    seq, fsdp = lax.axis_size("seq"), lax.axis_size("fsdp")
    devices = seq * fsdp
    depth = seq // 2
    rows, model = tokens.shape
    total = rows * devices
    key_width = KV_HEADS * HEAD_DIM
    query_width = HEADS * HEAD_DIM
    model_rows = q_weight.shape[0]
    units = gate_weight.shape[1] // seq
    first_row = lax.axis_index(AXES) * rows
    positions = first_row + jnp.arange(rows, dtype=jnp.int32)
    begin = begin_of(positions, lengths)
    cosine, sine_table = rope_tables(positions - begin, HEAD_DIM)
    score_scale = HEAD_DIM ** (-0.5)

    small = jnp.concatenate(
        [column(v, model_rows) for v in (attn_gain, q_bias, k_bias, v_bias, mlp_gain)]
        + [jnp.zeros((model_rows, 123), BF16)],
        axis=1,
    )
    pack = jnp.concatenate([q_weight, k_weight, v_weight, o_weight, small], axis=1)
    wide = jnp.stack([gate_weight, up_weight]).reshape(2, model_rows, seq, units)
    wide = wide.transpose(0, 2, 1, 3)
    pack_all, cot_all, wide_all, down_all = call_start(
        depth, 0, pack, cotangent, wide, down_weight
    )
    pack_all = pack_all.reshape(model, pack.shape[1])
    qkv_width = query_width + 2 * key_width
    w_qkv = pack_all[:, :qkv_width]
    w_out = pack_all[:, qkv_width : qkv_width + query_width]
    smalls = pack_all[:, qkv_width + query_width :].astype(F32)
    gain_one, b_query = smalls[:, 0], smalls[:, 1]
    gain_two = smalls[:, 4]
    kv_share = k_bias.shape[0]
    b_key = smalls[:, 2].reshape(devices, model_rows)[:, :kv_share].reshape(key_width)
    b_value = smalls[:, 3].reshape(devices, model_rows)[:, :kv_share].reshape(key_width)
    cot_all = cot_all.reshape(seq * rows, model)
    w_gate = wide_all[0].reshape(model, units)
    w_up = wide_all[1].reshape(model, units)
    w_down = down_all.reshape(units, model)

    inputs = tokens.astype(F32)
    inv_one = lax.rsqrt(jnp.mean(inputs * inputs, axis=-1, keepdims=True) + EPSILON)
    normed_one = inputs * inv_one
    hidden_one = (normed_one * gain_one).astype(BF16)
    lin = dot(hidden_one, w_qkv) + jnp.concatenate([b_query, b_key, b_value])
    queries = rotate(
        lin[:, :query_width].reshape(rows, HEADS, HEAD_DIM), cosine, sine_table, 1.0
    ).astype(BF16)
    queries = queries.transpose(1, 0, 2).reshape(KV_HEADS, GROUP * rows, HEAD_DIM)
    keys = rotate(
        lin[:, query_width : query_width + key_width].reshape(rows, KV_HEADS, HEAD_DIM),
        cosine,
        sine_table,
        1.0,
    ).reshape(rows, key_width)
    kv = jnp.concatenate([keys, lin[:, query_width + key_width :]], axis=1).astype(BF16)
    (kv_all,) = call_gathers(depth, 1, [True], [kv])
    kv_all = kv_all.reshape(total, 2 * key_width)
    all_keys, all_values = kv_all[:, :key_width], kv_all[:, key_width:]

    span = min(512, total)
    low = begin[0] // span
    high = (first_row + rows - 1) // span + 1
    info = jnp.stack([first_row, low, high]).astype(jnp.int32)
    begin_column = begin[:, None]
    mixed, lse = call_forward(span, info, begin_column, queries, all_keys, all_values)
    mixed_low = (
        mixed.reshape(HEADS, rows, HEAD_DIM)
        .transpose(1, 0, 2)
        .reshape(rows, query_width)
        .astype(BF16)
    )
    middle = inputs + dot(mixed_low, w_out)
    inv_two = lax.rsqrt(jnp.mean(middle * middle, axis=-1, keepdims=True) + EPSILON)
    normed_two = middle * inv_two
    hidden_two = (normed_two * gain_two).astype(BF16)

    (hidden_all,) = call_gathers(depth, 2, [False], [hidden_two])
    hidden_all = hidden_all.reshape(seq * rows, model)
    gate = dot(hidden_all, w_gate)
    up = dot(hidden_all, w_up)
    sigma = jax.nn.sigmoid(gate)
    silu = gate * sigma
    activated = (silu * up).astype(BF16)
    d_act = dot_t(cot_all, w_down)
    d_gate = (d_act * up * sigma * (1.0 + gate * (1.0 - sigma))).astype(BF16)
    d_up = (d_act * silu).astype(BF16)
    d_hidden_part = dot_t(d_gate, w_gate) + dot_t(d_up, w_up)
    out_part = dot(activated, w_down)
    shape = (depth, 2, rows, model)
    d_hidden_two, branch = call_reduces(
        depth,
        3,
        [False, False],
        [d_hidden_part.astype(BF16).reshape(shape), out_part.astype(BF16).reshape(shape)],
    )
    layer_out = (middle + branch).astype(BF16)
    gate_part = t_dot(hidden_all, d_gate).astype(BF16)
    up_part = t_dot(hidden_all, d_up).astype(BF16)
    down_part = t_dot(activated, cot_all).astype(BF16)

    gain_two_grad = jnp.sum(d_hidden_two * normed_two, axis=0)
    d_middle = cotangent.astype(F32) + norm_back(d_hidden_two, normed_two, inv_two, gain_two)

    d_branch = d_middle.astype(BF16)
    d_mixed = dot_t(d_branch, w_out).astype(BF16)
    d_mixed = (
        d_mixed.reshape(rows, HEADS, HEAD_DIM)
        .transpose(1, 0, 2)
        .reshape(KV_HEADS, GROUP * rows, HEAD_DIM)
    )
    d_query, d_kv_part = call_backward(
        span, info, begin_column, queries, all_keys, all_values, mixed, lse, d_mixed
    )
    (d_kv,) = call_reduces(
        depth, 4, [True], [d_kv_part.reshape(depth, 2, 2, 2, rows, 2 * key_width)]
    )
    d_query = d_query.reshape(HEADS, rows, HEAD_DIM).transpose(1, 0, 2)
    d_q = rotate(d_query * score_scale, cosine, sine_table, -1.0).reshape(rows, query_width)
    d_k = rotate(
        d_kv[:, :key_width].reshape(rows, KV_HEADS, HEAD_DIM) * score_scale,
        cosine,
        sine_table,
        -1.0,
    ).reshape(rows, key_width)
    d_lin = jnp.concatenate([d_q, d_k, d_kv[:, key_width:]], axis=1).astype(BF16)
    bias_grad = jnp.sum(d_lin.astype(F32), axis=0)
    d_hidden_one = dot_t(d_lin, w_qkv)
    gain_one_grad = jnp.sum(d_hidden_one * normed_one, axis=0)
    input_grad = d_middle + norm_back(d_hidden_one, normed_one, inv_one, gain_one)

    def spread(vector):
        parts = vector.reshape(devices, -1)
        return jnp.pad(parts, ((0, 0), (0, model_rows - parts.shape[1]))).reshape(model, 1)

    small_part = jnp.concatenate(
        [
            spread(gain_one_grad),
            spread(bias_grad[:query_width]),
            spread(bias_grad[query_width : query_width + key_width]),
            spread(bias_grad[query_width + key_width :]),
            spread(gain_two_grad),
            jnp.zeros((model, 123), F32),
        ],
        axis=1,
    )
    pack_part = jnp.concatenate(
        [
            t_dot(hidden_one, d_lin).astype(BF16),
            t_dot(mixed_low, d_branch).astype(BF16),
            small_part.astype(BF16),
        ],
        axis=1,
    ).reshape(depth, 2, 2, 2, model_rows, pack.shape[1])
    wide_part = jnp.stack([gate_part, up_part]).reshape(2, seq, fsdp, model_rows, units)
    down_part = down_part.reshape(fsdp, units // fsdp, model)
    pack_grad, wide_grad, down_grad = call_end(depth, 5, pack_part, wide_part, down_part)
    wide_grad = wide_grad.transpose(1, 2, 0, 3).reshape(2, model_rows, seq * units).astype(F32)
    small_grad = pack_grad[:, qkv_width + query_width :]
    return (
        layer_out,
        input_grad,
        small_grad[:, 0],
        pack_grad[:, :query_width],
        small_grad[:, 1],
        pack_grad[:, query_width : query_width + key_width],
        small_grad[:kv_share, 2],
        pack_grad[:, query_width + key_width : qkv_width],
        small_grad[:kv_share, 3],
        pack_grad[:, qkv_width : qkv_width + query_width],
        small_grad[:, 4],
        wide_grad[0],
        wide_grad[1],
        down_grad,
    )


def solution(mesh):
    matrix, vector = P(AXES, None), P(AXES)
    in_specs = (
        matrix,
        matrix,
        P(),
        vector,
        matrix,
        vector,
        matrix,
        vector,
        matrix,
        vector,
        matrix,
        vector,
        matrix,
        matrix,
        matrix,
    )
    out_specs = (
        matrix,
        matrix,
        vector,
        matrix,
        vector,
        matrix,
        vector,
        matrix,
        vector,
        matrix,
        vector,
        matrix,
        matrix,
        matrix,
    )
    return jax.shard_map(shards, mesh=mesh, in_specs=in_specs, out_specs=out_specs, check_vma=False)
```

```python
import functools

import jax
import jax.numpy as jnp
from jax import lax
from jax.experimental import pallas as pl
from jax.experimental.pallas import tpu as pltpu
from jax.sharding import PartitionSpec as P

HEADS = 12
KV_HEADS = 2
HEAD_DIM = 128
GROUP = HEADS // KV_HEADS
EPSILON = 1e-06
ROPE_BASE = 10000.0
LOG2E = 1.4426950408889634
AXES = ("seq", "fsdp")
VMEM_LIMIT = 56 << 20
VMEM_JOINED = 60 << 20
F32 = jnp.float32
BF16 = jnp.bfloat16
DMA = pltpu.SemaphoreType.DMA


class Place:
    def __init__(self, depth):
        self.depth = depth
        self.s = lax.axis_index("seq")
        self.f = lax.axis_index("fsdp")
        self.z = lax.div(self.s, 2)
        self.x = lax.rem(self.s, 2)
        self.y = lax.div(self.f, 2)
        self.c = lax.rem(self.f, 2)
        self.up = self.z + 1 < depth
        self.down = self.z > 0

    def flip_x(self):
        return (self.s + 1 - 2 * self.x, self.f)

    def flip_y(self):
        return (self.s, self.f + 2 - 4 * self.y)

    def flip_c(self):
        return (self.s, self.f + 1 - 2 * self.c)

    def z_up(self):
        return (self.s + 2, self.f)

    def z_down(self):
        return (self.s - 2, self.f)

    def first(self):
        return (
            self.s + (1 - self.c) * (1 - 2 * self.x),
            self.f + self.c * (2 - 4 * self.y),
        )

    def second(self):
        return (
            self.s + self.c * (1 - 2 * self.x),
            self.f + (1 - self.c) * (2 - 4 * self.y),
        )

    def corner(self, i, j):
        over_x = i * (1 - self.c) + j * self.c
        over_y = j * (1 - self.c) + i * self.c
        return (self.x + over_x * (1 - 2 * self.x), self.y + over_y * (1 - 2 * self.y))

    def wave(self, k):
        if k == 0:
            return [(self.z, None)]
        return [(self.z - k, self.z - k >= 0), (self.z + k, self.z + k < self.depth)]


def guard(condition, body):
    if condition is None:
        body()
    else:
        pl.when(condition)(body)


def greet(place, others=()):
    barrier = pltpu.get_barrier_semaphore()
    partners = [place.flip_x(), place.flip_y(), place.flip_c(), *others]
    for partner in partners:
        pl.semaphore_signal(barrier, inc=1, device_id=partner, device_id_type=pl.DeviceIdType.MESH)

    def tell_up():
        pl.semaphore_signal(
            barrier, inc=1, device_id=place.z_up(), device_id_type=pl.DeviceIdType.MESH
        )

    def tell_down():
        pl.semaphore_signal(
            barrier, inc=1, device_id=place.z_down(), device_id_type=pl.DeviceIdType.MESH
        )

    pl.when(place.up)(tell_up)
    pl.when(place.down)(tell_down)
    pl.semaphore_wait(
        barrier, len(partners) + place.up.astype(jnp.int32) + place.down.astype(jnp.int32)
    )


def remote(src, dst, send_sem, recv_sem, device):
    return pltpu.make_async_remote_copy(
        src_ref=src,
        dst_ref=dst,
        send_sem=send_sem,
        recv_sem=recv_sem,
        device_id=device,
        device_id_type=pl.DeviceIdType.MESH,
    )


def add_into(target, term, rows):
    step = 16 if rows % 16 == 0 else rows

    def body(number, carry):
        at = pl.ds(pl.multiple_of(number * step, step), step)
        target[at, :] = (target[at, :].astype(F32) + term[at, :].astype(F32)).astype(BF16)
        return carry

    lax.fori_loop(0, rows // step, body, 0)


class Gather:
    def __init__(self, place, wide, own, out, sems):
        self.place, self.wide, self.own, self.out, self.sems = place, wide, own, out, sems
        self.sent = []

    @staticmethod
    def semaphores(depth, wide):
        base = [DMA((1,)), DMA((2 * depth,)), DMA((depth,)), DMA((depth,)), DMA((depth,))]
        if wide:
            base += [DMA((2 * depth,)), DMA((2 * depth,)), DMA((4 * depth,)), DMA((4 * depth,))]
        return base

    def at(self, zi, i, j):
        place = self.place
        if self.wide:
            x, y = place.corner(i, j)
            return self.out.at[zi, x, y, place.c]
        return self.out.at[zi, place.x + i * (1 - 2 * place.x)]

    def send(self, src, dst, send_sem, recv_sem, device, condition):
        copy = remote(src, dst, send_sem, recv_sem, device)
        guard(condition, copy.start)
        self.sent.append((copy, condition))

    def local(self):
        copy = pltpu.make_async_copy(
            self.own, self.at(self.place.z, 0, 0), self.sems[0].at[0]
        )
        return copy

    def arrive(self, k):
        place, depth = self.place, self.place.depth
        z_send, z_recv, a_send, a_recv = self.sems[1:5]
        across = place.first() if self.wide else place.flip_x()
        for side, (zi, ok) in enumerate(place.wave(k)):
            block = self.at(zi, 0, 0)
            source = self.own if k == 0 else block
            if k > 0:
                landed = remote(block, block, z_send.at[0], z_recv.at[zi], place.z_up())
                guard(ok, landed.wait_recv)
            both = lambda a, b: a if b is None else jnp.logical_and(a, b)
            if k == 0 or side == 0:
                self.send(
                    source, block, z_send.at[k], z_recv.at[zi], place.z_up(), both(place.up, ok)
                )
            if k == 0 or side == 1:
                self.send(
                    source,
                    block,
                    z_send.at[depth + k],
                    z_recv.at[zi],
                    place.z_down(),
                    both(place.down, ok),
                )
            self.send(source, block, a_send.at[zi], a_recv.at[zi], across, ok)
            if self.wide:
                b_send, b_recv = self.sems[5:7]
                self.send(
                    source, block, b_send.at[2 * zi], b_recv.at[2 * zi], place.second(), ok
                )

    def across(self, k):
        place = self.place
        a_send, a_recv = self.sems[3:5]
        for zi, ok in place.wave(k):
            block = self.at(zi, 1, 0)
            landed = remote(block, block, a_send.at[0], a_recv.at[zi], place.first())
            guard(ok, landed.wait_recv)
            if self.wide:
                b_send, b_recv = self.sems[5:7]
                self.send(
                    block, block, b_send.at[2 * zi + 1], b_recv.at[2 * zi + 1], place.second(), ok
                )

    def hand(self, k):
        place = self.place
        b_send, b_recv, c_send, c_recv = self.sems[5:9]
        for zi, ok in place.wave(k):
            for i in range(2):
                block = self.at(zi, i, 1)
                landed = remote(block, block, b_send.at[0], b_recv.at[2 * zi + i], place.second())
                guard(ok, landed.wait_recv)
            for x in range(2):
                for y in range(2):
                    block = self.out.at[zi, x, y, place.c]
                    slot = 4 * zi + 2 * x + y
                    self.send(
                        block, block, c_send.at[slot], c_recv.at[slot], place.flip_c(), ok
                    )

    def take(self, k):
        place = self.place
        c_send, c_recv = self.sems[7:9]
        for zi, ok in place.wave(k):
            for x in range(2):
                for y in range(2):
                    block = self.out.at[zi, x, y, 1 - place.c]
                    slot = 4 * zi + 2 * x + y
                    landed = remote(block, block, c_send.at[0], c_recv.at[slot], place.flip_c())
                    guard(ok, landed.wait_recv)

    def settle(self):
        for copy, condition in self.sent:
            guard(condition, copy.wait_send)


def drive_gathers(place, gathers):
    depth = place.depth
    locals_ = [gather.local() for gather in gathers]
    for copy in locals_:
        copy.start()
    for step in range(depth + 3):
        for gather in gathers:
            if step < depth:
                gather.arrive(step)
        if step == 0:
            for copy in locals_:
                copy.wait()
        for gather in gathers:
            if 0 <= step - 1 < depth:
                gather.across(step - 1)
        for gather in gathers:
            if gather.wide and 0 <= step - 2 < depth:
                gather.hand(step - 2)
        for gather in gathers:
            if gather.wide and 0 <= step - 3 < depth:
                gather.take(step - 3)
    for gather in gathers:
        gather.settle()


def gather_shape(depth, wide, own):
    lead = (depth, 2, 2, 2) if wide else (depth, 2)
    return jax.ShapeDtypeStruct(lead + own.shape, own.dtype)


def call_gathers(depth, collective_id, wides, owns):
    def kernel(*refs):
        count = len(owns)
        place = Place(depth)
        greet(place)
        gathers, used = [], 2 * count
        for number, wide in enumerate(wides):
            need = len(Gather.semaphores(depth, wide))
            gathers.append(
                Gather(place, wide, refs[number], refs[count + number], refs[used : used + need])
            )
            used += need
        drive_gathers(place, gathers)

    scratch = []
    for wide in wides:
        scratch += Gather.semaphores(depth, wide)
    return pl.pallas_call(
        kernel,
        out_shape=[gather_shape(depth, wide, own) for wide, own in zip(wides, owns)],
        in_specs=[pl.BlockSpec(memory_space=pl.ANY)] * len(owns),
        out_specs=[pl.BlockSpec(memory_space=pl.ANY)] * len(owns),
        scratch_shapes=scratch,
        compiler_params=pltpu.CompilerParams(
            collective_id=collective_id, has_side_effects=True, vmem_limit_bytes=VMEM_LIMIT
        ),
    )(*owns)


def start_kernel(depth, *refs):
    (pack, cot, wide_in, down_in, pack_out, cot_out, wide_out, down_out), sems = refs[:8], refs[8:]
    place = Place(depth)
    count = 2 * depth
    partners = []
    for offset in range(1, count):
        partners.append((lax.rem(place.s + offset, count), place.f))
    greet(place, partners)
    first = len(Gather.semaphores(depth, True))
    second = first + len(Gather.semaphores(depth, False))
    gathers = [
        Gather(place, True, pack, pack_out, sems[:first]),
        Gather(place, False, cot, cot_out, sems[first:second]),
    ]
    local_sem, e_send, e_recv, y_send, y_recv, c_send, c_recv, d_sem, d_send, d_recv = sems[second:]
    sent = []

    def send(src, dst, send_sem, recv_sem, device):
        copy = remote(src, dst, send_sem, recv_sem, device)
        copy.start()
        sent.append(copy)

    locals_ = [gather.local() for gather in gathers]
    locals_.append(
        pltpu.make_async_copy(
            wide_in.at[:, place.s], wide_out.at[:, place.s, place.f], local_sem.at[0]
        )
    )
    locals_.append(pltpu.make_async_copy(down_in, down_out.at[place.f], d_sem.at[0]))
    for copy in locals_:
        copy.start()

    y_f = place.f + 2 - 4 * place.y
    c_f = place.f + 1 - 2 * place.c
    yc_f = y_f + 1 - 2 * place.c

    def exchange(offset):
        to = lax.rem(place.s + offset, count)
        send(
            wide_in.at[:, to],
            wide_out.at[:, place.s, place.f],
            e_send.at[offset],
            e_recv.at[offset],
            (to, place.f),
        )

    def onward(offset):
        origin = lax.rem(place.s + count - offset, count)
        block = wide_out.at[:, origin, place.f]
        if offset > 0:
            remote(block, block, e_send.at[0], e_recv.at[offset], place.flip_y()).wait_recv()
        send(block, block, y_send.at[offset], y_recv.at[offset], place.flip_y())
        send(block, block, c_send.at[2 * offset], c_recv.at[2 * offset], place.flip_c())

    def sideways(offset):
        origin = lax.rem(place.s + count - offset, count)
        block = wide_out.at[:, origin, y_f]
        remote(block, block, y_send.at[0], y_recv.at[offset], place.flip_y()).wait_recv()
        send(block, block, c_send.at[2 * offset + 1], c_recv.at[2 * offset + 1], place.flip_c())

    def last(offset):
        origin = lax.rem(place.s + count - offset, count)
        for slot, owner in ((2 * offset, c_f), (2 * offset + 1, yc_f)):
            block = wide_out.at[:, origin, owner]
            remote(block, block, c_send.at[0], c_recv.at[slot], place.flip_c()).wait_recv()

    for gather in gathers:
        gather.arrive(0)
    send(down_in, down_out.at[place.f], d_send.at[0], d_recv.at[0], place.flip_y())
    send(down_in, down_out.at[place.f], d_send.at[1], d_recv.at[1], place.flip_c())
    for offset in range(1, count):
        exchange(offset)
    for copy in locals_:
        copy.wait()
    onward(0)
    total = depth + 3
    for step in range(1, total):
        for gather in gathers:
            if step < depth:
                gather.arrive(step)
        for gather in gathers:
            if 0 <= step - 1 < depth:
                gather.across(step - 1)
        for gather in gathers:
            if gather.wide and 0 <= step - 2 < depth:
                gather.hand(step - 2)
        for gather in gathers:
            if gather.wide and 0 <= step - 3 < depth:
                gather.take(step - 3)
    block = down_out.at[y_f]
    remote(block, block, d_send.at[0], d_recv.at[0], place.flip_y()).wait_recv()
    send(block, block, d_send.at[2], d_recv.at[2], place.flip_c())
    for offset in range(1, count):
        onward(offset)
        sideways(offset - 1)
    sideways(count - 1)
    for offset in range(count):
        last(offset)
    for slot, owner in ((1, c_f), (2, yc_f)):
        block = down_out.at[owner]
        remote(block, block, d_send.at[0], d_recv.at[slot], place.flip_c()).wait_recv()
    for gather in gathers:
        gather.settle()
    for copy in sent:
        copy.wait_send()


def call_start(depth, collective_id, pack, cot, wide, down):
    count = 2 * depth
    _, _, rows, columns = wide.shape
    scratch = Gather.semaphores(depth, True) + Gather.semaphores(depth, False)
    scratch += [DMA((1,)), DMA((count,)), DMA((count,)), DMA((count,)), DMA((count,))]
    scratch += [DMA((2 * count,)), DMA((2 * count,)), DMA((1,)), DMA((3,)), DMA((3,))]
    return pl.pallas_call(
        functools.partial(start_kernel, depth),
        out_shape=[
            gather_shape(depth, True, pack),
            gather_shape(depth, False, cot),
            jax.ShapeDtypeStruct((2, count, 4, rows, columns), BF16),
            jax.ShapeDtypeStruct((4,) + down.shape, BF16),
        ],
        in_specs=[pl.BlockSpec(memory_space=pl.ANY)] * 4,
        out_specs=[pl.BlockSpec(memory_space=pl.ANY)] * 4,
        scratch_shapes=scratch,
        compiler_params=pltpu.CompilerParams(
            collective_id=collective_id, has_side_effects=True, vmem_limit_bytes=VMEM_LIMIT
        ),
    )(pack, cot, wide, down)


class Reduce:
    def __init__(self, place, wide, rows, own, out, buffers, sems, near=None, causal=False):
        self.place, self.wide, self.rows = place, wide, rows
        self.own, self.out, self.buffers, self.sems = own, out, buffers, sems
        self.near = near
        self.causal = causal
        self.sent = []

    def wave(self, k):
        waves = self.place.wave(k)
        return waves[:1] if self.causal else waves

    def near_block(self, zi):
        return self.own.at[zi, self.place.x] if self.near is None else self.near.at[zi]

    @staticmethod
    def scratch(depth, wide, block):
        buffers = [
            pltpu.VMEM((depth,) + block, BF16),
            pltpu.VMEM((depth + 1,) + block, BF16),
        ]
        sems = [DMA((depth,)), DMA((depth,)), DMA((2 * depth,)), DMA((2 * depth,))]
        if wide:
            buffers += [
                pltpu.VMEM((depth, 2, 2) + block, BF16),
                pltpu.VMEM((depth, 2) + block, BF16),
            ]
            sems += [DMA((4 * depth,)), DMA((4 * depth,)), DMA((2 * depth,)), DMA((2 * depth,))]
        return buffers, sems

    def send(self, src, dst, send_sem, recv_sem, device, condition):
        copy = remote(src, dst, send_sem, recv_sem, device)
        guard(condition, copy.start)
        self.sent.append((copy, condition))

    def cores(self, k):
        place = self.place
        c_send, c_recv = self.sems[4:6]
        got = self.buffers[2]
        for zi, ok in self.wave(k):
            for x in range(2):
                for y in range(2):
                    slot = 4 * zi + 2 * x + y
                    self.send(
                        self.own.at[zi, x, y, 1 - place.c],
                        got.at[zi, x, y],
                        c_send.at[slot],
                        c_recv.at[slot],
                        place.flip_c(),
                        ok,
                    )

    def over_second(self, k):
        place = self.place
        c_send, c_recv, b_send, b_recv = self.sems[4:8]
        got, next_ = self.buffers[2:4]
        for zi, ok in self.wave(k):

            def body(zi=zi):
                for j in (1, 0):
                    for i in (1, 0):
                        x, y = place.corner(i, j)
                        block = got.at[zi, x, y]
                        slot = 4 * zi + 2 * x + y
                        remote(
                            block, block, c_send.at[0], c_recv.at[slot], place.flip_c()
                        ).wait_recv()
                        add_into(block, self.own.at[zi, x, y, place.c], self.rows)
                        if j == 1:
                            remote(
                                block,
                                next_.at[zi, i],
                                b_send.at[2 * zi + i],
                                b_recv.at[2 * zi + i],
                                place.second(),
                            ).start()

            guard(ok, body)
            for i in (1, 0):
                x, y = place.corner(i, 1)
                copy = remote(
                    got.at[zi, x, y],
                    next_.at[zi, i],
                    b_send.at[2 * zi + i],
                    b_recv.at[2 * zi + i],
                    place.second(),
                )
                self.sent.append((copy, ok))

    def over_first(self, k):
        place = self.place
        a_send, a_recv = self.sems[0:2]
        got = self.buffers[0]
        for zi, ok in self.wave(k):
            if self.wide:
                b_send, b_recv = self.sems[6:8]
                before, held = self.buffers[2:4]

                def body(zi=zi):
                    for i in (1, 0):
                        block = held.at[zi, i]
                        x, y = place.corner(i, 0)
                        remote(
                            block, block, b_send.at[0], b_recv.at[2 * zi + i], place.second()
                        ).wait_recv()
                        add_into(block, before.at[zi, x, y], self.rows)
                        if i == 1:
                            remote(
                                block, got.at[zi], a_send.at[zi], a_recv.at[zi], place.first()
                            ).start()

                guard(ok, body)
                copy = remote(
                    held.at[zi, 1], got.at[zi], a_send.at[zi], a_recv.at[zi], place.first()
                )
                self.sent.append((copy, ok))
            else:
                self.send(
                    self.own.at[zi, 1 - place.x],
                    got.at[zi],
                    a_send.at[zi],
                    a_recv.at[zi],
                    place.flip_x(),
                    ok,
                )

    def along(self, k):
        place, depth = self.place, self.place.depth
        a_send, a_recv, z_send, z_recv = self.sems[0:4]
        held, line = self.buffers[0:2]
        for side, (zi, ok) in enumerate(self.wave(k)):
            block = held.at[zi]

            def body(zi=zi, side=side, block=block):
                remote(block, block, a_send.at[0], a_recv.at[zi], place.first()).wait_recv()
                if self.wide:
                    add_into(block, self.buffers[3].at[zi, 0], self.rows)
                else:
                    add_into(block, self.near_block(zi), self.rows)

                def more(direction):
                    slot = direction * depth + zi
                    term = line.at[depth if k == 0 and direction == 1 else zi]
                    remote(term, term, z_send.at[0], z_recv.at[slot], place.z_up()).wait_recv()
                    add_into(block, term, self.rows)

                def pass_on(direction, to):
                    slot = direction * depth + zi
                    there = line.at[depth if k == 1 and direction == 1 else zi]
                    remote(block, there, z_send.at[slot], z_recv.at[slot], to).start()

                if k == 0:
                    if not self.causal:
                        pl.when(place.down)(functools.partial(more, 0))
                    pl.when(place.up)(functools.partial(more, 1))
                elif side == 0:
                    pl.when(place.up)(functools.partial(more, 1))
                    pass_on(1, place.z_down())
                else:
                    pl.when(place.down)(functools.partial(more, 0))
                    pass_on(0, place.z_up())

            guard(ok, body)
            if k > 0:
                direction = 1 - side
                slot = direction * depth + zi
                to = place.z_up() if side == 1 else place.z_down()
                there = line.at[depth if k == 1 and direction == 1 else zi]
                copy = remote(block, there, z_send.at[slot], z_recv.at[slot], to)
                self.sent.append((copy, ok))

    def finish(self):
        self.out[...] = self.buffers[0][self.place.z].astype(self.out.dtype)

    def settle(self):
        for copy, condition in self.sent:
            guard(condition, copy.wait_send)


def drive_reduces(place, reduces):
    depth = place.depth
    order = list(range(depth - 1, -1, -1))
    for reduce in reduces:
        for k in order:
            reduce.cores(k) if reduce.wide else reduce.over_first(k)
    for step in range(depth + 2):
        for reduce in reduces:
            if not reduce.wide:
                if step < depth:
                    reduce.along(order[step])
                continue
            if step < depth:
                reduce.over_second(order[step])
            if 0 <= step - 1 < depth:
                reduce.over_first(order[step - 1])
            if 0 <= step - 2 < depth:
                reduce.along(order[step - 2])
    for reduce in reduces:
        reduce.finish()
    for reduce in reduces:
        reduce.settle()


def call_reduces(depth, collective_id, wides, owns):
    count = len(owns)
    blocks = [own.shape[-2:] for own in owns]
    parts = [Reduce.scratch(depth, wide, block) for wide, block in zip(wides, blocks)]
    scratch = []
    for buffers, sems in parts:
        scratch += buffers + sems

    def kernel(*refs):
        place = Place(depth)
        greet(place)
        reduces, used = [], 2 * count
        for number, (buffers, sems) in enumerate(parts):
            middle, end = used + len(buffers), used + len(buffers) + len(sems)
            reduces.append(
                Reduce(
                    place,
                    wides[number],
                    blocks[number][0],
                    refs[number],
                    refs[count + number],
                    refs[used:middle],
                    refs[middle:end],
                )
            )
            used = end
        drive_reduces(place, reduces)

    return pl.pallas_call(
        kernel,
        out_shape=[jax.ShapeDtypeStruct(block, F32) for block in blocks],
        in_specs=[pl.BlockSpec(memory_space=pltpu.VMEM)] * count,
        out_specs=[pl.BlockSpec(memory_space=pltpu.VMEM)] * count,
        scratch_shapes=scratch,
        compiler_params=pltpu.CompilerParams(
            collective_id=collective_id, has_side_effects=True, vmem_limit_bytes=VMEM_LIMIT
        ),
    )(*owns)


def end_kernel(depth, shapes, *refs):
    pack, wide, down, pack_out, wide_out, down_out = refs[:6]
    block, wide_block, down_block = shapes
    buffers, sems = Reduce.scratch(depth, True, block)
    used = 6 + len(buffers)
    place = Place(depth)
    count = 2 * depth
    partners = []
    for offset in range(1, count):
        partners.append((lax.rem(place.s + offset, count), place.f))
    greet(place, partners)
    reduce = Reduce(
        place, True, block[0], pack, pack_out, refs[6:used], refs[used : used + len(sems)]
    )
    used += len(sems)
    w_core, w_y, d_core, d_y = refs[used : used + 4]
    wc_send, wc_recv, wy_send, wy_recv, e_send, e_recv, e_sem = refs[used + 4 : used + 11]
    dc_send, dc_recv, dy_send, dy_recv = refs[used + 11 :]
    sent = []
    wide_rows, down_rows = wide_block[1], down_block[0]

    def send(src, dst, send_sem, recv_sem, device):
        copy = remote(src, dst, send_sem, recv_sem, device)
        copy.start()
        sent.append(copy)

    def landed(ref, recv_sem):
        remote(ref, ref, e_send.at[0], recv_sem, place.flip_c()).wait_recv()

    mine_y, other_y = place.y, 1 - place.y
    offsets = list(range(1, count)) + [0]
    for y in range(2):
        side = other_y if y == 0 else mine_y
        send(
            down.at[2 * side + 1 - place.c],
            d_core.at[side],
            dc_send.at[side],
            dc_recv.at[side],
            place.flip_c(),
        )
    for offset in offsets:
        to = lax.rem(place.s + offset, count)
        for y in range(2):
            send(
                wide.at[:, to, 2 * y + 1 - place.c],
                w_core.at[y, offset],
                wc_send.at[2 * offset + y],
                wc_recv.at[2 * offset + y],
                place.flip_c(),
            )
    order = list(range(depth - 1, -1, -1))
    for k in order:
        reduce.cores(k)

    def wide_add(target, term):
        for part in range(2):
            add_into(target.at[part], term.at[part], wide_rows)

    def wide_cores(offset):
        to = lax.rem(place.s + offset, count)
        for side in (other_y, mine_y):
            landed(w_core.at[side, offset], wc_recv.at[2 * offset + side])
            wide_add(w_core.at[side, offset], wide.at[:, to, 2 * side + place.c])
            if side is other_y:
                send(
                    w_core.at[side, offset],
                    w_y.at[offset],
                    wy_send.at[offset],
                    wy_recv.at[offset],
                    place.flip_y(),
                )

    def wide_across(offset):
        landed(w_y.at[offset], wy_recv.at[offset])
        wide_add(w_y.at[offset], w_core.at[mine_y, offset])
        to = lax.rem(place.s + offset, count)
        if offset > 0:
            send(
                w_y.at[offset],
                wide_out.at[place.s],
                e_send.at[offset],
                e_recv.at[offset],
                (to, place.f),
            )
        else:
            pltpu.make_async_copy(w_y.at[0], wide_out.at[place.s], e_sem.at[0]).start()

    for offset in offsets[: count // 2]:
        wide_cores(offset)
    for step in range(depth):
        reduce.over_second(order[step])
        if step >= 1:
            reduce.over_first(order[step - 1])
        if step == 0:
            for offset in offsets[count // 2 :]:
                wide_cores(offset)
            for side in (other_y, mine_y):
                landed(d_core.at[side], dc_recv.at[side])
                add_into(d_core.at[side], down.at[2 * side + place.c], down_rows)
                if side is other_y:
                    send(d_core.at[side], d_y.at[0], dy_send.at[0], dy_recv.at[0], place.flip_y())
        for offset in offsets[step * count // depth : (step + 1) * count // depth]:
            wide_across(offset)
        if step >= 2:
            reduce.along(order[step - 2])
    reduce.over_first(order[depth - 1])
    for step in range(max(depth - 2, 0), depth):
        reduce.along(order[step])
    reduce.finish()
    landed(d_y.at[0], dy_recv.at[0])
    down_out[...] = d_y[0].astype(F32) + d_core[mine_y].astype(F32)
    for offset in range(1, count):
        origin = lax.rem(place.s + count - offset, count)
        landed(wide_out.at[origin], e_recv.at[offset])
    pltpu.make_async_copy(w_y.at[0], wide_out.at[place.s], e_sem.at[0]).wait()
    reduce.settle()
    for copy in sent:
        copy.wait_send()


def call_end(depth, collective_id, pack, wide, down):
    count = 2 * depth
    block = pack.shape[-2:]
    wide_block = (2,) + wide.shape[-2:]
    down_block = down.shape[-2:]
    buffers, sems = Reduce.scratch(depth, True, block)
    scratch = buffers + sems
    scratch += [
        pltpu.VMEM((2, count) + wide_block, BF16),
        pltpu.VMEM((count,) + wide_block, BF16),
        pltpu.VMEM((2,) + down_block, BF16),
        pltpu.VMEM((1,) + down_block, BF16),
    ]
    scratch += [DMA((2 * count,)), DMA((2 * count,)), DMA((count,)), DMA((count,))]
    scratch += [DMA((count,)), DMA((count,)), DMA((1,))]
    scratch += [DMA((2,)), DMA((2,)), DMA((1,)), DMA((1,))]
    vmem = pl.BlockSpec(memory_space=pltpu.VMEM)
    return pl.pallas_call(
        functools.partial(end_kernel, depth, (block, wide_block, down_block)),
        out_shape=[
            jax.ShapeDtypeStruct(block, F32),
            jax.ShapeDtypeStruct((count,) + wide_block, BF16),
            jax.ShapeDtypeStruct(down_block, F32),
        ],
        in_specs=[vmem] * 3,
        out_specs=[vmem, vmem, vmem],
        scratch_shapes=scratch,
        compiler_params=pltpu.CompilerParams(
            collective_id=collective_id, has_side_effects=True, vmem_limit_bytes=VMEM_LIMIT
        ),
    )(pack, wide, down)


def forward_kernel(span, info, begin, query, key, value, mixed, lse, m_acc, l_acc, o_acc):
    rows = begin.shape[0]
    first_row, low, high = info[0], info[1], info[2]
    scale = HEAD_DIM ** (-0.5) * LOG2E
    m_acc[...] = jnp.full_like(m_acc, -1e30)
    l_acc[...] = jnp.zeros_like(l_acc)
    o_acc[...] = jnp.zeros_like(o_acc)
    places = first_row + lax.broadcasted_iota(jnp.int32, (rows, span), 0)
    offsets = lax.broadcasted_iota(jnp.int32, (rows, span), 1)

    def step(number, carry):
        base = pl.multiple_of(number * span, span)
        keys_at = base + offsets
        visible = jnp.logical_and(keys_at >= begin[...], keys_at <= places)
        for g in range(KV_HEADS):
            lanes = slice(g * HEAD_DIM, (g + 1) * HEAD_DIM)
            scores = lax.dot_general(
                query[g],
                key[pl.ds(base, span), lanes],
                (((1,), (1,)), ((), ())),
                preferred_element_type=F32,
            )
            scores = scores.reshape(GROUP, rows, span) * scale
            scores = jnp.where(visible[None], scores, -1e30).reshape(GROUP * rows, span)
            old = m_acc[g]
            new = jnp.maximum(old, jnp.max(scores, axis=-1, keepdims=True))
            weights = jnp.exp2(scores - new[:, :1])
            weights = jnp.where(
                visible[None], weights.reshape(GROUP, rows, span), 0.0
            ).reshape(GROUP * rows, span)
            fade = jnp.exp2(old - new)
            l_acc[g] = l_acc[g] * fade + jnp.sum(weights, axis=-1, keepdims=True)
            o_acc[g] = o_acc[g] * fade + jnp.dot(
                weights.astype(BF16),
                value[pl.ds(base, span), lanes],
                preferred_element_type=F32,
            )
            m_acc[g] = new
        return carry

    lax.fori_loop(low, high, step, 0)
    for g in range(KV_HEADS):
        mixed[g] = o_acc[g] / l_acc[g]
        lse[g] = m_acc[g] + jnp.log2(l_acc[g])


def call_forward(span, info, begin, query, key, value):
    stacked = query.shape[1]
    vmem = pl.BlockSpec(memory_space=pltpu.VMEM)
    return pl.pallas_call(
        functools.partial(forward_kernel, span),
        out_shape=[
            jax.ShapeDtypeStruct((KV_HEADS, stacked, HEAD_DIM), F32),
            jax.ShapeDtypeStruct((KV_HEADS, stacked, HEAD_DIM), F32),
        ],
        in_specs=[pl.BlockSpec(memory_space=pltpu.SMEM)] + [vmem] * 4,
        out_specs=[vmem, vmem],
        scratch_shapes=[pltpu.VMEM((KV_HEADS, stacked, HEAD_DIM), F32)] * 3,
        compiler_params=pltpu.CompilerParams(vmem_limit_bytes=VMEM_LIMIT),
    )(info, begin, query, key, value)


def backward_kernel(
    span, info, begin, query, key, value, mixed, lse, grad, dquery, dkeys, delta
):
    rows = begin.shape[0]
    first_row, low, high = info[0], info[1], info[2]
    scale = HEAD_DIM ** (-0.5) * LOG2E
    dquery[...] = jnp.zeros_like(dquery)
    width = KV_HEADS * HEAD_DIM
    for g in range(KV_HEADS):
        delta[g] = jnp.broadcast_to(
            jnp.sum(grad[g].astype(F32) * mixed[g], axis=-1, keepdims=True), delta.shape[1:]
        )
    places = first_row + lax.broadcasted_iota(jnp.int32, (rows, span), 0)
    offsets = lax.broadcasted_iota(jnp.int32, (rows, span), 1)

    def clear(number, carry):
        base = pl.multiple_of(number * span, span)
        dkeys[pl.ds(base, span), :] = jnp.zeros((span, dkeys.shape[1]), BF16)
        return carry

    lax.fori_loop(0, low, clear, 0)
    lax.fori_loop(high, dkeys.shape[0] // span, clear, 0)

    def step(number, carry):
        base = pl.multiple_of(number * span, span)
        keys_at = base + offsets
        visible = jnp.logical_and(keys_at >= begin[...], keys_at <= places)
        for g in range(KV_HEADS):
            lanes = slice(g * HEAD_DIM, (g + 1) * HEAD_DIM)
            key_rows = key[pl.ds(base, span), lanes]
            value_rows = value[pl.ds(base, span), lanes]
            scores = lax.dot_general(
                query[g], key_rows, (((1,), (1,)), ((), ())), preferred_element_type=F32
            )
            dprobs = lax.dot_general(
                grad[g], value_rows, (((1,), (1,)), ((), ())), preferred_element_type=F32
            )
            probs = jnp.exp2(scores * scale - lse[g][:, :1])
            probs = jnp.where(
                visible[None], probs.reshape(GROUP, rows, span), 0.0
            ).reshape(GROUP * rows, span)
            dscores = (probs * (dprobs - delta[g][:, :1])).astype(BF16)
            dquery[g] += jnp.dot(dscores, key_rows, preferred_element_type=F32)
            dkeys[pl.ds(base, span), lanes] = lax.dot_general(
                dscores, query[g], (((0,), (0,)), ((), ())), preferred_element_type=F32
            ).astype(BF16)
            dkeys[
                pl.ds(base, span), width + g * HEAD_DIM : width + (g + 1) * HEAD_DIM
            ] = lax.dot_general(
                probs.astype(BF16),
                grad[g],
                (((0,), (0,)), ((), ())),
                preferred_element_type=F32,
            ).astype(BF16)
        return carry

    lax.fori_loop(low, high, step, 0)


def call_backward(span, info, begin, query, key, value, mixed, lse, grad):
    stacked = query.shape[1]
    vmem = pl.BlockSpec(memory_space=pltpu.VMEM)
    return pl.pallas_call(
        functools.partial(backward_kernel, span),
        out_shape=[
            jax.ShapeDtypeStruct((KV_HEADS, stacked, HEAD_DIM), F32),
            jax.ShapeDtypeStruct((key.shape[0], 2 * key.shape[1]), BF16),
        ],
        in_specs=[pl.BlockSpec(memory_space=pltpu.SMEM)] + [vmem] * 7,
        out_specs=[vmem, vmem],
        scratch_shapes=[pltpu.VMEM((KV_HEADS, stacked, HEAD_DIM), F32)],
        compiler_params=pltpu.CompilerParams(vmem_limit_bytes=VMEM_LIMIT),
    )(info, begin, query, key, value, mixed, lse, grad)


class Exchange:
    def __init__(self, place, own, out, sems):
        self.place, self.own, self.out, self.sems = place, own, out, sems
        self.count = 2 * place.depth
        self.sent = []
        self.y_f = place.f + 2 - 4 * place.y
        self.c_f = place.f + 1 - 2 * place.c
        self.yc_f = self.y_f + 1 - 2 * place.c

    @staticmethod
    def semaphores(depth):
        count = 2 * depth
        return [
            DMA((1,)),
            DMA((count,)),
            DMA((count,)),
            DMA((count,)),
            DMA((count,)),
            DMA((2 * count,)),
            DMA((2 * count,)),
        ]

    def send(self, block, send_sem, recv_sem, device, source=None):
        copy = remote(block if source is None else source, block, send_sem, recv_sem, device)
        copy.start()
        self.sent.append(copy)

    def block(self, offset, owner):
        origin = lax.rem(self.place.s + self.count - offset, self.count)
        return self.out.at[:, origin, owner]

    def landed(self, block, recv_sem):
        remote(block, block, self.sems[1].at[0], recv_sem, self.place.flip_c()).wait_recv()

    def local(self):
        return pltpu.make_async_copy(
            self.own.at[:, self.place.s], self.block(0, self.place.f), self.sems[0].at[0]
        )

    def depart(self, offset):
        place = self.place
        to = lax.rem(place.s + offset, self.count)
        self.send(
            self.block(0, place.f),
            self.sems[1].at[offset],
            self.sems[2].at[offset],
            (to, place.f),
            self.own.at[:, to],
        )

    def onward(self, offset):
        place = self.place
        block = self.block(offset, place.f)
        if offset > 0:
            self.landed(block, self.sems[2].at[offset])
        self.send(block, self.sems[3].at[offset], self.sems[4].at[offset], place.flip_y())
        slot = 2 * offset
        self.send(block, self.sems[5].at[slot], self.sems[6].at[slot], place.flip_c())

    def sideways(self, offset):
        block = self.block(offset, self.y_f)
        self.landed(block, self.sems[4].at[offset])
        slot = 2 * offset + 1
        self.send(block, self.sems[5].at[slot], self.sems[6].at[slot], self.place.flip_c())

    def last(self, offset):
        self.landed(self.block(offset, self.c_f), self.sems[6].at[2 * offset])
        self.landed(self.block(offset, self.yc_f), self.sems[6].at[2 * offset + 1])

    def settle(self):
        for copy in self.sent:
            copy.wait_send()


class Quarter:
    def __init__(self, place, own, out, sems):
        self.place, self.own, self.out, self.sems = place, own, out, sems
        self.sent = []

    @staticmethod
    def semaphores():
        return [DMA((1,)), DMA((3,)), DMA((3,))]

    def local(self):
        return pltpu.make_async_copy(self.own, self.out.at[self.place.f], self.sems[0].at[0])

    def send(self, source, block, slot, device):
        copy = remote(source, block, self.sems[1].at[slot], self.sems[2].at[slot], device)
        copy.start()
        self.sent.append(copy)

    def depart(self):
        place = self.place
        self.send(self.own, self.out.at[place.f], 0, place.flip_y())
        self.send(self.own, self.out.at[place.f], 1, place.flip_c())

    def landed(self, owner, slot):
        block = self.out.at[owner]
        remote(block, block, self.sems[1].at[0], self.sems[2].at[slot], self.place.flip_c()).wait_recv()

    def sideways(self):
        place = self.place
        y_f = place.f + 2 - 4 * place.y
        self.landed(y_f, 0)
        self.send(self.out.at[y_f], self.out.at[y_f], 2, place.flip_c())

    def last(self):
        place = self.place
        self.landed(place.f + 1 - 2 * place.c, 1)
        self.landed(place.f + 2 - 4 * place.y + 1 - 2 * place.c, 2)

    def settle(self):
        for copy in self.sent:
            copy.wait_send()


def stage(gather, step):
    depth = gather.place.depth
    if step < depth:
        gather.arrive(step)
    if 0 <= step - 1 < depth:
        gather.across(step - 1)
    if gather.wide and 0 <= step - 2 < depth:
        gather.hand(step - 2)
    if gather.wide and 0 <= step - 3 < depth:
        gather.take(step - 3)


def turned(vector, cosine, sine):
    return vector * cosine + pltpu.roll(vector, HEAD_DIM // 2, 1) * sine


HEAD_INS = 9
HEAD_OUTS = 13


def head_kernel(depth, *refs):
    (pack, o_own, cot, wide, down, tokens, cosine, sine, begin) = refs[:HEAD_INS]
    (
        pack_out,
        o_out,
        kv_out,
        cot_out,
        wide_out,
        down_out,
        hidden_out,
        queries,
        mixed,
        lse,
        middle,
        hidden_one,
        mixed_low,
    ) = refs[HEAD_INS : HEAD_INS + HEAD_OUTS]
    vectors = refs[HEAD_INS + HEAD_OUTS]
    rest = refs[HEAD_INS + HEAD_OUTS + 1 :]
    pack_all, o_all, kv_all, kv_own, hidden_two, lin, m_acc, l_acc, o_acc = rest[:9]
    sems = list(rest[9:])

    def take(count):
        taken = sems[:count]
        del sems[:count]
        return taken

    wide_need = len(Gather.semaphores(depth, True))
    line_need = len(Gather.semaphores(depth, False))
    count = 2 * depth
    devices = 4 * count
    rows, model = tokens.shape
    query_width, key_width = HEADS * HEAD_DIM, KV_HEADS * HEAD_DIM
    qkv_width = query_width + 2 * key_width

    place = Place(depth)
    greet(place, [(lax.rem(place.s + offset, count), place.f) for offset in range(1, count)])
    g_pack = Gather(place, True, pack, pack_all, take(wide_need))
    g_o = Gather(place, True, o_own, o_all, take(wide_need))
    g_kv = Gather(place, True, kv_own, kv_all, take(wide_need))
    g_cot = Gather(place, False, cot, cot_out, take(line_need))
    g_hidden = Gather(place, False, hidden_two, hidden_out, take(line_need))
    x_wide = Exchange(place, wide, wide_out, take(len(Exchange.semaphores(depth))))
    x_down = Quarter(place, down, down_out, take(len(Quarter.semaphores())))
    (out_sem,) = take(1)

    g_pack.arrive(0)
    locals_ = [job.local() for job in (g_pack, g_o, g_cot, x_wide, x_down)]
    for copy in locals_:
        copy.start()
    inputs = tokens[...].astype(F32)
    inv_one = lax.rsqrt(jnp.mean(inputs * inputs, axis=-1, keepdims=True) + EPSILON)
    share = key_width // devices
    chosen = lax.broadcasted_iota(jnp.int32, (model, key_width), 1)
    chosen = lax.div(chosen, share) * (model // devices) + lax.rem(chosen, share)
    chosen = (lax.broadcasted_iota(jnp.int32, (model, key_width), 0) == chosen).astype(BF16)
    for copy in locals_:
        copy.wait()
    for step in range(1, depth):
        stage(g_pack, step)
    for offset in range(1, count):
        x_wide.depart(offset)
    for step in range(depth, depth + 3):
        stage(g_pack, step)
        if step == depth:
            x_down.depart()

    small = pack_all[:, :, :, :, :, qkv_width:].reshape(model, 128).astype(F32).T
    vectors[...] = small[:8]
    spread = jnp.dot(small[:8].astype(BF16), chosen, preferred_element_type=F32)
    hidden_one[...] = (inputs * inv_one * small[0:1]).astype(BF16)
    part = model // depth
    for zi in range(depth):
        weights = pack_all[zi][:, :, :, :, :qkv_width].reshape(part, qkv_width)
        term = jnp.dot(
            hidden_one[:, zi * part : (zi + 1) * part], weights, preferred_element_type=F32
        )
        if zi == 0:
            lin[...] = term
        else:
            lin[...] += term
    for g in range(KV_HEADS):
        lanes = slice(query_width + g * HEAD_DIM, query_width + (g + 1) * HEAD_DIM)
        own = slice(g * HEAD_DIM, (g + 1) * HEAD_DIM)
        head = lin[:, lanes] + spread[2:3, own]
        kv_own[:, own] = turned(head, cosine[...], sine[...]).astype(BF16)
    values = lin[:, query_width + key_width :] + spread[3:4]
    kv_own[:, key_width:] = values.astype(BF16)
    kv_local = g_kv.local()
    kv_local.start()
    g_kv.arrive(0)
    g_o.arrive(0)
    for h in range(HEADS):
        lanes = slice(h * HEAD_DIM, (h + 1) * HEAD_DIM)
        at = (h % GROUP) * rows
        head = lin[:, lanes] + small[1:2, lanes]
        queries[h // GROUP, at : at + rows, :] = turned(head, cosine[...], sine[...]).astype(BF16)
    kv_local.wait()
    for step in range(1, depth + 3):
        stage(g_kv, step)
        if step >= 2:
            x_wide.onward(step - 2)
    done_onward = depth + 1
    for step in range(1, depth):
        stage(g_o, step)
    g_cot.arrive(0)

    span = 4 * rows
    scale = HEAD_DIM ** (-0.5) * LOG2E
    m_acc[...] = jnp.full_like(m_acc, -1e30)
    l_acc[...] = jnp.zeros_like(l_acc)
    o_acc[...] = jnp.zeros_like(o_acc)
    first_row = (place.s * 4 + place.f) * rows
    places = first_row + lax.broadcasted_iota(jnp.int32, (rows, span), 0)
    offsets = lax.broadcasted_iota(jnp.int32, (rows, span), 1)

    def attend(number, carry):
        keys_at = number * span + offsets
        visible = jnp.logical_and(keys_at >= begin[...], keys_at <= places)
        block = kv_all.at[lax.div(number, 2), lax.rem(number, 2)]
        for g in range(KV_HEADS):
            key = block[:, :, :, g * HEAD_DIM : (g + 1) * HEAD_DIM].reshape(span, HEAD_DIM)
            value = block[
                :, :, :, key_width + g * HEAD_DIM : key_width + (g + 1) * HEAD_DIM
            ].reshape(span, HEAD_DIM)
            scores = lax.dot_general(
                queries[g], key, (((1,), (1,)), ((), ())), preferred_element_type=F32
            )
            scores = scores.reshape(GROUP, rows, span) * scale
            scores = jnp.where(visible[None], scores, -1e30).reshape(GROUP * rows, span)
            old = m_acc[g]
            new = jnp.maximum(old, jnp.max(scores, axis=-1, keepdims=True))
            weights = jnp.exp2(scores - new[:, :1])
            weights = jnp.where(
                visible[None], weights.reshape(GROUP, rows, span), 0.0
            ).reshape(GROUP * rows, span)
            fade = jnp.exp2(old - new)
            l_acc[g] = l_acc[g] * fade + jnp.sum(weights, axis=-1, keepdims=True)
            o_acc[g] = o_acc[g] * fade + jnp.dot(
                weights.astype(BF16), value, preferred_element_type=F32
            )
            m_acc[g] = new
        return carry

    pieces = 4
    for piece in range(pieces):
        low, high = piece * count // pieces, (piece + 1) * count // pieces
        lax.fori_loop(
            jnp.minimum(low, place.s + 1), jnp.minimum(high, place.s + 1), attend, 0
        )
        if depth + piece < depth + 3:
            stage(g_o, depth + piece)
        if piece > 0:
            stage(g_cot, piece)
        if done_onward < count:
            x_wide.onward(done_onward)
            done_onward += 1
    for g in range(KV_HEADS):
        total = o_acc[g] / l_acc[g]
        mixed[g] = total
        lse[g] = m_acc[g] + jnp.log2(l_acc[g])
        for j in range(GROUP):
            lanes = slice((g * GROUP + j) * HEAD_DIM, (g * GROUP + j + 1) * HEAD_DIM)
            mixed_low[:, lanes] = total[j * rows : (j + 1) * rows].astype(BF16)
    after = inputs
    for zi in range(depth):
        after = after + jnp.dot(
            mixed_low[:, zi * part : (zi + 1) * part],
            o_all[zi].reshape(part, model),
            preferred_element_type=F32,
        )
    middle[...] = after
    inv_two = lax.rsqrt(jnp.mean(after * after, axis=-1, keepdims=True) + EPSILON)
    hidden_two[...] = (after * inv_two * small[4:5]).astype(BF16)
    hidden_local = g_hidden.local()
    hidden_local.start()
    g_hidden.arrive(0)

    keeps = []
    for number, (source, target) in enumerate(
        ((pack_all, pack_out), (o_all, o_out), (kv_all, kv_out))
    ):
        copy = pltpu.make_async_copy(source, target, out_sem.at[number])
        copy.start()
        keeps.append(copy)
    while done_onward < count:
        x_wide.onward(done_onward)
        done_onward += 1
    hidden_local.wait()
    sideways = 0
    for step in range(1, depth + 1):
        stage(g_hidden, step)
        if step == 1:
            for later in range(pieces, depth + 1):
                stage(g_cot, later)
            x_down.sideways()
        while sideways < step * count // depth:
            x_wide.sideways(sideways)
            sideways += 1
    for offset in range(count):
        x_wide.last(offset)
    x_down.last()
    for copy in keeps:
        copy.wait()
    for job in (g_pack, g_o, g_kv, g_cot, g_hidden, x_wide, x_down):
        job.settle()


def call_head(depth, collective_id, pack, o_own, cot, wide, down, tokens, cosine, sine, begin):
    count = 2 * depth
    rows, model = tokens.shape
    key_width = KV_HEADS * HEAD_DIM
    stacked = GROUP * rows
    kv_own = jax.ShapeDtypeStruct((rows, 2 * key_width), BF16)
    any_, vmem = pl.BlockSpec(memory_space=pl.ANY), pl.BlockSpec(memory_space=pltpu.VMEM)
    heads = (KV_HEADS, stacked, HEAD_DIM)
    outs = [
        gather_shape(depth, True, pack),
        gather_shape(depth, True, o_own),
        gather_shape(depth, True, kv_own),
        gather_shape(depth, False, cot),
        jax.ShapeDtypeStruct((2, count, 4) + wide.shape[2:], BF16),
        jax.ShapeDtypeStruct((4,) + down.shape, BF16),
        gather_shape(depth, False, tokens),
        jax.ShapeDtypeStruct(heads, BF16),
        jax.ShapeDtypeStruct(heads, F32),
        jax.ShapeDtypeStruct(heads, F32),
        jax.ShapeDtypeStruct((rows, model), F32),
        jax.ShapeDtypeStruct((rows, model), BF16),
        jax.ShapeDtypeStruct((rows, model), BF16),
        jax.ShapeDtypeStruct((8, model), F32),
    ]
    scratch = [pltpu.VMEM(out.shape, BF16) for out in outs[:3]]
    scratch += [
        pltpu.VMEM(kv_own.shape, BF16),
        pltpu.VMEM((rows, model), BF16),
        pltpu.VMEM((rows, (HEADS + 2 * KV_HEADS) * HEAD_DIM), F32),
        pltpu.VMEM(heads, F32),
        pltpu.VMEM(heads, F32),
        pltpu.VMEM(heads, F32),
    ]
    scratch += Gather.semaphores(depth, True) * 3 + Gather.semaphores(depth, False) * 2
    scratch += Exchange.semaphores(depth) + Quarter.semaphores() + [DMA((3,))]
    return pl.pallas_call(
        functools.partial(head_kernel, depth),
        out_shape=outs,
        in_specs=[any_] * 5 + [vmem] * 4,
        out_specs=[any_] * 7 + [vmem] * 7,
        scratch_shapes=scratch,
        compiler_params=pltpu.CompilerParams(
            collective_id=collective_id, has_side_effects=True, vmem_limit_bytes=VMEM_LIMIT
        ),
    )(pack, o_own, cot, wide, down, tokens, cosine, sine, begin)


def t_mul(left, right):
    return lax.dot_general(left, right, (((0,), (0,)), ((), ())), preferred_element_type=F32)


def mul_t(left, right):
    return lax.dot_general(left, right, (((1,), (1,)), ((), ())), preferred_element_type=F32)


def middle_kernel(depth, *refs):
    (dh_part, out_part, hidden_all, cot_all, act, d_gate, d_up, o_own) = refs[:8]
    (middle, cotangent, vectors) = refs[8:11]
    (layer_out, d_middle, d_mixed, d_branch, gain_two, down_out, wide_out) = refs[11:18]
    (dh_near, out_near, dh_sum, out_sum, wide_tokens, left_tokens, right_tokens) = refs[18:25]
    (w_part, w_core, w_y, d_part, d_core, d_y, o_all) = refs[25:32]
    rest = list(refs[32:])

    def take(count):
        taken = rest[:count]
        del rest[:count]
        return taken

    count = 2 * depth
    rows, model = middle.shape
    units = act.shape[1]
    part = model // depth
    block = (rows, model)
    buffers, sems = Reduce.scratch(depth, False, block)
    place = Place(depth)
    greet(place)
    r_dh = Reduce(
        place, False, rows, dh_part, dh_sum, take(len(buffers)), take(len(sems)), dh_near
    )
    r_out = Reduce(
        place, False, rows, out_part, out_sum, take(len(buffers)), take(len(sems)), out_near
    )
    load_sem, wc_send, wc_recv, wy_send, wy_recv, dc_send, dc_recv, dy_send, dy_recv = take(9)
    sent = []

    def send(src, dst, send_sem, recv_sem, device):
        copy = remote(src, dst, send_sem, recv_sem, device)
        copy.start()
        sent.append(copy)

    def landed(ref, recv_sem):
        remote(ref, ref, wc_send.at[0], recv_sem, place.flip_c()).wait_recv()

    order = list(range(depth - 1, -1, -1))
    for k in order:
        r_dh.over_first(k)
    loads = [
        pltpu.make_async_copy(source, target, load_sem.at[number])
        for number, (source, target) in enumerate(
            (
                (hidden_all, wide_tokens),
                (d_gate, left_tokens),
                (d_up, right_tokens),
                (dh_part.at[:, place.x], dh_near),
                (out_part.at[:, place.x], out_near),
                (o_own, o_all),
            )
        )
    ]
    for copy in loads:
        copy.start()
    for k in order:
        r_out.over_first(k)
    mine_y, other_y = place.y, 1 - place.y
    wide_rows = w_part.shape[-2]

    def wide_chunk(k):
        lanes = slice(k * part, (k + 1) * part)
        tokens = wide_tokens[:, :, :, lanes].reshape(count * rows, part)
        for side, grad in enumerate((left_tokens, right_tokens)):
            term = t_mul(tokens, grad[...]).astype(BF16)
            w_part[side, 2 * k : 2 * k + 2] = term.reshape(2, 2, 2, wide_rows, units)
        for to in (2 * k, 2 * k + 1):
            for y in range(2):
                send(
                    w_part.at[:, to, y, 1 - place.c],
                    w_core.at[y, to],
                    wc_send.at[2 * to + y],
                    wc_recv.at[2 * to + y],
                    place.flip_c(),
                )

    def wide_cores(to):
        for y in (other_y, mine_y):
            landed(w_core.at[y, to], wc_recv.at[2 * to + y])
            for side in range(2):
                add_into(
                    w_core.at[y, to, side], w_part.at[side, to, y, place.c], wide_rows
                )
            if y is other_y:
                send(w_core.at[y, to], w_y.at[to], wy_send.at[to], wy_recv.at[to], place.flip_y())

    def wide_across(to):
        landed(w_y.at[to], wy_recv.at[to])
        for side in range(2):
            wide_out[to, side] = (
                w_y[to, side].astype(F32) + w_core[mine_y, to, side].astype(F32)
            ).astype(BF16)

    for copy in loads[:3]:
        copy.wait()
    for k in range(depth):
        wide_chunk(k)
        if k == 1:
            for copy in loads[3:5]:
                copy.wait()
        if k >= 1:
            for to in (2 * k - 2, 2 * k - 1):
                wide_cores(to)
            r_dh.along(order[k - 1])
    second = [
        pltpu.make_async_copy(cot_all, wide_tokens, load_sem.at[0]),
        pltpu.make_async_copy(act, left_tokens, load_sem.at[1]),
    ]
    for copy in second:
        copy.start()
    for to in (count - 2, count - 1):
        wide_cores(to)
    loads[5].wait()
    for copy in second:
        copy.wait()
    down_rows = d_part.shape[1]
    for k in range(depth):
        lanes = slice(k * part, (k + 1) * part)
        tokens = wide_tokens[:, :, :, lanes].reshape(count * rows, part)
        term = t_mul(left_tokens[...], tokens)
        for owner in range(4):
            d_part[owner, :, lanes] = term[
                owner * down_rows : (owner + 1) * down_rows
            ].astype(BF16)
    for y in (other_y, mine_y):
        send(
            d_part.at[2 * y + 1 - place.c],
            d_core.at[y],
            dc_send.at[y],
            dc_recv.at[y],
            place.flip_c(),
        )
    r_dh.along(order[depth - 1])
    r_dh.finish()
    for y in (other_y, mine_y):
        landed(d_core.at[y], dc_recv.at[y])
        add_into(d_core.at[y], d_part.at[2 * y + place.c], down_rows)
        if y is other_y:
            send(d_core.at[y], d_y.at[0], dy_send.at[0], dy_recv.at[0], place.flip_y())

    after = middle[...]
    inv_two = lax.rsqrt(jnp.mean(after * after, axis=-1, keepdims=True) + EPSILON)
    normed = after * inv_two
    d_hidden = dh_sum[...]
    gain_two[...] = jnp.broadcast_to(
        jnp.sum(d_hidden * normed, axis=0, keepdims=True), gain_two.shape
    )
    scaled = d_hidden * vectors[4:5]
    total = cotangent[...].astype(F32) + inv_two * (
        scaled - normed * jnp.mean(scaled * normed, axis=-1, keepdims=True)
    )
    d_middle[...] = total
    d_branch[...] = total.astype(BF16)
    for zi in range(depth):
        term = mul_t(d_branch[...], o_all[zi].reshape(part, model)).astype(BF16)
        for piece in range(part // HEAD_DIM):
            h = zi * (part // HEAD_DIM) + piece
            at = (h % GROUP) * rows
            d_mixed[h // GROUP, at : at + rows, :] = term[
                :, piece * HEAD_DIM : (piece + 1) * HEAD_DIM
            ]
    for step in range(depth):
        r_out.along(order[step])
        for to in range(step * count // depth, (step + 1) * count // depth):
            wide_across(to)
    r_out.finish()
    layer_out[...] = (middle[...] + out_sum[...]).astype(BF16)
    landed(d_y.at[0], dy_recv.at[0])
    down_out[...] = d_y[0].astype(F32) + d_core[mine_y].astype(F32)
    r_dh.settle()
    r_out.settle()
    for copy in sent:
        copy.wait_send()


def call_middle(
    depth, collective_id, dh, out, hidden, cot, act, d_gate, d_up, o_all, middle, cotangent, vectors
):
    count = 2 * depth
    rows, model = middle.shape
    units = act.shape[1]
    wide_rows, down_rows = model // (4 * count), units // 4
    any_, vmem = pl.BlockSpec(memory_space=pl.ANY), pl.BlockSpec(memory_space=pltpu.VMEM)
    buffers, sems = Reduce.scratch(depth, False, (rows, model))
    scratch = [pltpu.VMEM((depth, rows, model), BF16)] * 2
    scratch += [pltpu.VMEM((rows, model), F32)] * 2
    scratch += [
        pltpu.VMEM((depth, 2, rows, model), BF16),
        pltpu.VMEM((count * rows, units), BF16),
        pltpu.VMEM((count * rows, units), BF16),
        pltpu.VMEM((2, count, 2, 2, wide_rows, units), BF16),
        pltpu.VMEM((2, count, 2, wide_rows, units), BF16),
        pltpu.VMEM((count, 2, wide_rows, units), BF16),
        pltpu.VMEM((4, down_rows, model), BF16),
        pltpu.VMEM((2, down_rows, model), BF16),
        pltpu.VMEM((1, down_rows, model), BF16),
        pltpu.VMEM(o_all.shape, BF16),
    ]
    scratch += buffers + sems + buffers + sems
    scratch += [DMA((6,)), DMA((2 * count,)), DMA((2 * count,)), DMA((count,)), DMA((count,))]
    scratch += [DMA((2,)), DMA((2,)), DMA((1,)), DMA((1,))]
    return pl.pallas_call(
        functools.partial(middle_kernel, depth),
        out_shape=[
            jax.ShapeDtypeStruct((rows, model), BF16),
            jax.ShapeDtypeStruct((rows, model), F32),
            jax.ShapeDtypeStruct((KV_HEADS, GROUP * rows, HEAD_DIM), BF16),
            jax.ShapeDtypeStruct((rows, model), BF16),
            jax.ShapeDtypeStruct((8, model), F32),
            jax.ShapeDtypeStruct((down_rows, model), F32),
            jax.ShapeDtypeStruct((count, 2, wide_rows, units), BF16),
        ],
        in_specs=[any_] * 8 + [vmem] * 3,
        out_specs=[vmem] * 7,
        scratch_shapes=scratch,
        compiler_params=pltpu.CompilerParams(
            collective_id=collective_id, has_side_effects=True, vmem_limit_bytes=VMEM_JOINED
        ),
    )(dh, out, hidden, cot, act, d_gate, d_up, o_all, middle, cotangent, vectors)


def last_kernel(depth, *refs):
    (kv_own, pack_own, wide) = refs[:3]
    (queries, mixed, lse, d_mixed, cosine, sine, begin) = refs[3:10]
    (tokens, d_middle, vectors, gain_two, hidden_one, mixed_low, d_branch) = refs[10:17]
    (input_grad, q_out, kvs_out, o_out, wide_out) = refs[17:22]
    (kv_all, weights, d_query, delta, d_lin, d_keys, d_kv, o_part, q_part, kvs_part) = refs[22:32]
    rest = list(refs[32:])

    def take(number):
        taken = rest[:number]
        del rest[:number]
        return taken

    count = 2 * depth
    devices = 4 * count
    rows, model = tokens.shape
    part = model // depth
    query_width, key_width = HEADS * HEAD_DIM, KV_HEADS * HEAD_DIM
    qkv_width = query_width + 2 * key_width
    model_rows = model // devices
    share = key_width // devices
    span = 4 * rows
    score_scale = HEAD_DIM ** (-0.5)
    scale = score_scale * LOG2E

    place = Place(depth)
    greet(place, [(lax.rem(place.s + offset, count), place.f) for offset in range(1, count)])

    def reduce_of(own, out, causal=False):
        block = own.shape[-2:]
        buffers, sems = Reduce.scratch(depth, True, block)
        return Reduce(
            place,
            True,
            block[0],
            own,
            out,
            take(len(buffers)),
            take(len(sems)),
            causal=causal,
        )

    r_kv = reduce_of(d_keys, d_kv, True)
    r_o = reduce_of(o_part, o_out)
    r_q = reduce_of(q_part, q_out)
    r_kvs = reduce_of(kvs_part, kvs_out)
    load_sem, e_send, e_recv = take(3)
    order = list(range(depth - 1, -1, -1))
    sent = []

    def depart(offset):
        to = lax.rem(place.s + offset, count)
        copy = remote(
            wide.at[to], wide_out.at[place.s], e_send.at[offset], e_recv.at[offset], (to, place.f)
        )
        copy.start()
        sent.append(copy)

    kv_load = pltpu.make_async_copy(kv_own, kv_all, load_sem.at[0])
    kv_load.start()
    own_wide = pltpu.make_async_copy(wide.at[place.s], wide_out.at[place.s], load_sem.at[1])
    own_wide.start()
    for offset in range(2, count, 2):
        depart(offset)
    for zi in range(depth):
        lanes = slice(zi * part, (zi + 1) * part)
        term = t_mul(mixed_low[:, lanes], d_branch[...]).astype(BF16)
        o_part[zi] = term.reshape(2, 2, 2, model_rows, model)
    for k in order:
        r_o.cores(k)
    for g in range(KV_HEADS):
        delta[g] = jnp.broadcast_to(
            jnp.sum(d_mixed[g].astype(F32) * mixed[g], axis=-1, keepdims=True), delta.shape[1:]
        )
    d_query[...] = jnp.zeros_like(d_query)
    kv_load.wait()
    r_o.over_second(order[0])
    first_row = (place.s * 4 + place.f) * rows
    places = first_row + lax.broadcasted_iota(jnp.int32, (rows, span), 0)
    offsets = lax.broadcasted_iota(jnp.int32, (rows, span), 1)

    def attend(number, carry):
        keys_at = number * span + offsets
        visible = jnp.logical_and(keys_at >= begin[...], keys_at <= places)
        z, x = lax.div(number, 2), lax.rem(number, 2)
        block = kv_all.at[z, x]
        target = d_keys.at[z, x]
        for g in range(KV_HEADS):
            lanes = slice(g * HEAD_DIM, (g + 1) * HEAD_DIM)
            others = slice(key_width + g * HEAD_DIM, key_width + (g + 1) * HEAD_DIM)
            key = block[:, :, :, lanes].reshape(span, HEAD_DIM)
            value = block[:, :, :, others].reshape(span, HEAD_DIM)
            scores = mul_t(queries[g], key)
            d_probs = mul_t(d_mixed[g], value)
            probs = jnp.exp2(scores * scale - lse[g][:, :1])
            probs = jnp.where(
                visible[None], probs.reshape(GROUP, rows, span), 0.0
            ).reshape(GROUP * rows, span)
            d_scores = (probs * (d_probs - delta[g][:, :1])).astype(BF16)
            d_query[g] += jnp.dot(d_scores, key, preferred_element_type=F32)
            d_key = t_mul(d_scores, queries[g]).astype(BF16)
            d_value = t_mul(probs.astype(BF16), d_mixed[g]).astype(BF16)
            target[:, :, :, lanes] = d_key.reshape(2, 2, rows, HEAD_DIM)
            target[:, :, :, others] = d_value.reshape(2, 2, rows, HEAD_DIM)
        return carry

    for step in range(depth):
        k = order[step]
        zi = place.z - k
        low = jnp.maximum(2 * zi, 0)
        high = jnp.minimum(jnp.maximum(2 * zi + 2, 0), place.s + 1)
        lax.fori_loop(low, high, attend, 0)
        if k == 0:

            def clear():
                d_keys[place.z, 1] = jnp.zeros(d_keys.shape[2:], BF16)

            pl.when(place.x == 0)(clear)
        r_kv.cores(k)
        if step >= 1:
            r_kv.over_second(order[step - 1])
        if step >= 2:
            r_kv.over_first(order[step - 2])
        if step + 1 < depth:
            r_o.over_second(order[step + 1])
        if step >= 1:
            r_o.over_first(order[step - 1])
        if step == 0:
            for offset in range(1, count, 2):
                depart(offset)

    for h in range(HEADS):
        lanes = slice(h * HEAD_DIM, (h + 1) * HEAD_DIM)
        at = (h % GROUP) * rows
        head = d_query[h // GROUP, at : at + rows, :] * score_scale
        d_lin[:, lanes] = turned(head, cosine[...], -sine[...]).astype(BF16)
    r_kv.over_second(order[depth - 1])
    if depth >= 2:
        r_kv.over_first(order[depth - 2])
    for step in range(max(depth - 2, 0)):
        r_kv.along(order[step])
    for zi in range(depth):
        lanes = slice(zi * part, (zi + 1) * part)
        term = t_mul(hidden_one[:, lanes], d_lin[:, :query_width]).astype(BF16)
        q_part[zi] = term.reshape(2, 2, 2, model_rows, query_width)
    for k in order:
        r_q.cores(k)
    r_kv.over_first(order[depth - 1])
    r_o.over_first(order[depth - 1])
    for step in range(max(depth - 2, 0), depth):
        r_kv.along(order[step])
    r_kv.finish()
    for step in range(depth):
        r_q.over_second(order[step])
    for step in range(depth):
        r_o.along(order[step])
    r_o.finish()

    for g in range(KV_HEADS):
        lanes = slice(g * HEAD_DIM, (g + 1) * HEAD_DIM)
        to = slice(query_width + g * HEAD_DIM, query_width + (g + 1) * HEAD_DIM)
        d_lin[:, to] = turned(d_kv[:, lanes] * score_scale, cosine[...], -sine[...]).astype(BF16)
    d_lin[:, query_width + key_width :] = d_kv[:, key_width:].astype(BF16)
    inputs = tokens[...].astype(F32)
    inv_one = lax.rsqrt(jnp.mean(inputs * inputs, axis=-1, keepdims=True) + EPSILON)
    normed = inputs * inv_one
    loads = [
        pltpu.make_async_copy(pack_own.at[zi], weights.at[zi % 2], load_sem.at[2 + zi])
        for zi in range(depth)
    ]
    for copy in loads[:2]:
        copy.start()
    pieces = []
    for zi in range(depth):
        lanes = slice(zi * part, (zi + 1) * part)
        term = t_mul(hidden_one[:, lanes], d_lin[:, query_width:]).astype(BF16)
        kvs_part[zi, :, :, :, :, : 2 * key_width] = term.reshape(
            2, 2, 2, model_rows, 2 * key_width
        )
        loads[zi].wait()
        block = weights[zi % 2][:, :, :, :, :qkv_width].reshape(part, qkv_width)
        pieces.append(mul_t(d_lin[...], block))
        if zi + 2 < depth:
            loads[zi + 2].start()
    d_hidden = jnp.concatenate(pieces, axis=1)
    for step in range(depth):
        r_q.over_first(order[step])
    gain_one = jnp.sum(d_hidden * normed, axis=0, keepdims=True)
    bias = jnp.sum(d_lin[...].astype(F32), axis=0, keepdims=True)
    chosen = lax.broadcasted_iota(jnp.int32, (key_width, model), 0)
    chosen = lax.div(chosen, share) * model_rows + lax.rem(chosen, share)
    chosen = (lax.broadcasted_iota(jnp.int32, (key_width, model), 1) == chosen).astype(BF16)
    pair = jnp.concatenate(
        [
            bias[:, query_width : query_width + key_width],
            bias[:, query_width + key_width :],
            jnp.zeros((6, key_width), F32),
        ],
        axis=0,
    )
    spread = jnp.dot(pair.astype(BF16), chosen, preferred_element_type=F32)
    small = jnp.concatenate(
        [
            gain_one,
            bias[:, :query_width],
            spread[0:2],
            gain_two[0:1],
            jnp.zeros((123, model), F32),
        ],
        axis=0,
    ).T.astype(BF16)
    for zi in range(depth):
        kvs_part[zi, :, :, :, :, 2 * key_width :] = small[zi * part : (zi + 1) * part].reshape(
            2, 2, 2, model_rows, 128
        )
    for k in order:
        r_kvs.cores(k)
    scaled = d_hidden * vectors[0:1]
    input_grad[...] = d_middle[...] + inv_one * (
        scaled - normed * jnp.mean(scaled * normed, axis=-1, keepdims=True)
    )
    for step in range(depth + 2):
        if step < depth:
            r_kvs.over_second(order[step])
        if 0 <= step - 1 < depth:
            r_kvs.over_first(order[step - 1])
        if step < depth:
            r_q.along(order[step])
        if 0 <= step - 2 < depth:
            r_kvs.along(order[step - 2])
    r_q.finish()
    r_kvs.finish()
    for offset in range(1, count):
        origin = lax.rem(place.s + count - offset, count)
        block = wide_out.at[origin]
        remote(block, block, e_send.at[0], e_recv.at[offset], place.flip_c()).wait_recv()
    own_wide.wait()
    for job in (r_kv, r_o, r_q, r_kvs):
        job.settle()
    for copy in sent:
        copy.wait_send()


def call_last(depth, collective_id, hbm, vmems):
    kv_all, pack_all, wide = hbm
    tokens = vmems[7]
    count = 2 * depth
    rows, model = tokens.shape
    model_rows = model // (4 * count)
    query_width, key_width = HEADS * HEAD_DIM, KV_HEADS * HEAD_DIM
    heads = (KV_HEADS, GROUP * rows, HEAD_DIM)
    lead = (depth, 2, 2, 2)
    small_width = 2 * key_width + 128
    blocks = [
        (rows, 2 * key_width),
        (model_rows, model),
        (model_rows, query_width),
        (model_rows, small_width),
    ]
    scratch = [
        pltpu.VMEM(kv_all.shape, BF16),
        pltpu.VMEM((2,) + pack_all.shape[1:], BF16),
        pltpu.VMEM(heads, F32),
        pltpu.VMEM(heads, F32),
        pltpu.VMEM((rows, query_width + 2 * key_width), BF16),
        pltpu.VMEM(lead + blocks[0], BF16),
        pltpu.VMEM(blocks[0], F32),
    ]
    scratch += [pltpu.VMEM(lead + block, BF16) for block in blocks[1:]]
    for block in blocks:
        buffers, sems = Reduce.scratch(depth, True, block)
        scratch += buffers + sems
    scratch += [DMA((2 + depth,)), DMA((count,)), DMA((count,))]
    any_, vmem = pl.BlockSpec(memory_space=pl.ANY), pl.BlockSpec(memory_space=pltpu.VMEM)
    return pl.pallas_call(
        functools.partial(last_kernel, depth),
        out_shape=[
            jax.ShapeDtypeStruct((rows, model), F32),
            jax.ShapeDtypeStruct(blocks[2], F32),
            jax.ShapeDtypeStruct(blocks[3], F32),
            jax.ShapeDtypeStruct(blocks[1], F32),
            jax.ShapeDtypeStruct(wide.shape, BF16),
        ],
        in_specs=[any_] * 3 + [vmem] * len(vmems),
        out_specs=[vmem] * 4 + [any_],
        scratch_shapes=scratch,
        compiler_params=pltpu.CompilerParams(
            collective_id=collective_id, has_side_effects=True, vmem_limit_bytes=VMEM_JOINED
        ),
    )(*hbm, *vmems)


def begin_of(positions, lengths):
    ends = jnp.cumsum(lengths)
    starts = ends - lengths
    inside = (positions[:, None] >= starts[None, :]) & (positions[:, None] < ends[None, :])
    return jnp.sum(jnp.where(inside, starts[None, :], 0), axis=1)


def rope_tables(places, head_size):
    half_size = head_size // 2
    frequency = ROPE_BASE ** (-2.0 * jnp.arange(half_size, dtype=F32) / head_size)
    angles = places.astype(F32)[:, None] * frequency[None, :]
    return (jnp.cos(angles), jnp.sin(angles))


def rotate(vector, cosine, sine_table, direction):
    half_size = vector.shape[-1] // 2
    front_half = vector[..., :half_size]
    back_half = vector[..., half_size:]
    cosine = cosine[:, None, :]
    sine_table = direction * sine_table[:, None, :]
    return jnp.concatenate(
        [
            front_half * cosine - back_half * sine_table,
            back_half * cosine + front_half * sine_table,
        ],
        axis=-1,
    )


def norm_back(grad_normed, normed, inverse, gain_row):
    scaled = grad_normed * gain_row
    return inverse * (scaled - normed * jnp.mean(scaled * normed, axis=-1, keepdims=True))


def dot(left, right):
    return jnp.dot(left, right, preferred_element_type=F32)


def dot_t(left, right):
    return lax.dot_general(left, right, (((1,), (1,)), ((), ())), preferred_element_type=F32)


def t_dot(left, right):
    return lax.dot_general(left, right, (((0,), (0,)), ((), ())), preferred_element_type=F32)


def column(vector, rows):
    return jnp.pad(vector, (0, rows - vector.shape[0]))[:, None]


def shards_apart(
    tokens,
    cotangent,
    lengths,
    attn_gain,
    q_weight,
    q_bias,
    k_weight,
    k_bias,
    v_weight,
    v_bias,
    o_weight,
    mlp_gain,
    gate_weight,
    up_weight,
    down_weight,
):
    seq, fsdp = lax.axis_size("seq"), lax.axis_size("fsdp")
    devices = seq * fsdp
    depth = seq // 2
    rows, model = tokens.shape
    total = rows * devices
    key_width = KV_HEADS * HEAD_DIM
    query_width = HEADS * HEAD_DIM
    model_rows = q_weight.shape[0]
    units = gate_weight.shape[1] // seq
    first_row = lax.axis_index(AXES) * rows
    positions = first_row + jnp.arange(rows, dtype=jnp.int32)
    begin = begin_of(positions, lengths)
    cosine, sine_table = rope_tables(positions - begin, HEAD_DIM)
    score_scale = HEAD_DIM ** (-0.5)

    small = jnp.concatenate(
        [column(v, model_rows) for v in (attn_gain, q_bias, k_bias, v_bias, mlp_gain)]
        + [jnp.zeros((model_rows, 123), BF16)],
        axis=1,
    )
    pack = jnp.concatenate([q_weight, k_weight, v_weight, o_weight, small], axis=1)
    wide = jnp.stack([gate_weight, up_weight]).reshape(2, model_rows, seq, units)
    wide = wide.transpose(0, 2, 1, 3)
    pack_all, cot_all, wide_all, down_all = call_start(
        depth, 0, pack, cotangent, wide, down_weight
    )
    pack_all = pack_all.reshape(model, pack.shape[1])
    qkv_width = query_width + 2 * key_width
    w_qkv = pack_all[:, :qkv_width]
    w_out = pack_all[:, qkv_width : qkv_width + query_width]
    smalls = pack_all[:, qkv_width + query_width :].astype(F32)
    gain_one, b_query = smalls[:, 0], smalls[:, 1]
    gain_two = smalls[:, 4]
    kv_share = k_bias.shape[0]
    b_key = smalls[:, 2].reshape(devices, model_rows)[:, :kv_share].reshape(key_width)
    b_value = smalls[:, 3].reshape(devices, model_rows)[:, :kv_share].reshape(key_width)
    cot_all = cot_all.reshape(seq * rows, model)
    w_gate = wide_all[0].reshape(model, units)
    w_up = wide_all[1].reshape(model, units)
    w_down = down_all.reshape(units, model)

    inputs = tokens.astype(F32)
    inv_one = lax.rsqrt(jnp.mean(inputs * inputs, axis=-1, keepdims=True) + EPSILON)
    normed_one = inputs * inv_one
    hidden_one = (normed_one * gain_one).astype(BF16)
    lin = dot(hidden_one, w_qkv) + jnp.concatenate([b_query, b_key, b_value])
    queries = rotate(
        lin[:, :query_width].reshape(rows, HEADS, HEAD_DIM), cosine, sine_table, 1.0
    ).astype(BF16)
    queries = queries.transpose(1, 0, 2).reshape(KV_HEADS, GROUP * rows, HEAD_DIM)
    keys = rotate(
        lin[:, query_width : query_width + key_width].reshape(rows, KV_HEADS, HEAD_DIM),
        cosine,
        sine_table,
        1.0,
    ).reshape(rows, key_width)
    kv = jnp.concatenate([keys, lin[:, query_width + key_width :]], axis=1).astype(BF16)
    (kv_all,) = call_gathers(depth, 1, [True], [kv])
    kv_all = kv_all.reshape(total, 2 * key_width)
    all_keys, all_values = kv_all[:, :key_width], kv_all[:, key_width:]

    span = min(512, total)
    low = begin[0] // span
    high = (first_row + rows - 1) // span + 1
    info = jnp.stack([first_row, low, high]).astype(jnp.int32)
    begin_column = begin[:, None]
    mixed, lse = call_forward(span, info, begin_column, queries, all_keys, all_values)
    mixed_low = (
        mixed.reshape(HEADS, rows, HEAD_DIM)
        .transpose(1, 0, 2)
        .reshape(rows, query_width)
        .astype(BF16)
    )
    middle = inputs + dot(mixed_low, w_out)
    inv_two = lax.rsqrt(jnp.mean(middle * middle, axis=-1, keepdims=True) + EPSILON)
    normed_two = middle * inv_two
    hidden_two = (normed_two * gain_two).astype(BF16)

    (hidden_all,) = call_gathers(depth, 2, [False], [hidden_two])
    hidden_all = hidden_all.reshape(seq * rows, model)
    gate = dot(hidden_all, w_gate)
    up = dot(hidden_all, w_up)
    sigma = jax.nn.sigmoid(gate)
    silu = gate * sigma
    activated = (silu * up).astype(BF16)
    d_act = dot_t(cot_all, w_down)
    d_gate = (d_act * up * sigma * (1.0 + gate * (1.0 - sigma))).astype(BF16)
    d_up = (d_act * silu).astype(BF16)
    d_hidden_part = dot_t(d_gate, w_gate) + dot_t(d_up, w_up)
    out_part = dot(activated, w_down)
    shape = (depth, 2, rows, model)
    d_hidden_two, branch = call_reduces(
        depth,
        3,
        [False, False],
        [d_hidden_part.astype(BF16).reshape(shape), out_part.astype(BF16).reshape(shape)],
    )
    layer_out = (middle + branch).astype(BF16)
    gate_part = t_dot(hidden_all, d_gate).astype(BF16)
    up_part = t_dot(hidden_all, d_up).astype(BF16)
    down_part = t_dot(activated, cot_all).astype(BF16)

    gain_two_grad = jnp.sum(d_hidden_two * normed_two, axis=0)
    d_middle = cotangent.astype(F32) + norm_back(d_hidden_two, normed_two, inv_two, gain_two)

    d_branch = d_middle.astype(BF16)
    d_mixed = dot_t(d_branch, w_out).astype(BF16)
    d_mixed = (
        d_mixed.reshape(rows, HEADS, HEAD_DIM)
        .transpose(1, 0, 2)
        .reshape(KV_HEADS, GROUP * rows, HEAD_DIM)
    )
    d_query, d_kv_part = call_backward(
        span, info, begin_column, queries, all_keys, all_values, mixed, lse, d_mixed
    )
    (d_kv,) = call_reduces(
        depth, 4, [True], [d_kv_part.reshape(depth, 2, 2, 2, rows, 2 * key_width)]
    )
    d_query = d_query.reshape(HEADS, rows, HEAD_DIM).transpose(1, 0, 2)
    d_q = rotate(d_query * score_scale, cosine, sine_table, -1.0).reshape(rows, query_width)
    d_k = rotate(
        d_kv[:, :key_width].reshape(rows, KV_HEADS, HEAD_DIM) * score_scale,
        cosine,
        sine_table,
        -1.0,
    ).reshape(rows, key_width)
    d_lin = jnp.concatenate([d_q, d_k, d_kv[:, key_width:]], axis=1).astype(BF16)
    bias_grad = jnp.sum(d_lin.astype(F32), axis=0)
    d_hidden_one = dot_t(d_lin, w_qkv)
    gain_one_grad = jnp.sum(d_hidden_one * normed_one, axis=0)
    input_grad = d_middle + norm_back(d_hidden_one, normed_one, inv_one, gain_one)

    def spread(vector):
        parts = vector.reshape(devices, -1)
        return jnp.pad(parts, ((0, 0), (0, model_rows - parts.shape[1]))).reshape(model, 1)

    small_part = jnp.concatenate(
        [
            spread(gain_one_grad),
            spread(bias_grad[:query_width]),
            spread(bias_grad[query_width : query_width + key_width]),
            spread(bias_grad[query_width + key_width :]),
            spread(gain_two_grad),
            jnp.zeros((model, 123), F32),
        ],
        axis=1,
    )
    pack_part = jnp.concatenate(
        [
            t_dot(hidden_one, d_lin).astype(BF16),
            t_dot(mixed_low, d_branch).astype(BF16),
            small_part.astype(BF16),
        ],
        axis=1,
    ).reshape(depth, 2, 2, 2, model_rows, pack.shape[1])
    wide_part = jnp.stack([gate_part, up_part]).reshape(2, seq, fsdp, model_rows, units)
    down_part = down_part.reshape(fsdp, units // fsdp, model)
    pack_grad, wide_grad, down_grad = call_end(depth, 5, pack_part, wide_part, down_part)
    wide_grad = wide_grad.transpose(1, 2, 0, 3).reshape(2, model_rows, seq * units).astype(F32)
    small_grad = pack_grad[:, qkv_width + query_width :]
    return (
        layer_out,
        input_grad,
        small_grad[:, 0],
        pack_grad[:, :query_width],
        small_grad[:, 1],
        pack_grad[:, query_width : query_width + key_width],
        small_grad[:kv_share, 2],
        pack_grad[:, query_width + key_width : qkv_width],
        small_grad[:kv_share, 3],
        pack_grad[:, qkv_width : qkv_width + query_width],
        small_grad[:, 4],
        wide_grad[0],
        wide_grad[1],
        down_grad,
    )


def shards_joined(
    tokens,
    cotangent,
    lengths,
    attn_gain,
    q_weight,
    q_bias,
    k_weight,
    k_bias,
    v_weight,
    v_bias,
    o_weight,
    mlp_gain,
    gate_weight,
    up_weight,
    down_weight,
):
    seq, fsdp = lax.axis_size("seq"), lax.axis_size("fsdp")
    devices = seq * fsdp
    depth = seq // 2
    rows, model = tokens.shape
    key_width = KV_HEADS * HEAD_DIM
    model_rows = q_weight.shape[0]
    kv_share = k_bias.shape[0]
    units = gate_weight.shape[1] // seq
    first_row = lax.axis_index(AXES) * rows
    positions = first_row + jnp.arange(rows, dtype=jnp.int32)
    begin = begin_of(positions, lengths)
    cosine, sine_table = rope_tables(positions - begin, HEAD_DIM)
    cosine_row = jnp.concatenate([cosine, cosine], axis=1)
    sine_row = jnp.concatenate([-sine_table, sine_table], axis=1)

    small = jnp.concatenate(
        [column(v, model_rows) for v in (attn_gain, q_bias, k_bias, v_bias, mlp_gain)]
        + [jnp.zeros((model_rows, 123), BF16)],
        axis=1,
    )
    pack = jnp.concatenate([q_weight, k_weight, v_weight, small], axis=1)
    wide = jnp.stack([gate_weight, up_weight]).reshape(2, model_rows, seq, units)
    wide = wide.transpose(0, 2, 1, 3)
    begin_column = begin[:, None]
    (
        pack_all,
        o_all,
        kv_all,
        cot_all,
        wide_all,
        down_all,
        hidden_all,
        queries,
        mixed,
        lse,
        middle,
        hidden_one,
        mixed_low,
        vectors,
    ) = call_head(
        depth,
        6,
        pack,
        o_weight,
        cotangent,
        wide,
        down_weight,
        tokens,
        cosine_row,
        sine_row,
        begin_column,
    )
    w_gate = wide_all[0].reshape(model, units)
    w_up = wide_all[1].reshape(model, units)
    w_down = down_all.reshape(units, model)
    tokens_all = hidden_all.reshape(seq * rows, model)
    grads_all = cot_all.reshape(seq * rows, model)

    gate = dot(tokens_all, w_gate)
    up = dot(tokens_all, w_up)
    sigma = jax.nn.sigmoid(gate)
    silu = gate * sigma
    activated = (silu * up).astype(BF16)
    d_act = dot_t(grads_all, w_down)
    d_gate = (d_act * up * sigma * (1.0 + gate * (1.0 - sigma))).astype(BF16)
    d_up = (d_act * silu).astype(BF16)
    d_hidden_part = dot_t(d_gate, w_gate) + dot_t(d_up, w_up)
    out_part = dot(activated, w_down)
    shape = (depth, 2, rows, model)
    layer_out, d_middle, d_mixed, d_branch, gain_two_grad, down_grad, wide_part = call_middle(
        depth,
        7,
        d_hidden_part.astype(BF16).reshape(shape),
        out_part.astype(BF16).reshape(shape),
        hidden_all,
        cot_all,
        activated,
        d_gate,
        d_up,
        o_all,
        middle,
        cotangent,
        vectors,
    )
    input_grad, q_grad, kvs_grad, o_grad, wide_grad = call_last(
        depth,
        8,
        (kv_all, pack_all, wide_part),
        (
            queries,
            mixed,
            lse,
            d_mixed,
            cosine_row,
            sine_row,
            begin_column,
            tokens,
            d_middle,
            vectors,
            gain_two_grad,
            hidden_one,
            mixed_low,
            d_branch,
        ),
    )
    wide_grad = wide_grad.transpose(1, 2, 0, 3).reshape(2, model_rows, seq * units).astype(F32)
    small_grad = kvs_grad[:, 2 * key_width :]
    return (
        layer_out,
        input_grad,
        small_grad[:, 0],
        q_grad,
        small_grad[:, 1],
        kvs_grad[:, :key_width],
        small_grad[:kv_share, 2],
        kvs_grad[:, key_width : 2 * key_width],
        small_grad[:kv_share, 3],
        o_grad,
        small_grad[:, 4],
        wide_grad[0],
        wide_grad[1],
        down_grad,
    )


def shards(*arguments):
    model_rows, rows = arguments[4].shape[0], arguments[0].shape[0]
    if model_rows % 16 == 0 and rows % 128 == 0:
        return shards_joined(*arguments)
    return shards_apart(*arguments)


def solution(mesh):
    matrix, vector = P(AXES, None), P(AXES)
    in_specs = (
        matrix,
        matrix,
        P(),
        vector,
        matrix,
        vector,
        matrix,
        vector,
        matrix,
        vector,
        matrix,
        vector,
        matrix,
        matrix,
        matrix,
    )
    out_specs = (
        matrix,
        matrix,
        vector,
        matrix,
        vector,
        matrix,
        vector,
        matrix,
        vector,
        matrix,
        vector,
        matrix,
        matrix,
        matrix,
    )
    return jax.shard_map(shards, mesh=mesh, in_specs=in_specs, out_specs=out_specs, check_vma=False)
```

```python
import functools

import jax
import jax.numpy as jnp
from jax import lax
from jax.experimental import pallas as pl
from jax.experimental.pallas import tpu as pltpu
from jax.sharding import PartitionSpec as P

HEADS = 12
KV_HEADS = 2
HEAD_DIM = 128
GROUP = HEADS // KV_HEADS
EPSILON = 1e-06
ROPE_BASE = 10000.0
LOG2E = 1.4426950408889634
AXES = ("seq", "fsdp")
VMEM_LIMIT = 56 << 20
VMEM_JOINED = 60 << 20
F32 = jnp.float32
BF16 = jnp.bfloat16
DMA = pltpu.SemaphoreType.DMA


class Place:
    def __init__(self, depth):
        self.depth = depth
        self.s = lax.axis_index("seq")
        self.f = lax.axis_index("fsdp")
        self.z = lax.div(self.s, 2)
        self.x = lax.rem(self.s, 2)
        self.y = lax.div(self.f, 2)
        self.c = lax.rem(self.f, 2)
        self.up = self.z + 1 < depth
        self.down = self.z > 0

    def flip_x(self):
        return (self.s + 1 - 2 * self.x, self.f)

    def flip_y(self):
        return (self.s, self.f + 2 - 4 * self.y)

    def flip_c(self):
        return (self.s, self.f + 1 - 2 * self.c)

    def z_up(self):
        return (self.s + 2, self.f)

    def z_down(self):
        return (self.s - 2, self.f)

    def first(self):
        return (
            self.s + (1 - self.c) * (1 - 2 * self.x),
            self.f + self.c * (2 - 4 * self.y),
        )

    def second(self):
        return (
            self.s + self.c * (1 - 2 * self.x),
            self.f + (1 - self.c) * (2 - 4 * self.y),
        )

    def corner(self, i, j):
        over_x = i * (1 - self.c) + j * self.c
        over_y = j * (1 - self.c) + i * self.c
        return (self.x + over_x * (1 - 2 * self.x), self.y + over_y * (1 - 2 * self.y))

    def wave(self, k):
        if k == 0:
            return [(self.z, None)]
        return [(self.z - k, self.z - k >= 0), (self.z + k, self.z + k < self.depth)]


def guard(condition, body):
    if condition is None:
        body()
    else:
        pl.when(condition)(body)


def both(one, other):
    return one if other is None else jnp.logical_and(one, other)


def greet(place, others=()):
    barrier = pltpu.get_barrier_semaphore()
    partners = [place.flip_x(), place.flip_y(), place.flip_c(), *others]
    for partner in partners:
        pl.semaphore_signal(barrier, inc=1, device_id=partner, device_id_type=pl.DeviceIdType.MESH)

    def tell_up():
        pl.semaphore_signal(
            barrier, inc=1, device_id=place.z_up(), device_id_type=pl.DeviceIdType.MESH
        )

    def tell_down():
        pl.semaphore_signal(
            barrier, inc=1, device_id=place.z_down(), device_id_type=pl.DeviceIdType.MESH
        )

    pl.when(place.up)(tell_up)
    pl.when(place.down)(tell_down)
    pl.semaphore_wait(
        barrier, len(partners) + place.up.astype(jnp.int32) + place.down.astype(jnp.int32)
    )


def remote(src, dst, send_sem, recv_sem, device):
    return pltpu.make_async_remote_copy(
        src_ref=src,
        dst_ref=dst,
        send_sem=send_sem,
        recv_sem=recv_sem,
        device_id=device,
        device_id_type=pl.DeviceIdType.MESH,
    )


def add_into(target, term, rows):
    step = 16 if rows % 16 == 0 else rows

    def body(number, carry):
        at = pl.ds(pl.multiple_of(number * step, step), step)
        target[at, :] = (target[at, :].astype(F32) + term[at, :].astype(F32)).astype(BF16)
        return carry

    lax.fori_loop(0, rows // step, body, 0)


class Gather:
    def __init__(self, place, wide, own, out, sems, mixed=False):
        self.place, self.wide, self.own, self.out, self.sems = place, wide, own, out, sems
        self.mixed = mixed
        self.sent = []

    @staticmethod
    def semaphores(depth, wide, mixed=False):
        base = [DMA((1,)), DMA((2 * depth,)), DMA((depth,)), DMA((depth,)), DMA((depth,))]
        if mixed:
            base += [DMA((2 * depth,)), DMA((depth,))]
        if wide:
            base += [DMA((2 * depth,)), DMA((2 * depth,)), DMA((4 * depth,)), DMA((4 * depth,))]
        return base

    def at(self, zi, i, j):
        place = self.place
        if self.wide:
            x, y = place.corner(i, j)
            return self.out.at[zi, x, y, place.c]
        return self.out.at[zi, place.x + i * (1 - 2 * place.x)]

    def send(self, src, dst, send_sem, recv_sem, device, condition):
        copy = remote(src, dst, send_sem, recv_sem, device)
        guard(condition, copy.start)
        self.sent.append((copy, condition))

    def local(self):
        copy = pltpu.make_async_copy(
            self.own, self.at(self.place.z, 0, 0), self.sems[0].at[0]
        )
        return copy

    def along(self, k, zi, side, ok, column, z_send, z_recv, source=None):
        place, depth = self.place, self.place.depth
        block = self.at(zi, column, 0)
        source = block if source is None else source
        if k == 0 or side == 0:
            self.send(
                source, block, z_send.at[k], z_recv.at[zi], place.z_up(), both(place.up, ok)
            )
        if k == 0 or side == 1:
            self.send(
                source,
                block,
                z_send.at[depth + k],
                z_recv.at[zi],
                place.z_down(),
                both(place.down, ok),
            )

    def arrive(self, k):
        place = self.place
        z_send, z_recv, a_send, a_recv = self.sems[1:5]
        across = place.first() if self.wide else place.flip_x()
        for side, (zi, ok) in enumerate(place.wave(k)):
            block = self.at(zi, 0, 0)
            source = self.own if k == 0 else block
            if k > 0:
                landed = remote(block, block, z_send.at[0], z_recv.at[zi], place.z_up())
                guard(ok, landed.wait_recv)
            self.along(k, zi, side, ok, 0, z_send, z_recv, source)
            crossing = both(place.c == 0, ok) if self.mixed and k > 0 else ok
            self.send(source, block, a_send.at[zi], a_recv.at[zi], across, crossing)
            if self.wide:
                b_send, b_recv = self.sems[5:7]
                self.send(
                    source, block, b_send.at[2 * zi], b_recv.at[2 * zi], place.second(), ok
                )

    def across(self, k):
        place = self.place
        a_send, a_recv = self.sems[3:5]
        for side, (zi, ok) in enumerate(place.wave(k)):
            block = self.at(zi, 1, 0)
            crossing = both(place.c == 0, ok) if self.mixed and k > 0 else ok
            landed = remote(block, block, a_send.at[0], a_recv.at[zi], place.first())
            guard(crossing, landed.wait_recv)
            if self.mixed:
                z_send, z_recv = self.sems[5:7]
                carried = both(place.c == 1, ok)
                if k > 0:
                    landed = remote(block, block, z_send.at[0], z_recv.at[zi], place.z_up())
                    guard(carried, landed.wait_recv)
                self.along(k, zi, side, carried, 1, z_send, z_recv)
            if self.wide:
                b_send, b_recv = self.sems[5:7]
                self.send(
                    block, block, b_send.at[2 * zi + 1], b_recv.at[2 * zi + 1], place.second(), ok
                )

    def hand(self, k):
        place = self.place
        b_send, b_recv, c_send, c_recv = self.sems[5:9]
        for zi, ok in place.wave(k):
            for i in range(2):
                block = self.at(zi, i, 1)
                landed = remote(block, block, b_send.at[0], b_recv.at[2 * zi + i], place.second())
                guard(ok, landed.wait_recv)
            for x in range(2):
                for y in range(2):
                    block = self.out.at[zi, x, y, place.c]
                    slot = 4 * zi + 2 * x + y
                    self.send(
                        block, block, c_send.at[slot], c_recv.at[slot], place.flip_c(), ok
                    )

    def take(self, k):
        place = self.place
        c_send, c_recv = self.sems[7:9]
        for zi, ok in place.wave(k):
            for x in range(2):
                for y in range(2):
                    block = self.out.at[zi, x, y, 1 - place.c]
                    slot = 4 * zi + 2 * x + y
                    landed = remote(block, block, c_send.at[0], c_recv.at[slot], place.flip_c())
                    guard(ok, landed.wait_recv)

    def settle(self):
        for copy, condition in self.sent:
            guard(condition, copy.wait_send)


def drive_gathers(place, gathers):
    depth = place.depth
    locals_ = [gather.local() for gather in gathers]
    for copy in locals_:
        copy.start()
    for step in range(depth + 3):
        for gather in gathers:
            if step < depth:
                gather.arrive(step)
        if step == 0:
            for copy in locals_:
                copy.wait()
        for gather in gathers:
            if 0 <= step - 1 < depth:
                gather.across(step - 1)
        for gather in gathers:
            if gather.wide and 0 <= step - 2 < depth:
                gather.hand(step - 2)
        for gather in gathers:
            if gather.wide and 0 <= step - 3 < depth:
                gather.take(step - 3)
    for gather in gathers:
        gather.settle()


def gather_shape(depth, wide, own):
    lead = (depth, 2, 2, 2) if wide else (depth, 2)
    return jax.ShapeDtypeStruct(lead + own.shape, own.dtype)


def call_gathers(depth, collective_id, wides, owns):
    def kernel(*refs):
        count = len(owns)
        place = Place(depth)
        greet(place)
        gathers, used = [], 2 * count
        for number, wide in enumerate(wides):
            need = len(Gather.semaphores(depth, wide))
            gathers.append(
                Gather(place, wide, refs[number], refs[count + number], refs[used : used + need])
            )
            used += need
        drive_gathers(place, gathers)

    scratch = []
    for wide in wides:
        scratch += Gather.semaphores(depth, wide)
    return pl.pallas_call(
        kernel,
        out_shape=[gather_shape(depth, wide, own) for wide, own in zip(wides, owns)],
        in_specs=[pl.BlockSpec(memory_space=pl.ANY)] * len(owns),
        out_specs=[pl.BlockSpec(memory_space=pl.ANY)] * len(owns),
        scratch_shapes=scratch,
        compiler_params=pltpu.CompilerParams(
            collective_id=collective_id, has_side_effects=True, vmem_limit_bytes=VMEM_LIMIT
        ),
    )(*owns)


def start_kernel(depth, *refs):
    (pack, cot, wide_in, down_in, pack_out, cot_out, wide_out, down_out), sems = refs[:8], refs[8:]
    place = Place(depth)
    count = 2 * depth
    partners = []
    for offset in range(1, count):
        partners.append((lax.rem(place.s + offset, count), place.f))
    greet(place, partners)
    first = len(Gather.semaphores(depth, True))
    second = first + len(Gather.semaphores(depth, False))
    gathers = [
        Gather(place, True, pack, pack_out, sems[:first]),
        Gather(place, False, cot, cot_out, sems[first:second]),
    ]
    local_sem, e_send, e_recv, y_send, y_recv, c_send, c_recv, d_sem, d_send, d_recv = sems[second:]
    sent = []

    def send(src, dst, send_sem, recv_sem, device):
        copy = remote(src, dst, send_sem, recv_sem, device)
        copy.start()
        sent.append(copy)

    locals_ = [gather.local() for gather in gathers]
    locals_.append(
        pltpu.make_async_copy(
            wide_in.at[:, place.s], wide_out.at[:, place.s, place.f], local_sem.at[0]
        )
    )
    locals_.append(pltpu.make_async_copy(down_in, down_out.at[place.f], d_sem.at[0]))
    for copy in locals_:
        copy.start()

    y_f = place.f + 2 - 4 * place.y
    c_f = place.f + 1 - 2 * place.c
    yc_f = y_f + 1 - 2 * place.c

    def exchange(offset):
        to = lax.rem(place.s + offset, count)
        send(
            wide_in.at[:, to],
            wide_out.at[:, place.s, place.f],
            e_send.at[offset],
            e_recv.at[offset],
            (to, place.f),
        )

    def onward(offset):
        origin = lax.rem(place.s + count - offset, count)
        block = wide_out.at[:, origin, place.f]
        if offset > 0:
            remote(block, block, e_send.at[0], e_recv.at[offset], place.flip_y()).wait_recv()
        send(block, block, y_send.at[offset], y_recv.at[offset], place.flip_y())
        send(block, block, c_send.at[2 * offset], c_recv.at[2 * offset], place.flip_c())

    def sideways(offset):
        origin = lax.rem(place.s + count - offset, count)
        block = wide_out.at[:, origin, y_f]
        remote(block, block, y_send.at[0], y_recv.at[offset], place.flip_y()).wait_recv()
        send(block, block, c_send.at[2 * offset + 1], c_recv.at[2 * offset + 1], place.flip_c())

    def last(offset):
        origin = lax.rem(place.s + count - offset, count)
        for slot, owner in ((2 * offset, c_f), (2 * offset + 1, yc_f)):
            block = wide_out.at[:, origin, owner]
            remote(block, block, c_send.at[0], c_recv.at[slot], place.flip_c()).wait_recv()

    for gather in gathers:
        gather.arrive(0)
    send(down_in, down_out.at[place.f], d_send.at[0], d_recv.at[0], place.flip_y())
    send(down_in, down_out.at[place.f], d_send.at[1], d_recv.at[1], place.flip_c())
    for offset in range(1, count):
        exchange(offset)
    for copy in locals_:
        copy.wait()
    onward(0)
    total = depth + 3
    for step in range(1, total):
        for gather in gathers:
            if step < depth:
                gather.arrive(step)
        for gather in gathers:
            if 0 <= step - 1 < depth:
                gather.across(step - 1)
        for gather in gathers:
            if gather.wide and 0 <= step - 2 < depth:
                gather.hand(step - 2)
        for gather in gathers:
            if gather.wide and 0 <= step - 3 < depth:
                gather.take(step - 3)
    block = down_out.at[y_f]
    remote(block, block, d_send.at[0], d_recv.at[0], place.flip_y()).wait_recv()
    send(block, block, d_send.at[2], d_recv.at[2], place.flip_c())
    for offset in range(1, count):
        onward(offset)
        sideways(offset - 1)
    sideways(count - 1)
    for offset in range(count):
        last(offset)
    for slot, owner in ((1, c_f), (2, yc_f)):
        block = down_out.at[owner]
        remote(block, block, d_send.at[0], d_recv.at[slot], place.flip_c()).wait_recv()
    for gather in gathers:
        gather.settle()
    for copy in sent:
        copy.wait_send()


def call_start(depth, collective_id, pack, cot, wide, down):
    count = 2 * depth
    _, _, rows, columns = wide.shape
    scratch = Gather.semaphores(depth, True) + Gather.semaphores(depth, False)
    scratch += [DMA((1,)), DMA((count,)), DMA((count,)), DMA((count,)), DMA((count,))]
    scratch += [DMA((2 * count,)), DMA((2 * count,)), DMA((1,)), DMA((3,)), DMA((3,))]
    return pl.pallas_call(
        functools.partial(start_kernel, depth),
        out_shape=[
            gather_shape(depth, True, pack),
            gather_shape(depth, False, cot),
            jax.ShapeDtypeStruct((2, count, 4, rows, columns), BF16),
            jax.ShapeDtypeStruct((4,) + down.shape, BF16),
        ],
        in_specs=[pl.BlockSpec(memory_space=pl.ANY)] * 4,
        out_specs=[pl.BlockSpec(memory_space=pl.ANY)] * 4,
        scratch_shapes=scratch,
        compiler_params=pltpu.CompilerParams(
            collective_id=collective_id, has_side_effects=True, vmem_limit_bytes=VMEM_LIMIT
        ),
    )(pack, cot, wide, down)


class Reduce:
    def __init__(self, place, wide, rows, own, out, buffers, sems, near=None, causal=False):
        self.place, self.wide, self.rows = place, wide, rows
        self.own, self.out, self.buffers, self.sems = own, out, buffers, sems
        self.near = near
        self.causal = causal
        self.sent = []

    def wave(self, k):
        waves = self.place.wave(k)
        return waves[:1] if self.causal else waves

    def near_block(self, zi):
        return self.own.at[zi, self.place.x] if self.near is None else self.near.at[zi]

    @staticmethod
    def scratch(depth, wide, block):
        buffers = [
            pltpu.VMEM((depth,) + block, BF16),
            pltpu.VMEM((depth + 1,) + block, BF16),
        ]
        sems = [DMA((depth,)), DMA((depth,)), DMA((2 * depth,)), DMA((2 * depth,))]
        if wide:
            buffers += [
                pltpu.VMEM((depth, 2, 2) + block, BF16),
                pltpu.VMEM((depth, 2) + block, BF16),
            ]
            sems += [DMA((4 * depth,)), DMA((4 * depth,)), DMA((2 * depth,)), DMA((2 * depth,))]
        return buffers, sems

    def send(self, src, dst, send_sem, recv_sem, device, condition):
        copy = remote(src, dst, send_sem, recv_sem, device)
        guard(condition, copy.start)
        self.sent.append((copy, condition))

    def cores(self, k):
        place = self.place
        c_send, c_recv = self.sems[4:6]
        got = self.buffers[2]
        for zi, ok in self.wave(k):
            for x in range(2):
                for y in range(2):
                    slot = 4 * zi + 2 * x + y
                    self.send(
                        self.own.at[zi, x, y, 1 - place.c],
                        got.at[zi, x, y],
                        c_send.at[slot],
                        c_recv.at[slot],
                        place.flip_c(),
                        ok,
                    )

    def over_second(self, k):
        place = self.place
        c_send, c_recv, b_send, b_recv = self.sems[4:8]
        got, next_ = self.buffers[2:4]
        for zi, ok in self.wave(k):

            def body(zi=zi):
                for j in (1, 0):
                    for i in (1, 0):
                        x, y = place.corner(i, j)
                        block = got.at[zi, x, y]
                        slot = 4 * zi + 2 * x + y
                        remote(
                            block, block, c_send.at[0], c_recv.at[slot], place.flip_c()
                        ).wait_recv()
                        add_into(block, self.own.at[zi, x, y, place.c], self.rows)
                        if j == 1:
                            remote(
                                block,
                                next_.at[zi, i],
                                b_send.at[2 * zi + i],
                                b_recv.at[2 * zi + i],
                                place.second(),
                            ).start()

            guard(ok, body)
            for i in (1, 0):
                x, y = place.corner(i, 1)
                copy = remote(
                    got.at[zi, x, y],
                    next_.at[zi, i],
                    b_send.at[2 * zi + i],
                    b_recv.at[2 * zi + i],
                    place.second(),
                )
                self.sent.append((copy, ok))

    def over_first(self, k):
        place = self.place
        a_send, a_recv = self.sems[0:2]
        got = self.buffers[0]
        for zi, ok in self.wave(k):
            if self.wide:
                b_send, b_recv = self.sems[6:8]
                before, held = self.buffers[2:4]

                def body(zi=zi):
                    for i in (1, 0):
                        block = held.at[zi, i]
                        x, y = place.corner(i, 0)
                        remote(
                            block, block, b_send.at[0], b_recv.at[2 * zi + i], place.second()
                        ).wait_recv()
                        add_into(block, before.at[zi, x, y], self.rows)
                        if i == 1:
                            remote(
                                block, got.at[zi], a_send.at[zi], a_recv.at[zi], place.first()
                            ).start()

                guard(ok, body)
                copy = remote(
                    held.at[zi, 1], got.at[zi], a_send.at[zi], a_recv.at[zi], place.first()
                )
                self.sent.append((copy, ok))
            else:
                self.send(
                    self.own.at[zi, 1 - place.x],
                    got.at[zi],
                    a_send.at[zi],
                    a_recv.at[zi],
                    place.flip_x(),
                    ok,
                )

    def cross_copy(self, zi):
        place = self.place
        return remote(
            self.own.at[zi, 1 - place.x],
            self.buffers[0].at[zi],
            self.sems[0].at[zi],
            self.sems[1].at[zi],
            place.flip_x(),
        )

    def cross(self, zi):
        self.cross_copy(zi).start()

    def crossed(self):
        for zi in range(self.place.depth):
            self.sent.append((self.cross_copy(zi), None))

    def along(self, k):
        place, depth = self.place, self.place.depth
        a_send, a_recv, z_send, z_recv = self.sems[0:4]
        held, line = self.buffers[0:2]
        for side, (zi, ok) in enumerate(self.wave(k)):
            block = held.at[zi]

            def body(zi=zi, side=side, block=block):
                remote(block, block, a_send.at[0], a_recv.at[zi], place.first()).wait_recv()
                if self.wide:
                    add_into(block, self.buffers[3].at[zi, 0], self.rows)
                else:
                    add_into(block, self.near_block(zi), self.rows)

                def more(direction):
                    slot = direction * depth + zi
                    term = line.at[depth if k == 0 and direction == 1 else zi]
                    remote(term, term, z_send.at[0], z_recv.at[slot], place.z_up()).wait_recv()
                    add_into(block, term, self.rows)

                def pass_on(direction, to):
                    slot = direction * depth + zi
                    there = line.at[depth if k == 1 and direction == 1 else zi]
                    remote(block, there, z_send.at[slot], z_recv.at[slot], to).start()

                if k == 0:
                    if not self.causal:
                        pl.when(place.down)(functools.partial(more, 0))
                    pl.when(place.up)(functools.partial(more, 1))
                elif side == 0:
                    pl.when(place.up)(functools.partial(more, 1))
                    pass_on(1, place.z_down())
                else:
                    pl.when(place.down)(functools.partial(more, 0))
                    pass_on(0, place.z_up())

            guard(ok, body)
            if k > 0:
                direction = 1 - side
                slot = direction * depth + zi
                to = place.z_up() if side == 1 else place.z_down()
                there = line.at[depth if k == 1 and direction == 1 else zi]
                copy = remote(block, there, z_send.at[slot], z_recv.at[slot], to)
                self.sent.append((copy, ok))

    def finish(self):
        self.out[...] = self.buffers[0][self.place.z].astype(self.out.dtype)

    def settle(self):
        for copy, condition in self.sent:
            guard(condition, copy.wait_send)


def drive_reduces(place, reduces):
    depth = place.depth
    order = list(range(depth - 1, -1, -1))
    for reduce in reduces:
        for k in order:
            reduce.cores(k) if reduce.wide else reduce.over_first(k)
    for step in range(depth + 2):
        for reduce in reduces:
            if not reduce.wide:
                if step < depth:
                    reduce.along(order[step])
                continue
            if step < depth:
                reduce.over_second(order[step])
            if 0 <= step - 1 < depth:
                reduce.over_first(order[step - 1])
            if 0 <= step - 2 < depth:
                reduce.along(order[step - 2])
    for reduce in reduces:
        reduce.finish()
    for reduce in reduces:
        reduce.settle()


def call_reduces(depth, collective_id, wides, owns):
    count = len(owns)
    blocks = [own.shape[-2:] for own in owns]
    parts = [Reduce.scratch(depth, wide, block) for wide, block in zip(wides, blocks)]
    scratch = []
    for buffers, sems in parts:
        scratch += buffers + sems

    def kernel(*refs):
        place = Place(depth)
        greet(place)
        reduces, used = [], 2 * count
        for number, (buffers, sems) in enumerate(parts):
            middle, end = used + len(buffers), used + len(buffers) + len(sems)
            reduces.append(
                Reduce(
                    place,
                    wides[number],
                    blocks[number][0],
                    refs[number],
                    refs[count + number],
                    refs[used:middle],
                    refs[middle:end],
                )
            )
            used = end
        drive_reduces(place, reduces)

    return pl.pallas_call(
        kernel,
        out_shape=[jax.ShapeDtypeStruct(block, F32) for block in blocks],
        in_specs=[pl.BlockSpec(memory_space=pltpu.VMEM)] * count,
        out_specs=[pl.BlockSpec(memory_space=pltpu.VMEM)] * count,
        scratch_shapes=scratch,
        compiler_params=pltpu.CompilerParams(
            collective_id=collective_id, has_side_effects=True, vmem_limit_bytes=VMEM_LIMIT
        ),
    )(*owns)


def end_kernel(depth, shapes, *refs):
    pack, wide, down, pack_out, wide_out, down_out = refs[:6]
    block, wide_block, down_block = shapes
    buffers, sems = Reduce.scratch(depth, True, block)
    used = 6 + len(buffers)
    place = Place(depth)
    count = 2 * depth
    partners = []
    for offset in range(1, count):
        partners.append((lax.rem(place.s + offset, count), place.f))
    greet(place, partners)
    reduce = Reduce(
        place, True, block[0], pack, pack_out, refs[6:used], refs[used : used + len(sems)]
    )
    used += len(sems)
    w_core, w_y, d_core, d_y = refs[used : used + 4]
    wc_send, wc_recv, wy_send, wy_recv, e_send, e_recv, e_sem = refs[used + 4 : used + 11]
    dc_send, dc_recv, dy_send, dy_recv = refs[used + 11 :]
    sent = []
    wide_rows, down_rows = wide_block[1], down_block[0]

    def send(src, dst, send_sem, recv_sem, device):
        copy = remote(src, dst, send_sem, recv_sem, device)
        copy.start()
        sent.append(copy)

    def landed(ref, recv_sem):
        remote(ref, ref, e_send.at[0], recv_sem, place.flip_c()).wait_recv()

    mine_y, other_y = place.y, 1 - place.y
    offsets = list(range(1, count)) + [0]
    for y in range(2):
        side = other_y if y == 0 else mine_y
        send(
            down.at[2 * side + 1 - place.c],
            d_core.at[side],
            dc_send.at[side],
            dc_recv.at[side],
            place.flip_c(),
        )
    for offset in offsets:
        to = lax.rem(place.s + offset, count)
        for y in range(2):
            send(
                wide.at[:, to, 2 * y + 1 - place.c],
                w_core.at[y, offset],
                wc_send.at[2 * offset + y],
                wc_recv.at[2 * offset + y],
                place.flip_c(),
            )
    order = list(range(depth - 1, -1, -1))
    for k in order:
        reduce.cores(k)

    def wide_add(target, term):
        for part in range(2):
            add_into(target.at[part], term.at[part], wide_rows)

    def wide_cores(offset):
        to = lax.rem(place.s + offset, count)
        for side in (other_y, mine_y):
            landed(w_core.at[side, offset], wc_recv.at[2 * offset + side])
            wide_add(w_core.at[side, offset], wide.at[:, to, 2 * side + place.c])
            if side is other_y:
                send(
                    w_core.at[side, offset],
                    w_y.at[offset],
                    wy_send.at[offset],
                    wy_recv.at[offset],
                    place.flip_y(),
                )

    def wide_across(offset):
        landed(w_y.at[offset], wy_recv.at[offset])
        wide_add(w_y.at[offset], w_core.at[mine_y, offset])
        to = lax.rem(place.s + offset, count)
        if offset > 0:
            send(
                w_y.at[offset],
                wide_out.at[place.s],
                e_send.at[offset],
                e_recv.at[offset],
                (to, place.f),
            )
        else:
            pltpu.make_async_copy(w_y.at[0], wide_out.at[place.s], e_sem.at[0]).start()

    for offset in offsets[: count // 2]:
        wide_cores(offset)
    for step in range(depth):
        reduce.over_second(order[step])
        if step >= 1:
            reduce.over_first(order[step - 1])
        if step == 0:
            for offset in offsets[count // 2 :]:
                wide_cores(offset)
            for side in (other_y, mine_y):
                landed(d_core.at[side], dc_recv.at[side])
                add_into(d_core.at[side], down.at[2 * side + place.c], down_rows)
                if side is other_y:
                    send(d_core.at[side], d_y.at[0], dy_send.at[0], dy_recv.at[0], place.flip_y())
        for offset in offsets[step * count // depth : (step + 1) * count // depth]:
            wide_across(offset)
        if step >= 2:
            reduce.along(order[step - 2])
    reduce.over_first(order[depth - 1])
    for step in range(max(depth - 2, 0), depth):
        reduce.along(order[step])
    reduce.finish()
    landed(d_y.at[0], dy_recv.at[0])
    down_out[...] = d_y[0].astype(F32) + d_core[mine_y].astype(F32)
    for offset in range(1, count):
        origin = lax.rem(place.s + count - offset, count)
        landed(wide_out.at[origin], e_recv.at[offset])
    pltpu.make_async_copy(w_y.at[0], wide_out.at[place.s], e_sem.at[0]).wait()
    reduce.settle()
    for copy in sent:
        copy.wait_send()


def call_end(depth, collective_id, pack, wide, down):
    count = 2 * depth
    block = pack.shape[-2:]
    wide_block = (2,) + wide.shape[-2:]
    down_block = down.shape[-2:]
    buffers, sems = Reduce.scratch(depth, True, block)
    scratch = buffers + sems
    scratch += [
        pltpu.VMEM((2, count) + wide_block, BF16),
        pltpu.VMEM((count,) + wide_block, BF16),
        pltpu.VMEM((2,) + down_block, BF16),
        pltpu.VMEM((1,) + down_block, BF16),
    ]
    scratch += [DMA((2 * count,)), DMA((2 * count,)), DMA((count,)), DMA((count,))]
    scratch += [DMA((count,)), DMA((count,)), DMA((1,))]
    scratch += [DMA((2,)), DMA((2,)), DMA((1,)), DMA((1,))]
    vmem = pl.BlockSpec(memory_space=pltpu.VMEM)
    return pl.pallas_call(
        functools.partial(end_kernel, depth, (block, wide_block, down_block)),
        out_shape=[
            jax.ShapeDtypeStruct(block, F32),
            jax.ShapeDtypeStruct((count,) + wide_block, BF16),
            jax.ShapeDtypeStruct(down_block, F32),
        ],
        in_specs=[vmem] * 3,
        out_specs=[vmem, vmem, vmem],
        scratch_shapes=scratch,
        compiler_params=pltpu.CompilerParams(
            collective_id=collective_id, has_side_effects=True, vmem_limit_bytes=VMEM_LIMIT
        ),
    )(pack, wide, down)


def forward_kernel(span, info, begin, query, key, value, mixed, lse, m_acc, l_acc, o_acc):
    rows = begin.shape[0]
    first_row, low, high = info[0], info[1], info[2]
    scale = HEAD_DIM ** (-0.5) * LOG2E
    m_acc[...] = jnp.full_like(m_acc, -1e30)
    l_acc[...] = jnp.zeros_like(l_acc)
    o_acc[...] = jnp.zeros_like(o_acc)
    places = first_row + lax.broadcasted_iota(jnp.int32, (rows, span), 0)
    offsets = lax.broadcasted_iota(jnp.int32, (rows, span), 1)

    def step(number, carry):
        base = pl.multiple_of(number * span, span)
        keys_at = base + offsets
        visible = jnp.logical_and(keys_at >= begin[...], keys_at <= places)
        for g in range(KV_HEADS):
            lanes = slice(g * HEAD_DIM, (g + 1) * HEAD_DIM)
            scores = lax.dot_general(
                query[g],
                key[pl.ds(base, span), lanes],
                (((1,), (1,)), ((), ())),
                preferred_element_type=F32,
            )
            scores = scores.reshape(GROUP, rows, span) * scale
            scores = jnp.where(visible[None], scores, -1e30).reshape(GROUP * rows, span)
            old = m_acc[g]
            new = jnp.maximum(old, jnp.max(scores, axis=-1, keepdims=True))
            weights = jnp.exp2(scores - new[:, :1])
            weights = jnp.where(
                visible[None], weights.reshape(GROUP, rows, span), 0.0
            ).reshape(GROUP * rows, span)
            fade = jnp.exp2(old - new)
            l_acc[g] = l_acc[g] * fade + jnp.sum(weights, axis=-1, keepdims=True)
            o_acc[g] = o_acc[g] * fade + jnp.dot(
                weights.astype(BF16),
                value[pl.ds(base, span), lanes],
                preferred_element_type=F32,
            )
            m_acc[g] = new
        return carry

    lax.fori_loop(low, high, step, 0)
    for g in range(KV_HEADS):
        mixed[g] = o_acc[g] / l_acc[g]
        lse[g] = m_acc[g] + jnp.log2(l_acc[g])


def call_forward(span, info, begin, query, key, value):
    stacked = query.shape[1]
    vmem = pl.BlockSpec(memory_space=pltpu.VMEM)
    return pl.pallas_call(
        functools.partial(forward_kernel, span),
        out_shape=[
            jax.ShapeDtypeStruct((KV_HEADS, stacked, HEAD_DIM), F32),
            jax.ShapeDtypeStruct((KV_HEADS, stacked, HEAD_DIM), F32),
        ],
        in_specs=[pl.BlockSpec(memory_space=pltpu.SMEM)] + [vmem] * 4,
        out_specs=[vmem, vmem],
        scratch_shapes=[pltpu.VMEM((KV_HEADS, stacked, HEAD_DIM), F32)] * 3,
        compiler_params=pltpu.CompilerParams(vmem_limit_bytes=VMEM_LIMIT),
    )(info, begin, query, key, value)


def backward_kernel(
    span, info, begin, query, key, value, mixed, lse, grad, dquery, dkeys, delta
):
    rows = begin.shape[0]
    first_row, low, high = info[0], info[1], info[2]
    scale = HEAD_DIM ** (-0.5) * LOG2E
    dquery[...] = jnp.zeros_like(dquery)
    width = KV_HEADS * HEAD_DIM
    for g in range(KV_HEADS):
        delta[g] = jnp.broadcast_to(
            jnp.sum(grad[g].astype(F32) * mixed[g], axis=-1, keepdims=True), delta.shape[1:]
        )
    places = first_row + lax.broadcasted_iota(jnp.int32, (rows, span), 0)
    offsets = lax.broadcasted_iota(jnp.int32, (rows, span), 1)

    def clear(number, carry):
        base = pl.multiple_of(number * span, span)
        dkeys[pl.ds(base, span), :] = jnp.zeros((span, dkeys.shape[1]), BF16)
        return carry

    lax.fori_loop(0, low, clear, 0)
    lax.fori_loop(high, dkeys.shape[0] // span, clear, 0)

    def step(number, carry):
        base = pl.multiple_of(number * span, span)
        keys_at = base + offsets
        visible = jnp.logical_and(keys_at >= begin[...], keys_at <= places)
        for g in range(KV_HEADS):
            lanes = slice(g * HEAD_DIM, (g + 1) * HEAD_DIM)
            key_rows = key[pl.ds(base, span), lanes]
            value_rows = value[pl.ds(base, span), lanes]
            scores = lax.dot_general(
                query[g], key_rows, (((1,), (1,)), ((), ())), preferred_element_type=F32
            )
            dprobs = lax.dot_general(
                grad[g], value_rows, (((1,), (1,)), ((), ())), preferred_element_type=F32
            )
            probs = jnp.exp2(scores * scale - lse[g][:, :1])
            probs = jnp.where(
                visible[None], probs.reshape(GROUP, rows, span), 0.0
            ).reshape(GROUP * rows, span)
            dscores = (probs * (dprobs - delta[g][:, :1])).astype(BF16)
            dquery[g] += jnp.dot(dscores, key_rows, preferred_element_type=F32)
            dkeys[pl.ds(base, span), lanes] = lax.dot_general(
                dscores, query[g], (((0,), (0,)), ((), ())), preferred_element_type=F32
            ).astype(BF16)
            dkeys[
                pl.ds(base, span), width + g * HEAD_DIM : width + (g + 1) * HEAD_DIM
            ] = lax.dot_general(
                probs.astype(BF16),
                grad[g],
                (((0,), (0,)), ((), ())),
                preferred_element_type=F32,
            ).astype(BF16)
        return carry

    lax.fori_loop(low, high, step, 0)


def call_backward(span, info, begin, query, key, value, mixed, lse, grad):
    stacked = query.shape[1]
    vmem = pl.BlockSpec(memory_space=pltpu.VMEM)
    return pl.pallas_call(
        functools.partial(backward_kernel, span),
        out_shape=[
            jax.ShapeDtypeStruct((KV_HEADS, stacked, HEAD_DIM), F32),
            jax.ShapeDtypeStruct((key.shape[0], 2 * key.shape[1]), BF16),
        ],
        in_specs=[pl.BlockSpec(memory_space=pltpu.SMEM)] + [vmem] * 7,
        out_specs=[vmem, vmem],
        scratch_shapes=[pltpu.VMEM((KV_HEADS, stacked, HEAD_DIM), F32)],
        compiler_params=pltpu.CompilerParams(vmem_limit_bytes=VMEM_LIMIT),
    )(info, begin, query, key, value, mixed, lse, grad)


class Exchange:
    def __init__(self, place, own, out, sems):
        self.place, self.own, self.out, self.sems = place, own, out, sems
        self.count = 2 * place.depth
        self.sent = []
        self.y_f = place.f + 2 - 4 * place.y
        self.c_f = place.f + 1 - 2 * place.c
        self.yc_f = self.y_f + 1 - 2 * place.c

    @staticmethod
    def semaphores(depth):
        count = 2 * depth
        return [
            DMA((1,)),
            DMA((count,)),
            DMA((count,)),
            DMA((count,)),
            DMA((count,)),
            DMA((2 * count,)),
            DMA((2 * count,)),
        ]

    def send(self, block, send_sem, recv_sem, device, source=None):
        copy = remote(block if source is None else source, block, send_sem, recv_sem, device)
        copy.start()
        self.sent.append(copy)

    def block(self, offset, owner):
        origin = lax.rem(self.place.s + self.count - offset, self.count)
        return self.out.at[:, origin, owner]

    def landed(self, block, recv_sem):
        remote(block, block, self.sems[1].at[0], recv_sem, self.place.flip_c()).wait_recv()

    def local(self):
        return pltpu.make_async_copy(
            self.own.at[:, self.place.s], self.block(0, self.place.f), self.sems[0].at[0]
        )

    def depart(self, offset):
        place = self.place
        to = lax.rem(place.s + offset, self.count)
        self.send(
            self.block(0, place.f),
            self.sems[1].at[offset],
            self.sems[2].at[offset],
            (to, place.f),
            self.own.at[:, to],
        )

    def onward(self, offset):
        place = self.place
        block = self.block(offset, place.f)
        if offset > 0:
            self.landed(block, self.sems[2].at[offset])
        self.send(block, self.sems[3].at[offset], self.sems[4].at[offset], place.flip_y())
        slot = 2 * offset
        self.send(block, self.sems[5].at[slot], self.sems[6].at[slot], place.flip_c())

    def sideways(self, offset):
        block = self.block(offset, self.y_f)
        self.landed(block, self.sems[4].at[offset])
        slot = 2 * offset + 1
        self.send(block, self.sems[5].at[slot], self.sems[6].at[slot], self.place.flip_c())

    def last(self, offset):
        self.landed(self.block(offset, self.c_f), self.sems[6].at[2 * offset])
        self.landed(self.block(offset, self.yc_f), self.sems[6].at[2 * offset + 1])

    def settle(self):
        for copy in self.sent:
            copy.wait_send()


class Quarter:
    def __init__(self, place, own, out, sems):
        self.place, self.own, self.out, self.sems = place, own, out, sems
        self.sent = []

    @staticmethod
    def semaphores():
        return [DMA((1,)), DMA((3,)), DMA((3,))]

    def local(self):
        return pltpu.make_async_copy(self.own, self.out.at[self.place.f], self.sems[0].at[0])

    def send(self, source, block, slot, device):
        copy = remote(source, block, self.sems[1].at[slot], self.sems[2].at[slot], device)
        copy.start()
        self.sent.append(copy)

    def depart(self):
        place = self.place
        self.send(self.own, self.out.at[place.f], 0, place.flip_y())
        self.send(self.own, self.out.at[place.f], 1, place.flip_c())

    def landed(self, owner, slot):
        block = self.out.at[owner]
        remote(block, block, self.sems[1].at[0], self.sems[2].at[slot], self.place.flip_c()).wait_recv()

    def sideways(self):
        place = self.place
        y_f = place.f + 2 - 4 * place.y
        self.landed(y_f, 0)
        self.send(self.out.at[y_f], self.out.at[y_f], 2, place.flip_c())

    def last(self):
        place = self.place
        self.landed(place.f + 1 - 2 * place.c, 1)
        self.landed(place.f + 2 - 4 * place.y + 1 - 2 * place.c, 2)

    def settle(self):
        for copy in self.sent:
            copy.wait_send()


def stage(gather, step):
    depth = gather.place.depth
    if step < depth:
        gather.arrive(step)
    if 0 <= step - 1 < depth:
        gather.across(step - 1)
    if gather.wide and 0 <= step - 2 < depth:
        gather.hand(step - 2)
    if gather.wide and 0 <= step - 3 < depth:
        gather.take(step - 3)


def turned(vector, cosine, sine):
    return vector * cosine + pltpu.roll(vector, HEAD_DIM // 2, 1) * sine


HEAD_PLAN = {
    "z": ("d1", "d2"),
    "gap": ("d7", "n0", "d5"),
    "kv0": ("o0",),
    "kv": ("d6", "o1"),
    "a0": ("c0",),
    "a1": ("o2",),
    "a2": ("n2", "d4", "o3", "d3", "o4", "c1"),
    "a3": ("o5",),
    "b": ("n5", "n7", "o6"),
    "e": ("s5", "h0", "n3", "c2", "s7", "s0", "n1", "h1", "D", "h2", "n6", "n4", "s3", "s1", "c3", "S", "s2", "h3", "s6", "s4", "c4", "h4"),
}
HEAD_INS = 12
HEAD_OUTS = 13


def head_kernel(depth, *refs):
    (o_own, q_own, k_own, v_own, small_own, gate_own, up_own, down_own) = refs[:8]
    (tokens, cot, angles, begin) = refs[8:HEAD_INS]
    (
        pack_out,
        o_out,
        kv_out,
        cot_out,
        wide_out,
        down_out,
        hidden_out,
        queries,
        mixed,
        lse,
        middle,
        hidden_one,
        mixed_low,
    ) = refs[HEAD_INS : HEAD_INS + HEAD_OUTS]
    vectors = refs[HEAD_INS + HEAD_OUTS]
    rest = refs[HEAD_INS + HEAD_OUTS + 1 :]
    pack_all, o_all, kv_all, kv_own, hidden_two, lin, m_acc, l_acc, o_acc = rest[:9]
    pack, wide, down = rest[9:12]
    sems = list(rest[12:])
    cosine, sine = angles.at[0], angles.at[1]

    def take(count):
        taken = sems[:count]
        del sems[:count]
        return taken

    wide_need = len(Gather.semaphores(depth, True))
    line_need = len(Gather.semaphores(depth, False))
    count = 2 * depth
    devices = 4 * count
    rows, model = tokens.shape
    query_width, key_width = HEADS * HEAD_DIM, KV_HEADS * HEAD_DIM
    qkv_width = query_width + 2 * key_width

    place = Place(depth)
    at = 0
    for source in (q_own, k_own, v_own, small_own):
        width = source.shape[1]
        pack[:, at : at + width] = source[...]
        at += width
    greet(place, [(lax.rem(place.s + offset, count), place.f) for offset in range(1, count)])
    g_pack = Gather(place, True, pack, pack_all, take(wide_need))
    g_o = Gather(place, True, o_own, o_all, take(wide_need))
    g_kv = Gather(place, True, kv_own, kv_all, take(wide_need))
    g_cot = Gather(place, False, cot, cot_out, take(line_need + 2), True)
    g_hidden = Gather(place, False, hidden_two, hidden_out, take(line_need))
    x_wide = Exchange(place, wide, wide_out, take(len(Exchange.semaphores(depth))))
    x_down = Quarter(place, down, down_out, take(len(Quarter.semaphores())))
    (out_sem,) = take(1)

    g_pack.arrive(0)
    few = down_own.shape[0]
    filled = down.shape[0]
    for side, source in enumerate((gate_own, up_own)):
        for to in range(count):
            parts = []
            for owner in range(4):
                low = (4 * to + owner) * few
                parts.append(source[:, low : low + few])
                parts.append(jnp.zeros((wide.shape[2], filled - few), BF16))
            wide[side, to] = jnp.concatenate(parts, axis=1)
    down[...] = jnp.concatenate(
        [down_own[...], jnp.zeros((filled - few, model), BF16)], axis=0
    )
    locals_ = [job.local() for job in (g_pack, g_o, g_cot, x_wide, x_down)]
    for copy in locals_:
        copy.start()
    inputs = tokens[...].astype(F32)
    inv_one = lax.rsqrt(jnp.mean(inputs * inputs, axis=-1, keepdims=True) + EPSILON)
    share = key_width // devices
    chosen = lax.broadcasted_iota(jnp.int32, (model, key_width), 1)
    chosen = lax.div(chosen, share) * (model // devices) + lax.rem(chosen, share)
    chosen = (lax.broadcasted_iota(jnp.int32, (model, key_width), 0) == chosen).astype(BF16)
    for copy in locals_:
        copy.wait()
    jobs = {"o": g_o, "c": g_cot, "h": g_hidden}
    moves = {"d": x_wide.depart, "n": x_wide.onward, "s": x_wide.sideways}

    def follow(spot):
        for word in HEAD_PLAN[spot]:
            if word == "D":
                x_down.depart()
            elif word == "S":
                x_down.sideways()
            elif word[0] in jobs:
                stage(jobs[word[0]], int(word[1:]))
            else:
                moves[word[0]](int(word[1:]))

    for step in range(1, depth):
        stage(g_pack, step)
    follow("z")
    stage(g_pack, depth)
    follow("gap")
    stage(g_pack, depth + 1)
    stage(g_pack, depth + 2)

    small = pack_all[:, :, :, :, :, qkv_width:].reshape(model, 128).astype(F32).T
    vectors[...] = small[:8]
    spread = jnp.dot(small[:8].astype(BF16), chosen, preferred_element_type=F32)
    hidden_one[...] = (inputs * inv_one * small[0:1]).astype(BF16)
    part = model // depth
    for zi in range(depth):
        weights = pack_all[zi][:, :, :, :, :qkv_width].reshape(part, qkv_width)
        term = jnp.dot(
            hidden_one[:, zi * part : (zi + 1) * part], weights, preferred_element_type=F32
        )
        if zi == 0:
            lin[...] = term
        else:
            lin[...] += term
    for g in range(KV_HEADS):
        lanes = slice(query_width + g * HEAD_DIM, query_width + (g + 1) * HEAD_DIM)
        own = slice(g * HEAD_DIM, (g + 1) * HEAD_DIM)
        head = lin[:, lanes] + spread[2:3, own]
        kv_own[:, own] = turned(head, cosine[...], sine[...]).astype(BF16)
    values = lin[:, query_width + key_width :] + spread[3:4]
    kv_own[:, key_width:] = values.astype(BF16)
    kv_local = g_kv.local()
    kv_local.start()
    g_kv.arrive(0)
    follow("kv0")
    for h in range(HEADS):
        lanes = slice(h * HEAD_DIM, (h + 1) * HEAD_DIM)
        at = (h % GROUP) * rows
        head = lin[:, lanes] + small[1:2, lanes]
        queries[h // GROUP, at : at + rows, :] = turned(head, cosine[...], sine[...]).astype(BF16)
    kv_local.wait()
    for step in range(1, depth + 3):
        stage(g_kv, step)
        if step == depth:
            follow("kv")

    span = 4 * rows
    scale = HEAD_DIM ** (-0.5) * LOG2E
    m_acc[...] = jnp.full_like(m_acc, -1e30)
    l_acc[...] = jnp.zeros_like(l_acc)
    o_acc[...] = jnp.zeros_like(o_acc)
    first_row = (place.s * 4 + place.f) * rows
    places = first_row + lax.broadcasted_iota(jnp.int32, (rows, span), 0)
    offsets = lax.broadcasted_iota(jnp.int32, (rows, span), 1)

    def attend(number, carry):
        keys_at = number * span + offsets
        visible = jnp.logical_and(keys_at >= begin[...], keys_at <= places)
        block = kv_all.at[lax.div(number, 2), lax.rem(number, 2)]
        for g in range(KV_HEADS):
            key = block[:, :, :, g * HEAD_DIM : (g + 1) * HEAD_DIM].reshape(span, HEAD_DIM)
            value = block[
                :, :, :, key_width + g * HEAD_DIM : key_width + (g + 1) * HEAD_DIM
            ].reshape(span, HEAD_DIM)
            scores = lax.dot_general(
                queries[g], key, (((1,), (1,)), ((), ())), preferred_element_type=F32
            )
            scores = scores.reshape(GROUP, rows, span) * scale
            scores = jnp.where(visible[None], scores, -1e30).reshape(GROUP * rows, span)
            old = m_acc[g]
            new = jnp.maximum(old, jnp.max(scores, axis=-1, keepdims=True))
            weights = jnp.exp2(scores - new[:, :1])
            weights = jnp.where(
                visible[None], weights.reshape(GROUP, rows, span), 0.0
            ).reshape(GROUP * rows, span)
            fade = jnp.exp2(old - new)
            l_acc[g] = l_acc[g] * fade + jnp.sum(weights, axis=-1, keepdims=True)
            o_acc[g] = o_acc[g] * fade + jnp.dot(
                weights.astype(BF16), value, preferred_element_type=F32
            )
            m_acc[g] = new
        return carry

    pieces = 4
    for piece in range(pieces):
        follow("a%d" % piece)
        low, high = piece * count // pieces, (piece + 1) * count // pieces
        lax.fori_loop(
            jnp.minimum(low, place.s + 1), jnp.minimum(high, place.s + 1), attend, 0
        )
    follow("b")
    for g in range(KV_HEADS):
        total = o_acc[g] / l_acc[g]
        mixed[g] = total
        lse[g] = m_acc[g] + jnp.log2(l_acc[g])
        for j in range(GROUP):
            lanes = slice((g * GROUP + j) * HEAD_DIM, (g * GROUP + j + 1) * HEAD_DIM)
            mixed_low[:, lanes] = total[j * rows : (j + 1) * rows].astype(BF16)
    after = inputs
    for zi in range(depth):
        after = after + jnp.dot(
            mixed_low[:, zi * part : (zi + 1) * part],
            o_all[zi].reshape(part, model),
            preferred_element_type=F32,
        )
    middle[...] = after
    inv_two = lax.rsqrt(jnp.mean(after * after, axis=-1, keepdims=True) + EPSILON)
    hidden_two[...] = (after * inv_two * small[4:5]).astype(BF16)
    hidden_local = g_hidden.local()
    hidden_local.start()

    keeps = []
    for number, (source, target) in enumerate(
        ((pack_all, pack_out), (o_all, o_out), (kv_all, kv_out))
    ):
        copy = pltpu.make_async_copy(source, target, out_sem.at[number])
        copy.start()
        keeps.append(copy)
    follow("e")
    hidden_local.wait()
    for offset in range(count):
        x_wide.last(offset)
    x_down.last()
    for copy in keeps:
        copy.wait()
    for job in (g_pack, g_o, g_kv, g_cot, g_hidden, x_wide, x_down):
        job.settle()


def call_head(depth, collective_id, hbm, vmems):
    (o_own,) = hbm
    q_own, k_own, v_own, small_own, gate_own, _, down_own, tokens, cot = vmems[:9]
    count = 2 * depth
    few = down_own.shape[0]
    filled = -(-few // 16) * 16
    width = q_own.shape[1] + k_own.shape[1] + v_own.shape[1] + small_own.shape[1]
    pack = jax.ShapeDtypeStruct((q_own.shape[0], width), BF16)
    wide = jax.ShapeDtypeStruct((2, count, gate_own.shape[0], 4 * filled), BF16)
    down = jax.ShapeDtypeStruct((filled, down_own.shape[1]), BF16)
    rows, model = tokens.shape
    key_width = KV_HEADS * HEAD_DIM
    stacked = GROUP * rows
    kv_own = jax.ShapeDtypeStruct((rows, 2 * key_width), BF16)
    any_, vmem = pl.BlockSpec(memory_space=pl.ANY), pl.BlockSpec(memory_space=pltpu.VMEM)
    heads = (KV_HEADS, stacked, HEAD_DIM)
    outs = [
        gather_shape(depth, True, pack),
        gather_shape(depth, True, o_own),
        gather_shape(depth, True, kv_own),
        gather_shape(depth, False, cot),
        jax.ShapeDtypeStruct((2, count, 4) + wide.shape[2:], BF16),
        jax.ShapeDtypeStruct((4,) + down.shape, BF16),
        gather_shape(depth, False, tokens),
        jax.ShapeDtypeStruct(heads, BF16),
        jax.ShapeDtypeStruct(heads, F32),
        jax.ShapeDtypeStruct(heads, F32),
        jax.ShapeDtypeStruct((rows, model), F32),
        jax.ShapeDtypeStruct((rows, model), BF16),
        jax.ShapeDtypeStruct((rows, model), BF16),
        jax.ShapeDtypeStruct((8, model), F32),
    ]
    scratch = [pltpu.VMEM(out.shape, BF16) for out in outs[:3]]
    scratch += [
        pltpu.VMEM(kv_own.shape, BF16),
        pltpu.VMEM((rows, model), BF16),
        pltpu.VMEM((rows, (HEADS + 2 * KV_HEADS) * HEAD_DIM), F32),
        pltpu.VMEM(heads, F32),
        pltpu.VMEM(heads, F32),
        pltpu.VMEM(heads, F32),
        pltpu.VMEM(pack.shape, BF16),
        pltpu.VMEM(wide.shape, BF16),
        pltpu.VMEM(down.shape, BF16),
    ]
    scratch += Gather.semaphores(depth, True) * 3
    scratch += Gather.semaphores(depth, False, True) + Gather.semaphores(depth, False)
    scratch += Exchange.semaphores(depth) + Quarter.semaphores() + [DMA((3,))]
    return pl.pallas_call(
        functools.partial(head_kernel, depth),
        out_shape=outs,
        in_specs=[any_] + [vmem] * len(vmems),
        out_specs=[any_] * 7 + [vmem] * 7,
        scratch_shapes=scratch,
        compiler_params=pltpu.CompilerParams(
            collective_id=collective_id, has_side_effects=True, vmem_limit_bytes=VMEM_LIMIT
        ),
    )(*hbm, *vmems)


def t_mul(left, right):
    return lax.dot_general(left, right, (((0,), (0,)), ((), ())), preferred_element_type=F32)


def mul_t(left, right):
    return lax.dot_general(left, right, (((1,), (1,)), ((), ())), preferred_element_type=F32)


CUTS = ((0, 512), (512, 1024), (1024, 1152))


def middle_kernel(depth, *refs):
    (hidden_all, cot_all, wide_all, down_all, o_own) = refs[:5]
    (middle, cotangent, vectors) = refs[5:8]
    (layer_out, d_middle, d_mixed, d_branch, gain_two, down_out, wide_out) = refs[8:15]
    (tokens_v, grads_v, w_part, d_part, act, d_gate, d_up, dh_part, out_part) = refs[15:24]
    (dh_sum, out_sum, w_core, w_y, d_core, o_all) = refs[24:30]
    rest = list(refs[30:])

    def take(count):
        taken = rest[:count]
        del rest[:count]
        return taken

    count = 2 * depth
    rows, model = middle.shape
    units = act.shape[2]
    part = model // depth
    buffers, sems = Reduce.scratch(depth, False, (rows, model))
    place = Place(depth)
    greet(place)
    r_dh = Reduce(place, False, rows, dh_part, dh_sum, take(len(buffers)), take(len(sems)))
    r_out = Reduce(place, False, rows, out_part, out_sum, take(len(buffers)), take(len(sems)))
    load_sem, wc_send, wc_recv, wy_send, wy_recv, dc_send, dc_recv = take(7)
    sent = []

    def send(src, dst, send_sem, recv_sem, device):
        copy = remote(src, dst, send_sem, recv_sem, device)
        copy.start()
        sent.append(copy)

    def landed(ref, recv_sem):
        remote(ref, ref, wc_send.at[0], recv_sem, place.flip_c()).wait_recv()

    loads = [
        pltpu.make_async_copy(source, target, load_sem.at[number])
        for number, (source, target) in enumerate(
            (
                (hidden_all, tokens_v),
                (wide_all, w_part),
                (cot_all, grads_v),
                (down_all, d_part),
            )
        )
    ]
    for copy in loads:
        copy.start()
    mine_y, other_y = place.y, 1 - place.y
    wide_rows = w_part.shape[-2]
    half = lax.div(place.z, 2)
    tiles = [3 - 3 * half, 2 - half, 1 + 4 * half - place.z, place.z]
    for copy in loads:
        copy.wait()

    def weights(side, low, high):
        return w_part[side, :, :, :, :, low:high].reshape(model, high - low)

    def forward(zi):
        tokens = tokens_v[zi].reshape(2 * rows, model)
        grads = grads_v[zi].reshape(2 * rows, model)
        out = None
        for low, high in CUTS:
            gate = jnp.dot(tokens, weights(0, low, high), preferred_element_type=F32)
            up = jnp.dot(tokens, weights(1, low, high), preferred_element_type=F32)
            d_act = mul_t(grads, d_part[low:high, :])
            sigma = jax.nn.sigmoid(gate)
            silu = gate * sigma
            act[zi, :, low:high] = (silu * up).astype(BF16)
            d_gate[zi, :, low:high] = (
                d_act * up * sigma * (1.0 + gate * (1.0 - sigma))
            ).astype(BF16)
            d_up[zi, :, low:high] = (d_act * silu).astype(BF16)
        total = mul_t(d_gate[zi], weights(0, 0, units)) + mul_t(d_up[zi], weights(1, 0, units))
        dh_part[zi] = total.astype(BF16).reshape(2, rows, model)
        out = jnp.dot(act[zi], d_part[...], preferred_element_type=F32)
        out_part[zi] = out.astype(BF16).reshape(2, rows, model)

    def tile(number, carry):
        zi = jnp.where(
            number == 0,
            tiles[0],
            jnp.where(number == 1, tiles[1], jnp.where(number == 2, tiles[2], tiles[3])),
        )
        forward(zi)
        r_dh.cross(zi)
        return carry

    lax.fori_loop(0, depth, tile, 0)
    for zi in tiles:
        r_out.cross(zi)
    r_dh.crossed()
    r_out.crossed()

    def wide_chunk(k, carry):
        lanes = pl.ds(pl.multiple_of(k * part, part), part)
        tokens = tokens_v[:, :, :, lanes].reshape(count * rows, part)
        for side, grad in enumerate((d_gate, d_up)):
            term = t_mul(tokens, grad[...].reshape(count * rows, units)).astype(BF16)
            w_part[side, pl.ds(2 * k, 2)] = term.reshape(2, 2, 2, wide_rows, units)
        for step in range(2):
            to = 2 * k + step
            for y in range(2):
                remote(
                    w_part.at[:, to, y, 1 - place.c],
                    w_core.at[y, to],
                    wc_send.at[2 * to + y],
                    wc_recv.at[2 * to + y],
                    place.flip_c(),
                ).start()
        return carry

    def wide_cores(to):
        for y in (other_y, mine_y):
            landed(w_core.at[y, to], wc_recv.at[2 * to + y])
            for side in range(2):
                add_into(
                    w_core.at[y, to, side], w_part.at[side, to, y, place.c], wide_rows
                )
            if y is other_y:
                remote(
                    w_core.at[y, to], w_y.at[to], wy_send.at[to], wy_recv.at[to], place.flip_y()
                ).start()

    def wide_across(to, carry):
        landed(w_y.at[to], wy_recv.at[to])
        for side in range(2):
            add_into(w_y.at[to, side], w_core.at[mine_y, to, side], wide_rows)
        pltpu.make_async_copy(w_y.at[to], wide_out.at[to], load_sem.at[to]).start()
        return carry

    def wide_step(k, carry):
        wide_chunk(k, 0)
        pl.when(k > 0)(lambda: wide_cores(2 * k - 2))
        pl.when(k > 0)(lambda: wide_cores(2 * k - 1))
        return carry

    order = list(range(depth - 1, -1, -1))
    lax.fori_loop(0, depth - 2, wide_step, 0)
    r_dh.along(order[0])
    r_dh.along(order[1])
    lax.fori_loop(depth - 2, depth, wide_step, 0)
    wide_cores(count - 2)
    wide_cores(count - 1)
    r_dh.along(order[2])
    pieces = [
        pltpu.make_async_copy(o_own.at[zi], o_all.at[zi % 2], load_sem.at[zi])
        for zi in range(depth)
    ]
    for copy in pieces[:2]:
        copy.start()

    def down_chunk(k, carry):
        lanes = pl.ds(pl.multiple_of(k * part, part), part)
        grads = grads_v[:, :, :, lanes].reshape(count * rows, part)
        d_part[:, lanes] = t_mul(act[...].reshape(count * rows, units), grads).astype(BF16)
        return carry

    lax.fori_loop(0, depth, down_chunk, 0)
    down_rows = units // 4

    def down_block(owner):
        return d_part.at[pl.ds(pl.multiple_of(owner * down_rows, down_rows), down_rows)]

    for y in (other_y, mine_y):
        send(
            down_block(2 * y + 1 - place.c),
            d_core.at[y],
            dc_send.at[y],
            dc_recv.at[y],
            place.flip_c(),
        )
    r_dh.along(order[3])
    r_dh.finish()

    after = middle[...]
    inv_two = lax.rsqrt(jnp.mean(after * after, axis=-1, keepdims=True) + EPSILON)
    normed = after * inv_two
    d_hidden = dh_sum[...]
    gain_two[...] = jnp.broadcast_to(
        jnp.sum(d_hidden * normed, axis=0, keepdims=True), gain_two.shape
    )
    scaled = d_hidden * vectors[4:5]
    total = cotangent[...].astype(F32) + inv_two * (
        scaled - normed * jnp.mean(scaled * normed, axis=-1, keepdims=True)
    )
    d_middle[...] = total
    d_branch[...] = total.astype(BF16)
    for zi in range(depth):
        pieces[zi].wait()
        term = mul_t(d_branch[...], o_all[zi % 2].reshape(part, model)).astype(BF16)
        for piece in range(part // HEAD_DIM):
            h = zi * (part // HEAD_DIM) + piece
            at = (h % GROUP) * rows
            d_mixed[h // GROUP, at : at + rows, :] = term[
                :, piece * HEAD_DIM : (piece + 1) * HEAD_DIM
            ]
        if zi + 2 < depth:
            pieces[zi + 2].start()
    for y in (other_y, mine_y):
        landed(d_core.at[y], dc_recv.at[y])
        add_into(d_core.at[y], down_block(2 * y + place.c), down_rows)
    keep = pltpu.make_async_copy(d_core, down_out, load_sem.at[count])
    keep.start()
    for step in range(depth):
        r_out.along(order[step])
        lax.fori_loop(2 * step, 2 * step + 2, wide_across, 0)
    r_out.finish()
    layer_out[...] = (middle[...] + out_sum[...]).astype(BF16)
    keep.wait()

    def end(to, carry):
        pltpu.make_async_copy(w_y.at[to], wide_out.at[to], load_sem.at[to]).wait()
        for y in range(2):
            slot = 2 * to + y
            remote(
                w_core.at[y, to], w_core.at[y, to], wc_send.at[slot], wc_recv.at[slot], place.flip_c()
            ).wait_send()
        remote(
            w_y.at[to], w_y.at[to], wy_send.at[to], wy_recv.at[to], place.flip_y()
        ).wait_send()
        return carry

    lax.fori_loop(0, count, end, 0)
    r_dh.settle()
    r_out.settle()
    for copy in sent:
        copy.wait_send()


def call_middle(depth, collective_id, hbm, vmems):
    hidden, cot, wide, down, o_all = hbm
    count = 2 * depth
    rows, model = vmems[0].shape
    units, wide_rows = wide.shape[-1], wide.shape[-2]
    any_, vmem = pl.BlockSpec(memory_space=pl.ANY), pl.BlockSpec(memory_space=pltpu.VMEM)
    buffers, sems = Reduce.scratch(depth, False, (rows, model))
    scratch = [pltpu.VMEM((depth, 2, rows, model), BF16)] * 2
    scratch += [pltpu.VMEM(wide.shape, BF16), pltpu.VMEM(down.shape, BF16)]
    scratch += [pltpu.VMEM((depth, 2 * rows, units), BF16)] * 3
    scratch += [pltpu.VMEM((depth, 2, rows, model), BF16)] * 2
    scratch += [pltpu.VMEM((rows, model), F32)] * 2
    scratch += [
        pltpu.VMEM((2, count, 2, wide_rows, units), BF16),
        pltpu.VMEM((count, 2, wide_rows, units), BF16),
        pltpu.VMEM((2, units // 4, model), BF16),
        pltpu.VMEM((2,) + o_all.shape[1:], BF16),
    ]
    scratch += buffers + sems + buffers + sems
    scratch += [DMA((count + 1,)), DMA((2 * count,)), DMA((2 * count,))]
    scratch += [DMA((count,)), DMA((count,)), DMA((2,)), DMA((2,))]
    return pl.pallas_call(
        functools.partial(middle_kernel, depth),
        out_shape=[
            jax.ShapeDtypeStruct((rows, model), BF16),
            jax.ShapeDtypeStruct((rows, model), F32),
            jax.ShapeDtypeStruct((KV_HEADS, GROUP * rows, HEAD_DIM), BF16),
            jax.ShapeDtypeStruct((rows, model), BF16),
            jax.ShapeDtypeStruct((8, model), F32),
            jax.ShapeDtypeStruct((2, units // 4, model), BF16),
            jax.ShapeDtypeStruct((count, 2, wide_rows, units), BF16),
        ],
        in_specs=[any_] * 5 + [vmem] * 3,
        out_specs=[vmem] * 5 + [any_] * 2,
        scratch_shapes=scratch,
        compiler_params=pltpu.CompilerParams(
            collective_id=collective_id, has_side_effects=True, vmem_limit_bytes=VMEM_JOINED
        ),
    )(*hbm, *vmems)


LAST_PLAN = (
    ("down", "d7", "delta", "out", "d1", "d5", "a0", "Ck0", "a1"),
    ("d6", "a2", "d3", "Co2", "Bk0", "Co0", "d4", "a3", "d2"),
    ("Ck3", "Co1", "Bo2", "Bo0", "Ck2", "Bo1", "turn", "Ck1", "Co3"),
    ("query", "Bk1", "Ak0", "Ao0", "hq", "Bk2", "Bk3", "Zk0", "Cq0"),
    ("Bo3", "Ak1", "Bq0", "Ak3", "Ak2", "Zk1", "Cq2", "Ao1", "Ao2"),
    ("Zo0", "Zk2", "Cq1", "Bq2", "Zo1", "Zk3", "Bq1", "key", "Cq3"),
    ("Zo2", "hk", "Aq0", "Bq3", "Ao3", "small", "Cs0", "Aq1", "Zq0"),
    ("Cs1", "input", "Aq2", "Zq1", "Cs2", "Cs3", "Bs0", "Zo3", "Bs1"),
    ("Aq3", "Zq2", "As0", "Bs2", "Zs0", "As1", "Zq3", "Bs3", "Zs1"),
    ("As2", "Zs2", "As3", "Zs3"),
)


def follow_last(plan, works, depart, attend_wave, jobs):
    depth = 4
    steps = {"C": "cores", "B": "over_second", "A": "over_first", "Z": "along"}
    for words in plan:
        for word in words:
            if word in works:
                works[word]()
            elif word[0] == "d":
                depart(int(word[1:]))
            elif word[0] == "a":
                attend_wave(int(word[1:]))
            else:
                getattr(jobs[word[1]], steps[word[0]])(depth - 1 - int(word[2:]))


def last_kernel(depth, *refs):
    (kv_own, pack_own, wide, down) = refs[:4]
    (queries, mixed, lse, d_mixed, angles, begin) = refs[4:10]
    (tokens, d_middle, vectors, gain_two, hidden_one, mixed_low, d_branch) = refs[10:17]
    (input_grad, q_out, kvs_out, o_out, down_out, wide_out) = refs[17:23]
    (kv_all, weights, d_query, delta, d_lin, d_keys, d_kv, o_part, q_part, kvs_part) = refs[23:33]
    d_near, d_far, d_hidden, kv_weights = refs[33:37]
    rest = list(refs[37:])
    cosine, sine = angles.at[0], angles.at[1]

    def take(number):
        taken = rest[:number]
        del rest[:number]
        return taken

    count = 2 * depth
    devices = 4 * count
    rows, model = tokens.shape
    part = model // depth
    query_width, key_width = HEADS * HEAD_DIM, KV_HEADS * HEAD_DIM
    qkv_width = query_width + 2 * key_width
    model_rows = model // devices
    share = key_width // devices
    span = 4 * rows
    score_scale = HEAD_DIM ** (-0.5)
    scale = score_scale * LOG2E

    place = Place(depth)
    greet(place, [(lax.rem(place.s + offset, count), place.f) for offset in range(1, count)])

    def reduce_of(own, out, causal=False):
        block = own.shape[-2:]
        buffers, sems = Reduce.scratch(depth, True, block)
        return Reduce(
            place,
            True,
            block[0],
            own,
            out,
            take(len(buffers)),
            take(len(sems)),
            causal=causal,
        )

    r_kv = reduce_of(d_keys, d_kv, True)
    r_o = reduce_of(o_part, o_out)
    r_q = reduce_of(q_part, q_out)
    r_kvs = reduce_of(kvs_part, kvs_out)
    load_sem, e_send, e_recv, y_send, y_recv = take(5)
    order = list(range(depth - 1, -1, -1))
    sent = []

    def depart(offset):
        to = lax.rem(place.s + offset, count)
        copy = remote(
            wide.at[to], wide_out.at[place.s], e_send.at[offset], e_recv.at[offset], (to, place.f)
        )
        copy.start()
        sent.append(copy)

    kv_load = pltpu.make_async_copy(kv_own, kv_all, load_sem.at[0])
    kv_load.start()
    own_wide = pltpu.make_async_copy(wide.at[place.s], wide_out.at[place.s], load_sem.at[1])
    own_wide.start()
    down_load = pltpu.make_async_copy(down.at[place.y], d_near, load_sem.at[2 + depth])
    down_load.start()
    down_copy = remote(
        down.at[1 - place.y], d_far, y_send.at[0], y_recv.at[0], place.flip_y()
    )
    loads = [
        pltpu.make_async_copy(pack_own.at[zi], weights.at[zi % 2], load_sem.at[2 + zi])
        for zi in range(depth)
    ]

    first_row = (place.s * 4 + place.f) * rows
    places = first_row + lax.broadcasted_iota(jnp.int32, (rows, span), 0)
    offsets = lax.broadcasted_iota(jnp.int32, (rows, span), 1)

    def attend(number, carry):
        keys_at = number * span + offsets
        visible = jnp.logical_and(keys_at >= begin[...], keys_at <= places)
        z, x = lax.div(number, 2), lax.rem(number, 2)
        block = kv_all.at[z, x]
        target = d_keys.at[z, x]
        for g in range(KV_HEADS):
            lanes = slice(g * HEAD_DIM, (g + 1) * HEAD_DIM)
            others = slice(key_width + g * HEAD_DIM, key_width + (g + 1) * HEAD_DIM)
            key = block[:, :, :, lanes].reshape(span, HEAD_DIM)
            value = block[:, :, :, others].reshape(span, HEAD_DIM)
            scores = mul_t(queries[g], key)
            d_probs = mul_t(d_mixed[g], value)
            probs = jnp.exp2(scores * scale - lse[g][:, :1])
            probs = jnp.where(
                visible[None], probs.reshape(GROUP, rows, span), 0.0
            ).reshape(GROUP * rows, span)
            d_scores = (probs * (d_probs - delta[g][:, :1])).astype(BF16)
            d_query[g] += jnp.dot(d_scores, key, preferred_element_type=F32)
            d_key = t_mul(d_scores, queries[g]).astype(BF16)
            d_value = t_mul(probs.astype(BF16), d_mixed[g]).astype(BF16)
            target[:, :, :, lanes] = d_key.reshape(2, 2, rows, HEAD_DIM)
            target[:, :, :, others] = d_value.reshape(2, 2, rows, HEAD_DIM)
        return carry

    inputs = tokens[...].astype(F32)
    inv_one = lax.rsqrt(jnp.mean(inputs * inputs, axis=-1, keepdims=True) + EPSILON)
    normed = inputs * inv_one

    def out_gradient():
        for copy in loads[:2]:
            copy.start()
        for zi in range(depth):
            lanes = slice(zi * part, (zi + 1) * part)
            term = t_mul(mixed_low[:, lanes], d_branch[...]).astype(BF16)
            o_part[zi] = term.reshape(2, 2, 2, model_rows, model)

    def deltas():
        for g in range(KV_HEADS):
            delta[g] = jnp.broadcast_to(
                jnp.sum(d_mixed[g].astype(F32) * mixed[g], axis=-1, keepdims=True),
                delta.shape[1:],
            )
        d_query[...] = jnp.zeros_like(d_query)
        kv_load.wait()

    def attend_wave(step):
        k = order[step]
        zi = place.z - k
        low = jnp.maximum(2 * zi, 0)
        high = jnp.minimum(jnp.maximum(2 * zi + 2, 0), place.s + 1)
        lax.fori_loop(low, high, attend, 0)
        if k == 0:

            def clear():
                d_keys[place.z, 1] = jnp.zeros(d_keys.shape[2:], BF16)

            pl.when(place.x == 0)(clear)

    def query_turn():
        for h in range(HEADS):
            lanes = slice(h * HEAD_DIM, (h + 1) * HEAD_DIM)
            at = (h % GROUP) * rows
            head = d_query[h // GROUP, at : at + rows, :] * score_scale
            d_lin[:, lanes] = turned(head, cosine[...], -sine[...]).astype(BF16)

    def query_gradient():
        for zi in range(depth):
            lanes = slice(zi * part, (zi + 1) * part)
            term = t_mul(hidden_one[:, lanes], d_lin[:, :query_width]).astype(BF16)
            q_part[zi] = term.reshape(2, 2, 2, model_rows, query_width)

    def key_turn():
        r_kv.finish()
        for g in range(KV_HEADS):
            lanes = slice(g * HEAD_DIM, (g + 1) * HEAD_DIM)
            to = slice(query_width + g * HEAD_DIM, query_width + (g + 1) * HEAD_DIM)
            d_lin[:, to] = turned(d_kv[:, lanes] * score_scale, cosine[...], -sine[...]).astype(
                BF16
            )
        d_lin[:, query_width + key_width :] = d_kv[:, key_width:].astype(BF16)

    def hidden_query():
        for zi in range(depth):
            lanes = slice(zi * part, (zi + 1) * part)
            loads[zi].wait()
            block = weights[zi % 2][:, :, :, :, :query_width].reshape(part, query_width)
            d_hidden[:, lanes] = mul_t(d_lin[:, :query_width], block)
            block = weights[zi % 2][:, :, :, :, query_width:qkv_width]
            kv_weights[lanes, :] = block.reshape(part, 2 * key_width)
            if zi + 2 < depth:
                loads[zi + 2].start()

    def hidden_key():
        for zi in range(depth):
            lanes = slice(zi * part, (zi + 1) * part)
            term = t_mul(hidden_one[:, lanes], d_lin[:, query_width:]).astype(BF16)
            kvs_part[zi, :, :, :, :, : 2 * key_width] = term.reshape(
                2, 2, 2, model_rows, 2 * key_width
            )
            d_hidden[:, lanes] += mul_t(d_lin[:, query_width:], kv_weights[lanes, :])

    def small_gradients():
        gain_one = jnp.sum(d_hidden[...] * normed, axis=0, keepdims=True)
        bias = jnp.sum(d_lin[...].astype(F32), axis=0, keepdims=True)
        chosen = lax.broadcasted_iota(jnp.int32, (key_width, model), 0)
        chosen = lax.div(chosen, share) * model_rows + lax.rem(chosen, share)
        chosen = (lax.broadcasted_iota(jnp.int32, (key_width, model), 1) == chosen).astype(BF16)
        pair = jnp.concatenate(
            [
                bias[:, query_width : query_width + key_width],
                bias[:, query_width + key_width :],
                jnp.zeros((6, key_width), F32),
            ],
            axis=0,
        )
        spread = jnp.dot(pair.astype(BF16), chosen, preferred_element_type=F32)
        small = jnp.concatenate(
            [
                gain_one,
                bias[:, :query_width],
                spread[0:2],
                gain_two[0:1],
                jnp.zeros((123, model), F32),
            ],
            axis=0,
        ).T.astype(BF16)
        for zi in range(depth):
            kvs_part[zi, :, :, :, :, 2 * key_width :] = small[
                zi * part : (zi + 1) * part
            ].reshape(2, 2, 2, model_rows, 128)

    def input_gradient():
        scaled = d_hidden[...] * vectors[0:1]
        input_grad[...] = d_middle[...] + inv_one * (
            scaled - normed * jnp.mean(scaled * normed, axis=-1, keepdims=True)
        )

    works = {
        "out": out_gradient,
        "delta": deltas,
        "turn": query_turn,
        "query": query_gradient,
        "key": key_turn,
        "hq": hidden_query,
        "hk": hidden_key,
        "small": small_gradients,
        "input": input_gradient,
        "down": down_copy.start,
    }
    follow_last(LAST_PLAN, works, depart, attend_wave, {"o": r_o, "k": r_kv, "q": r_q, "s": r_kvs})
    for job in (r_o, r_q, r_kvs):
        job.finish()
    for offset in range(1, count):
        origin = lax.rem(place.s + count - offset, count)
        block = wide_out.at[origin]
        remote(block, block, e_send.at[0], e_recv.at[offset], place.flip_c()).wait_recv()
    own_wide.wait()
    down_load.wait()
    down_copy.wait()
    down_out[...] = d_near[...].astype(F32) + d_far[...].astype(F32)
    for job in (r_kv, r_o, r_q, r_kvs):
        job.settle()
    for copy in sent:
        copy.wait_send()


def call_last(depth, collective_id, hbm, vmems):
    kv_all, pack_all, wide, down = hbm
    tokens = vmems[6]
    count = 2 * depth
    rows, model = tokens.shape
    model_rows = model // (4 * count)
    query_width, key_width = HEADS * HEAD_DIM, KV_HEADS * HEAD_DIM
    heads = (KV_HEADS, GROUP * rows, HEAD_DIM)
    lead = (depth, 2, 2, 2)
    small_width = 2 * key_width + 128
    blocks = [
        (rows, 2 * key_width),
        (model_rows, model),
        (model_rows, query_width),
        (model_rows, small_width),
    ]
    scratch = [
        pltpu.VMEM(kv_all.shape, BF16),
        pltpu.VMEM((2,) + pack_all.shape[1:], BF16),
        pltpu.VMEM(heads, F32),
        pltpu.VMEM(heads, F32),
        pltpu.VMEM((rows, query_width + 2 * key_width), BF16),
        pltpu.VMEM(lead + blocks[0], BF16),
        pltpu.VMEM(blocks[0], F32),
    ]
    scratch += [pltpu.VMEM(lead + block, BF16) for block in blocks[1:]]
    scratch += [pltpu.VMEM(down.shape[1:], BF16)] * 2
    scratch += [pltpu.VMEM((rows, model), F32), pltpu.VMEM((model, 2 * key_width), BF16)]
    for block in blocks:
        buffers, sems = Reduce.scratch(depth, True, block)
        scratch += buffers + sems
    scratch += [DMA((3 + depth,)), DMA((count,)), DMA((count,)), DMA((1,)), DMA((1,))]
    any_, vmem = pl.BlockSpec(memory_space=pl.ANY), pl.BlockSpec(memory_space=pltpu.VMEM)
    return pl.pallas_call(
        functools.partial(last_kernel, depth),
        out_shape=[
            jax.ShapeDtypeStruct((rows, model), F32),
            jax.ShapeDtypeStruct(blocks[2], F32),
            jax.ShapeDtypeStruct(blocks[3], F32),
            jax.ShapeDtypeStruct(blocks[1], F32),
            jax.ShapeDtypeStruct(down.shape[1:], F32),
            jax.ShapeDtypeStruct(wide.shape, BF16),
        ],
        in_specs=[any_] * 4 + [vmem] * len(vmems),
        out_specs=[vmem] * 6,
        scratch_shapes=scratch,
        compiler_params=pltpu.CompilerParams(
            collective_id=collective_id, has_side_effects=True, vmem_limit_bytes=VMEM_JOINED
        ),
    )(*hbm, *vmems)


def finish_kernel(few, plain, *refs):
    wide, down, kvs = refs[:3]
    sources = refs[3 : 3 + plain]
    gate_out, up_out, down_out, k_out, v_out, vectors = refs[3 + plain : 9 + plain]
    targets = refs[9 + plain : 9 + 2 * plain]
    for source, target in zip(sources, targets):
        target[...] = source[...]
    down_out[...] = down[:few, :]
    filled = wide.shape[3] // 4
    for side, out in enumerate((gate_out, up_out)):
        for place in range(wide.shape[0]):
            block = wide[place, side].astype(F32)
            for owner in range(4):
                low = (4 * place + owner) * few
                out[:, low : low + few] = block[:, owner * filled : owner * filled + few]
    key_width = k_out.shape[1]
    k_out[...] = kvs[:, :key_width]
    v_out[...] = kvs[:, key_width : 2 * key_width]
    vectors[...] = kvs[:, 2 * key_width :].T[:8]


def call_finish(few, wide, down, kvs, plain):
    seq, _, rows, _ = wide.shape
    key_width = KV_HEADS * HEAD_DIM
    units = seq * 4 * few
    vmem = pl.BlockSpec(memory_space=pltpu.VMEM)
    out_shape = [
        jax.ShapeDtypeStruct((rows, units), F32),
        jax.ShapeDtypeStruct((rows, units), F32),
        jax.ShapeDtypeStruct((few, down.shape[1]), F32),
        jax.ShapeDtypeStruct((rows, key_width), F32),
        jax.ShapeDtypeStruct((rows, key_width), F32),
        jax.ShapeDtypeStruct((8, rows), F32),
    ] + [jax.ShapeDtypeStruct(array.shape, array.dtype) for array in plain]
    return pl.pallas_call(
        functools.partial(finish_kernel, few, len(plain)),
        out_shape=out_shape,
        in_specs=[vmem] * (3 + len(plain)),
        out_specs=[vmem] * len(out_shape),
        compiler_params=pltpu.CompilerParams(vmem_limit_bytes=VMEM_LIMIT),
    )(wide, down, kvs, *plain)


def begin_of(positions, lengths):
    ends = jnp.cumsum(lengths)
    starts = ends - lengths
    inside = (positions[:, None] >= starts[None, :]) & (positions[:, None] < ends[None, :])
    return jnp.sum(jnp.where(inside, starts[None, :], 0), axis=1)


def rope_tables(places, head_size):
    half_size = head_size // 2
    frequency = ROPE_BASE ** (-2.0 * jnp.arange(half_size, dtype=F32) / head_size)
    angles = places.astype(F32)[:, None] * frequency[None, :]
    return (jnp.cos(angles), jnp.sin(angles))


def rotate(vector, cosine, sine_table, direction):
    half_size = vector.shape[-1] // 2
    front_half = vector[..., :half_size]
    back_half = vector[..., half_size:]
    cosine = cosine[:, None, :]
    sine_table = direction * sine_table[:, None, :]
    return jnp.concatenate(
        [
            front_half * cosine - back_half * sine_table,
            back_half * cosine + front_half * sine_table,
        ],
        axis=-1,
    )


def norm_back(grad_normed, normed, inverse, gain_row):
    scaled = grad_normed * gain_row
    return inverse * (scaled - normed * jnp.mean(scaled * normed, axis=-1, keepdims=True))


def dot(left, right):
    return jnp.dot(left, right, preferred_element_type=F32)


def dot_t(left, right):
    return lax.dot_general(left, right, (((1,), (1,)), ((), ())), preferred_element_type=F32)


def t_dot(left, right):
    return lax.dot_general(left, right, (((0,), (0,)), ((), ())), preferred_element_type=F32)


def column(vector, rows):
    return jnp.pad(vector, (0, rows - vector.shape[0]))[:, None]


def shards_apart(
    tokens,
    cotangent,
    lengths,
    attn_gain,
    q_weight,
    q_bias,
    k_weight,
    k_bias,
    v_weight,
    v_bias,
    o_weight,
    mlp_gain,
    gate_weight,
    up_weight,
    down_weight,
):
    seq, fsdp = lax.axis_size("seq"), lax.axis_size("fsdp")
    devices = seq * fsdp
    depth = seq // 2
    rows, model = tokens.shape
    total = rows * devices
    key_width = KV_HEADS * HEAD_DIM
    query_width = HEADS * HEAD_DIM
    model_rows = q_weight.shape[0]
    units = gate_weight.shape[1] // seq
    first_row = lax.axis_index(AXES) * rows
    positions = first_row + jnp.arange(rows, dtype=jnp.int32)
    begin = begin_of(positions, lengths)
    cosine, sine_table = rope_tables(positions - begin, HEAD_DIM)
    score_scale = HEAD_DIM ** (-0.5)

    small = jnp.concatenate(
        [column(v, model_rows) for v in (attn_gain, q_bias, k_bias, v_bias, mlp_gain)]
        + [jnp.zeros((model_rows, 123), BF16)],
        axis=1,
    )
    pack = jnp.concatenate([q_weight, k_weight, v_weight, o_weight, small], axis=1)
    wide = jnp.stack([gate_weight, up_weight]).reshape(2, model_rows, seq, units)
    wide = wide.transpose(0, 2, 1, 3)
    pack_all, cot_all, wide_all, down_all = call_start(
        depth, 0, pack, cotangent, wide, down_weight
    )
    pack_all = pack_all.reshape(model, pack.shape[1])
    qkv_width = query_width + 2 * key_width
    w_qkv = pack_all[:, :qkv_width]
    w_out = pack_all[:, qkv_width : qkv_width + query_width]
    smalls = pack_all[:, qkv_width + query_width :].astype(F32)
    gain_one, b_query = smalls[:, 0], smalls[:, 1]
    gain_two = smalls[:, 4]
    kv_share = k_bias.shape[0]
    b_key = smalls[:, 2].reshape(devices, model_rows)[:, :kv_share].reshape(key_width)
    b_value = smalls[:, 3].reshape(devices, model_rows)[:, :kv_share].reshape(key_width)
    cot_all = cot_all.reshape(seq * rows, model)
    w_gate = wide_all[0].reshape(model, units)
    w_up = wide_all[1].reshape(model, units)
    w_down = down_all.reshape(units, model)

    inputs = tokens.astype(F32)
    inv_one = lax.rsqrt(jnp.mean(inputs * inputs, axis=-1, keepdims=True) + EPSILON)
    normed_one = inputs * inv_one
    hidden_one = (normed_one * gain_one).astype(BF16)
    lin = dot(hidden_one, w_qkv) + jnp.concatenate([b_query, b_key, b_value])
    queries = rotate(
        lin[:, :query_width].reshape(rows, HEADS, HEAD_DIM), cosine, sine_table, 1.0
    ).astype(BF16)
    queries = queries.transpose(1, 0, 2).reshape(KV_HEADS, GROUP * rows, HEAD_DIM)
    keys = rotate(
        lin[:, query_width : query_width + key_width].reshape(rows, KV_HEADS, HEAD_DIM),
        cosine,
        sine_table,
        1.0,
    ).reshape(rows, key_width)
    kv = jnp.concatenate([keys, lin[:, query_width + key_width :]], axis=1).astype(BF16)
    (kv_all,) = call_gathers(depth, 1, [True], [kv])
    kv_all = kv_all.reshape(total, 2 * key_width)
    all_keys, all_values = kv_all[:, :key_width], kv_all[:, key_width:]

    span = min(512, total)
    low = begin[0] // span
    high = (first_row + rows - 1) // span + 1
    info = jnp.stack([first_row, low, high]).astype(jnp.int32)
    begin_column = begin[:, None]
    mixed, lse = call_forward(span, info, begin_column, queries, all_keys, all_values)
    mixed_low = (
        mixed.reshape(HEADS, rows, HEAD_DIM)
        .transpose(1, 0, 2)
        .reshape(rows, query_width)
        .astype(BF16)
    )
    middle = inputs + dot(mixed_low, w_out)
    inv_two = lax.rsqrt(jnp.mean(middle * middle, axis=-1, keepdims=True) + EPSILON)
    normed_two = middle * inv_two
    hidden_two = (normed_two * gain_two).astype(BF16)

    (hidden_all,) = call_gathers(depth, 2, [False], [hidden_two])
    hidden_all = hidden_all.reshape(seq * rows, model)
    gate = dot(hidden_all, w_gate)
    up = dot(hidden_all, w_up)
    sigma = jax.nn.sigmoid(gate)
    silu = gate * sigma
    activated = (silu * up).astype(BF16)
    d_act = dot_t(cot_all, w_down)
    d_gate = (d_act * up * sigma * (1.0 + gate * (1.0 - sigma))).astype(BF16)
    d_up = (d_act * silu).astype(BF16)
    d_hidden_part = dot_t(d_gate, w_gate) + dot_t(d_up, w_up)
    out_part = dot(activated, w_down)
    shape = (depth, 2, rows, model)
    d_hidden_two, branch = call_reduces(
        depth,
        3,
        [False, False],
        [d_hidden_part.astype(BF16).reshape(shape), out_part.astype(BF16).reshape(shape)],
    )
    layer_out = (middle + branch).astype(BF16)
    gate_part = t_dot(hidden_all, d_gate).astype(BF16)
    up_part = t_dot(hidden_all, d_up).astype(BF16)
    down_part = t_dot(activated, cot_all).astype(BF16)

    gain_two_grad = jnp.sum(d_hidden_two * normed_two, axis=0)
    d_middle = cotangent.astype(F32) + norm_back(d_hidden_two, normed_two, inv_two, gain_two)

    d_branch = d_middle.astype(BF16)
    d_mixed = dot_t(d_branch, w_out).astype(BF16)
    d_mixed = (
        d_mixed.reshape(rows, HEADS, HEAD_DIM)
        .transpose(1, 0, 2)
        .reshape(KV_HEADS, GROUP * rows, HEAD_DIM)
    )
    d_query, d_kv_part = call_backward(
        span, info, begin_column, queries, all_keys, all_values, mixed, lse, d_mixed
    )
    (d_kv,) = call_reduces(
        depth, 4, [True], [d_kv_part.reshape(depth, 2, 2, 2, rows, 2 * key_width)]
    )
    d_query = d_query.reshape(HEADS, rows, HEAD_DIM).transpose(1, 0, 2)
    d_q = rotate(d_query * score_scale, cosine, sine_table, -1.0).reshape(rows, query_width)
    d_k = rotate(
        d_kv[:, :key_width].reshape(rows, KV_HEADS, HEAD_DIM) * score_scale,
        cosine,
        sine_table,
        -1.0,
    ).reshape(rows, key_width)
    d_lin = jnp.concatenate([d_q, d_k, d_kv[:, key_width:]], axis=1).astype(BF16)
    bias_grad = jnp.sum(d_lin.astype(F32), axis=0)
    d_hidden_one = dot_t(d_lin, w_qkv)
    gain_one_grad = jnp.sum(d_hidden_one * normed_one, axis=0)
    input_grad = d_middle + norm_back(d_hidden_one, normed_one, inv_one, gain_one)

    def spread(vector):
        parts = vector.reshape(devices, -1)
        return jnp.pad(parts, ((0, 0), (0, model_rows - parts.shape[1]))).reshape(model, 1)

    small_part = jnp.concatenate(
        [
            spread(gain_one_grad),
            spread(bias_grad[:query_width]),
            spread(bias_grad[query_width : query_width + key_width]),
            spread(bias_grad[query_width + key_width :]),
            spread(gain_two_grad),
            jnp.zeros((model, 123), F32),
        ],
        axis=1,
    )
    pack_part = jnp.concatenate(
        [
            t_dot(hidden_one, d_lin).astype(BF16),
            t_dot(mixed_low, d_branch).astype(BF16),
            small_part.astype(BF16),
        ],
        axis=1,
    ).reshape(depth, 2, 2, 2, model_rows, pack.shape[1])
    wide_part = jnp.stack([gate_part, up_part]).reshape(2, seq, fsdp, model_rows, units)
    down_part = down_part.reshape(fsdp, units // fsdp, model)
    pack_grad, wide_grad, down_grad = call_end(depth, 5, pack_part, wide_part, down_part)
    wide_grad = wide_grad.transpose(1, 2, 0, 3).reshape(2, model_rows, seq * units).astype(F32)
    small_grad = pack_grad[:, qkv_width + query_width :]
    return (
        layer_out,
        input_grad,
        small_grad[:, 0],
        pack_grad[:, :query_width],
        small_grad[:, 1],
        pack_grad[:, query_width : query_width + key_width],
        small_grad[:kv_share, 2],
        pack_grad[:, query_width + key_width : qkv_width],
        small_grad[:kv_share, 3],
        pack_grad[:, qkv_width : qkv_width + query_width],
        small_grad[:, 4],
        wide_grad[0],
        wide_grad[1],
        down_grad,
    )


def shards_joined(
    tokens,
    cotangent,
    lengths,
    attn_gain,
    q_weight,
    q_bias,
    k_weight,
    k_bias,
    v_weight,
    v_bias,
    o_weight,
    mlp_gain,
    gate_weight,
    up_weight,
    down_weight,
):
    seq, fsdp = lax.axis_size("seq"), lax.axis_size("fsdp")
    devices = seq * fsdp
    depth = seq // 2
    rows, model = tokens.shape
    key_width = KV_HEADS * HEAD_DIM
    model_rows = q_weight.shape[0]
    kv_share = k_bias.shape[0]
    first_row = lax.axis_index(AXES) * rows
    positions = first_row + jnp.arange(rows, dtype=jnp.int32)
    begin = begin_of(positions, lengths)
    cosine, sine_table = rope_tables(positions - begin, HEAD_DIM)
    angles = jnp.stack(
        [
            jnp.concatenate([cosine, cosine], axis=1),
            jnp.concatenate([-sine_table, sine_table], axis=1),
        ]
    )

    small = jnp.stack(
        [jnp.pad(v, (0, model_rows - v.shape[0])) for v in (attn_gain, q_bias, k_bias, v_bias, mlp_gain)],
        axis=1,
    )
    small = jnp.pad(small, ((0, 0), (0, 123)))
    few = down_weight.shape[0]
    filled = fsdp * (few + -few % 16)
    begin_column = begin[:, None]
    (
        pack_all,
        o_all,
        kv_all,
        cot_all,
        wide_all,
        down_all,
        hidden_all,
        queries,
        mixed,
        lse,
        middle,
        hidden_one,
        mixed_low,
        vectors,
    ) = call_head(
        depth,
        6,
        (o_weight,),
        (
            q_weight,
            k_weight,
            v_weight,
            small,
            gate_weight,
            up_weight,
            down_weight,
            tokens,
            cotangent,
            angles,
            begin_column,
        ),
    )
    layer_out, d_middle, d_mixed, d_branch, gain_two_grad, down_part, wide_part = call_middle(
        depth,
        7,
        (
            hidden_all,
            cot_all,
            wide_all.reshape(2, seq, 2, 2, model_rows, filled),
            down_all.reshape(filled, model),
            o_all,
        ),
        (middle, cotangent, vectors),
    )
    input_grad, q_grad, kvs_grad, o_grad, down_grad, wide_grad = call_last(
        depth,
        8,
        (kv_all, pack_all, wide_part, down_part),
        (
            queries,
            mixed,
            lse,
            d_mixed,
            angles,
            begin_column,
            tokens,
            d_middle,
            vectors,
            gain_two_grad,
            hidden_one,
            mixed_low,
            d_branch,
        ),
    )
    gate_grad, up_grad, down_grad, k_grad, v_grad, small_grad, *plain = call_finish(
        few, wide_grad, down_grad, kvs_grad, (layer_out, input_grad, q_grad, o_grad)
    )
    layer_out, input_grad, q_grad, o_grad = plain
    return (
        layer_out,
        input_grad,
        small_grad[0],
        q_grad,
        small_grad[1],
        k_grad,
        small_grad[2, :kv_share],
        v_grad,
        small_grad[3, :kv_share],
        o_grad,
        small_grad[4],
        gate_grad,
        up_grad,
        down_grad,
    )


def shards(*arguments):
    model_rows, rows = arguments[4].shape[0], arguments[0].shape[0]
    if model_rows % 16 == 0 and rows % 128 == 0 and lax.axis_size("seq") == 8:
        return shards_joined(*arguments)
    return shards_apart(*arguments)


def solution(mesh):
    matrix, vector = P(AXES, None), P(AXES)
    in_specs = (
        matrix,
        matrix,
        P(),
        vector,
        matrix,
        vector,
        matrix,
        vector,
        matrix,
        vector,
        matrix,
        vector,
        matrix,
        matrix,
        matrix,
    )
    out_specs = (
        matrix,
        matrix,
        vector,
        matrix,
        vector,
        matrix,
        vector,
        matrix,
        vector,
        matrix,
        vector,
        matrix,
        matrix,
        matrix,
    )
    return jax.shard_map(shards, mesh=mesh, in_specs=in_specs, out_specs=out_specs, check_vma=False)
```

```python
import functools

import jax
import jax.numpy as jnp
from jax import lax
from jax.experimental import pallas as pl
from jax.experimental.pallas import tpu as pltpu
from jax.sharding import PartitionSpec as P

HEADS = 12
KV_HEADS = 2
HEAD_DIM = 128
GROUP = HEADS // KV_HEADS
EPSILON = 1e-06
ROPE_BASE = 10000.0
LOG2E = 1.4426950408889634
AXES = ("seq", "fsdp")
VMEM_LIMIT = 56 << 20
VMEM_JOINED = 60 << 20
F32 = jnp.float32
BF16 = jnp.bfloat16
DMA = pltpu.SemaphoreType.DMA


class Place:
    def __init__(self, depth):
        self.depth = depth
        self.s = lax.axis_index("seq")
        self.f = lax.axis_index("fsdp")
        self.z = lax.div(self.s, 2)
        self.x = lax.rem(self.s, 2)
        self.y = lax.div(self.f, 2)
        self.c = lax.rem(self.f, 2)
        self.up = self.z + 1 < depth
        self.down = self.z > 0

    def flip_x(self):
        return (self.s + 1 - 2 * self.x, self.f)

    def flip_y(self):
        return (self.s, self.f + 2 - 4 * self.y)

    def flip_c(self):
        return (self.s, self.f + 1 - 2 * self.c)

    def z_up(self):
        return (self.s + 2, self.f)

    def z_down(self):
        return (self.s - 2, self.f)

    def first(self):
        return (
            self.s + (1 - self.c) * (1 - 2 * self.x),
            self.f + self.c * (2 - 4 * self.y),
        )

    def second(self):
        return (
            self.s + self.c * (1 - 2 * self.x),
            self.f + (1 - self.c) * (2 - 4 * self.y),
        )

    def corner(self, i, j):
        over_x = i * (1 - self.c) + j * self.c
        over_y = j * (1 - self.c) + i * self.c
        return (self.x + over_x * (1 - 2 * self.x), self.y + over_y * (1 - 2 * self.y))

    def wave(self, k):
        if k == 0:
            return [(self.z, None)]
        return [(self.z - k, self.z - k >= 0), (self.z + k, self.z + k < self.depth)]


def guard(condition, body):
    if condition is None:
        body()
    else:
        pl.when(condition)(body)


def both(one, other):
    return one if other is None else jnp.logical_and(one, other)


def greet(place, others=()):
    barrier = pltpu.get_barrier_semaphore()
    partners = [place.flip_x(), place.flip_y(), place.flip_c(), *others]
    for partner in partners:
        pl.semaphore_signal(barrier, inc=1, device_id=partner, device_id_type=pl.DeviceIdType.MESH)

    def tell_up():
        pl.semaphore_signal(
            barrier, inc=1, device_id=place.z_up(), device_id_type=pl.DeviceIdType.MESH
        )

    def tell_down():
        pl.semaphore_signal(
            barrier, inc=1, device_id=place.z_down(), device_id_type=pl.DeviceIdType.MESH
        )

    pl.when(place.up)(tell_up)
    pl.when(place.down)(tell_down)
    pl.semaphore_wait(
        barrier, len(partners) + place.up.astype(jnp.int32) + place.down.astype(jnp.int32)
    )


def remote(src, dst, send_sem, recv_sem, device):
    return pltpu.make_async_remote_copy(
        src_ref=src,
        dst_ref=dst,
        send_sem=send_sem,
        recv_sem=recv_sem,
        device_id=device,
        device_id_type=pl.DeviceIdType.MESH,
    )


def add_into(target, term, rows):
    step = 16 if rows % 16 == 0 else rows

    def body(number, carry):
        at = pl.ds(pl.multiple_of(number * step, step), step)
        target[at, :] = (target[at, :].astype(F32) + term[at, :].astype(F32)).astype(BF16)
        return carry

    lax.fori_loop(0, rows // step, body, 0)


class Gather:
    def __init__(self, place, wide, own, out, sems, mixed=False):
        self.place, self.wide, self.own, self.out, self.sems = place, wide, own, out, sems
        self.mixed = mixed
        self.sent = []

    @staticmethod
    def semaphores(depth, wide, mixed=False):
        base = [DMA((1,)), DMA((2 * depth,)), DMA((depth,)), DMA((depth,)), DMA((depth,))]
        if mixed:
            base += [DMA((2 * depth,)), DMA((depth,))]
        if wide:
            base += [DMA((2 * depth,)), DMA((2 * depth,)), DMA((4 * depth,)), DMA((4 * depth,))]
        return base

    def at(self, zi, i, j):
        place = self.place
        if self.wide:
            x, y = place.corner(i, j)
            return self.out.at[zi, x, y, place.c]
        return self.out.at[zi, place.x + i * (1 - 2 * place.x)]

    def send(self, src, dst, send_sem, recv_sem, device, condition):
        copy = remote(src, dst, send_sem, recv_sem, device)
        guard(condition, copy.start)
        self.sent.append((copy, condition))

    def local(self):
        copy = pltpu.make_async_copy(
            self.own, self.at(self.place.z, 0, 0), self.sems[0].at[0]
        )
        return copy

    def along(self, k, zi, side, ok, column, z_send, z_recv, source=None):
        place, depth = self.place, self.place.depth
        block = self.at(zi, column, 0)
        source = block if source is None else source
        if k == 0 or side == 0:
            self.send(
                source, block, z_send.at[k], z_recv.at[zi], place.z_up(), both(place.up, ok)
            )
        if k == 0 or side == 1:
            self.send(
                source,
                block,
                z_send.at[depth + k],
                z_recv.at[zi],
                place.z_down(),
                both(place.down, ok),
            )

    def arrive(self, k):
        place = self.place
        z_send, z_recv, a_send, a_recv = self.sems[1:5]
        across = place.first() if self.wide else place.flip_x()
        for side, (zi, ok) in enumerate(place.wave(k)):
            block = self.at(zi, 0, 0)
            source = self.own if k == 0 else block
            if k > 0:
                landed = remote(block, block, z_send.at[0], z_recv.at[zi], place.z_up())
                guard(ok, landed.wait_recv)
            self.along(k, zi, side, ok, 0, z_send, z_recv, source)
            crossing = both(place.c == 0, ok) if self.mixed and k > 0 else ok
            self.send(source, block, a_send.at[zi], a_recv.at[zi], across, crossing)
            if self.wide:
                b_send, b_recv = self.sems[5:7]
                self.send(
                    source, block, b_send.at[2 * zi], b_recv.at[2 * zi], place.second(), ok
                )

    def across(self, k):
        place = self.place
        a_send, a_recv = self.sems[3:5]
        for side, (zi, ok) in enumerate(place.wave(k)):
            block = self.at(zi, 1, 0)
            crossing = both(place.c == 0, ok) if self.mixed and k > 0 else ok
            landed = remote(block, block, a_send.at[0], a_recv.at[zi], place.first())
            guard(crossing, landed.wait_recv)
            if self.mixed:
                z_send, z_recv = self.sems[5:7]
                carried = both(place.c == 1, ok)
                if k > 0:
                    landed = remote(block, block, z_send.at[0], z_recv.at[zi], place.z_up())
                    guard(carried, landed.wait_recv)
                self.along(k, zi, side, carried, 1, z_send, z_recv)
            if self.wide:
                b_send, b_recv = self.sems[5:7]
                self.send(
                    block, block, b_send.at[2 * zi + 1], b_recv.at[2 * zi + 1], place.second(), ok
                )

    def hand(self, k):
        place = self.place
        b_send, b_recv, c_send, c_recv = self.sems[5:9]
        for zi, ok in place.wave(k):
            for i in range(2):
                block = self.at(zi, i, 1)
                landed = remote(block, block, b_send.at[0], b_recv.at[2 * zi + i], place.second())
                guard(ok, landed.wait_recv)
            for x in range(2):
                for y in range(2):
                    block = self.out.at[zi, x, y, place.c]
                    slot = 4 * zi + 2 * x + y
                    self.send(
                        block, block, c_send.at[slot], c_recv.at[slot], place.flip_c(), ok
                    )

    def take(self, k):
        place = self.place
        c_send, c_recv = self.sems[7:9]
        for zi, ok in place.wave(k):
            for x in range(2):
                for y in range(2):
                    block = self.out.at[zi, x, y, 1 - place.c]
                    slot = 4 * zi + 2 * x + y
                    landed = remote(block, block, c_send.at[0], c_recv.at[slot], place.flip_c())
                    guard(ok, landed.wait_recv)

    def settle(self):
        for copy, condition in self.sent:
            guard(condition, copy.wait_send)


def drive_gathers(place, gathers):
    depth = place.depth
    locals_ = [gather.local() for gather in gathers]
    for copy in locals_:
        copy.start()
    for step in range(depth + 3):
        for gather in gathers:
            if step < depth:
                gather.arrive(step)
        if step == 0:
            for copy in locals_:
                copy.wait()
        for gather in gathers:
            if 0 <= step - 1 < depth:
                gather.across(step - 1)
        for gather in gathers:
            if gather.wide and 0 <= step - 2 < depth:
                gather.hand(step - 2)
        for gather in gathers:
            if gather.wide and 0 <= step - 3 < depth:
                gather.take(step - 3)
    for gather in gathers:
        gather.settle()


def gather_shape(depth, wide, own):
    lead = (depth, 2, 2, 2) if wide else (depth, 2)
    return jax.ShapeDtypeStruct(lead + own.shape, own.dtype)


def call_gathers(depth, collective_id, wides, owns):
    def kernel(*refs):
        count = len(owns)
        place = Place(depth)
        greet(place)
        gathers, used = [], 2 * count
        for number, wide in enumerate(wides):
            need = len(Gather.semaphores(depth, wide))
            gathers.append(
                Gather(place, wide, refs[number], refs[count + number], refs[used : used + need])
            )
            used += need
        drive_gathers(place, gathers)

    scratch = []
    for wide in wides:
        scratch += Gather.semaphores(depth, wide)
    return pl.pallas_call(
        kernel,
        out_shape=[gather_shape(depth, wide, own) for wide, own in zip(wides, owns)],
        in_specs=[pl.BlockSpec(memory_space=pl.ANY)] * len(owns),
        out_specs=[pl.BlockSpec(memory_space=pl.ANY)] * len(owns),
        scratch_shapes=scratch,
        compiler_params=pltpu.CompilerParams(
            collective_id=collective_id, has_side_effects=True, vmem_limit_bytes=VMEM_LIMIT
        ),
    )(*owns)


def start_kernel(depth, *refs):
    (pack, cot, wide_in, down_in, pack_out, cot_out, wide_out, down_out), sems = refs[:8], refs[8:]
    place = Place(depth)
    count = 2 * depth
    partners = []
    for offset in range(1, count):
        partners.append((lax.rem(place.s + offset, count), place.f))
    greet(place, partners)
    first = len(Gather.semaphores(depth, True))
    second = first + len(Gather.semaphores(depth, False))
    gathers = [
        Gather(place, True, pack, pack_out, sems[:first]),
        Gather(place, False, cot, cot_out, sems[first:second]),
    ]
    local_sem, e_send, e_recv, y_send, y_recv, c_send, c_recv, d_sem, d_send, d_recv = sems[second:]
    sent = []

    def send(src, dst, send_sem, recv_sem, device):
        copy = remote(src, dst, send_sem, recv_sem, device)
        copy.start()
        sent.append(copy)

    locals_ = [gather.local() for gather in gathers]
    locals_.append(
        pltpu.make_async_copy(
            wide_in.at[:, place.s], wide_out.at[:, place.s, place.f], local_sem.at[0]
        )
    )
    locals_.append(pltpu.make_async_copy(down_in, down_out.at[place.f], d_sem.at[0]))
    for copy in locals_:
        copy.start()

    y_f = place.f + 2 - 4 * place.y
    c_f = place.f + 1 - 2 * place.c
    yc_f = y_f + 1 - 2 * place.c

    def exchange(offset):
        to = lax.rem(place.s + offset, count)
        send(
            wide_in.at[:, to],
            wide_out.at[:, place.s, place.f],
            e_send.at[offset],
            e_recv.at[offset],
            (to, place.f),
        )

    def onward(offset):
        origin = lax.rem(place.s + count - offset, count)
        block = wide_out.at[:, origin, place.f]
        if offset > 0:
            remote(block, block, e_send.at[0], e_recv.at[offset], place.flip_y()).wait_recv()
        send(block, block, y_send.at[offset], y_recv.at[offset], place.flip_y())
        send(block, block, c_send.at[2 * offset], c_recv.at[2 * offset], place.flip_c())

    def sideways(offset):
        origin = lax.rem(place.s + count - offset, count)
        block = wide_out.at[:, origin, y_f]
        remote(block, block, y_send.at[0], y_recv.at[offset], place.flip_y()).wait_recv()
        send(block, block, c_send.at[2 * offset + 1], c_recv.at[2 * offset + 1], place.flip_c())

    def last(offset):
        origin = lax.rem(place.s + count - offset, count)
        for slot, owner in ((2 * offset, c_f), (2 * offset + 1, yc_f)):
            block = wide_out.at[:, origin, owner]
            remote(block, block, c_send.at[0], c_recv.at[slot], place.flip_c()).wait_recv()

    for gather in gathers:
        gather.arrive(0)
    send(down_in, down_out.at[place.f], d_send.at[0], d_recv.at[0], place.flip_y())
    send(down_in, down_out.at[place.f], d_send.at[1], d_recv.at[1], place.flip_c())
    for offset in range(1, count):
        exchange(offset)
    for copy in locals_:
        copy.wait()
    onward(0)
    total = depth + 3
    for step in range(1, total):
        for gather in gathers:
            if step < depth:
                gather.arrive(step)
        for gather in gathers:
            if 0 <= step - 1 < depth:
                gather.across(step - 1)
        for gather in gathers:
            if gather.wide and 0 <= step - 2 < depth:
                gather.hand(step - 2)
        for gather in gathers:
            if gather.wide and 0 <= step - 3 < depth:
                gather.take(step - 3)
    block = down_out.at[y_f]
    remote(block, block, d_send.at[0], d_recv.at[0], place.flip_y()).wait_recv()
    send(block, block, d_send.at[2], d_recv.at[2], place.flip_c())
    for offset in range(1, count):
        onward(offset)
        sideways(offset - 1)
    sideways(count - 1)
    for offset in range(count):
        last(offset)
    for slot, owner in ((1, c_f), (2, yc_f)):
        block = down_out.at[owner]
        remote(block, block, d_send.at[0], d_recv.at[slot], place.flip_c()).wait_recv()
    for gather in gathers:
        gather.settle()
    for copy in sent:
        copy.wait_send()


def call_start(depth, collective_id, pack, cot, wide, down):
    count = 2 * depth
    _, _, rows, columns = wide.shape
    scratch = Gather.semaphores(depth, True) + Gather.semaphores(depth, False)
    scratch += [DMA((1,)), DMA((count,)), DMA((count,)), DMA((count,)), DMA((count,))]
    scratch += [DMA((2 * count,)), DMA((2 * count,)), DMA((1,)), DMA((3,)), DMA((3,))]
    return pl.pallas_call(
        functools.partial(start_kernel, depth),
        out_shape=[
            gather_shape(depth, True, pack),
            gather_shape(depth, False, cot),
            jax.ShapeDtypeStruct((2, count, 4, rows, columns), BF16),
            jax.ShapeDtypeStruct((4,) + down.shape, BF16),
        ],
        in_specs=[pl.BlockSpec(memory_space=pl.ANY)] * 4,
        out_specs=[pl.BlockSpec(memory_space=pl.ANY)] * 4,
        scratch_shapes=scratch,
        compiler_params=pltpu.CompilerParams(
            collective_id=collective_id, has_side_effects=True, vmem_limit_bytes=VMEM_LIMIT
        ),
    )(pack, cot, wide, down)


class Reduce:
    def __init__(self, place, wide, rows, own, out, buffers, sems, near=None, causal=False):
        self.place, self.wide, self.rows = place, wide, rows
        self.own, self.out, self.buffers, self.sems = own, out, buffers, sems
        self.near = near
        self.causal = causal
        self.sent = []

    def wave(self, k):
        waves = self.place.wave(k)
        return waves[:1] if self.causal else waves

    def near_block(self, zi):
        return self.own.at[zi, self.place.x] if self.near is None else self.near.at[zi]

    @staticmethod
    def scratch(depth, wide, block):
        buffers = [
            pltpu.VMEM((depth,) + block, BF16),
            pltpu.VMEM((depth + 1,) + block, BF16),
        ]
        sems = [DMA((depth,)), DMA((depth,)), DMA((2 * depth,)), DMA((2 * depth,))]
        if wide:
            buffers += [
                pltpu.VMEM((depth, 2, 2) + block, BF16),
                pltpu.VMEM((depth, 2) + block, BF16),
            ]
            sems += [DMA((4 * depth,)), DMA((4 * depth,)), DMA((2 * depth,)), DMA((2 * depth,))]
        return buffers, sems

    def send(self, src, dst, send_sem, recv_sem, device, condition):
        copy = remote(src, dst, send_sem, recv_sem, device)
        guard(condition, copy.start)
        self.sent.append((copy, condition))

    def cores(self, k):
        place = self.place
        c_send, c_recv = self.sems[4:6]
        got = self.buffers[2]
        for zi, ok in self.wave(k):
            for x in range(2):
                for y in range(2):
                    slot = 4 * zi + 2 * x + y
                    self.send(
                        self.own.at[zi, x, y, 1 - place.c],
                        got.at[zi, x, y],
                        c_send.at[slot],
                        c_recv.at[slot],
                        place.flip_c(),
                        ok,
                    )

    def over_second(self, k):
        place = self.place
        c_send, c_recv, b_send, b_recv = self.sems[4:8]
        got, next_ = self.buffers[2:4]
        for zi, ok in self.wave(k):

            def body(zi=zi):
                for j in (1, 0):
                    for i in (1, 0):
                        x, y = place.corner(i, j)
                        block = got.at[zi, x, y]
                        slot = 4 * zi + 2 * x + y
                        remote(
                            block, block, c_send.at[0], c_recv.at[slot], place.flip_c()
                        ).wait_recv()
                        add_into(block, self.own.at[zi, x, y, place.c], self.rows)
                        if j == 1:
                            remote(
                                block,
                                next_.at[zi, i],
                                b_send.at[2 * zi + i],
                                b_recv.at[2 * zi + i],
                                place.second(),
                            ).start()

            guard(ok, body)
            for i in (1, 0):
                x, y = place.corner(i, 1)
                copy = remote(
                    got.at[zi, x, y],
                    next_.at[zi, i],
                    b_send.at[2 * zi + i],
                    b_recv.at[2 * zi + i],
                    place.second(),
                )
                self.sent.append((copy, ok))

    def over_first(self, k):
        place = self.place
        a_send, a_recv = self.sems[0:2]
        got = self.buffers[0]
        for zi, ok in self.wave(k):
            if self.wide:
                b_send, b_recv = self.sems[6:8]
                before, held = self.buffers[2:4]

                def body(zi=zi):
                    for i in (1, 0):
                        block = held.at[zi, i]
                        x, y = place.corner(i, 0)
                        remote(
                            block, block, b_send.at[0], b_recv.at[2 * zi + i], place.second()
                        ).wait_recv()
                        add_into(block, before.at[zi, x, y], self.rows)
                        if i == 1:
                            remote(
                                block, got.at[zi], a_send.at[zi], a_recv.at[zi], place.first()
                            ).start()

                guard(ok, body)
                copy = remote(
                    held.at[zi, 1], got.at[zi], a_send.at[zi], a_recv.at[zi], place.first()
                )
                self.sent.append((copy, ok))
            else:
                self.send(
                    self.own.at[zi, 1 - place.x],
                    got.at[zi],
                    a_send.at[zi],
                    a_recv.at[zi],
                    place.flip_x(),
                    ok,
                )

    def cross_copy(self, zi):
        place = self.place
        return remote(
            self.own.at[zi, 1 - place.x],
            self.buffers[0].at[zi],
            self.sems[0].at[zi],
            self.sems[1].at[zi],
            place.flip_x(),
        )

    def cross(self, zi):
        self.cross_copy(zi).start()

    def crossed(self):
        for zi in range(self.place.depth):
            self.sent.append((self.cross_copy(zi), None))

    def along(self, k):
        place, depth = self.place, self.place.depth
        a_send, a_recv, z_send, z_recv = self.sems[0:4]
        held, line = self.buffers[0:2]
        for side, (zi, ok) in enumerate(self.wave(k)):
            block = held.at[zi]

            def body(zi=zi, side=side, block=block):
                remote(block, block, a_send.at[0], a_recv.at[zi], place.first()).wait_recv()
                if self.wide:
                    add_into(block, self.buffers[3].at[zi, 0], self.rows)
                else:
                    add_into(block, self.near_block(zi), self.rows)

                def more(direction):
                    slot = direction * depth + zi
                    term = line.at[depth if k == 0 and direction == 1 else zi]
                    remote(term, term, z_send.at[0], z_recv.at[slot], place.z_up()).wait_recv()
                    add_into(block, term, self.rows)

                def pass_on(direction, to):
                    slot = direction * depth + zi
                    there = line.at[depth if k == 1 and direction == 1 else zi]
                    remote(block, there, z_send.at[slot], z_recv.at[slot], to).start()

                if k == 0:
                    if not self.causal:
                        pl.when(place.down)(functools.partial(more, 0))
                    pl.when(place.up)(functools.partial(more, 1))
                elif side == 0:
                    pl.when(place.up)(functools.partial(more, 1))
                    pass_on(1, place.z_down())
                else:
                    pl.when(place.down)(functools.partial(more, 0))
                    pass_on(0, place.z_up())

            guard(ok, body)
            if k > 0:
                direction = 1 - side
                slot = direction * depth + zi
                to = place.z_up() if side == 1 else place.z_down()
                there = line.at[depth if k == 1 and direction == 1 else zi]
                copy = remote(block, there, z_send.at[slot], z_recv.at[slot], to)
                self.sent.append((copy, ok))

    def finish(self):
        self.out[...] = self.buffers[0][self.place.z].astype(self.out.dtype)

    def settle(self):
        for copy, condition in self.sent:
            guard(condition, copy.wait_send)


def drive_reduces(place, reduces):
    depth = place.depth
    order = list(range(depth - 1, -1, -1))
    for reduce in reduces:
        for k in order:
            reduce.cores(k) if reduce.wide else reduce.over_first(k)
    for step in range(depth + 2):
        for reduce in reduces:
            if not reduce.wide:
                if step < depth:
                    reduce.along(order[step])
                continue
            if step < depth:
                reduce.over_second(order[step])
            if 0 <= step - 1 < depth:
                reduce.over_first(order[step - 1])
            if 0 <= step - 2 < depth:
                reduce.along(order[step - 2])
    for reduce in reduces:
        reduce.finish()
    for reduce in reduces:
        reduce.settle()


def call_reduces(depth, collective_id, wides, owns):
    count = len(owns)
    blocks = [own.shape[-2:] for own in owns]
    parts = [Reduce.scratch(depth, wide, block) for wide, block in zip(wides, blocks)]
    scratch = []
    for buffers, sems in parts:
        scratch += buffers + sems

    def kernel(*refs):
        place = Place(depth)
        greet(place)
        reduces, used = [], 2 * count
        for number, (buffers, sems) in enumerate(parts):
            middle, end = used + len(buffers), used + len(buffers) + len(sems)
            reduces.append(
                Reduce(
                    place,
                    wides[number],
                    blocks[number][0],
                    refs[number],
                    refs[count + number],
                    refs[used:middle],
                    refs[middle:end],
                )
            )
            used = end
        drive_reduces(place, reduces)

    return pl.pallas_call(
        kernel,
        out_shape=[jax.ShapeDtypeStruct(block, F32) for block in blocks],
        in_specs=[pl.BlockSpec(memory_space=pltpu.VMEM)] * count,
        out_specs=[pl.BlockSpec(memory_space=pltpu.VMEM)] * count,
        scratch_shapes=scratch,
        compiler_params=pltpu.CompilerParams(
            collective_id=collective_id, has_side_effects=True, vmem_limit_bytes=VMEM_LIMIT
        ),
    )(*owns)


def end_kernel(depth, shapes, *refs):
    pack, wide, down, pack_out, wide_out, down_out = refs[:6]
    block, wide_block, down_block = shapes
    buffers, sems = Reduce.scratch(depth, True, block)
    used = 6 + len(buffers)
    place = Place(depth)
    count = 2 * depth
    partners = []
    for offset in range(1, count):
        partners.append((lax.rem(place.s + offset, count), place.f))
    greet(place, partners)
    reduce = Reduce(
        place, True, block[0], pack, pack_out, refs[6:used], refs[used : used + len(sems)]
    )
    used += len(sems)
    w_core, w_y, d_core, d_y = refs[used : used + 4]
    wc_send, wc_recv, wy_send, wy_recv, e_send, e_recv, e_sem = refs[used + 4 : used + 11]
    dc_send, dc_recv, dy_send, dy_recv = refs[used + 11 :]
    sent = []
    wide_rows, down_rows = wide_block[1], down_block[0]

    def send(src, dst, send_sem, recv_sem, device):
        copy = remote(src, dst, send_sem, recv_sem, device)
        copy.start()
        sent.append(copy)

    def landed(ref, recv_sem):
        remote(ref, ref, e_send.at[0], recv_sem, place.flip_c()).wait_recv()

    mine_y, other_y = place.y, 1 - place.y
    offsets = list(range(1, count)) + [0]
    for y in range(2):
        side = other_y if y == 0 else mine_y
        send(
            down.at[2 * side + 1 - place.c],
            d_core.at[side],
            dc_send.at[side],
            dc_recv.at[side],
            place.flip_c(),
        )
    for offset in offsets:
        to = lax.rem(place.s + offset, count)
        for y in range(2):
            send(
                wide.at[:, to, 2 * y + 1 - place.c],
                w_core.at[y, offset],
                wc_send.at[2 * offset + y],
                wc_recv.at[2 * offset + y],
                place.flip_c(),
            )
    order = list(range(depth - 1, -1, -1))
    for k in order:
        reduce.cores(k)

    def wide_add(target, term):
        for part in range(2):
            add_into(target.at[part], term.at[part], wide_rows)

    def wide_cores(offset):
        to = lax.rem(place.s + offset, count)
        for side in (other_y, mine_y):
            landed(w_core.at[side, offset], wc_recv.at[2 * offset + side])
            wide_add(w_core.at[side, offset], wide.at[:, to, 2 * side + place.c])
            if side is other_y:
                send(
                    w_core.at[side, offset],
                    w_y.at[offset],
                    wy_send.at[offset],
                    wy_recv.at[offset],
                    place.flip_y(),
                )

    def wide_across(offset):
        landed(w_y.at[offset], wy_recv.at[offset])
        wide_add(w_y.at[offset], w_core.at[mine_y, offset])
        to = lax.rem(place.s + offset, count)
        if offset > 0:
            send(
                w_y.at[offset],
                wide_out.at[place.s],
                e_send.at[offset],
                e_recv.at[offset],
                (to, place.f),
            )
        else:
            pltpu.make_async_copy(w_y.at[0], wide_out.at[place.s], e_sem.at[0]).start()

    for offset in offsets[: count // 2]:
        wide_cores(offset)
    for step in range(depth):
        reduce.over_second(order[step])
        if step >= 1:
            reduce.over_first(order[step - 1])
        if step == 0:
            for offset in offsets[count // 2 :]:
                wide_cores(offset)
            for side in (other_y, mine_y):
                landed(d_core.at[side], dc_recv.at[side])
                add_into(d_core.at[side], down.at[2 * side + place.c], down_rows)
                if side is other_y:
                    send(d_core.at[side], d_y.at[0], dy_send.at[0], dy_recv.at[0], place.flip_y())
        for offset in offsets[step * count // depth : (step + 1) * count // depth]:
            wide_across(offset)
        if step >= 2:
            reduce.along(order[step - 2])
    reduce.over_first(order[depth - 1])
    for step in range(max(depth - 2, 0), depth):
        reduce.along(order[step])
    reduce.finish()
    landed(d_y.at[0], dy_recv.at[0])
    down_out[...] = d_y[0].astype(F32) + d_core[mine_y].astype(F32)
    for offset in range(1, count):
        origin = lax.rem(place.s + count - offset, count)
        landed(wide_out.at[origin], e_recv.at[offset])
    pltpu.make_async_copy(w_y.at[0], wide_out.at[place.s], e_sem.at[0]).wait()
    reduce.settle()
    for copy in sent:
        copy.wait_send()


def call_end(depth, collective_id, pack, wide, down):
    count = 2 * depth
    block = pack.shape[-2:]
    wide_block = (2,) + wide.shape[-2:]
    down_block = down.shape[-2:]
    buffers, sems = Reduce.scratch(depth, True, block)
    scratch = buffers + sems
    scratch += [
        pltpu.VMEM((2, count) + wide_block, BF16),
        pltpu.VMEM((count,) + wide_block, BF16),
        pltpu.VMEM((2,) + down_block, BF16),
        pltpu.VMEM((1,) + down_block, BF16),
    ]
    scratch += [DMA((2 * count,)), DMA((2 * count,)), DMA((count,)), DMA((count,))]
    scratch += [DMA((count,)), DMA((count,)), DMA((1,))]
    scratch += [DMA((2,)), DMA((2,)), DMA((1,)), DMA((1,))]
    vmem = pl.BlockSpec(memory_space=pltpu.VMEM)
    return pl.pallas_call(
        functools.partial(end_kernel, depth, (block, wide_block, down_block)),
        out_shape=[
            jax.ShapeDtypeStruct(block, F32),
            jax.ShapeDtypeStruct((count,) + wide_block, BF16),
            jax.ShapeDtypeStruct(down_block, F32),
        ],
        in_specs=[vmem] * 3,
        out_specs=[vmem, vmem, vmem],
        scratch_shapes=scratch,
        compiler_params=pltpu.CompilerParams(
            collective_id=collective_id, has_side_effects=True, vmem_limit_bytes=VMEM_LIMIT
        ),
    )(pack, wide, down)


def forward_kernel(span, info, begin, query, key, value, mixed, lse, m_acc, l_acc, o_acc):
    rows = begin.shape[0]
    first_row, low, high = info[0], info[1], info[2]
    scale = HEAD_DIM ** (-0.5) * LOG2E
    m_acc[...] = jnp.full_like(m_acc, -1e30)
    l_acc[...] = jnp.zeros_like(l_acc)
    o_acc[...] = jnp.zeros_like(o_acc)
    places = first_row + lax.broadcasted_iota(jnp.int32, (rows, span), 0)
    offsets = lax.broadcasted_iota(jnp.int32, (rows, span), 1)

    def step(number, carry):
        base = pl.multiple_of(number * span, span)
        keys_at = base + offsets
        visible = jnp.logical_and(keys_at >= begin[...], keys_at <= places)
        for g in range(KV_HEADS):
            lanes = slice(g * HEAD_DIM, (g + 1) * HEAD_DIM)
            scores = lax.dot_general(
                query[g],
                key[pl.ds(base, span), lanes],
                (((1,), (1,)), ((), ())),
                preferred_element_type=F32,
            )
            scores = scores.reshape(GROUP, rows, span) * scale
            scores = jnp.where(visible[None], scores, -1e30).reshape(GROUP * rows, span)
            old = m_acc[g]
            new = jnp.maximum(old, jnp.max(scores, axis=-1, keepdims=True))
            weights = jnp.exp2(scores - new[:, :1])
            weights = jnp.where(
                visible[None], weights.reshape(GROUP, rows, span), 0.0
            ).reshape(GROUP * rows, span)
            fade = jnp.exp2(old - new)
            l_acc[g] = l_acc[g] * fade + jnp.sum(weights, axis=-1, keepdims=True)
            o_acc[g] = o_acc[g] * fade + jnp.dot(
                weights.astype(BF16),
                value[pl.ds(base, span), lanes],
                preferred_element_type=F32,
            )
            m_acc[g] = new
        return carry

    lax.fori_loop(low, high, step, 0)
    for g in range(KV_HEADS):
        mixed[g] = o_acc[g] / l_acc[g]
        lse[g] = m_acc[g] + jnp.log2(l_acc[g])


def call_forward(span, info, begin, query, key, value):
    stacked = query.shape[1]
    vmem = pl.BlockSpec(memory_space=pltpu.VMEM)
    return pl.pallas_call(
        functools.partial(forward_kernel, span),
        out_shape=[
            jax.ShapeDtypeStruct((KV_HEADS, stacked, HEAD_DIM), F32),
            jax.ShapeDtypeStruct((KV_HEADS, stacked, HEAD_DIM), F32),
        ],
        in_specs=[pl.BlockSpec(memory_space=pltpu.SMEM)] + [vmem] * 4,
        out_specs=[vmem, vmem],
        scratch_shapes=[pltpu.VMEM((KV_HEADS, stacked, HEAD_DIM), F32)] * 3,
        compiler_params=pltpu.CompilerParams(vmem_limit_bytes=VMEM_LIMIT),
    )(info, begin, query, key, value)


def backward_kernel(
    span, info, begin, query, key, value, mixed, lse, grad, dquery, dkeys, delta
):
    rows = begin.shape[0]
    first_row, low, high = info[0], info[1], info[2]
    scale = HEAD_DIM ** (-0.5) * LOG2E
    dquery[...] = jnp.zeros_like(dquery)
    width = KV_HEADS * HEAD_DIM
    for g in range(KV_HEADS):
        delta[g] = jnp.broadcast_to(
            jnp.sum(grad[g].astype(F32) * mixed[g], axis=-1, keepdims=True), delta.shape[1:]
        )
    places = first_row + lax.broadcasted_iota(jnp.int32, (rows, span), 0)
    offsets = lax.broadcasted_iota(jnp.int32, (rows, span), 1)

    def clear(number, carry):
        base = pl.multiple_of(number * span, span)
        dkeys[pl.ds(base, span), :] = jnp.zeros((span, dkeys.shape[1]), BF16)
        return carry

    lax.fori_loop(0, low, clear, 0)
    lax.fori_loop(high, dkeys.shape[0] // span, clear, 0)

    def step(number, carry):
        base = pl.multiple_of(number * span, span)
        keys_at = base + offsets
        visible = jnp.logical_and(keys_at >= begin[...], keys_at <= places)
        for g in range(KV_HEADS):
            lanes = slice(g * HEAD_DIM, (g + 1) * HEAD_DIM)
            key_rows = key[pl.ds(base, span), lanes]
            value_rows = value[pl.ds(base, span), lanes]
            scores = lax.dot_general(
                query[g], key_rows, (((1,), (1,)), ((), ())), preferred_element_type=F32
            )
            dprobs = lax.dot_general(
                grad[g], value_rows, (((1,), (1,)), ((), ())), preferred_element_type=F32
            )
            probs = jnp.exp2(scores * scale - lse[g][:, :1])
            probs = jnp.where(
                visible[None], probs.reshape(GROUP, rows, span), 0.0
            ).reshape(GROUP * rows, span)
            dscores = (probs * (dprobs - delta[g][:, :1])).astype(BF16)
            dquery[g] += jnp.dot(dscores, key_rows, preferred_element_type=F32)
            dkeys[pl.ds(base, span), lanes] = lax.dot_general(
                dscores, query[g], (((0,), (0,)), ((), ())), preferred_element_type=F32
            ).astype(BF16)
            dkeys[
                pl.ds(base, span), width + g * HEAD_DIM : width + (g + 1) * HEAD_DIM
            ] = lax.dot_general(
                probs.astype(BF16),
                grad[g],
                (((0,), (0,)), ((), ())),
                preferred_element_type=F32,
            ).astype(BF16)
        return carry

    lax.fori_loop(low, high, step, 0)


def call_backward(span, info, begin, query, key, value, mixed, lse, grad):
    stacked = query.shape[1]
    vmem = pl.BlockSpec(memory_space=pltpu.VMEM)
    return pl.pallas_call(
        functools.partial(backward_kernel, span),
        out_shape=[
            jax.ShapeDtypeStruct((KV_HEADS, stacked, HEAD_DIM), F32),
            jax.ShapeDtypeStruct((key.shape[0], 2 * key.shape[1]), BF16),
        ],
        in_specs=[pl.BlockSpec(memory_space=pltpu.SMEM)] + [vmem] * 7,
        out_specs=[vmem, vmem],
        scratch_shapes=[pltpu.VMEM((KV_HEADS, stacked, HEAD_DIM), F32)],
        compiler_params=pltpu.CompilerParams(vmem_limit_bytes=VMEM_LIMIT),
    )(info, begin, query, key, value, mixed, lse, grad)


class PairGather:
    def __init__(self, place, own, out, sems, crossing):
        self.place, self.own, self.out, self.sems = place, own, out, sems
        self.crossing = crossing
        self.sent = []

    @staticmethod
    def semaphores(depth):
        return [
            DMA((1,)),
            DMA((1,)),
            DMA((1,)),
            DMA((2 * depth,)),
            DMA((depth,)),
            DMA((depth,)),
            DMA((depth,)),
            DMA((2 * depth,)),
            DMA((2 * depth,)),
        ]

    def send(self, src, dst, send_sem, recv_sem, device, condition=None):
        copy = remote(src, dst, send_sem, recv_sem, device)
        guard(condition, copy.start)
        self.sent.append((copy, condition))

    def block(self, zi, y, c):
        return self.out.at[zi, :, y, c]

    def landed(self, ref, recv_sem, condition=None):
        guard(condition, remote(ref, ref, self.sems[3].at[0], recv_sem, self.place.flip_c()).wait_recv)

    def local(self):
        place = self.place
        if self.crossing:
            return pltpu.make_async_copy(
                self.own.at[place.x],
                self.out.at[place.z, place.x, place.y, place.c],
                self.sems[0].at[0],
            )
        return pltpu.make_async_copy(
            self.own, self.block(place.z, place.y, place.c), self.sems[0].at[0]
        )

    def begin(self):
        place = self.place
        if self.crossing:
            self.send(
                self.own.at[1 - place.x],
                self.out.at[place.z, place.x, place.y, place.c],
                self.sems[1].at[0],
                self.sems[2].at[0],
                place.flip_x(),
            )

    def arrive(self, k):
        place, depth = self.place, self.place.depth
        z_send, z_recv, y_send, y_recv, c_send, c_recv = self.sems[3:9]
        for side, (zi, ok) in enumerate(place.wave(k)):
            block = self.block(zi, place.y, place.c)
            source = self.own if k == 0 and not self.crossing else block
            if k > 0:
                self.landed(block, z_recv.at[zi], ok)
            elif self.crossing:
                self.landed(
                    self.out.at[place.z, 1 - place.x, place.y, place.c], self.sems[2].at[0]
                )
            if k == 0 or side == 0:
                self.send(
                    source, block, z_send.at[k], z_recv.at[zi], place.z_up(), both(place.up, ok)
                )
            if k == 0 or side == 1:
                self.send(
                    source,
                    block,
                    z_send.at[depth + k],
                    z_recv.at[zi],
                    place.z_down(),
                    both(place.down, ok),
                )
            self.send(source, block, y_send.at[zi], y_recv.at[zi], place.flip_y(), ok)
            self.send(
                source, block, c_send.at[2 * zi], c_recv.at[2 * zi], place.flip_c(), ok
            )

    def across(self, k):
        place = self.place
        y_recv, c_send, c_recv = self.sems[6:9]
        for zi, ok in place.wave(k):
            block = self.block(zi, 1 - place.y, place.c)
            self.landed(block, y_recv.at[zi], ok)
            slot = 2 * zi + 1
            self.send(block, block, c_send.at[slot], c_recv.at[slot], place.flip_c(), ok)

    def take(self, k):
        place = self.place
        c_recv = self.sems[8]
        for zi, ok in place.wave(k):
            self.landed(self.block(zi, place.y, 1 - place.c), c_recv.at[2 * zi], ok)
            self.landed(self.block(zi, 1 - place.y, 1 - place.c), c_recv.at[2 * zi + 1], ok)

    def settle(self):
        for copy, condition in self.sent:
            guard(condition, copy.wait_send)


class PairReduce:
    def __init__(self, place, own, out, buffers, sems, causal=False, crossing=False):
        self.place, self.own, self.out, self.sems = place, own, out, sems
        self.from_core, self.from_y, self.line, self.from_x = buffers
        self.causal, self.crossing = causal, crossing
        self.sent = []

    @staticmethod
    def scratch(depth, block):
        buffers = [
            pltpu.VMEM((depth, 2, 2) + block, BF16),
            pltpu.VMEM((depth, 2) + block, BF16),
            pltpu.VMEM((depth + 1, 2) + block, BF16),
            pltpu.VMEM((1,) + block, BF16),
        ]
        sems = [DMA((2 * depth,)), DMA((2 * depth,)), DMA((depth,)), DMA((depth,))]
        sems += [DMA((2 * depth,)), DMA((2 * depth,)), DMA((1,)), DMA((1,))]
        return buffers, sems

    def wave(self, k):
        waves = self.place.wave(k)
        return waves[:1] if self.causal else waves

    def send(self, src, dst, send_sem, recv_sem, device, condition=None):
        copy = remote(src, dst, send_sem, recv_sem, device)
        guard(condition, copy.start)
        self.sent.append((copy, condition))

    def landed(self, ref, recv_sem):
        remote(ref, ref, self.sems[0].at[0], recv_sem, self.place.flip_c()).wait_recv()

    def add(self, target, term):
        for x in range(2):
            add_into(target.at[x], term.at[x], target.shape[1])

    def cores(self, k):
        place = self.place
        for zi, ok in self.wave(k):
            for y in range(2):
                slot = 2 * zi + y
                self.send(
                    self.own.at[zi, :, y, 1 - place.c],
                    self.from_core.at[zi, y],
                    self.sems[0].at[slot],
                    self.sems[1].at[slot],
                    place.flip_c(),
                    ok,
                )

    def over(self, k):
        place = self.place
        for zi, ok in self.wave(k):

            def body(zi=zi):
                for y in (1 - place.y, place.y):
                    block = self.from_core.at[zi, y]
                    self.landed(block, self.sems[1].at[2 * zi + y])
                    self.add(block, self.own.at[zi, :, y, place.c])
                    if y is not place.y:
                        self.y_copy(zi).start()

            guard(ok, body)
            self.sent.append((self.y_copy(zi), ok))

    def y_copy(self, zi):
        place = self.place
        return remote(
            self.from_core.at[zi, 1 - place.y],
            self.from_y.at[zi],
            self.sems[2].at[zi],
            self.sems[3].at[zi],
            place.flip_y(),
        )

    def z_copy(self, k, side, zi):
        depth = self.place.depth
        direction = 1 - side
        slot = direction * depth + zi
        there = self.line.at[depth if k == 1 and direction == 1 else zi]
        to = self.place.z_up() if side == 1 else self.place.z_down()
        return remote(
            self.from_y.at[zi], there, self.sems[4].at[slot], self.sems[5].at[slot], to
        )

    def along(self, k):
        place, depth = self.place, self.place.depth
        for side, (zi, ok) in enumerate(self.wave(k)):
            block = self.from_y.at[zi]

            def body(zi=zi, side=side, block=block):
                self.landed(block, self.sems[3].at[zi])
                self.add(block, self.from_core.at[zi, place.y])

                def more(direction):
                    term = self.line.at[depth if k == 0 and direction == 1 else zi]
                    self.landed(term, self.sems[5].at[direction * depth + zi])
                    self.add(block, term)

                if k == 0:
                    if not self.causal:
                        pl.when(place.down)(functools.partial(more, 0))
                    pl.when(place.up)(functools.partial(more, 1))
                elif side == 0:
                    pl.when(place.up)(functools.partial(more, 1))
                else:
                    pl.when(place.down)(functools.partial(more, 0))
                if k > 0:
                    self.z_copy(k, side, zi).start()

            guard(ok, body)
            if k > 0:
                self.sent.append((self.z_copy(k, side, zi), ok))

    def swap(self):
        place = self.place
        self.send(
            self.from_y.at[place.z, 1 - place.x],
            self.from_x.at[0],
            self.sems[6].at[0],
            self.sems[7].at[0],
            place.flip_x(),
        )

    def finish(self):
        place = self.place
        if self.crossing:
            self.landed(self.from_x.at[0], self.sems[7].at[0])
            self.out[place.x] = self.from_y[place.z, place.x].astype(self.out.dtype)
            self.out[1 - place.x] = self.from_x[0].astype(self.out.dtype)
        else:
            self.out[...] = self.from_y[place.z].astype(self.out.dtype)

    def settle(self):
        for copy, condition in self.sent:
            guard(condition, copy.wait_send)


class Exchange:
    def __init__(self, place, own, out, sems):
        self.place, self.own, self.out, self.sems = place, own, out, sems
        self.count = 2 * place.depth
        self.sent = []
        self.y_f = place.f + 2 - 4 * place.y
        self.c_f = place.f + 1 - 2 * place.c
        self.yc_f = self.y_f + 1 - 2 * place.c

    @staticmethod
    def semaphores(depth):
        count = 2 * depth
        return [
            DMA((1,)),
            DMA((count,)),
            DMA((count,)),
            DMA((count,)),
            DMA((count,)),
            DMA((2 * count,)),
            DMA((2 * count,)),
        ]

    def send(self, block, send_sem, recv_sem, device, source=None):
        copy = remote(block if source is None else source, block, send_sem, recv_sem, device)
        copy.start()
        self.sent.append(copy)

    def block(self, offset, owner):
        origin = lax.rem(self.place.s + self.count - offset, self.count)
        return self.out.at[:, origin, owner]

    def landed(self, block, recv_sem):
        remote(block, block, self.sems[1].at[0], recv_sem, self.place.flip_c()).wait_recv()

    def local(self):
        return pltpu.make_async_copy(
            self.own.at[:, self.place.s], self.block(0, self.place.f), self.sems[0].at[0]
        )

    def depart(self, offset):
        place = self.place
        to = lax.rem(place.s + offset, self.count)
        self.send(
            self.block(0, place.f),
            self.sems[1].at[offset],
            self.sems[2].at[offset],
            (to, place.f),
            self.own.at[:, to],
        )

    def onward(self, offset):
        place = self.place
        block = self.block(offset, place.f)
        if offset > 0:
            self.landed(block, self.sems[2].at[offset])
        self.send(block, self.sems[3].at[offset], self.sems[4].at[offset], place.flip_y())
        slot = 2 * offset
        self.send(block, self.sems[5].at[slot], self.sems[6].at[slot], place.flip_c())

    def sideways(self, offset):
        block = self.block(offset, self.y_f)
        self.landed(block, self.sems[4].at[offset])
        slot = 2 * offset + 1
        self.send(block, self.sems[5].at[slot], self.sems[6].at[slot], self.place.flip_c())

    def last(self, offset):
        self.landed(self.block(offset, self.c_f), self.sems[6].at[2 * offset])
        self.landed(self.block(offset, self.yc_f), self.sems[6].at[2 * offset + 1])

    def settle(self):
        for copy in self.sent:
            copy.wait_send()


class Quarter:
    def __init__(self, place, own, out, sems):
        self.place, self.own, self.out, self.sems = place, own, out, sems
        self.sent = []

    @staticmethod
    def semaphores():
        return [DMA((1,)), DMA((3,)), DMA((3,))]

    def local(self):
        return pltpu.make_async_copy(self.own, self.out.at[self.place.f], self.sems[0].at[0])

    def send(self, source, block, slot, device):
        copy = remote(source, block, self.sems[1].at[slot], self.sems[2].at[slot], device)
        copy.start()
        self.sent.append(copy)

    def depart(self):
        place = self.place
        self.send(self.own, self.out.at[place.f], 0, place.flip_y())
        self.send(self.own, self.out.at[place.f], 1, place.flip_c())

    def landed(self, owner, slot):
        block = self.out.at[owner]
        remote(block, block, self.sems[1].at[0], self.sems[2].at[slot], self.place.flip_c()).wait_recv()

    def sideways(self):
        place = self.place
        y_f = place.f + 2 - 4 * place.y
        self.landed(y_f, 0)
        self.send(self.out.at[y_f], self.out.at[y_f], 2, place.flip_c())

    def last(self):
        place = self.place
        self.landed(place.f + 1 - 2 * place.c, 1)
        self.landed(place.f + 2 - 4 * place.y + 1 - 2 * place.c, 2)

    def settle(self):
        for copy in self.sent:
            copy.wait_send()


def stage(gather, step):
    depth = gather.place.depth
    if step < depth:
        gather.arrive(step)
    if 0 <= step - 1 < depth:
        gather.across(step - 1)
    if isinstance(gather, PairGather):
        if 0 <= step - 2 < depth:
            gather.take(step - 2)
        return
    if gather.wide and 0 <= step - 2 < depth:
        gather.hand(step - 2)
    if gather.wide and 0 <= step - 3 < depth:
        gather.take(step - 3)


def turned(vector, cosine, sine):
    return vector * cosine + pltpu.roll(vector, HEAD_DIM // 2, 1) * sine


HEAD_PLAN = (
    ("P0", "P1", "P2", "d1", "d5", "P3", "o0", "d7", "P4", "P5", "project", "K0", "o1", "c0", "n7"),
    ("K1", "K2", "d2", "K3", "K4", "o2", "d6", "c1", "K5", "n0", "A0", "d4", "A1", "o3", "A2"),
    ("o4", "s0", "n6", "A3", "s7", "o5", "mix", "n1", "n5", "d3", "o6", "D", "after", "h0", "h1"),
    ("c2", "s1", "n4", "n3", "s6", "s5", "h2", "n2", "c3", "S", "s3", "s4", "s2", "h3", "h4", "c4"),
)
HEAD_INS = 12
HEAD_OUTS = 13


def head_kernel(depth, *refs):
    (o_own, q_own, k_own, v_own, small_own, gate_own, up_own, down_own) = refs[:8]
    (tokens, cot, angles, begin) = refs[8:HEAD_INS]
    (
        pack_out,
        o_out,
        kv_out,
        cot_out,
        wide_out,
        down_out,
        hidden_out,
        queries,
        mixed,
        lse,
        middle,
        hidden_pair,
        mixed_low,
    ) = refs[HEAD_INS : HEAD_INS + HEAD_OUTS]
    vectors = refs[HEAD_INS + HEAD_OUTS]
    rest = refs[HEAD_INS + HEAD_OUTS + 1 :]
    pack_all, o_all, kv_all, kv_own, hidden_two, lin, m_acc, l_acc, o_acc = rest[:9]
    pack, wide, down, pair, mixed_pair, mixed_far, spread = rest[9:16]
    sems = list(rest[16:])

    def take(count):
        taken = sems[:count]
        del sems[:count]
        return taken

    wide_need = len(Gather.semaphores(depth, True))
    line_need = len(Gather.semaphores(depth, False))
    count = 2 * depth
    devices = 4 * count
    rows, model = tokens.shape
    key_width = KV_HEADS * HEAD_DIM
    group_width = GROUP * HEAD_DIM
    qkv_width = group_width + 2 * HEAD_DIM

    place = Place(depth)
    for g in range(KV_HEADS):
        at = 0
        for source in (q_own, k_own, v_own):
            width = source.shape[1] // KV_HEADS
            pack[g, :, at : at + width] = source[:, g * width : (g + 1) * width]
            at += width
        pack[g, :, at:] = small_own[...]
    greet(place, [(lax.rem(place.s + offset, count), place.f) for offset in range(1, count)])
    pair_need = len(PairGather.semaphores(depth))
    g_pack = PairGather(place, pack, pack_all, take(pair_need), True)
    g_o = Gather(place, True, o_own, o_all, take(wide_need))
    g_kv = PairGather(place, kv_own, kv_all, take(pair_need), False)
    g_cot = Gather(place, False, cot, cot_out, take(line_need + 2), True)
    g_hidden = Gather(place, False, hidden_two, hidden_out, take(line_need))
    x_wide = Exchange(place, wide, wide_out, take(len(Exchange.semaphores(depth))))
    x_down = Quarter(place, down, down_out, take(len(Quarter.semaphores())))
    out_sem, x_send, x_recv = take(3)

    g_pack.begin()
    token_copy = remote(
        tokens, pair.at[place.x], x_send.at[0], x_recv.at[0], place.flip_x()
    )
    token_copy.start()
    pair[place.x] = tokens[...]
    pack_local = g_pack.local()
    pack_local.start()
    pack_local.wait()
    stage(g_pack, 0)
    few = down_own.shape[0]
    filled = down.shape[0]
    for side, source in enumerate((gate_own, up_own)):
        for to in range(count):
            parts = []
            for owner in range(4):
                low = (4 * to + owner) * few
                parts.append(source[:, low : low + few])
                parts.append(jnp.zeros((wide.shape[2], filled - few), BF16))
            wide[side, to] = jnp.concatenate(parts, axis=1)
    down[...] = jnp.concatenate(
        [down_own[...], jnp.zeros((filled - few, model), BF16)], axis=0
    )
    locals_ = [job.local() for job in (g_o, g_cot, x_wide, x_down)]
    for copy in locals_:
        copy.start()
    inputs = tokens[...].astype(F32)
    inv_one = lax.rsqrt(jnp.mean(inputs * inputs, axis=-1, keepdims=True) + EPSILON)
    share = key_width // devices
    chosen = lax.broadcasted_iota(jnp.int32, (model, key_width), 1)
    chosen = lax.div(chosen, share) * (model // devices) + lax.rem(chosen, share)
    chosen = (lax.broadcasted_iota(jnp.int32, (model, key_width), 0) == chosen).astype(BF16)
    for copy in locals_:
        copy.wait()
    part = model // depth
    own_head = pl.ds(pl.multiple_of(place.x * HEAD_DIM, HEAD_DIM), HEAD_DIM)
    own_heads = pl.ds(pl.multiple_of(place.x * group_width, group_width), group_width)
    kv_local = g_kv.local()
    hidden_local = g_hidden.local()
    mixed_copy = remote(
        mixed_pair.at[1 - place.x], mixed_far, x_send.at[1], x_recv.at[1], place.flip_x()
    )

    def project():
        small = pack_all[:, :, :, :, :, qkv_width:].reshape(model, 128).astype(F32).T
        vectors[...] = small[:8]
        spread[...] = jnp.dot(small[:8].astype(BF16), chosen, preferred_element_type=F32)
        token_copy.wait_recv()
        pair_inputs = pair[...].reshape(2 * rows, model).astype(F32)
        inv_pair = lax.rsqrt(jnp.mean(pair_inputs * pair_inputs, axis=-1, keepdims=True) + EPSILON)
        hidden_pair[...] = (pair_inputs * inv_pair * small[0:1]).astype(BF16)
        for zi in range(depth):
            weights = pack_all[zi][:, :, :, :, :qkv_width].reshape(part, qkv_width)
            term = jnp.dot(
                hidden_pair[:, zi * part : (zi + 1) * part], weights, preferred_element_type=F32
            )
            if zi == 0:
                lin[...] = term
            else:
                lin[...] += term
        for x in range(2):
            at = slice(x * rows, (x + 1) * rows)
            head = lin[at, group_width : group_width + HEAD_DIM] + spread[2:3, own_head]
            kv_own[x, :, :HEAD_DIM] = turned(head, angles[x, 0], angles[x, 1]).astype(BF16)
            values = lin[at, group_width + HEAD_DIM :] + spread[3:4, own_head]
            kv_own[x, :, HEAD_DIM:] = values.astype(BF16)
        kv_local.start()

    def queries_of():
        query_bias = vectors[1:2, own_heads]
        for x in range(2):
            for j in range(GROUP):
                lanes = slice(j * HEAD_DIM, (j + 1) * HEAD_DIM)
                head = lin[x * rows : (x + 1) * rows, lanes] + query_bias[:, lanes]
                queries[x, j * rows : (j + 1) * rows, :] = turned(
                    head, angles[x, 0], angles[x, 1]
                ).astype(BF16)
        kv_local.wait()

    span = 4 * rows
    scale = HEAD_DIM ** (-0.5) * LOG2E
    m_acc[...] = jnp.full_like(m_acc, -1e30)
    l_acc[...] = jnp.zeros_like(l_acc)
    o_acc[...] = jnp.zeros_like(o_acc)
    local_rows = lax.broadcasted_iota(jnp.int32, (rows, span), 0)
    offsets = lax.broadcasted_iota(jnp.int32, (rows, span), 1)

    def attend(number, carry):
        keys_at = number * span + offsets
        block = kv_all.at[lax.div(number, 2), lax.rem(number, 2)]
        key = block[:, :, :, :HEAD_DIM].reshape(span, HEAD_DIM)
        value = block[:, :, :, HEAD_DIM:].reshape(span, HEAD_DIM)
        for x in range(2):
            places = ((2 * place.z + x) * 4 + place.f) * rows + local_rows
            visible = jnp.logical_and(keys_at >= begin[x], keys_at <= places)
            scores = mul_t(queries[x], key)
            scores = scores.reshape(GROUP, rows, span) * scale
            scores = jnp.where(visible[None], scores, -1e30).reshape(GROUP * rows, span)
            old = m_acc[x]
            new = jnp.maximum(old, jnp.max(scores, axis=-1, keepdims=True))
            weights = jnp.exp2(scores - new[:, :1])
            weights = jnp.where(
                visible[None], weights.reshape(GROUP, rows, span), 0.0
            ).reshape(GROUP * rows, span)
            fade = jnp.exp2(old - new)
            l_acc[x] = l_acc[x] * fade + jnp.sum(weights, axis=-1, keepdims=True)
            o_acc[x] = o_acc[x] * fade + jnp.dot(
                weights.astype(BF16), value, preferred_element_type=F32
            )
            m_acc[x] = new
        return carry

    def attend_quarter(piece):
        low, high = piece * count // 4, (piece + 1) * count // 4
        reach = 2 * place.z + 2
        lax.fori_loop(jnp.minimum(low, reach), jnp.minimum(high, reach), attend, 0)

    def mix():
        for x in range(2):
            total = o_acc[x] / l_acc[x]
            mixed[x] = total
            lse[x] = m_acc[x] + jnp.log2(l_acc[x])
            mixed_pair[x] = total.astype(BF16)
        mixed_copy.start()

    def after_attention():
        mixed_copy.wait_recv()
        for j in range(GROUP):
            at = slice(j * rows, (j + 1) * rows)
            near = pl.multiple_of((place.x * GROUP + j) * HEAD_DIM, HEAD_DIM)
            far = pl.multiple_of(((1 - place.x) * GROUP + j) * HEAD_DIM, HEAD_DIM)
            mixed_low[:, pl.ds(near, HEAD_DIM)] = mixed_pair[place.x, at, :]
            mixed_low[:, pl.ds(far, HEAD_DIM)] = mixed_far[at, :]
        after = inputs
        for zi in range(depth):
            after = after + jnp.dot(
                mixed_low[:, zi * part : (zi + 1) * part],
                o_all[zi].reshape(part, model),
                preferred_element_type=F32,
            )
        middle[...] = after
        inv_two = lax.rsqrt(jnp.mean(after * after, axis=-1, keepdims=True) + EPSILON)
        hidden_two[...] = (after * inv_two * vectors[4:5]).astype(BF16)
        hidden_local.start()

    jobs = {"P": g_pack, "K": g_kv, "o": g_o, "c": g_cot, "h": g_hidden}
    moves = {"d": x_wide.depart, "n": x_wide.onward, "s": x_wide.sideways, "A": attend_quarter}
    works = {
        "project": project,
        "mix": mix,
        "after": after_attention,
        "D": x_down.depart,
        "S": x_down.sideways,
    }
    for words in HEAD_PLAN:
        for word in words:
            if word in works:
                works[word]()
            elif word[0] in moves:
                moves[word[0]](int(word[1:]))
            elif word != "P0":
                stage(jobs[word[0]], int(word[1:]))
                if word == "K0":
                    queries_of()

    keeps = []
    for number, (source, target) in enumerate(
        ((pack_all, pack_out), (o_all, o_out), (kv_all, kv_out))
    ):
        copy = pltpu.make_async_copy(source, target, out_sem.at[number])
        copy.start()
        keeps.append(copy)
    hidden_local.wait()
    for offset in range(count):
        x_wide.last(offset)
    x_down.last()
    for copy in keeps:
        copy.wait()
    token_copy.wait_send()
    mixed_copy.wait_send()
    for job in (g_pack, g_o, g_kv, g_cot, g_hidden, x_wide, x_down):
        job.settle()


def call_head(depth, collective_id, hbm, vmems):
    (o_own,) = hbm
    q_own, k_own, v_own, small_own, gate_own, _, down_own, tokens, cot = vmems[:9]
    count = 2 * depth
    few = down_own.shape[0]
    filled = -(-few // 16) * 16
    qkv_width = (GROUP + 2) * HEAD_DIM
    width = qkv_width + small_own.shape[1]
    pack = jax.ShapeDtypeStruct((q_own.shape[0], width), BF16)
    wide = jax.ShapeDtypeStruct((2, count, gate_own.shape[0], 4 * filled), BF16)
    down = jax.ShapeDtypeStruct((filled, down_own.shape[1]), BF16)
    rows, model = tokens.shape
    key_width = KV_HEADS * HEAD_DIM
    stacked = GROUP * rows
    kv_own = jax.ShapeDtypeStruct((rows, 2 * HEAD_DIM), BF16)
    any_, vmem = pl.BlockSpec(memory_space=pl.ANY), pl.BlockSpec(memory_space=pltpu.VMEM)
    heads = (KV_HEADS, stacked, HEAD_DIM)
    outs = [
        gather_shape(depth, True, pack),
        gather_shape(depth, True, o_own),
        gather_shape(depth, True, kv_own),
        gather_shape(depth, False, cot),
        jax.ShapeDtypeStruct((2, count, 4) + wide.shape[2:], BF16),
        jax.ShapeDtypeStruct((4,) + down.shape, BF16),
        gather_shape(depth, False, tokens),
        jax.ShapeDtypeStruct(heads, BF16),
        jax.ShapeDtypeStruct(heads, F32),
        jax.ShapeDtypeStruct(heads, F32),
        jax.ShapeDtypeStruct((rows, model), F32),
        jax.ShapeDtypeStruct((2 * rows, model), BF16),
        jax.ShapeDtypeStruct((rows, model), BF16),
        jax.ShapeDtypeStruct((8, model), F32),
    ]
    scratch = [pltpu.VMEM(out.shape, BF16) for out in outs[:3]]
    scratch += [
        pltpu.VMEM((2,) + kv_own.shape, BF16),
        pltpu.VMEM((rows, model), BF16),
        pltpu.VMEM((2 * rows, qkv_width), F32),
        pltpu.VMEM(heads, F32),
        pltpu.VMEM(heads, F32),
        pltpu.VMEM(heads, F32),
        pltpu.VMEM((KV_HEADS,) + pack.shape, BF16),
        pltpu.VMEM(wide.shape, BF16),
        pltpu.VMEM(down.shape, BF16),
        pltpu.VMEM((2, rows, model), BF16),
        pltpu.VMEM(heads, BF16),
        pltpu.VMEM(heads[1:], BF16),
        pltpu.VMEM((8, key_width), F32),
    ]
    scratch += PairGather.semaphores(depth) + Gather.semaphores(depth, True)
    scratch += PairGather.semaphores(depth)
    scratch += Gather.semaphores(depth, False, True) + Gather.semaphores(depth, False)
    scratch += Exchange.semaphores(depth) + Quarter.semaphores()
    scratch += [DMA((3,)), DMA((2,)), DMA((2,))]
    return pl.pallas_call(
        functools.partial(head_kernel, depth),
        out_shape=outs,
        in_specs=[any_] + [vmem] * len(vmems),
        out_specs=[any_] * 7 + [vmem] * 7,
        scratch_shapes=scratch,
        compiler_params=pltpu.CompilerParams(
            collective_id=collective_id, has_side_effects=True, vmem_limit_bytes=VMEM_LIMIT
        ),
    )(*hbm, *vmems)


def t_mul(left, right):
    return lax.dot_general(left, right, (((0,), (0,)), ((), ())), preferred_element_type=F32)


def mul_t(left, right):
    return lax.dot_general(left, right, (((1,), (1,)), ((), ())), preferred_element_type=F32)


CUTS = ((0, 512), (512, 1024), (1024, 1152))


def middle_kernel(depth, *refs):
    (hidden_all, cot_all, wide_all, down_all, o_own) = refs[:5]
    (middle, cotangent, vectors) = refs[5:8]
    (layer_out, d_middle, d_mixed, d_branch, gain_two, down_out, wide_out) = refs[8:15]
    (tokens_v, grads_v, w_part, d_part, act, d_gate, d_up, dh_part, out_part) = refs[15:24]
    (dh_sum, out_sum, w_core, w_y, d_core, o_all) = refs[24:30]
    rest = list(refs[30:])

    def take(count):
        taken = rest[:count]
        del rest[:count]
        return taken

    count = 2 * depth
    rows, model = middle.shape
    units = act.shape[2]
    part = model // depth
    buffers, sems = Reduce.scratch(depth, False, (rows, model))
    place = Place(depth)
    greet(place)
    r_dh = Reduce(place, False, rows, dh_part, dh_sum, take(len(buffers)), take(len(sems)))
    r_out = Reduce(place, False, rows, out_part, out_sum, take(len(buffers)), take(len(sems)))
    load_sem, wc_send, wc_recv, wy_send, wy_recv, dc_send, dc_recv = take(7)
    sent = []

    def send(src, dst, send_sem, recv_sem, device):
        copy = remote(src, dst, send_sem, recv_sem, device)
        copy.start()
        sent.append(copy)

    def landed(ref, recv_sem):
        remote(ref, ref, wc_send.at[0], recv_sem, place.flip_c()).wait_recv()

    loads = [
        pltpu.make_async_copy(source, target, load_sem.at[number])
        for number, (source, target) in enumerate(
            (
                (hidden_all, tokens_v),
                (wide_all, w_part),
                (cot_all, grads_v),
                (down_all, d_part),
            )
        )
    ]
    for copy in loads:
        copy.start()
    mine_y, other_y = place.y, 1 - place.y
    wide_rows = w_part.shape[-2]
    half = lax.div(place.z, 2)
    tiles = [3 - 3 * half, 2 - half, 1 + 4 * half - place.z, place.z]
    for copy in loads:
        copy.wait()

    def weights(side, low, high):
        return w_part[side, :, :, :, :, low:high].reshape(model, high - low)

    def forward(zi):
        tokens = tokens_v[zi].reshape(2 * rows, model)
        grads = grads_v[zi].reshape(2 * rows, model)
        out = None
        for low, high in CUTS:
            gate = jnp.dot(tokens, weights(0, low, high), preferred_element_type=F32)
            up = jnp.dot(tokens, weights(1, low, high), preferred_element_type=F32)
            d_act = mul_t(grads, d_part[low:high, :])
            sigma = jax.nn.sigmoid(gate)
            silu = gate * sigma
            act[zi, :, low:high] = (silu * up).astype(BF16)
            d_gate[zi, :, low:high] = (
                d_act * up * sigma * (1.0 + gate * (1.0 - sigma))
            ).astype(BF16)
            d_up[zi, :, low:high] = (d_act * silu).astype(BF16)
        total = mul_t(d_gate[zi], weights(0, 0, units)) + mul_t(d_up[zi], weights(1, 0, units))
        dh_part[zi] = total.astype(BF16).reshape(2, rows, model)
        out = jnp.dot(act[zi], d_part[...], preferred_element_type=F32)
        out_part[zi] = out.astype(BF16).reshape(2, rows, model)

    def tile(number, carry):
        zi = jnp.where(
            number == 0,
            tiles[0],
            jnp.where(number == 1, tiles[1], jnp.where(number == 2, tiles[2], tiles[3])),
        )
        forward(zi)
        r_dh.cross(zi)
        return carry

    lax.fori_loop(0, depth, tile, 0)
    for zi in tiles:
        r_out.cross(zi)
    r_dh.crossed()
    r_out.crossed()

    def wide_chunk(k, carry):
        lanes = pl.ds(pl.multiple_of(k * part, part), part)
        tokens = tokens_v[:, :, :, lanes].reshape(count * rows, part)
        for side, grad in enumerate((d_gate, d_up)):
            term = t_mul(tokens, grad[...].reshape(count * rows, units)).astype(BF16)
            w_part[side, pl.ds(2 * k, 2)] = term.reshape(2, 2, 2, wide_rows, units)
        for step in range(2):
            to = 2 * k + step
            for y in range(2):
                remote(
                    w_part.at[:, to, y, 1 - place.c],
                    w_core.at[y, to],
                    wc_send.at[2 * to + y],
                    wc_recv.at[2 * to + y],
                    place.flip_c(),
                ).start()
        return carry

    def wide_cores(to):
        for y in (other_y, mine_y):
            landed(w_core.at[y, to], wc_recv.at[2 * to + y])
            for side in range(2):
                add_into(
                    w_core.at[y, to, side], w_part.at[side, to, y, place.c], wide_rows
                )
            if y is other_y:
                remote(
                    w_core.at[y, to], w_y.at[to], wy_send.at[to], wy_recv.at[to], place.flip_y()
                ).start()

    def wide_across(to, carry):
        landed(w_y.at[to], wy_recv.at[to])
        for side in range(2):
            add_into(w_y.at[to, side], w_core.at[mine_y, to, side], wide_rows)
        pltpu.make_async_copy(w_y.at[to], wide_out.at[to], load_sem.at[to]).start()
        return carry

    def wide_step(k, carry):
        wide_chunk(k, 0)
        pl.when(k > 0)(lambda: wide_cores(2 * k - 2))
        pl.when(k > 0)(lambda: wide_cores(2 * k - 1))
        return carry

    order = list(range(depth - 1, -1, -1))
    lax.fori_loop(0, depth - 2, wide_step, 0)
    r_dh.along(order[0])
    r_dh.along(order[1])
    lax.fori_loop(depth - 2, depth, wide_step, 0)
    wide_cores(count - 2)
    wide_cores(count - 1)
    r_dh.along(order[2])
    pieces = [
        pltpu.make_async_copy(o_own.at[zi], o_all.at[zi % 2], load_sem.at[zi])
        for zi in range(depth)
    ]
    for copy in pieces[:2]:
        copy.start()

    def down_chunk(k, carry):
        lanes = pl.ds(pl.multiple_of(k * part, part), part)
        grads = grads_v[:, :, :, lanes].reshape(count * rows, part)
        d_part[:, lanes] = t_mul(act[...].reshape(count * rows, units), grads).astype(BF16)
        return carry

    lax.fori_loop(0, depth, down_chunk, 0)
    down_rows = units // 4

    def down_block(owner):
        return d_part.at[pl.ds(pl.multiple_of(owner * down_rows, down_rows), down_rows)]

    for y in (other_y, mine_y):
        send(
            down_block(2 * y + 1 - place.c),
            d_core.at[y],
            dc_send.at[y],
            dc_recv.at[y],
            place.flip_c(),
        )
    r_dh.along(order[3])
    r_dh.finish()

    after = middle[...]
    inv_two = lax.rsqrt(jnp.mean(after * after, axis=-1, keepdims=True) + EPSILON)
    normed = after * inv_two
    d_hidden = dh_sum[...]
    gain_two[...] = jnp.broadcast_to(
        jnp.sum(d_hidden * normed, axis=0, keepdims=True), gain_two.shape
    )
    scaled = d_hidden * vectors[4:5]
    total = cotangent[...].astype(F32) + inv_two * (
        scaled - normed * jnp.mean(scaled * normed, axis=-1, keepdims=True)
    )
    d_middle[...] = total
    d_branch[...] = total.astype(BF16)
    for zi in range(depth):
        pieces[zi].wait()
        term = mul_t(d_branch[...], o_all[zi % 2].reshape(part, model)).astype(BF16)
        for piece in range(part // HEAD_DIM):
            h = zi * (part // HEAD_DIM) + piece
            at = (h % GROUP) * rows
            d_mixed[h // GROUP, at : at + rows, :] = term[
                :, piece * HEAD_DIM : (piece + 1) * HEAD_DIM
            ]
        if zi + 2 < depth:
            pieces[zi + 2].start()
    for y in (other_y, mine_y):
        landed(d_core.at[y], dc_recv.at[y])
        add_into(d_core.at[y], down_block(2 * y + place.c), down_rows)
    keep = pltpu.make_async_copy(d_core, down_out, load_sem.at[count])
    keep.start()
    for step in range(depth):
        r_out.along(order[step])
        lax.fori_loop(2 * step, 2 * step + 2, wide_across, 0)
    r_out.finish()
    layer_out[...] = (middle[...] + out_sum[...]).astype(BF16)
    keep.wait()

    def end(to, carry):
        pltpu.make_async_copy(w_y.at[to], wide_out.at[to], load_sem.at[to]).wait()
        for y in range(2):
            slot = 2 * to + y
            remote(
                w_core.at[y, to], w_core.at[y, to], wc_send.at[slot], wc_recv.at[slot], place.flip_c()
            ).wait_send()
        remote(
            w_y.at[to], w_y.at[to], wy_send.at[to], wy_recv.at[to], place.flip_y()
        ).wait_send()
        return carry

    lax.fori_loop(0, count, end, 0)
    r_dh.settle()
    r_out.settle()
    for copy in sent:
        copy.wait_send()


def call_middle(depth, collective_id, hbm, vmems):
    hidden, cot, wide, down, o_all = hbm
    count = 2 * depth
    rows, model = vmems[0].shape
    units, wide_rows = wide.shape[-1], wide.shape[-2]
    any_, vmem = pl.BlockSpec(memory_space=pl.ANY), pl.BlockSpec(memory_space=pltpu.VMEM)
    buffers, sems = Reduce.scratch(depth, False, (rows, model))
    scratch = [pltpu.VMEM((depth, 2, rows, model), BF16)] * 2
    scratch += [pltpu.VMEM(wide.shape, BF16), pltpu.VMEM(down.shape, BF16)]
    scratch += [pltpu.VMEM((depth, 2 * rows, units), BF16)] * 3
    scratch += [pltpu.VMEM((depth, 2, rows, model), BF16)] * 2
    scratch += [pltpu.VMEM((rows, model), F32)] * 2
    scratch += [
        pltpu.VMEM((2, count, 2, wide_rows, units), BF16),
        pltpu.VMEM((count, 2, wide_rows, units), BF16),
        pltpu.VMEM((2, units // 4, model), BF16),
        pltpu.VMEM((2,) + o_all.shape[1:], BF16),
    ]
    scratch += buffers + sems + buffers + sems
    scratch += [DMA((count + 1,)), DMA((2 * count,)), DMA((2 * count,))]
    scratch += [DMA((count,)), DMA((count,)), DMA((2,)), DMA((2,))]
    return pl.pallas_call(
        functools.partial(middle_kernel, depth),
        out_shape=[
            jax.ShapeDtypeStruct((rows, model), BF16),
            jax.ShapeDtypeStruct((rows, model), F32),
            jax.ShapeDtypeStruct((KV_HEADS, GROUP * rows, HEAD_DIM), BF16),
            jax.ShapeDtypeStruct((rows, model), BF16),
            jax.ShapeDtypeStruct((8, model), F32),
            jax.ShapeDtypeStruct((2, units // 4, model), BF16),
            jax.ShapeDtypeStruct((count, 2, wide_rows, units), BF16),
        ],
        in_specs=[any_] * 5 + [vmem] * 3,
        out_specs=[vmem] * 5 + [any_] * 2,
        scratch_shapes=scratch,
        compiler_params=pltpu.CompilerParams(
            collective_id=collective_id, has_side_effects=True, vmem_limit_bytes=VMEM_JOINED
        ),
    )(*hbm, *vmems)


LAST_PLAN = (
    ("down", "d4", "out", "delta", "Co0", "a0", "d1", "d5", "Ck0"),
    ("a1", "Bo0", "a2", "Ck2", "d3", "Co2", "a3", "Ck1", "Co3"),
    ("d2", "Bo2", "Yk0", "Co1", "Yk1", "Ao0", "Yk2", "Ck3", "d7"),
    ("Bo3", "Yk3", "Zk0", "Zk1", "Zo0", "turn", "Bo1", "query", "Zk2"),
    ("Ao2", "Cq2", "hq", "Zk3", "Cq3", "key", "Cq0", "hk", "Ao1"),
    ("Cq1", "kg", "Cs0", "d6", "Yq0", "Cs2", "Ys0", "Yq3", "Ys2"),
    ("Yq1", "hw", "Zo1", "Zq0", "Cs1", "small", "Ct1", "Ct0", "Ao3"),
    ("Cs3", "Yt0", "Yq2", "Ct3", "Zo2", "Ys1", "Zs0", "Yt1", "Ct2"),
    ("Ys3", "input", "Zt0", "Zq1", "Zo3", "Zs1", "Zt1", "Zq2", "Yt2"),
    ("Zs2", "Zt2", "Yt3", "Zq3", "Xq", "Zt3", "Xt", "Zs3", "Xs"),
)


def follow_last(plan, works, depart, attend_wave, jobs):
    depth = 4
    steps = {"C": "cores", "B": "over_second", "A": "over_first", "Z": "along", "Y": "over"}
    for words in plan:
        for word in words:
            if word in works:
                works[word]()
            elif word[0] == "d":
                depart(int(word[1:]))
            elif word[0] == "a":
                attend_wave(int(word[1:]))
            else:
                getattr(jobs[word[1]], steps[word[0]])(depth - 1 - int(word[2:]))


def last_kernel(depth, *refs):
    (kv_own, pack_own, wide, down) = refs[:4]
    (queries, mixed, lse, d_mixed, angles, begin) = refs[4:10]
    (tokens, d_middle, vectors, gain_two, hidden_pair, mixed_low, d_branch) = refs[10:17]
    (input_grad, q_out, kv_out, small_out, o_out, down_out, wide_out) = refs[17:24]
    (kv_all, weights, d_query, delta, d_lin, d_keys, d_kv) = refs[24:31]
    (o_part, q_part, kv_part, small_part) = refs[31:35]
    (d_near, d_far, d_hidden, kv_weights, d_pair, h_send, h_far, lines, pairs) = refs[35:44]
    rest = list(refs[44:])

    def take(number):
        taken = rest[:number]
        del rest[:number]
        return taken

    count = 2 * depth
    devices = 4 * count
    rows, model = tokens.shape
    part = model // depth
    key_width = KV_HEADS * HEAD_DIM
    group_width = GROUP * HEAD_DIM
    qkv_width = group_width + 2 * HEAD_DIM
    model_rows = model // devices
    share = key_width // devices
    span = 4 * rows
    score_scale = HEAD_DIM ** (-0.5)
    scale = score_scale * LOG2E

    place = Place(depth)
    greet(place, [(lax.rem(place.s + offset, count), place.f) for offset in range(1, count)])
    buffers, sems = Reduce.scratch(depth, True, o_part.shape[-2:])
    r_o = Reduce(
        place, True, model_rows, o_part, o_out, take(len(buffers)), take(len(sems))
    )

    def reduce_of(own, out, causal=False, crossing=True):
        buffers, sems = PairReduce.scratch(depth, own.shape[-2:])
        return PairReduce(
            place, own, out, take(len(buffers)), take(len(sems)), causal, crossing
        )

    r_kv = reduce_of(d_keys, d_kv, True, False)
    r_q = reduce_of(q_part, q_out)
    r_s = reduce_of(kv_part, kv_out)
    r_t = reduce_of(small_part, small_out)
    load_sem, e_send, e_recv, y_send, y_recv, x_send, x_recv = take(7)
    order = list(range(depth - 1, -1, -1))
    sent = []

    def depart(offset):
        to = lax.rem(place.s + offset, count)
        copy = remote(
            wide.at[to], wide_out.at[place.s], e_send.at[offset], e_recv.at[offset], (to, place.f)
        )
        copy.start()
        sent.append(copy)

    mixed_copy = remote(
        d_mixed.at[1 - place.x],
        d_pair.at[place.x],
        x_send.at[0],
        x_recv.at[0],
        place.flip_x(),
    )
    mixed_copy.start()
    sent.append(mixed_copy)
    d_pair[place.x] = d_mixed[place.x]
    kv_load = pltpu.make_async_copy(kv_own, kv_all, load_sem.at[0])
    kv_load.start()
    own_wide = pltpu.make_async_copy(wide.at[place.s], wide_out.at[place.s], load_sem.at[1])
    own_wide.start()
    down_load = pltpu.make_async_copy(down.at[place.y], d_near, load_sem.at[2 + depth])
    down_load.start()
    down_copy = remote(
        down.at[1 - place.y], d_far, y_send.at[0], y_recv.at[0], place.flip_y()
    )
    hidden_copy = remote(h_send, h_far, x_send.at[1], x_recv.at[1], place.flip_x())
    loads = [
        pltpu.make_async_copy(pack_own.at[zi], weights.at[zi % 2], load_sem.at[2 + zi])
        for zi in range(depth)
    ]

    local_rows = lax.broadcasted_iota(jnp.int32, (rows, span), 0)
    offsets = lax.broadcasted_iota(jnp.int32, (rows, span), 1)

    def attend(number, carry):
        keys_at = number * span + offsets
        z, x_at = lax.div(number, 2), lax.rem(number, 2)
        block = kv_all.at[z, x_at]
        key = block[:, :, :, :HEAD_DIM].reshape(span, HEAD_DIM)
        value = block[:, :, :, HEAD_DIM:].reshape(span, HEAD_DIM)
        d_key, d_value = None, None
        for x in range(2):
            places = ((2 * place.z + x) * 4 + place.f) * rows + local_rows
            visible = jnp.logical_and(keys_at >= begin[x], keys_at <= places)
            scores = mul_t(queries[x], key)
            d_probs = mul_t(d_pair[x], value)
            probs = jnp.exp2(scores * scale - lse[x][:, :1])
            probs = jnp.where(
                visible[None], probs.reshape(GROUP, rows, span), 0.0
            ).reshape(GROUP * rows, span)
            d_scores = (probs * (d_probs - delta[x][:, :1])).astype(BF16)
            d_query[x] += jnp.dot(d_scores, key, preferred_element_type=F32)
            key_term = t_mul(d_scores, queries[x])
            value_term = t_mul(probs.astype(BF16), d_pair[x])
            d_key = key_term if x == 0 else d_key + key_term
            d_value = value_term if x == 0 else d_value + value_term
        target = d_keys.at[z, x_at]
        target[:, :, :, :HEAD_DIM] = d_key.astype(BF16).reshape(2, 2, rows, HEAD_DIM)
        target[:, :, :, HEAD_DIM:] = d_value.astype(BF16).reshape(2, 2, rows, HEAD_DIM)
        return carry

    inputs = tokens[...].astype(F32)
    inv_one = lax.rsqrt(jnp.mean(inputs * inputs, axis=-1, keepdims=True) + EPSILON)
    normed = inputs * inv_one

    def out_gradient():
        for copy in loads[:2]:
            copy.start()
        for zi in range(depth):
            lanes = slice(zi * part, (zi + 1) * part)
            term = t_mul(mixed_low[:, lanes], d_branch[...]).astype(BF16)
            o_part[zi] = term.reshape(2, 2, 2, model_rows, model)

    def deltas():
        mixed_copy.wait_recv()
        for x in range(2):
            delta[x] = jnp.broadcast_to(
                jnp.sum(d_pair[x].astype(F32) * mixed[x], axis=-1, keepdims=True),
                delta.shape[1:],
            )
        d_query[...] = jnp.zeros_like(d_query)
        kv_load.wait()

    def attend_wave(step):
        zi = place.z - order[step]
        low = jnp.maximum(2 * zi, 0)
        high = jnp.maximum(2 * zi + 2, 0)
        lax.fori_loop(low, high, attend, 0)

    def query_turn():
        for x in range(2):
            for j in range(GROUP):
                lanes = slice(j * HEAD_DIM, (j + 1) * HEAD_DIM)
                head = d_query[x, j * rows : (j + 1) * rows, :] * score_scale
                d_lin[x * rows : (x + 1) * rows, lanes] = turned(
                    head, angles[x, 0], -angles[x, 1]
                ).astype(BF16)

    def query_gradient():
        for zi in range(depth):
            lanes = slice(zi * part, (zi + 1) * part)
            term = t_mul(hidden_pair[:, lanes], d_lin[:, :group_width]).astype(BF16)
            q_part[zi] = term.reshape(2, 2, 2, model_rows, group_width)

    def key_turn():
        r_kv.finish()
        for x in range(2):
            at = slice(x * rows, (x + 1) * rows)
            head = d_kv[x, :, :HEAD_DIM] * score_scale
            d_lin[at, group_width : group_width + HEAD_DIM] = turned(
                head, angles[x, 0], -angles[x, 1]
            ).astype(BF16)
            d_lin[at, group_width + HEAD_DIM :] = d_kv[x, :, HEAD_DIM:].astype(BF16)

    def hidden_query():
        for zi in range(depth):
            lanes = slice(zi * part, (zi + 1) * part)
            loads[zi].wait()
            block = weights[zi % 2][:, :, :, :, :group_width].reshape(part, group_width)
            term = mul_t(d_lin[:, :group_width], block)
            for x in range(2):
                d_hidden[x, :, lanes] = term[x * rows : (x + 1) * rows]
            block = weights[zi % 2][:, :, :, :, group_width:qkv_width]
            kv_weights[lanes, :] = block.reshape(part, 2 * HEAD_DIM)
            if zi + 2 < depth:
                loads[zi + 2].start()

    def hidden_key():
        for zi in range(depth):
            lanes = slice(zi * part, (zi + 1) * part)
            term = mul_t(d_lin[:, group_width:], kv_weights[lanes, :])
            for x in range(2):
                d_hidden[x, :, lanes] += term[x * rows : (x + 1) * rows]
        h_send[...] = d_hidden[1 - place.x].astype(BF16)
        hidden_copy.start()

    def key_gradient():
        for zi in range(depth):
            lanes = slice(zi * part, (zi + 1) * part)
            term = t_mul(hidden_pair[:, lanes], d_lin[:, group_width:]).astype(BF16)
            kv_part[zi] = term.reshape(2, 2, 2, model_rows, 2 * HEAD_DIM)

    def hidden_whole():
        hidden_copy.wait_recv()
        d_hidden[place.x] += h_far[...].astype(F32)

    def small_gradients():
        lines[...] = jnp.zeros_like(lines)
        pairs[...] = jnp.zeros_like(pairs)
        bias = jnp.sum(d_lin[...].astype(F32), axis=0, keepdims=True)
        own_head = pl.ds(pl.multiple_of(place.x * HEAD_DIM, HEAD_DIM), HEAD_DIM)
        own_heads = pl.ds(pl.multiple_of(place.x * group_width, group_width), group_width)
        lines[0:1, :] = jnp.sum(d_hidden[place.x] * normed, axis=0, keepdims=True)
        lines[1:2, own_heads] = bias[:, :group_width]
        lines[4:5, :] = gain_two[0:1]
        pairs[0:1, own_head] = bias[:, group_width : group_width + HEAD_DIM]
        pairs[1:2, own_head] = bias[:, group_width + HEAD_DIM :]
        chosen = lax.broadcasted_iota(jnp.int32, (key_width, model), 0)
        chosen = lax.div(chosen, share) * model_rows + lax.rem(chosen, share)
        chosen = (lax.broadcasted_iota(jnp.int32, (key_width, model), 1) == chosen).astype(BF16)
        spread = jnp.dot(pairs[...].astype(BF16), chosen, preferred_element_type=F32)
        lines[2:4, :] = spread[0:2]
        small = jnp.concatenate([lines[...], jnp.zeros((120, model), F32)], axis=0)
        small = small.T.astype(BF16)
        for zi in range(depth):
            small_part[zi] = small[zi * part : (zi + 1) * part].reshape(2, 2, 2, model_rows, 128)

    def input_gradient():
        scaled = d_hidden[place.x] * vectors[0:1]
        input_grad[...] = d_middle[...] + inv_one * (
            scaled - normed * jnp.mean(scaled * normed, axis=-1, keepdims=True)
        )

    works = {
        "out": out_gradient,
        "delta": deltas,
        "turn": query_turn,
        "query": query_gradient,
        "key": key_turn,
        "hq": hidden_query,
        "hk": hidden_key,
        "kg": key_gradient,
        "hw": hidden_whole,
        "Xq": r_q.swap,
        "Xs": r_s.swap,
        "Xt": r_t.swap,
        "small": small_gradients,
        "input": input_gradient,
        "down": down_copy.start,
    }
    jobs = {"o": r_o, "k": r_kv, "q": r_q, "s": r_s, "t": r_t}
    follow_last(LAST_PLAN, works, depart, attend_wave, jobs)
    for job in (r_o, r_q, r_s, r_t):
        job.finish()
    for offset in range(1, count):
        origin = lax.rem(place.s + count - offset, count)
        block = wide_out.at[origin]
        remote(block, block, e_send.at[0], e_recv.at[offset], place.flip_c()).wait_recv()
    own_wide.wait()
    down_load.wait()
    down_copy.wait()
    down_out[...] = d_near[...].astype(F32) + d_far[...].astype(F32)
    hidden_copy.wait_send()
    for job in (r_kv, r_o, r_q, r_s, r_t):
        job.settle()
    for copy in sent:
        copy.wait_send()


def call_last(depth, collective_id, hbm, vmems):
    kv_all, pack_all, wide, down = hbm
    tokens = vmems[6]
    count = 2 * depth
    rows, model = tokens.shape
    model_rows = model // (4 * count)
    key_width, group_width = KV_HEADS * HEAD_DIM, GROUP * HEAD_DIM
    heads = (2, GROUP * rows, HEAD_DIM)
    lead = (depth, 2, 2, 2)
    kv_block, o_block = (rows, 2 * HEAD_DIM), (model_rows, model)
    blocks = [
        (model_rows, group_width),
        (model_rows, 2 * HEAD_DIM),
        (model_rows, 128),
    ]
    scratch = [
        pltpu.VMEM(kv_all.shape, BF16),
        pltpu.VMEM((2,) + pack_all.shape[1:], BF16),
        pltpu.VMEM(heads, F32),
        pltpu.VMEM(heads, F32),
        pltpu.VMEM((2 * rows, group_width + 2 * HEAD_DIM), BF16),
        pltpu.VMEM(lead + kv_block, BF16),
        pltpu.VMEM((2,) + kv_block, F32),
        pltpu.VMEM(lead + o_block, BF16),
    ]
    scratch += [pltpu.VMEM(lead + block, BF16) for block in blocks]
    scratch += [pltpu.VMEM(down.shape[1:], BF16)] * 2
    scratch += [
        pltpu.VMEM((2, rows, model), F32),
        pltpu.VMEM((model, 2 * HEAD_DIM), BF16),
        pltpu.VMEM(heads, BF16),
        pltpu.VMEM((rows, model), BF16),
        pltpu.VMEM((rows, model), BF16),
        pltpu.VMEM((8, model), F32),
        pltpu.VMEM((8, key_width), F32),
    ]
    buffers, sems = Reduce.scratch(depth, True, o_block)
    scratch += buffers + sems
    for block in [kv_block] + blocks:
        buffers, sems = PairReduce.scratch(depth, block)
        scratch += buffers + sems
    scratch += [DMA((3 + depth,)), DMA((count,)), DMA((count,)), DMA((1,)), DMA((1,))]
    scratch += [DMA((2,)), DMA((2,))]
    any_, vmem = pl.BlockSpec(memory_space=pl.ANY), pl.BlockSpec(memory_space=pltpu.VMEM)
    return pl.pallas_call(
        functools.partial(last_kernel, depth),
        out_shape=[
            jax.ShapeDtypeStruct((rows, model), F32),
            jax.ShapeDtypeStruct((2,) + blocks[0], F32),
            jax.ShapeDtypeStruct((2,) + blocks[1], F32),
            jax.ShapeDtypeStruct((2,) + blocks[2], F32),
            jax.ShapeDtypeStruct(o_block, F32),
            jax.ShapeDtypeStruct(down.shape[1:], F32),
            jax.ShapeDtypeStruct(wide.shape, BF16),
        ],
        in_specs=[any_] * 4 + [vmem] * len(vmems),
        out_specs=[vmem] * 7,
        scratch_shapes=scratch,
        compiler_params=pltpu.CompilerParams(
            collective_id=collective_id, has_side_effects=True, vmem_limit_bytes=VMEM_JOINED
        ),
    )(*hbm, *vmems)


def finish_kernel(few, plain, *refs):
    wide, down, q_in, kv_in, small_in = refs[:5]
    sources = refs[5 : 5 + plain]
    gate_out, up_out, down_out, q_out, k_out, v_out, vectors = refs[5 + plain : 12 + plain]
    targets = refs[12 + plain : 12 + 2 * plain]
    for source, target in zip(sources, targets):
        target[...] = source[...]
    down_out[...] = down[:few, :]
    filled = wide.shape[3] // 4
    for side, out in enumerate((gate_out, up_out)):
        for place in range(wide.shape[0]):
            block = wide[place, side].astype(F32)
            for owner in range(4):
                low = (4 * place + owner) * few
                out[:, low : low + few] = block[:, owner * filled : owner * filled + few]
    for g in range(KV_HEADS):
        width = q_in.shape[2]
        q_out[:, g * width : (g + 1) * width] = q_in[g]
        lanes = slice(g * HEAD_DIM, (g + 1) * HEAD_DIM)
        k_out[:, lanes] = kv_in[g, :, :HEAD_DIM]
        v_out[:, lanes] = kv_in[g, :, HEAD_DIM:]
    vectors[...] = (small_in[0] + small_in[1]).T[:8]


def call_finish(few, wide, down, q_grad, kv_grad, small_grad, plain):
    seq, _, rows, _ = wide.shape
    key_width = KV_HEADS * HEAD_DIM
    units = seq * 4 * few
    vmem = pl.BlockSpec(memory_space=pltpu.VMEM)
    out_shape = [
        jax.ShapeDtypeStruct((rows, units), F32),
        jax.ShapeDtypeStruct((rows, units), F32),
        jax.ShapeDtypeStruct((few, down.shape[1]), F32),
        jax.ShapeDtypeStruct((rows, HEADS * HEAD_DIM), F32),
        jax.ShapeDtypeStruct((rows, key_width), F32),
        jax.ShapeDtypeStruct((rows, key_width), F32),
        jax.ShapeDtypeStruct((8, rows), F32),
    ] + [jax.ShapeDtypeStruct(array.shape, array.dtype) for array in plain]
    return pl.pallas_call(
        functools.partial(finish_kernel, few, len(plain)),
        out_shape=out_shape,
        in_specs=[vmem] * (5 + len(plain)),
        out_specs=[vmem] * len(out_shape),
        compiler_params=pltpu.CompilerParams(vmem_limit_bytes=VMEM_LIMIT),
    )(wide, down, q_grad, kv_grad, small_grad, *plain)


def begin_of(positions, lengths):
    ends = jnp.cumsum(lengths)
    starts = ends - lengths
    inside = (positions[:, None] >= starts[None, :]) & (positions[:, None] < ends[None, :])
    return jnp.sum(jnp.where(inside, starts[None, :], 0), axis=1)


def rope_tables(places, head_size):
    half_size = head_size // 2
    frequency = ROPE_BASE ** (-2.0 * jnp.arange(half_size, dtype=F32) / head_size)
    angles = places.astype(F32)[:, None] * frequency[None, :]
    return (jnp.cos(angles), jnp.sin(angles))


def rotate(vector, cosine, sine_table, direction):
    half_size = vector.shape[-1] // 2
    front_half = vector[..., :half_size]
    back_half = vector[..., half_size:]
    cosine = cosine[:, None, :]
    sine_table = direction * sine_table[:, None, :]
    return jnp.concatenate(
        [
            front_half * cosine - back_half * sine_table,
            back_half * cosine + front_half * sine_table,
        ],
        axis=-1,
    )


def norm_back(grad_normed, normed, inverse, gain_row):
    scaled = grad_normed * gain_row
    return inverse * (scaled - normed * jnp.mean(scaled * normed, axis=-1, keepdims=True))


def dot(left, right):
    return jnp.dot(left, right, preferred_element_type=F32)


def dot_t(left, right):
    return lax.dot_general(left, right, (((1,), (1,)), ((), ())), preferred_element_type=F32)


def t_dot(left, right):
    return lax.dot_general(left, right, (((0,), (0,)), ((), ())), preferred_element_type=F32)


def column(vector, rows):
    return jnp.pad(vector, (0, rows - vector.shape[0]))[:, None]


def shards_apart(
    tokens,
    cotangent,
    lengths,
    attn_gain,
    q_weight,
    q_bias,
    k_weight,
    k_bias,
    v_weight,
    v_bias,
    o_weight,
    mlp_gain,
    gate_weight,
    up_weight,
    down_weight,
):
    seq, fsdp = lax.axis_size("seq"), lax.axis_size("fsdp")
    devices = seq * fsdp
    depth = seq // 2
    rows, model = tokens.shape
    total = rows * devices
    key_width = KV_HEADS * HEAD_DIM
    query_width = HEADS * HEAD_DIM
    model_rows = q_weight.shape[0]
    units = gate_weight.shape[1] // seq
    first_row = lax.axis_index(AXES) * rows
    positions = first_row + jnp.arange(rows, dtype=jnp.int32)
    begin = begin_of(positions, lengths)
    cosine, sine_table = rope_tables(positions - begin, HEAD_DIM)
    score_scale = HEAD_DIM ** (-0.5)

    small = jnp.concatenate(
        [column(v, model_rows) for v in (attn_gain, q_bias, k_bias, v_bias, mlp_gain)]
        + [jnp.zeros((model_rows, 123), BF16)],
        axis=1,
    )
    pack = jnp.concatenate([q_weight, k_weight, v_weight, o_weight, small], axis=1)
    wide = jnp.stack([gate_weight, up_weight]).reshape(2, model_rows, seq, units)
    wide = wide.transpose(0, 2, 1, 3)
    pack_all, cot_all, wide_all, down_all = call_start(
        depth, 0, pack, cotangent, wide, down_weight
    )
    pack_all = pack_all.reshape(model, pack.shape[1])
    qkv_width = query_width + 2 * key_width
    w_qkv = pack_all[:, :qkv_width]
    w_out = pack_all[:, qkv_width : qkv_width + query_width]
    smalls = pack_all[:, qkv_width + query_width :].astype(F32)
    gain_one, b_query = smalls[:, 0], smalls[:, 1]
    gain_two = smalls[:, 4]
    kv_share = k_bias.shape[0]
    b_key = smalls[:, 2].reshape(devices, model_rows)[:, :kv_share].reshape(key_width)
    b_value = smalls[:, 3].reshape(devices, model_rows)[:, :kv_share].reshape(key_width)
    cot_all = cot_all.reshape(seq * rows, model)
    w_gate = wide_all[0].reshape(model, units)
    w_up = wide_all[1].reshape(model, units)
    w_down = down_all.reshape(units, model)

    inputs = tokens.astype(F32)
    inv_one = lax.rsqrt(jnp.mean(inputs * inputs, axis=-1, keepdims=True) + EPSILON)
    normed_one = inputs * inv_one
    hidden_one = (normed_one * gain_one).astype(BF16)
    lin = dot(hidden_one, w_qkv) + jnp.concatenate([b_query, b_key, b_value])
    queries = rotate(
        lin[:, :query_width].reshape(rows, HEADS, HEAD_DIM), cosine, sine_table, 1.0
    ).astype(BF16)
    queries = queries.transpose(1, 0, 2).reshape(KV_HEADS, GROUP * rows, HEAD_DIM)
    keys = rotate(
        lin[:, query_width : query_width + key_width].reshape(rows, KV_HEADS, HEAD_DIM),
        cosine,
        sine_table,
        1.0,
    ).reshape(rows, key_width)
    kv = jnp.concatenate([keys, lin[:, query_width + key_width :]], axis=1).astype(BF16)
    (kv_all,) = call_gathers(depth, 1, [True], [kv])
    kv_all = kv_all.reshape(total, 2 * key_width)
    all_keys, all_values = kv_all[:, :key_width], kv_all[:, key_width:]

    span = min(512, total)
    low = begin[0] // span
    high = (first_row + rows - 1) // span + 1
    info = jnp.stack([first_row, low, high]).astype(jnp.int32)
    begin_column = begin[:, None]
    mixed, lse = call_forward(span, info, begin_column, queries, all_keys, all_values)
    mixed_low = (
        mixed.reshape(HEADS, rows, HEAD_DIM)
        .transpose(1, 0, 2)
        .reshape(rows, query_width)
        .astype(BF16)
    )
    middle = inputs + dot(mixed_low, w_out)
    inv_two = lax.rsqrt(jnp.mean(middle * middle, axis=-1, keepdims=True) + EPSILON)
    normed_two = middle * inv_two
    hidden_two = (normed_two * gain_two).astype(BF16)

    (hidden_all,) = call_gathers(depth, 2, [False], [hidden_two])
    hidden_all = hidden_all.reshape(seq * rows, model)
    gate = dot(hidden_all, w_gate)
    up = dot(hidden_all, w_up)
    sigma = jax.nn.sigmoid(gate)
    silu = gate * sigma
    activated = (silu * up).astype(BF16)
    d_act = dot_t(cot_all, w_down)
    d_gate = (d_act * up * sigma * (1.0 + gate * (1.0 - sigma))).astype(BF16)
    d_up = (d_act * silu).astype(BF16)
    d_hidden_part = dot_t(d_gate, w_gate) + dot_t(d_up, w_up)
    out_part = dot(activated, w_down)
    shape = (depth, 2, rows, model)
    d_hidden_two, branch = call_reduces(
        depth,
        3,
        [False, False],
        [d_hidden_part.astype(BF16).reshape(shape), out_part.astype(BF16).reshape(shape)],
    )
    layer_out = (middle + branch).astype(BF16)
    gate_part = t_dot(hidden_all, d_gate).astype(BF16)
    up_part = t_dot(hidden_all, d_up).astype(BF16)
    down_part = t_dot(activated, cot_all).astype(BF16)

    gain_two_grad = jnp.sum(d_hidden_two * normed_two, axis=0)
    d_middle = cotangent.astype(F32) + norm_back(d_hidden_two, normed_two, inv_two, gain_two)

    d_branch = d_middle.astype(BF16)
    d_mixed = dot_t(d_branch, w_out).astype(BF16)
    d_mixed = (
        d_mixed.reshape(rows, HEADS, HEAD_DIM)
        .transpose(1, 0, 2)
        .reshape(KV_HEADS, GROUP * rows, HEAD_DIM)
    )
    d_query, d_kv_part = call_backward(
        span, info, begin_column, queries, all_keys, all_values, mixed, lse, d_mixed
    )
    (d_kv,) = call_reduces(
        depth, 4, [True], [d_kv_part.reshape(depth, 2, 2, 2, rows, 2 * key_width)]
    )
    d_query = d_query.reshape(HEADS, rows, HEAD_DIM).transpose(1, 0, 2)
    d_q = rotate(d_query * score_scale, cosine, sine_table, -1.0).reshape(rows, query_width)
    d_k = rotate(
        d_kv[:, :key_width].reshape(rows, KV_HEADS, HEAD_DIM) * score_scale,
        cosine,
        sine_table,
        -1.0,
    ).reshape(rows, key_width)
    d_lin = jnp.concatenate([d_q, d_k, d_kv[:, key_width:]], axis=1).astype(BF16)
    bias_grad = jnp.sum(d_lin.astype(F32), axis=0)
    d_hidden_one = dot_t(d_lin, w_qkv)
    gain_one_grad = jnp.sum(d_hidden_one * normed_one, axis=0)
    input_grad = d_middle + norm_back(d_hidden_one, normed_one, inv_one, gain_one)

    def spread(vector):
        parts = vector.reshape(devices, -1)
        return jnp.pad(parts, ((0, 0), (0, model_rows - parts.shape[1]))).reshape(model, 1)

    small_part = jnp.concatenate(
        [
            spread(gain_one_grad),
            spread(bias_grad[:query_width]),
            spread(bias_grad[query_width : query_width + key_width]),
            spread(bias_grad[query_width + key_width :]),
            spread(gain_two_grad),
            jnp.zeros((model, 123), F32),
        ],
        axis=1,
    )
    pack_part = jnp.concatenate(
        [
            t_dot(hidden_one, d_lin).astype(BF16),
            t_dot(mixed_low, d_branch).astype(BF16),
            small_part.astype(BF16),
        ],
        axis=1,
    ).reshape(depth, 2, 2, 2, model_rows, pack.shape[1])
    wide_part = jnp.stack([gate_part, up_part]).reshape(2, seq, fsdp, model_rows, units)
    down_part = down_part.reshape(fsdp, units // fsdp, model)
    pack_grad, wide_grad, down_grad = call_end(depth, 5, pack_part, wide_part, down_part)
    wide_grad = wide_grad.transpose(1, 2, 0, 3).reshape(2, model_rows, seq * units).astype(F32)
    small_grad = pack_grad[:, qkv_width + query_width :]
    return (
        layer_out,
        input_grad,
        small_grad[:, 0],
        pack_grad[:, :query_width],
        small_grad[:, 1],
        pack_grad[:, query_width : query_width + key_width],
        small_grad[:kv_share, 2],
        pack_grad[:, query_width + key_width : qkv_width],
        small_grad[:kv_share, 3],
        pack_grad[:, qkv_width : qkv_width + query_width],
        small_grad[:, 4],
        wide_grad[0],
        wide_grad[1],
        down_grad,
    )


def shards_joined(
    tokens,
    cotangent,
    lengths,
    attn_gain,
    q_weight,
    q_bias,
    k_weight,
    k_bias,
    v_weight,
    v_bias,
    o_weight,
    mlp_gain,
    gate_weight,
    up_weight,
    down_weight,
):
    seq, fsdp = lax.axis_size("seq"), lax.axis_size("fsdp")
    devices = seq * fsdp
    depth = seq // 2
    rows, model = tokens.shape
    key_width = KV_HEADS * HEAD_DIM
    model_rows = q_weight.shape[0]
    kv_share = k_bias.shape[0]
    place, fifth = lax.axis_index("seq") // 2 * 2, lax.axis_index("fsdp")
    starts = ((place + jnp.arange(2, dtype=jnp.int32)) * fsdp + fifth) * rows
    positions = (starts[:, None] + jnp.arange(rows, dtype=jnp.int32)).reshape(2 * rows)
    begin = begin_of(positions, lengths)
    cosine, sine_table = rope_tables(positions - begin, HEAD_DIM)
    cosine = jnp.concatenate([cosine, cosine], axis=1).reshape(2, rows, HEAD_DIM)
    sine_table = jnp.concatenate([-sine_table, sine_table], axis=1).reshape(2, rows, HEAD_DIM)
    angles = jnp.stack([cosine, sine_table], axis=1)

    small = jnp.stack(
        [jnp.pad(v, (0, model_rows - v.shape[0])) for v in (attn_gain, q_bias, k_bias, v_bias, mlp_gain)],
        axis=1,
    )
    small = jnp.pad(small, ((0, 0), (0, 123)))
    few = down_weight.shape[0]
    filled = fsdp * (few + -few % 16)
    begin_column = begin.reshape(2, rows, 1)
    (
        pack_all,
        o_all,
        kv_all,
        cot_all,
        wide_all,
        down_all,
        hidden_all,
        queries,
        mixed,
        lse,
        middle,
        hidden_pair,
        mixed_low,
        vectors,
    ) = call_head(
        depth,
        6,
        (o_weight,),
        (
            q_weight,
            k_weight,
            v_weight,
            small,
            gate_weight,
            up_weight,
            down_weight,
            tokens,
            cotangent,
            angles,
            begin_column,
        ),
    )
    layer_out, d_middle, d_mixed, d_branch, gain_two_grad, down_part, wide_part = call_middle(
        depth,
        7,
        (
            hidden_all,
            cot_all,
            wide_all.reshape(2, seq, 2, 2, model_rows, filled),
            down_all.reshape(filled, model),
            o_all,
        ),
        (middle, cotangent, vectors),
    )
    input_grad, q_grad, kv_grad, small_grad, o_grad, down_grad, wide_grad = call_last(
        depth,
        8,
        (kv_all, pack_all, wide_part, down_part),
        (
            queries,
            mixed,
            lse,
            d_mixed,
            angles,
            begin_column,
            tokens,
            d_middle,
            vectors,
            gain_two_grad,
            hidden_pair,
            mixed_low,
            d_branch,
        ),
    )
    gate_grad, up_grad, down_grad, q_grad, k_grad, v_grad, small_grad, *plain = call_finish(
        few, wide_grad, down_grad, q_grad, kv_grad, small_grad, (layer_out, input_grad, o_grad)
    )
    layer_out, input_grad, o_grad = plain
    return (
        layer_out,
        input_grad,
        small_grad[0],
        q_grad,
        small_grad[1],
        k_grad,
        small_grad[2, :kv_share],
        v_grad,
        small_grad[3, :kv_share],
        o_grad,
        small_grad[4],
        gate_grad,
        up_grad,
        down_grad,
    )


def shards(*arguments):
    model_rows, rows = arguments[4].shape[0], arguments[0].shape[0]
    if model_rows % 16 == 0 and rows % 128 == 0 and lax.axis_size("seq") == 8:
        return shards_joined(*arguments)
    return shards_apart(*arguments)


def solution(mesh):
    matrix, vector = P(AXES, None), P(AXES)
    in_specs = (
        matrix,
        matrix,
        P(),
        vector,
        matrix,
        vector,
        matrix,
        vector,
        matrix,
        vector,
        matrix,
        vector,
        matrix,
        matrix,
        matrix,
    )
    out_specs = (
        matrix,
        matrix,
        vector,
        matrix,
        vector,
        matrix,
        vector,
        matrix,
        vector,
        matrix,
        vector,
        matrix,
        matrix,
        matrix,
    )
    return jax.shard_map(shards, mesh=mesh, in_specs=in_specs, out_specs=out_specs, check_vma=False)
```

```python
import functools

import jax
import jax.numpy as jnp
import numpy as np
from jax import lax
from jax.experimental import pallas as pl
from jax.experimental.pallas import tpu as pltpu
from jax.sharding import PartitionSpec as P

HEADS = 12
KV_HEADS = 2
HEAD_DIM = 128
GROUP = HEADS // KV_HEADS
EPSILON = 1e-06
ROPE_BASE = 10000.0
LOG2E = 1.4426950408889634
AXES = ("seq", "fsdp")
VMEM_LIMIT = 56 << 20
VMEM_JOINED = 60 << 20
F32 = jnp.float32
BF16 = jnp.bfloat16
DMA = pltpu.SemaphoreType.DMA


class Place:
    def __init__(self, depth):
        self.depth = depth
        self.s = lax.axis_index("seq")
        self.f = lax.axis_index("fsdp")
        self.z = lax.div(self.s, 2)
        self.x = lax.rem(self.s, 2)
        self.y = lax.div(self.f, 2)
        self.c = lax.rem(self.f, 2)
        self.up = self.z + 1 < depth
        self.down = self.z > 0

    def flip_x(self):
        return (self.s + 1 - 2 * self.x, self.f)

    def flip_y(self):
        return (self.s, self.f + 2 - 4 * self.y)

    def flip_c(self):
        return (self.s, self.f + 1 - 2 * self.c)

    def z_up(self):
        return (self.s + 2, self.f)

    def z_down(self):
        return (self.s - 2, self.f)

    def first(self):
        return (
            self.s + (1 - self.c) * (1 - 2 * self.x),
            self.f + self.c * (2 - 4 * self.y),
        )

    def second(self):
        return (
            self.s + self.c * (1 - 2 * self.x),
            self.f + (1 - self.c) * (2 - 4 * self.y),
        )

    def corner(self, i, j):
        over_x = i * (1 - self.c) + j * self.c
        over_y = j * (1 - self.c) + i * self.c
        return (self.x + over_x * (1 - 2 * self.x), self.y + over_y * (1 - 2 * self.y))

    def wave(self, k):
        if k == 0:
            return [(self.z, None)]
        return [(self.z - k, self.z - k >= 0), (self.z + k, self.z + k < self.depth)]


def guard(condition, body):
    if condition is None:
        body()
    else:
        pl.when(condition)(body)


def both(one, other):
    return one if other is None else jnp.logical_and(one, other)


def greet(place, others=()):
    barrier = pltpu.get_barrier_semaphore()
    partners = [place.flip_x(), place.flip_y(), place.flip_c(), *others]
    for partner in partners:
        pl.semaphore_signal(barrier, inc=1, device_id=partner, device_id_type=pl.DeviceIdType.MESH)

    def tell_up():
        pl.semaphore_signal(
            barrier, inc=1, device_id=place.z_up(), device_id_type=pl.DeviceIdType.MESH
        )

    def tell_down():
        pl.semaphore_signal(
            barrier, inc=1, device_id=place.z_down(), device_id_type=pl.DeviceIdType.MESH
        )

    pl.when(place.up)(tell_up)
    pl.when(place.down)(tell_down)
    pl.semaphore_wait(
        barrier, len(partners) + place.up.astype(jnp.int32) + place.down.astype(jnp.int32)
    )


def remote(src, dst, send_sem, recv_sem, device):
    return pltpu.make_async_remote_copy(
        src_ref=src,
        dst_ref=dst,
        send_sem=send_sem,
        recv_sem=recv_sem,
        device_id=device,
        device_id_type=pl.DeviceIdType.MESH,
    )


def add_into(target, term, rows):
    step = 16 if rows % 16 == 0 else rows

    def body(number, carry):
        at = pl.ds(pl.multiple_of(number * step, step), step)
        target[at, :] = (target[at, :].astype(F32) + term[at, :].astype(F32)).astype(BF16)
        return carry

    lax.fori_loop(0, rows // step, body, 0)


class Gather:
    def __init__(self, place, wide, own, out, sems, mixed=False):
        self.place, self.wide, self.own, self.out, self.sems = place, wide, own, out, sems
        self.mixed = mixed
        self.sent = []

    @staticmethod
    def semaphores(depth, wide, mixed=False):
        base = [DMA((1,)), DMA((2 * depth,)), DMA((depth,)), DMA((depth,)), DMA((depth,))]
        if mixed:
            base += [DMA((2 * depth,)), DMA((depth,))]
        if wide:
            base += [DMA((2 * depth,)), DMA((2 * depth,)), DMA((4 * depth,)), DMA((4 * depth,))]
        return base

    def at(self, zi, i, j):
        place = self.place
        if self.wide:
            x, y = place.corner(i, j)
            return self.out.at[zi, x, y, place.c]
        return self.out.at[zi, place.x + i * (1 - 2 * place.x)]

    def send(self, src, dst, send_sem, recv_sem, device, condition):
        copy = remote(src, dst, send_sem, recv_sem, device)
        guard(condition, copy.start)
        self.sent.append((copy, condition))

    def local(self):
        copy = pltpu.make_async_copy(
            self.own, self.at(self.place.z, 0, 0), self.sems[0].at[0]
        )
        return copy

    def along(self, k, zi, side, ok, column, z_send, z_recv, source=None):
        place, depth = self.place, self.place.depth
        block = self.at(zi, column, 0)
        source = block if source is None else source
        if k == 0 or side == 0:
            self.send(
                source, block, z_send.at[k], z_recv.at[zi], place.z_up(), both(place.up, ok)
            )
        if k == 0 or side == 1:
            self.send(
                source,
                block,
                z_send.at[depth + k],
                z_recv.at[zi],
                place.z_down(),
                both(place.down, ok),
            )

    def arrive(self, k):
        place = self.place
        z_send, z_recv, a_send, a_recv = self.sems[1:5]
        across = place.first() if self.wide else place.flip_x()
        for side, (zi, ok) in enumerate(place.wave(k)):
            block = self.at(zi, 0, 0)
            source = self.own if k == 0 else block
            if k > 0:
                landed = remote(block, block, z_send.at[0], z_recv.at[zi], place.z_up())
                guard(ok, landed.wait_recv)
            self.along(k, zi, side, ok, 0, z_send, z_recv, source)
            crossing = both(place.c == 0, ok) if self.mixed and k > 0 else ok
            self.send(source, block, a_send.at[zi], a_recv.at[zi], across, crossing)
            if self.wide:
                b_send, b_recv = self.sems[5:7]
                self.send(
                    source, block, b_send.at[2 * zi], b_recv.at[2 * zi], place.second(), ok
                )

    def across(self, k):
        place = self.place
        a_send, a_recv = self.sems[3:5]
        for side, (zi, ok) in enumerate(place.wave(k)):
            block = self.at(zi, 1, 0)
            crossing = both(place.c == 0, ok) if self.mixed and k > 0 else ok
            landed = remote(block, block, a_send.at[0], a_recv.at[zi], place.first())
            guard(crossing, landed.wait_recv)
            if self.mixed:
                z_send, z_recv = self.sems[5:7]
                carried = both(place.c == 1, ok)
                if k > 0:
                    landed = remote(block, block, z_send.at[0], z_recv.at[zi], place.z_up())
                    guard(carried, landed.wait_recv)
                self.along(k, zi, side, carried, 1, z_send, z_recv)
            if self.wide:
                b_send, b_recv = self.sems[5:7]
                self.send(
                    block, block, b_send.at[2 * zi + 1], b_recv.at[2 * zi + 1], place.second(), ok
                )

    def hand(self, k):
        place = self.place
        b_send, b_recv, c_send, c_recv = self.sems[5:9]
        for zi, ok in place.wave(k):
            for i in range(2):
                block = self.at(zi, i, 1)
                landed = remote(block, block, b_send.at[0], b_recv.at[2 * zi + i], place.second())
                guard(ok, landed.wait_recv)
            for x in range(2):
                for y in range(2):
                    block = self.out.at[zi, x, y, place.c]
                    slot = 4 * zi + 2 * x + y
                    self.send(
                        block, block, c_send.at[slot], c_recv.at[slot], place.flip_c(), ok
                    )

    def take(self, k):
        place = self.place
        c_send, c_recv = self.sems[7:9]
        for zi, ok in place.wave(k):
            for x in range(2):
                for y in range(2):
                    block = self.out.at[zi, x, y, 1 - place.c]
                    slot = 4 * zi + 2 * x + y
                    landed = remote(block, block, c_send.at[0], c_recv.at[slot], place.flip_c())
                    guard(ok, landed.wait_recv)

    def settle(self):
        for copy, condition in self.sent:
            guard(condition, copy.wait_send)


def drive_gathers(place, gathers):
    depth = place.depth
    locals_ = [gather.local() for gather in gathers]
    for copy in locals_:
        copy.start()
    for step in range(depth + 3):
        for gather in gathers:
            if step < depth:
                gather.arrive(step)
        if step == 0:
            for copy in locals_:
                copy.wait()
        for gather in gathers:
            if 0 <= step - 1 < depth:
                gather.across(step - 1)
        for gather in gathers:
            if gather.wide and 0 <= step - 2 < depth:
                gather.hand(step - 2)
        for gather in gathers:
            if gather.wide and 0 <= step - 3 < depth:
                gather.take(step - 3)
    for gather in gathers:
        gather.settle()


def gather_shape(depth, wide, own):
    lead = (depth, 2, 2, 2) if wide else (depth, 2)
    return jax.ShapeDtypeStruct(lead + own.shape, own.dtype)


def call_gathers(depth, collective_id, wides, owns):
    def kernel(*refs):
        count = len(owns)
        place = Place(depth)
        greet(place)
        gathers, used = [], 2 * count
        for number, wide in enumerate(wides):
            need = len(Gather.semaphores(depth, wide))
            gathers.append(
                Gather(place, wide, refs[number], refs[count + number], refs[used : used + need])
            )
            used += need
        drive_gathers(place, gathers)

    scratch = []
    for wide in wides:
        scratch += Gather.semaphores(depth, wide)
    return pl.pallas_call(
        kernel,
        out_shape=[gather_shape(depth, wide, own) for wide, own in zip(wides, owns)],
        in_specs=[pl.BlockSpec(memory_space=pl.ANY)] * len(owns),
        out_specs=[pl.BlockSpec(memory_space=pl.ANY)] * len(owns),
        scratch_shapes=scratch,
        compiler_params=pltpu.CompilerParams(
            collective_id=collective_id, has_side_effects=True, vmem_limit_bytes=VMEM_LIMIT
        ),
    )(*owns)


def start_kernel(depth, *refs):
    (pack, cot, wide_in, down_in, pack_out, cot_out, wide_out, down_out), sems = refs[:8], refs[8:]
    place = Place(depth)
    count = 2 * depth
    partners = []
    for offset in range(1, count):
        partners.append((lax.rem(place.s + offset, count), place.f))
    greet(place, partners)
    first = len(Gather.semaphores(depth, True))
    second = first + len(Gather.semaphores(depth, False))
    gathers = [
        Gather(place, True, pack, pack_out, sems[:first]),
        Gather(place, False, cot, cot_out, sems[first:second]),
    ]
    local_sem, e_send, e_recv, y_send, y_recv, c_send, c_recv, d_sem, d_send, d_recv = sems[second:]
    sent = []

    def send(src, dst, send_sem, recv_sem, device):
        copy = remote(src, dst, send_sem, recv_sem, device)
        copy.start()
        sent.append(copy)

    locals_ = [gather.local() for gather in gathers]
    locals_.append(
        pltpu.make_async_copy(
            wide_in.at[:, place.s], wide_out.at[:, place.s, place.f], local_sem.at[0]
        )
    )
    locals_.append(pltpu.make_async_copy(down_in, down_out.at[place.f], d_sem.at[0]))
    for copy in locals_:
        copy.start()

    y_f = place.f + 2 - 4 * place.y
    c_f = place.f + 1 - 2 * place.c
    yc_f = y_f + 1 - 2 * place.c

    def exchange(offset):
        to = lax.rem(place.s + offset, count)
        send(
            wide_in.at[:, to],
            wide_out.at[:, place.s, place.f],
            e_send.at[offset],
            e_recv.at[offset],
            (to, place.f),
        )

    def onward(offset):
        origin = lax.rem(place.s + count - offset, count)
        block = wide_out.at[:, origin, place.f]
        if offset > 0:
            remote(block, block, e_send.at[0], e_recv.at[offset], place.flip_y()).wait_recv()
        send(block, block, y_send.at[offset], y_recv.at[offset], place.flip_y())
        send(block, block, c_send.at[2 * offset], c_recv.at[2 * offset], place.flip_c())

    def sideways(offset):
        origin = lax.rem(place.s + count - offset, count)
        block = wide_out.at[:, origin, y_f]
        remote(block, block, y_send.at[0], y_recv.at[offset], place.flip_y()).wait_recv()
        send(block, block, c_send.at[2 * offset + 1], c_recv.at[2 * offset + 1], place.flip_c())

    def last(offset):
        origin = lax.rem(place.s + count - offset, count)
        for slot, owner in ((2 * offset, c_f), (2 * offset + 1, yc_f)):
            block = wide_out.at[:, origin, owner]
            remote(block, block, c_send.at[0], c_recv.at[slot], place.flip_c()).wait_recv()

    for gather in gathers:
        gather.arrive(0)
    send(down_in, down_out.at[place.f], d_send.at[0], d_recv.at[0], place.flip_y())
    send(down_in, down_out.at[place.f], d_send.at[1], d_recv.at[1], place.flip_c())
    for offset in range(1, count):
        exchange(offset)
    for copy in locals_:
        copy.wait()
    onward(0)
    total = depth + 3
    for step in range(1, total):
        for gather in gathers:
            if step < depth:
                gather.arrive(step)
        for gather in gathers:
            if 0 <= step - 1 < depth:
                gather.across(step - 1)
        for gather in gathers:
            if gather.wide and 0 <= step - 2 < depth:
                gather.hand(step - 2)
        for gather in gathers:
            if gather.wide and 0 <= step - 3 < depth:
                gather.take(step - 3)
    block = down_out.at[y_f]
    remote(block, block, d_send.at[0], d_recv.at[0], place.flip_y()).wait_recv()
    send(block, block, d_send.at[2], d_recv.at[2], place.flip_c())
    for offset in range(1, count):
        onward(offset)
        sideways(offset - 1)
    sideways(count - 1)
    for offset in range(count):
        last(offset)
    for slot, owner in ((1, c_f), (2, yc_f)):
        block = down_out.at[owner]
        remote(block, block, d_send.at[0], d_recv.at[slot], place.flip_c()).wait_recv()
    for gather in gathers:
        gather.settle()
    for copy in sent:
        copy.wait_send()


def call_start(depth, collective_id, pack, cot, wide, down):
    count = 2 * depth
    _, _, rows, columns = wide.shape
    scratch = Gather.semaphores(depth, True) + Gather.semaphores(depth, False)
    scratch += [DMA((1,)), DMA((count,)), DMA((count,)), DMA((count,)), DMA((count,))]
    scratch += [DMA((2 * count,)), DMA((2 * count,)), DMA((1,)), DMA((3,)), DMA((3,))]
    return pl.pallas_call(
        functools.partial(start_kernel, depth),
        out_shape=[
            gather_shape(depth, True, pack),
            gather_shape(depth, False, cot),
            jax.ShapeDtypeStruct((2, count, 4, rows, columns), BF16),
            jax.ShapeDtypeStruct((4,) + down.shape, BF16),
        ],
        in_specs=[pl.BlockSpec(memory_space=pl.ANY)] * 4,
        out_specs=[pl.BlockSpec(memory_space=pl.ANY)] * 4,
        scratch_shapes=scratch,
        compiler_params=pltpu.CompilerParams(
            collective_id=collective_id, has_side_effects=True, vmem_limit_bytes=VMEM_LIMIT
        ),
    )(pack, cot, wide, down)


class Reduce:
    def __init__(self, place, wide, rows, own, out, buffers, sems, near=None, causal=False):
        self.place, self.wide, self.rows = place, wide, rows
        self.own, self.out, self.buffers, self.sems = own, out, buffers, sems
        self.near = near
        self.causal = causal
        self.sent = []

    def wave(self, k):
        waves = self.place.wave(k)
        return waves[:1] if self.causal else waves

    def near_block(self, zi):
        return self.own.at[zi, self.place.x] if self.near is None else self.near.at[zi]

    @staticmethod
    def scratch(depth, wide, block):
        buffers = [
            pltpu.VMEM((depth,) + block, BF16),
            pltpu.VMEM((depth + 1,) + block, BF16),
        ]
        sems = [DMA((depth,)), DMA((depth,)), DMA((2 * depth,)), DMA((2 * depth,))]
        if wide:
            buffers += [
                pltpu.VMEM((depth, 2, 2) + block, BF16),
                pltpu.VMEM((depth, 2) + block, BF16),
            ]
            sems += [DMA((4 * depth,)), DMA((4 * depth,)), DMA((2 * depth,)), DMA((2 * depth,))]
        return buffers, sems

    def send(self, src, dst, send_sem, recv_sem, device, condition):
        copy = remote(src, dst, send_sem, recv_sem, device)
        guard(condition, copy.start)
        self.sent.append((copy, condition))

    def cores(self, k):
        place = self.place
        c_send, c_recv = self.sems[4:6]
        got = self.buffers[2]
        for zi, ok in self.wave(k):
            for x in range(2):
                for y in range(2):
                    slot = 4 * zi + 2 * x + y
                    self.send(
                        self.own.at[zi, x, y, 1 - place.c],
                        got.at[zi, x, y],
                        c_send.at[slot],
                        c_recv.at[slot],
                        place.flip_c(),
                        ok,
                    )

    def over_second(self, k):
        place = self.place
        c_send, c_recv, b_send, b_recv = self.sems[4:8]
        got, next_ = self.buffers[2:4]
        for zi, ok in self.wave(k):

            def body(zi=zi):
                for j in (1, 0):
                    for i in (1, 0):
                        x, y = place.corner(i, j)
                        block = got.at[zi, x, y]
                        slot = 4 * zi + 2 * x + y
                        remote(
                            block, block, c_send.at[0], c_recv.at[slot], place.flip_c()
                        ).wait_recv()
                        add_into(block, self.own.at[zi, x, y, place.c], self.rows)
                        if j == 1:
                            remote(
                                block,
                                next_.at[zi, i],
                                b_send.at[2 * zi + i],
                                b_recv.at[2 * zi + i],
                                place.second(),
                            ).start()

            guard(ok, body)
            for i in (1, 0):
                x, y = place.corner(i, 1)
                copy = remote(
                    got.at[zi, x, y],
                    next_.at[zi, i],
                    b_send.at[2 * zi + i],
                    b_recv.at[2 * zi + i],
                    place.second(),
                )
                self.sent.append((copy, ok))

    def over_first(self, k):
        place = self.place
        a_send, a_recv = self.sems[0:2]
        got = self.buffers[0]
        for zi, ok in self.wave(k):
            if self.wide:
                b_send, b_recv = self.sems[6:8]
                before, held = self.buffers[2:4]

                def body(zi=zi):
                    for i in (1, 0):
                        block = held.at[zi, i]
                        x, y = place.corner(i, 0)
                        remote(
                            block, block, b_send.at[0], b_recv.at[2 * zi + i], place.second()
                        ).wait_recv()
                        add_into(block, before.at[zi, x, y], self.rows)
                        if i == 1:
                            remote(
                                block, got.at[zi], a_send.at[zi], a_recv.at[zi], place.first()
                            ).start()

                guard(ok, body)
                copy = remote(
                    held.at[zi, 1], got.at[zi], a_send.at[zi], a_recv.at[zi], place.first()
                )
                self.sent.append((copy, ok))
            else:
                self.send(
                    self.own.at[zi, 1 - place.x],
                    got.at[zi],
                    a_send.at[zi],
                    a_recv.at[zi],
                    place.flip_x(),
                    ok,
                )

    def cross_copy(self, zi):
        place = self.place
        return remote(
            self.own.at[zi, 1 - place.x],
            self.buffers[0].at[zi],
            self.sems[0].at[zi],
            self.sems[1].at[zi],
            place.flip_x(),
        )

    def cross(self, zi):
        self.cross_copy(zi).start()

    def crossed(self):
        for zi in range(self.place.depth):
            self.sent.append((self.cross_copy(zi), None))

    def along(self, k):
        place, depth = self.place, self.place.depth
        a_send, a_recv, z_send, z_recv = self.sems[0:4]
        held, line = self.buffers[0:2]
        for side, (zi, ok) in enumerate(self.wave(k)):
            block = held.at[zi]

            def body(zi=zi, side=side, block=block):
                remote(block, block, a_send.at[0], a_recv.at[zi], place.first()).wait_recv()
                if self.wide:
                    add_into(block, self.buffers[3].at[zi, 0], self.rows)
                else:
                    add_into(block, self.near_block(zi), self.rows)

                def more(direction):
                    slot = direction * depth + zi
                    term = line.at[depth if k == 0 and direction == 1 else zi]
                    remote(term, term, z_send.at[0], z_recv.at[slot], place.z_up()).wait_recv()
                    add_into(block, term, self.rows)

                def pass_on(direction, to):
                    slot = direction * depth + zi
                    there = line.at[depth if k == 1 and direction == 1 else zi]
                    remote(block, there, z_send.at[slot], z_recv.at[slot], to).start()

                if k == 0:
                    if not self.causal:
                        pl.when(place.down)(functools.partial(more, 0))
                    pl.when(place.up)(functools.partial(more, 1))
                elif side == 0:
                    pl.when(place.up)(functools.partial(more, 1))
                    pass_on(1, place.z_down())
                else:
                    pl.when(place.down)(functools.partial(more, 0))
                    pass_on(0, place.z_up())

            guard(ok, body)
            if k > 0:
                direction = 1 - side
                slot = direction * depth + zi
                to = place.z_up() if side == 1 else place.z_down()
                there = line.at[depth if k == 1 and direction == 1 else zi]
                copy = remote(block, there, z_send.at[slot], z_recv.at[slot], to)
                self.sent.append((copy, ok))

    def finish(self):
        self.out[...] = self.buffers[0][self.place.z].astype(self.out.dtype)

    def settle(self):
        for copy, condition in self.sent:
            guard(condition, copy.wait_send)


def drive_reduces(place, reduces):
    depth = place.depth
    order = list(range(depth - 1, -1, -1))
    for reduce in reduces:
        for k in order:
            reduce.cores(k) if reduce.wide else reduce.over_first(k)
    for step in range(depth + 2):
        for reduce in reduces:
            if not reduce.wide:
                if step < depth:
                    reduce.along(order[step])
                continue
            if step < depth:
                reduce.over_second(order[step])
            if 0 <= step - 1 < depth:
                reduce.over_first(order[step - 1])
            if 0 <= step - 2 < depth:
                reduce.along(order[step - 2])
    for reduce in reduces:
        reduce.finish()
    for reduce in reduces:
        reduce.settle()


def call_reduces(depth, collective_id, wides, owns):
    count = len(owns)
    blocks = [own.shape[-2:] for own in owns]
    parts = [Reduce.scratch(depth, wide, block) for wide, block in zip(wides, blocks)]
    scratch = []
    for buffers, sems in parts:
        scratch += buffers + sems

    def kernel(*refs):
        place = Place(depth)
        greet(place)
        reduces, used = [], 2 * count
        for number, (buffers, sems) in enumerate(parts):
            middle, end = used + len(buffers), used + len(buffers) + len(sems)
            reduces.append(
                Reduce(
                    place,
                    wides[number],
                    blocks[number][0],
                    refs[number],
                    refs[count + number],
                    refs[used:middle],
                    refs[middle:end],
                )
            )
            used = end
        drive_reduces(place, reduces)

    return pl.pallas_call(
        kernel,
        out_shape=[jax.ShapeDtypeStruct(block, F32) for block in blocks],
        in_specs=[pl.BlockSpec(memory_space=pltpu.VMEM)] * count,
        out_specs=[pl.BlockSpec(memory_space=pltpu.VMEM)] * count,
        scratch_shapes=scratch,
        compiler_params=pltpu.CompilerParams(
            collective_id=collective_id, has_side_effects=True, vmem_limit_bytes=VMEM_LIMIT
        ),
    )(*owns)


def end_kernel(depth, shapes, *refs):
    pack, wide, down, pack_out, wide_out, down_out = refs[:6]
    block, wide_block, down_block = shapes
    buffers, sems = Reduce.scratch(depth, True, block)
    used = 6 + len(buffers)
    place = Place(depth)
    count = 2 * depth
    partners = []
    for offset in range(1, count):
        partners.append((lax.rem(place.s + offset, count), place.f))
    greet(place, partners)
    reduce = Reduce(
        place, True, block[0], pack, pack_out, refs[6:used], refs[used : used + len(sems)]
    )
    used += len(sems)
    w_core, w_y, d_core, d_y = refs[used : used + 4]
    wc_send, wc_recv, wy_send, wy_recv, e_send, e_recv, e_sem = refs[used + 4 : used + 11]
    dc_send, dc_recv, dy_send, dy_recv = refs[used + 11 :]
    sent = []
    wide_rows, down_rows = wide_block[1], down_block[0]

    def send(src, dst, send_sem, recv_sem, device):
        copy = remote(src, dst, send_sem, recv_sem, device)
        copy.start()
        sent.append(copy)

    def landed(ref, recv_sem):
        remote(ref, ref, e_send.at[0], recv_sem, place.flip_c()).wait_recv()

    mine_y, other_y = place.y, 1 - place.y
    offsets = list(range(1, count)) + [0]
    for y in range(2):
        side = other_y if y == 0 else mine_y
        send(
            down.at[2 * side + 1 - place.c],
            d_core.at[side],
            dc_send.at[side],
            dc_recv.at[side],
            place.flip_c(),
        )
    for offset in offsets:
        to = lax.rem(place.s + offset, count)
        for y in range(2):
            send(
                wide.at[:, to, 2 * y + 1 - place.c],
                w_core.at[y, offset],
                wc_send.at[2 * offset + y],
                wc_recv.at[2 * offset + y],
                place.flip_c(),
            )
    order = list(range(depth - 1, -1, -1))
    for k in order:
        reduce.cores(k)

    def wide_add(target, term):
        for part in range(2):
            add_into(target.at[part], term.at[part], wide_rows)

    def wide_cores(offset):
        to = lax.rem(place.s + offset, count)
        for side in (other_y, mine_y):
            landed(w_core.at[side, offset], wc_recv.at[2 * offset + side])
            wide_add(w_core.at[side, offset], wide.at[:, to, 2 * side + place.c])
            if side is other_y:
                send(
                    w_core.at[side, offset],
                    w_y.at[offset],
                    wy_send.at[offset],
                    wy_recv.at[offset],
                    place.flip_y(),
                )

    def wide_across(offset):
        landed(w_y.at[offset], wy_recv.at[offset])
        wide_add(w_y.at[offset], w_core.at[mine_y, offset])
        to = lax.rem(place.s + offset, count)
        if offset > 0:
            send(
                w_y.at[offset],
                wide_out.at[place.s],
                e_send.at[offset],
                e_recv.at[offset],
                (to, place.f),
            )
        else:
            pltpu.make_async_copy(w_y.at[0], wide_out.at[place.s], e_sem.at[0]).start()

    for offset in offsets[: count // 2]:
        wide_cores(offset)
    for step in range(depth):
        reduce.over_second(order[step])
        if step >= 1:
            reduce.over_first(order[step - 1])
        if step == 0:
            for offset in offsets[count // 2 :]:
                wide_cores(offset)
            for side in (other_y, mine_y):
                landed(d_core.at[side], dc_recv.at[side])
                add_into(d_core.at[side], down.at[2 * side + place.c], down_rows)
                if side is other_y:
                    send(d_core.at[side], d_y.at[0], dy_send.at[0], dy_recv.at[0], place.flip_y())
        for offset in offsets[step * count // depth : (step + 1) * count // depth]:
            wide_across(offset)
        if step >= 2:
            reduce.along(order[step - 2])
    reduce.over_first(order[depth - 1])
    for step in range(max(depth - 2, 0), depth):
        reduce.along(order[step])
    reduce.finish()
    landed(d_y.at[0], dy_recv.at[0])
    down_out[...] = d_y[0].astype(F32) + d_core[mine_y].astype(F32)
    for offset in range(1, count):
        origin = lax.rem(place.s + count - offset, count)
        landed(wide_out.at[origin], e_recv.at[offset])
    pltpu.make_async_copy(w_y.at[0], wide_out.at[place.s], e_sem.at[0]).wait()
    reduce.settle()
    for copy in sent:
        copy.wait_send()


def call_end(depth, collective_id, pack, wide, down):
    count = 2 * depth
    block = pack.shape[-2:]
    wide_block = (2,) + wide.shape[-2:]
    down_block = down.shape[-2:]
    buffers, sems = Reduce.scratch(depth, True, block)
    scratch = buffers + sems
    scratch += [
        pltpu.VMEM((2, count) + wide_block, BF16),
        pltpu.VMEM((count,) + wide_block, BF16),
        pltpu.VMEM((2,) + down_block, BF16),
        pltpu.VMEM((1,) + down_block, BF16),
    ]
    scratch += [DMA((2 * count,)), DMA((2 * count,)), DMA((count,)), DMA((count,))]
    scratch += [DMA((count,)), DMA((count,)), DMA((1,))]
    scratch += [DMA((2,)), DMA((2,)), DMA((1,)), DMA((1,))]
    vmem = pl.BlockSpec(memory_space=pltpu.VMEM)
    return pl.pallas_call(
        functools.partial(end_kernel, depth, (block, wide_block, down_block)),
        out_shape=[
            jax.ShapeDtypeStruct(block, F32),
            jax.ShapeDtypeStruct((count,) + wide_block, BF16),
            jax.ShapeDtypeStruct(down_block, F32),
        ],
        in_specs=[vmem] * 3,
        out_specs=[vmem, vmem, vmem],
        scratch_shapes=scratch,
        compiler_params=pltpu.CompilerParams(
            collective_id=collective_id, has_side_effects=True, vmem_limit_bytes=VMEM_LIMIT
        ),
    )(pack, wide, down)


def forward_kernel(span, info, begin, query, key, value, mixed, lse, m_acc, l_acc, o_acc):
    rows = begin.shape[0]
    first_row, low, high = info[0], info[1], info[2]
    scale = HEAD_DIM ** (-0.5) * LOG2E
    m_acc[...] = jnp.full_like(m_acc, -1e30)
    l_acc[...] = jnp.zeros_like(l_acc)
    o_acc[...] = jnp.zeros_like(o_acc)
    places = first_row + lax.broadcasted_iota(jnp.int32, (rows, span), 0)
    offsets = lax.broadcasted_iota(jnp.int32, (rows, span), 1)

    def step(number, carry):
        base = pl.multiple_of(number * span, span)
        keys_at = base + offsets
        visible = jnp.logical_and(keys_at >= begin[...], keys_at <= places)
        for g in range(KV_HEADS):
            lanes = slice(g * HEAD_DIM, (g + 1) * HEAD_DIM)
            scores = lax.dot_general(
                query[g],
                key[pl.ds(base, span), lanes],
                (((1,), (1,)), ((), ())),
                preferred_element_type=F32,
            )
            scores = scores.reshape(GROUP, rows, span) * scale
            scores = jnp.where(visible[None], scores, -1e30).reshape(GROUP * rows, span)
            old = m_acc[g]
            new = jnp.maximum(old, jnp.max(scores, axis=-1, keepdims=True))
            weights = jnp.exp2(scores - new[:, :1])
            weights = jnp.where(
                visible[None], weights.reshape(GROUP, rows, span), 0.0
            ).reshape(GROUP * rows, span)
            fade = jnp.exp2(old - new)
            l_acc[g] = l_acc[g] * fade + jnp.sum(weights, axis=-1, keepdims=True)
            o_acc[g] = o_acc[g] * fade + jnp.dot(
                weights.astype(BF16),
                value[pl.ds(base, span), lanes],
                preferred_element_type=F32,
            )
            m_acc[g] = new
        return carry

    lax.fori_loop(low, high, step, 0)
    for g in range(KV_HEADS):
        mixed[g] = o_acc[g] / l_acc[g]
        lse[g] = m_acc[g] + jnp.log2(l_acc[g])


def call_forward(span, info, begin, query, key, value):
    stacked = query.shape[1]
    vmem = pl.BlockSpec(memory_space=pltpu.VMEM)
    return pl.pallas_call(
        functools.partial(forward_kernel, span),
        out_shape=[
            jax.ShapeDtypeStruct((KV_HEADS, stacked, HEAD_DIM), F32),
            jax.ShapeDtypeStruct((KV_HEADS, stacked, HEAD_DIM), F32),
        ],
        in_specs=[pl.BlockSpec(memory_space=pltpu.SMEM)] + [vmem] * 4,
        out_specs=[vmem, vmem],
        scratch_shapes=[pltpu.VMEM((KV_HEADS, stacked, HEAD_DIM), F32)] * 3,
        compiler_params=pltpu.CompilerParams(vmem_limit_bytes=VMEM_LIMIT),
    )(info, begin, query, key, value)


def backward_kernel(
    span, info, begin, query, key, value, mixed, lse, grad, dquery, dkeys, delta
):
    rows = begin.shape[0]
    first_row, low, high = info[0], info[1], info[2]
    scale = HEAD_DIM ** (-0.5) * LOG2E
    dquery[...] = jnp.zeros_like(dquery)
    width = KV_HEADS * HEAD_DIM
    for g in range(KV_HEADS):
        delta[g] = jnp.broadcast_to(
            jnp.sum(grad[g].astype(F32) * mixed[g], axis=-1, keepdims=True), delta.shape[1:]
        )
    places = first_row + lax.broadcasted_iota(jnp.int32, (rows, span), 0)
    offsets = lax.broadcasted_iota(jnp.int32, (rows, span), 1)

    def clear(number, carry):
        base = pl.multiple_of(number * span, span)
        dkeys[pl.ds(base, span), :] = jnp.zeros((span, dkeys.shape[1]), BF16)
        return carry

    lax.fori_loop(0, low, clear, 0)
    lax.fori_loop(high, dkeys.shape[0] // span, clear, 0)

    def step(number, carry):
        base = pl.multiple_of(number * span, span)
        keys_at = base + offsets
        visible = jnp.logical_and(keys_at >= begin[...], keys_at <= places)
        for g in range(KV_HEADS):
            lanes = slice(g * HEAD_DIM, (g + 1) * HEAD_DIM)
            key_rows = key[pl.ds(base, span), lanes]
            value_rows = value[pl.ds(base, span), lanes]
            scores = lax.dot_general(
                query[g], key_rows, (((1,), (1,)), ((), ())), preferred_element_type=F32
            )
            dprobs = lax.dot_general(
                grad[g], value_rows, (((1,), (1,)), ((), ())), preferred_element_type=F32
            )
            probs = jnp.exp2(scores * scale - lse[g][:, :1])
            probs = jnp.where(
                visible[None], probs.reshape(GROUP, rows, span), 0.0
            ).reshape(GROUP * rows, span)
            dscores = (probs * (dprobs - delta[g][:, :1])).astype(BF16)
            dquery[g] += jnp.dot(dscores, key_rows, preferred_element_type=F32)
            dkeys[pl.ds(base, span), lanes] = lax.dot_general(
                dscores, query[g], (((0,), (0,)), ((), ())), preferred_element_type=F32
            ).astype(BF16)
            dkeys[
                pl.ds(base, span), width + g * HEAD_DIM : width + (g + 1) * HEAD_DIM
            ] = lax.dot_general(
                probs.astype(BF16),
                grad[g],
                (((0,), (0,)), ((), ())),
                preferred_element_type=F32,
            ).astype(BF16)
        return carry

    lax.fori_loop(low, high, step, 0)


def call_backward(span, info, begin, query, key, value, mixed, lse, grad):
    stacked = query.shape[1]
    vmem = pl.BlockSpec(memory_space=pltpu.VMEM)
    return pl.pallas_call(
        functools.partial(backward_kernel, span),
        out_shape=[
            jax.ShapeDtypeStruct((KV_HEADS, stacked, HEAD_DIM), F32),
            jax.ShapeDtypeStruct((key.shape[0], 2 * key.shape[1]), BF16),
        ],
        in_specs=[pl.BlockSpec(memory_space=pltpu.SMEM)] + [vmem] * 7,
        out_specs=[vmem, vmem],
        scratch_shapes=[pltpu.VMEM((KV_HEADS, stacked, HEAD_DIM), F32)],
        compiler_params=pltpu.CompilerParams(vmem_limit_bytes=VMEM_LIMIT),
    )(info, begin, query, key, value, mixed, lse, grad)


class PairGather:
    def __init__(self, place, own, out, sems, crossing):
        self.place, self.own, self.out, self.sems = place, own, out, sems
        self.crossing = crossing
        self.sent = []

    @staticmethod
    def semaphores(depth):
        return [
            DMA((1,)),
            DMA((1,)),
            DMA((1,)),
            DMA((2 * depth,)),
            DMA((depth,)),
            DMA((depth,)),
            DMA((depth,)),
            DMA((2 * depth,)),
            DMA((2 * depth,)),
        ]

    def send(self, src, dst, send_sem, recv_sem, device, condition=None):
        copy = remote(src, dst, send_sem, recv_sem, device)
        guard(condition, copy.start)
        self.sent.append((copy, condition))

    def block(self, zi, y, c):
        return self.out.at[zi, :, y, c]

    def landed(self, ref, recv_sem, condition=None):
        guard(condition, remote(ref, ref, self.sems[3].at[0], recv_sem, self.place.flip_c()).wait_recv)

    def local(self):
        place = self.place
        if self.crossing:
            return pltpu.make_async_copy(
                self.own.at[place.x],
                self.out.at[place.z, place.x, place.y, place.c],
                self.sems[0].at[0],
            )
        return pltpu.make_async_copy(
            self.own, self.block(place.z, place.y, place.c), self.sems[0].at[0]
        )

    def begin(self):
        place = self.place
        if self.crossing:
            self.send(
                self.own.at[1 - place.x],
                self.out.at[place.z, place.x, place.y, place.c],
                self.sems[1].at[0],
                self.sems[2].at[0],
                place.flip_x(),
            )

    def arrive(self, k):
        place, depth = self.place, self.place.depth
        z_send, z_recv, y_send, y_recv, c_send, c_recv = self.sems[3:9]
        for side, (zi, ok) in enumerate(place.wave(k)):
            block = self.block(zi, place.y, place.c)
            source = self.own if k == 0 and not self.crossing else block
            if k > 0:
                self.landed(block, z_recv.at[zi], ok)
            elif self.crossing:
                self.landed(
                    self.out.at[place.z, 1 - place.x, place.y, place.c], self.sems[2].at[0]
                )
            if k == 0 or side == 0:
                self.send(
                    source, block, z_send.at[k], z_recv.at[zi], place.z_up(), both(place.up, ok)
                )
            if k == 0 or side == 1:
                self.send(
                    source,
                    block,
                    z_send.at[depth + k],
                    z_recv.at[zi],
                    place.z_down(),
                    both(place.down, ok),
                )
            self.send(source, block, y_send.at[zi], y_recv.at[zi], place.flip_y(), ok)
            self.send(
                source, block, c_send.at[2 * zi], c_recv.at[2 * zi], place.flip_c(), ok
            )

    def across(self, k):
        place = self.place
        y_recv, c_send, c_recv = self.sems[6:9]
        for zi, ok in place.wave(k):
            block = self.block(zi, 1 - place.y, place.c)
            self.landed(block, y_recv.at[zi], ok)
            slot = 2 * zi + 1
            self.send(block, block, c_send.at[slot], c_recv.at[slot], place.flip_c(), ok)

    def take(self, k):
        place = self.place
        c_recv = self.sems[8]
        for zi, ok in place.wave(k):
            self.landed(self.block(zi, place.y, 1 - place.c), c_recv.at[2 * zi], ok)
            self.landed(self.block(zi, 1 - place.y, 1 - place.c), c_recv.at[2 * zi + 1], ok)

    def settle(self):
        for copy, condition in self.sent:
            guard(condition, copy.wait_send)


class PairReduce:
    def __init__(self, place, own, out, buffers, sems, causal=False, crossing=False):
        self.place, self.own, self.out, self.sems = place, own, out, sems
        self.from_core, self.from_y, self.line, self.from_x = buffers
        self.causal, self.crossing = causal, crossing
        self.sent = []

    @staticmethod
    def scratch(depth, block):
        buffers = [
            pltpu.VMEM((depth, 2, 2) + block, BF16),
            pltpu.VMEM((depth, 2) + block, BF16),
            pltpu.VMEM((depth + 1, 2) + block, BF16),
            pltpu.VMEM((1,) + block, BF16),
        ]
        sems = [DMA((2 * depth,)), DMA((2 * depth,)), DMA((depth,)), DMA((depth,))]
        sems += [DMA((2 * depth,)), DMA((2 * depth,)), DMA((1,)), DMA((1,))]
        return buffers, sems

    def wave(self, k):
        waves = self.place.wave(k)
        return waves[:1] if self.causal else waves

    def send(self, src, dst, send_sem, recv_sem, device, condition=None):
        copy = remote(src, dst, send_sem, recv_sem, device)
        guard(condition, copy.start)
        self.sent.append((copy, condition))

    def landed(self, ref, recv_sem):
        remote(ref, ref, self.sems[0].at[0], recv_sem, self.place.flip_c()).wait_recv()

    def add(self, target, term):
        for x in range(2):
            add_into(target.at[x], term.at[x], target.shape[1])

    def cores(self, k):
        place = self.place
        for zi, ok in self.wave(k):
            for y in range(2):
                slot = 2 * zi + y
                self.send(
                    self.own.at[zi, :, y, 1 - place.c],
                    self.from_core.at[zi, y],
                    self.sems[0].at[slot],
                    self.sems[1].at[slot],
                    place.flip_c(),
                    ok,
                )

    def over(self, k):
        place = self.place
        for zi, ok in self.wave(k):

            def body(zi=zi):
                for y in (1 - place.y, place.y):
                    block = self.from_core.at[zi, y]
                    self.landed(block, self.sems[1].at[2 * zi + y])
                    self.add(block, self.own.at[zi, :, y, place.c])
                    if y is not place.y:
                        self.y_copy(zi).start()

            guard(ok, body)
            self.sent.append((self.y_copy(zi), ok))

    def y_copy(self, zi):
        place = self.place
        return remote(
            self.from_core.at[zi, 1 - place.y],
            self.from_y.at[zi],
            self.sems[2].at[zi],
            self.sems[3].at[zi],
            place.flip_y(),
        )

    def z_copy(self, k, side, zi):
        depth = self.place.depth
        direction = 1 - side
        slot = direction * depth + zi
        there = self.line.at[depth if k == 1 and direction == 1 else zi]
        to = self.place.z_up() if side == 1 else self.place.z_down()
        return remote(
            self.from_y.at[zi], there, self.sems[4].at[slot], self.sems[5].at[slot], to
        )

    def along(self, k):
        place, depth = self.place, self.place.depth
        for side, (zi, ok) in enumerate(self.wave(k)):
            block = self.from_y.at[zi]

            def body(zi=zi, side=side, block=block):
                self.landed(block, self.sems[3].at[zi])
                self.add(block, self.from_core.at[zi, place.y])

                def more(direction):
                    term = self.line.at[depth if k == 0 and direction == 1 else zi]
                    self.landed(term, self.sems[5].at[direction * depth + zi])
                    self.add(block, term)

                if k == 0:
                    if not self.causal:
                        pl.when(place.down)(functools.partial(more, 0))
                    pl.when(place.up)(functools.partial(more, 1))
                elif side == 0:
                    pl.when(place.up)(functools.partial(more, 1))
                else:
                    pl.when(place.down)(functools.partial(more, 0))
                if k > 0:
                    self.z_copy(k, side, zi).start()

            guard(ok, body)
            if k > 0:
                self.sent.append((self.z_copy(k, side, zi), ok))

    def swap(self):
        place = self.place
        self.send(
            self.from_y.at[place.z, 1 - place.x],
            self.from_x.at[0],
            self.sems[6].at[0],
            self.sems[7].at[0],
            place.flip_x(),
        )

    def finish(self):
        place = self.place
        if self.crossing:
            self.landed(self.from_x.at[0], self.sems[7].at[0])
            self.out[place.x] = self.from_y[place.z, place.x].astype(self.out.dtype)
            self.out[1 - place.x] = self.from_x[0].astype(self.out.dtype)
        else:
            self.out[...] = self.from_y[place.z].astype(self.out.dtype)

    def settle(self):
        for copy, condition in self.sent:
            guard(condition, copy.wait_send)


class Exchange:
    def __init__(self, place, own, out, sems):
        self.place, self.own, self.out, self.sems = place, own, out, sems
        self.count = 2 * place.depth
        self.sent = []
        self.y_f = place.f + 2 - 4 * place.y
        self.c_f = place.f + 1 - 2 * place.c
        self.yc_f = self.y_f + 1 - 2 * place.c

    @staticmethod
    def semaphores(depth):
        count = 2 * depth
        return [
            DMA((1,)),
            DMA((count,)),
            DMA((count,)),
            DMA((count,)),
            DMA((count,)),
            DMA((2 * count,)),
            DMA((2 * count,)),
        ]

    def send(self, block, send_sem, recv_sem, device, source=None):
        copy = remote(block if source is None else source, block, send_sem, recv_sem, device)
        copy.start()
        self.sent.append(copy)

    def block(self, offset, owner):
        origin = lax.rem(self.place.s + self.count - offset, self.count)
        return self.out.at[:, origin, owner]

    def landed(self, block, recv_sem):
        remote(block, block, self.sems[1].at[0], recv_sem, self.place.flip_c()).wait_recv()

    def local(self):
        return pltpu.make_async_copy(
            self.own.at[:, self.place.s], self.block(0, self.place.f), self.sems[0].at[0]
        )

    def depart(self, offset):
        place = self.place
        to = lax.rem(place.s + offset, self.count)
        self.send(
            self.block(0, place.f),
            self.sems[1].at[offset],
            self.sems[2].at[offset],
            (to, place.f),
            self.own.at[:, to],
        )

    def onward(self, offset):
        place = self.place
        block = self.block(offset, place.f)
        if offset > 0:
            self.landed(block, self.sems[2].at[offset])
        self.send(block, self.sems[3].at[offset], self.sems[4].at[offset], place.flip_y())
        slot = 2 * offset
        self.send(block, self.sems[5].at[slot], self.sems[6].at[slot], place.flip_c())

    def sideways(self, offset):
        block = self.block(offset, self.y_f)
        self.landed(block, self.sems[4].at[offset])
        slot = 2 * offset + 1
        self.send(block, self.sems[5].at[slot], self.sems[6].at[slot], self.place.flip_c())

    def last(self, offset):
        self.landed(self.block(offset, self.c_f), self.sems[6].at[2 * offset])
        self.landed(self.block(offset, self.yc_f), self.sems[6].at[2 * offset + 1])

    def settle(self):
        for copy in self.sent:
            copy.wait_send()


class Quarter:
    def __init__(self, place, own, out, sems):
        self.place, self.own, self.out, self.sems = place, own, out, sems
        self.sent = []

    @staticmethod
    def semaphores():
        return [DMA((1,)), DMA((3,)), DMA((3,))]

    def local(self):
        return pltpu.make_async_copy(self.own, self.out.at[self.place.f], self.sems[0].at[0])

    def send(self, source, block, slot, device):
        copy = remote(source, block, self.sems[1].at[slot], self.sems[2].at[slot], device)
        copy.start()
        self.sent.append(copy)

    def depart(self):
        place = self.place
        self.send(self.own, self.out.at[place.f], 0, place.flip_y())
        self.send(self.own, self.out.at[place.f], 1, place.flip_c())

    def landed(self, owner, slot):
        block = self.out.at[owner]
        remote(block, block, self.sems[1].at[0], self.sems[2].at[slot], self.place.flip_c()).wait_recv()

    def sideways(self):
        place = self.place
        y_f = place.f + 2 - 4 * place.y
        self.landed(y_f, 0)
        self.send(self.out.at[y_f], self.out.at[y_f], 2, place.flip_c())

    def last(self):
        place = self.place
        self.landed(place.f + 1 - 2 * place.c, 1)
        self.landed(place.f + 2 - 4 * place.y + 1 - 2 * place.c, 2)

    def settle(self):
        for copy in self.sent:
            copy.wait_send()


def stage(gather, step):
    depth = gather.place.depth
    if step < depth:
        gather.arrive(step)
    if 0 <= step - 1 < depth:
        gather.across(step - 1)
    if isinstance(gather, PairGather):
        if 0 <= step - 2 < depth:
            gather.take(step - 2)
        return
    if gather.wide and 0 <= step - 2 < depth:
        gather.hand(step - 2)
    if gather.wide and 0 <= step - 3 < depth:
        gather.take(step - 3)


def turned(vector, cosine, sine):
    return vector * cosine + pltpu.roll(vector, HEAD_DIM // 2, 1) * sine


HEAD_PLAN = (
    ("tables", "wide", "P1", "P2", "d1", "d5", "P3", "o0", "d7", "P4", "P5", "project", "K0", "o1", "c0", "n7"),
    ("K1", "K2", "d2", "K3", "K4", "o2", "d6", "c1", "K5", "n0", "A0", "d4", "A1", "o3", "A2"),
    ("o4", "s0", "n6", "A3", "s7", "o5", "mix", "n1", "n5", "d3", "o6", "D", "after", "h0", "h1"),
    ("c2", "s1", "n4", "n3", "s6", "s5", "h2", "n2", "c3", "S", "s3", "s4", "s2", "h3", "h4", "c4"),
)
HEAD_INS = 12
HEAD_OUTS = 16


def head_kernel(depth, *refs):
    (o_own, q_own, k_own, v_own, small_own, gate_own, up_own, down_own) = refs[:8]
    (tokens, cot, frequency, lengths) = refs[8:HEAD_INS]
    (
        pack_out,
        o_out,
        kv_out,
        cot_out,
        wide_out,
        down_out,
        hidden_out,
        queries,
        mixed,
        lse,
        middle,
        hidden_pair,
        mixed_low,
        pair,
        angles,
        begin,
    ) = refs[HEAD_INS : HEAD_INS + HEAD_OUTS]
    vectors = refs[HEAD_INS + HEAD_OUTS]
    rest = refs[HEAD_INS + HEAD_OUTS + 1 :]
    pack_all, o_all, kv_all, kv_own, hidden_two, lin, m_acc, l_acc, o_acc = rest[:9]
    pack, wide, down, mixed_pair, mixed_far, spread = rest[9:15]
    sems = list(rest[15:])

    def take(count):
        taken = sems[:count]
        del sems[:count]
        return taken

    wide_need = len(Gather.semaphores(depth, True))
    line_need = len(Gather.semaphores(depth, False))
    count = 2 * depth
    devices = 4 * count
    rows, model = tokens.shape
    key_width = KV_HEADS * HEAD_DIM
    group_width = GROUP * HEAD_DIM
    qkv_width = group_width + 2 * HEAD_DIM

    place = Place(depth)
    for g in range(KV_HEADS):
        at = 0
        for source in (q_own, k_own, v_own):
            width = source.shape[1] // KV_HEADS
            pack[g, :, at : at + width] = source[:, g * width : (g + 1) * width]
            at += width
        pack[g, :, at:] = small_own[...]
    greet(place, [(lax.rem(place.s + offset, count), place.f) for offset in range(1, count)])
    pair_need = len(PairGather.semaphores(depth))
    g_pack = PairGather(place, pack, pack_all, take(pair_need), True)
    g_o = Gather(place, True, o_own, o_all, take(wide_need))
    g_kv = PairGather(place, kv_own, kv_all, take(pair_need), False)
    g_cot = Gather(place, False, cot, cot_out, take(line_need + 2), True)
    g_hidden = Gather(place, False, hidden_two, hidden_out, take(line_need))
    x_wide = Exchange(place, wide, wide_out, take(len(Exchange.semaphores(depth))))
    x_down = Quarter(place, down, down_out, take(len(Quarter.semaphores())))
    out_sem, x_send, x_recv = take(3)

    g_pack.begin()
    token_copy = remote(
        tokens, pair.at[place.x], x_send.at[0], x_recv.at[0], place.flip_x()
    )
    token_copy.start()
    pair[place.x] = tokens[...]
    pack_local = g_pack.local()
    pack_local.start()
    pack_local.wait()
    stage(g_pack, 0)
    few = down_own.shape[0]
    filled = down.shape[0]
    locals_ = [job.local() for job in (g_o, g_cot, x_wide, x_down)]
    for copy in locals_[:2]:
        copy.start()
    inputs = tokens[...].astype(F32)

    def pack_wide():
        for side, source in enumerate((gate_own, up_own)):
            for to in range(count):
                parts = []
                for owner in range(4):
                    low = (4 * to + owner) * few
                    parts.append(source[:, low : low + few])
                    parts.append(jnp.zeros((wide.shape[2], filled - few), BF16))
                wide[side, to] = jnp.concatenate(parts, axis=1)
        locals_[2].start()

    def tables():
        down[...] = jnp.concatenate(
            [down_own[...], jnp.zeros((filled - few, model), BF16)], axis=0
        )
        locals_[3].start()
        ahead = lax.broadcasted_iota(jnp.int32, (1, HEAD_DIM), 1) < HEAD_DIM // 2
        for x in range(2):
            first_row = ((2 * place.z + x) * 4 + place.f) * rows
            positions = first_row + lax.broadcasted_iota(jnp.int32, (rows, 1), 0)
            start, found = jnp.int32(0), jnp.zeros((rows, 1), jnp.int32)
            for number in range(lengths.shape[0]):
                found = jnp.where(positions >= start, start, found)
                start = start + lengths[number]
            begin[x] = found
            turns = (positions - found).astype(F32) * frequency[...]
            angles[x, 0] = jnp.cos(turns)
            sine = jnp.sin(turns)
            angles[x, 1] = jnp.where(ahead, -sine, sine)

    part = model // depth
    own_head = pl.ds(pl.multiple_of(place.x * HEAD_DIM, HEAD_DIM), HEAD_DIM)
    own_heads = pl.ds(pl.multiple_of(place.x * group_width, group_width), group_width)
    kv_local = g_kv.local()
    hidden_local = g_hidden.local()
    mixed_copy = remote(
        mixed_pair.at[1 - place.x], mixed_far, x_send.at[1], x_recv.at[1], place.flip_x()
    )

    def project():
        share = key_width // devices
        chosen = lax.broadcasted_iota(jnp.int32, (model, key_width), 1)
        chosen = lax.div(chosen, share) * (model // devices) + lax.rem(chosen, share)
        chosen = lax.broadcasted_iota(jnp.int32, (model, key_width), 0) == chosen
        small = pack_all[:, :, :, :, :, qkv_width:].reshape(model, 128).astype(F32).T
        vectors[...] = small[:8]
        spread[...] = jnp.dot(
            small[:8].astype(BF16), chosen.astype(BF16), preferred_element_type=F32
        )
        for copy in locals_:
            copy.wait()
        token_copy.wait_recv()
        pair_inputs = pair[...].reshape(2 * rows, model).astype(F32)
        inv_pair = lax.rsqrt(jnp.mean(pair_inputs * pair_inputs, axis=-1, keepdims=True) + EPSILON)
        hidden_pair[...] = (pair_inputs * inv_pair * small[0:1]).astype(BF16)
        for zi in range(depth):
            weights = pack_all[zi][:, :, :, :, :qkv_width].reshape(part, qkv_width)
            term = jnp.dot(
                hidden_pair[:, zi * part : (zi + 1) * part], weights, preferred_element_type=F32
            )
            if zi == 0:
                lin[...] = term
            else:
                lin[...] += term
        for x in range(2):
            at = slice(x * rows, (x + 1) * rows)
            head = lin[at, group_width : group_width + HEAD_DIM] + spread[2:3, own_head]
            kv_own[x, :, :HEAD_DIM] = turned(head, angles[x, 0], angles[x, 1]).astype(BF16)
            values = lin[at, group_width + HEAD_DIM :] + spread[3:4, own_head]
            kv_own[x, :, HEAD_DIM:] = values.astype(BF16)
        kv_local.start()

    def queries_of():
        query_bias = vectors[1:2, own_heads]
        for x in range(2):
            for j in range(GROUP):
                lanes = slice(j * HEAD_DIM, (j + 1) * HEAD_DIM)
                head = lin[x * rows : (x + 1) * rows, lanes] + query_bias[:, lanes]
                queries[x, j * rows : (j + 1) * rows, :] = turned(
                    head, angles[x, 0], angles[x, 1]
                ).astype(BF16)
        kv_local.wait()

    span = 4 * rows
    scale = HEAD_DIM ** (-0.5) * LOG2E
    m_acc[...] = jnp.full_like(m_acc, -1e30)
    l_acc[...] = jnp.zeros_like(l_acc)
    o_acc[...] = jnp.zeros_like(o_acc)
    local_rows = lax.broadcasted_iota(jnp.int32, (rows, span), 0)
    offsets = lax.broadcasted_iota(jnp.int32, (rows, span), 1)

    def attend(number, carry):
        keys_at = number * span + offsets
        block = kv_all.at[lax.div(number, 2), lax.rem(number, 2)]
        key = block[:, :, :, :HEAD_DIM].reshape(span, HEAD_DIM)
        value = block[:, :, :, HEAD_DIM:].reshape(span, HEAD_DIM)
        for x in range(2):
            places = ((2 * place.z + x) * 4 + place.f) * rows + local_rows
            visible = jnp.logical_and(keys_at >= begin[x], keys_at <= places)
            scores = mul_t(queries[x], key)
            scores = scores.reshape(GROUP, rows, span) * scale
            scores = jnp.where(visible[None], scores, -1e30).reshape(GROUP * rows, span)
            old = m_acc[x]
            new = jnp.maximum(old, jnp.max(scores, axis=-1, keepdims=True))
            weights = jnp.exp2(scores - new[:, :1])
            fade = jnp.exp2(old - new)
            l_acc[x] = l_acc[x] * fade + jnp.sum(weights, axis=-1, keepdims=True)
            o_acc[x] = o_acc[x] * fade + jnp.dot(
                weights.astype(BF16), value, preferred_element_type=F32
            )
            m_acc[x] = new
        return carry

    def attend_quarter(piece):
        low, high = piece * count // 4, (piece + 1) * count // 4
        reach = 2 * place.z + 2
        lax.fori_loop(jnp.minimum(low, reach), jnp.minimum(high, reach), attend, 0)

    def mix():
        for x in range(2):
            total = o_acc[x] / l_acc[x]
            mixed[x] = total
            lse[x] = m_acc[x] + jnp.log2(l_acc[x])
            mixed_pair[x] = total.astype(BF16)
        mixed_copy.start()

    def after_attention():
        mixed_copy.wait_recv()
        for j in range(GROUP):
            at = slice(j * rows, (j + 1) * rows)
            near = pl.multiple_of((place.x * GROUP + j) * HEAD_DIM, HEAD_DIM)
            far = pl.multiple_of(((1 - place.x) * GROUP + j) * HEAD_DIM, HEAD_DIM)
            mixed_low[:, pl.ds(near, HEAD_DIM)] = mixed_pair[place.x, at, :]
            mixed_low[:, pl.ds(far, HEAD_DIM)] = mixed_far[at, :]
        after = inputs
        for zi in range(depth):
            after = after + jnp.dot(
                mixed_low[:, zi * part : (zi + 1) * part],
                o_all[zi].reshape(part, model),
                preferred_element_type=F32,
            )
        middle[...] = after
        inv_two = lax.rsqrt(jnp.mean(after * after, axis=-1, keepdims=True) + EPSILON)
        hidden_two[...] = (after * inv_two * vectors[4:5]).astype(BF16)
        hidden_local.start()

    jobs = {"P": g_pack, "K": g_kv, "o": g_o, "c": g_cot, "h": g_hidden}
    moves = {"d": x_wide.depart, "n": x_wide.onward, "s": x_wide.sideways, "A": attend_quarter}
    works = {
        "wide": pack_wide,
        "tables": tables,
        "project": project,
        "mix": mix,
        "after": after_attention,
        "D": x_down.depart,
        "S": x_down.sideways,
    }
    for words in HEAD_PLAN:
        for word in words:
            if word in works:
                works[word]()
            elif word[0] in moves:
                moves[word[0]](int(word[1:]))
            else:
                stage(jobs[word[0]], int(word[1:]))
                if word == "K0":
                    queries_of()

    keeps = []
    for number, (source, target) in enumerate(
        ((pack_all, pack_out), (o_all, o_out), (kv_all, kv_out))
    ):
        copy = pltpu.make_async_copy(source, target, out_sem.at[number])
        copy.start()
        keeps.append(copy)
    hidden_local.wait()
    for offset in range(count):
        x_wide.last(offset)
    x_down.last()
    for copy in keeps:
        copy.wait()
    token_copy.wait_send()
    mixed_copy.wait_send()
    for job in (g_pack, g_o, g_kv, g_cot, g_hidden, x_wide, x_down):
        job.settle()


def call_head(depth, collective_id, hbm, vmems, lengths):
    (o_own,) = hbm
    q_own, k_own, v_own, small_own, gate_own, _, down_own, tokens, cot = vmems[:9]
    count = 2 * depth
    few = down_own.shape[0]
    filled = -(-few // 16) * 16
    qkv_width = (GROUP + 2) * HEAD_DIM
    width = qkv_width + small_own.shape[1]
    pack = jax.ShapeDtypeStruct((q_own.shape[0], width), BF16)
    wide = jax.ShapeDtypeStruct((2, count, gate_own.shape[0], 4 * filled), BF16)
    down = jax.ShapeDtypeStruct((filled, down_own.shape[1]), BF16)
    rows, model = tokens.shape
    key_width = KV_HEADS * HEAD_DIM
    stacked = GROUP * rows
    kv_own = jax.ShapeDtypeStruct((rows, 2 * HEAD_DIM), BF16)
    any_, vmem = pl.BlockSpec(memory_space=pl.ANY), pl.BlockSpec(memory_space=pltpu.VMEM)
    heads = (KV_HEADS, stacked, HEAD_DIM)
    outs = [
        gather_shape(depth, True, pack),
        gather_shape(depth, True, o_own),
        gather_shape(depth, True, kv_own),
        gather_shape(depth, False, cot),
        jax.ShapeDtypeStruct((2, count, 4) + wide.shape[2:], BF16),
        jax.ShapeDtypeStruct((4,) + down.shape, BF16),
        gather_shape(depth, False, tokens),
        jax.ShapeDtypeStruct(heads, BF16),
        jax.ShapeDtypeStruct(heads, F32),
        jax.ShapeDtypeStruct(heads, F32),
        jax.ShapeDtypeStruct((rows, model), F32),
        jax.ShapeDtypeStruct((2 * rows, model), BF16),
        jax.ShapeDtypeStruct((rows, model), BF16),
        jax.ShapeDtypeStruct((2, rows, model), BF16),
        jax.ShapeDtypeStruct((2, 2, rows, HEAD_DIM), F32),
        jax.ShapeDtypeStruct((2, rows, 1), jnp.int32),
        jax.ShapeDtypeStruct((8, model), F32),
    ]
    scratch = [pltpu.VMEM(out.shape, BF16) for out in outs[:3]]
    scratch += [
        pltpu.VMEM((2,) + kv_own.shape, BF16),
        pltpu.VMEM((rows, model), BF16),
        pltpu.VMEM((2 * rows, qkv_width), F32),
        pltpu.VMEM(heads, F32),
        pltpu.VMEM(heads, F32),
        pltpu.VMEM(heads, F32),
        pltpu.VMEM((KV_HEADS,) + pack.shape, BF16),
        pltpu.VMEM(wide.shape, BF16),
        pltpu.VMEM(down.shape, BF16),
        pltpu.VMEM(heads, BF16),
        pltpu.VMEM(heads[1:], BF16),
        pltpu.VMEM((8, key_width), F32),
    ]
    scratch += PairGather.semaphores(depth) + Gather.semaphores(depth, True)
    scratch += PairGather.semaphores(depth)
    scratch += Gather.semaphores(depth, False, True) + Gather.semaphores(depth, False)
    scratch += Exchange.semaphores(depth) + Quarter.semaphores()
    scratch += [DMA((3,)), DMA((2,)), DMA((2,))]
    return pl.pallas_call(
        functools.partial(head_kernel, depth),
        out_shape=outs,
        in_specs=[any_] + [vmem] * len(vmems) + [pl.BlockSpec(memory_space=pltpu.SMEM)],
        out_specs=[any_] * 7 + [vmem] * 10,
        scratch_shapes=scratch,
        compiler_params=pltpu.CompilerParams(
            collective_id=collective_id, has_side_effects=True, vmem_limit_bytes=VMEM_LIMIT
        ),
    )(*hbm, *vmems, lengths)


def t_mul(left, right):
    return lax.dot_general(left, right, (((0,), (0,)), ((), ())), preferred_element_type=F32)


def mul_t(left, right):
    return lax.dot_general(left, right, (((1,), (1,)), ((), ())), preferred_element_type=F32)


CUTS = ((0, 512), (512, 1024), (1024, 1152))


def middle_kernel(depth, *refs):
    (hidden_all, cot_all, wide_all, down_all, o_own) = refs[:5]
    (middle, cotangent, vectors) = refs[5:8]
    (layer_out, d_middle, d_mixed, d_branch, gain_two, down_out, wide_out) = refs[8:15]
    (tokens_v, grads_v, w_part, d_part, act, d_both, dh_part, out_part) = refs[15:23]
    (dh_sum, out_sum, w_core, w_y, d_core, o_all) = refs[23:29]
    rest = list(refs[29:])

    def take(count):
        taken = rest[:count]
        del rest[:count]
        return taken

    count = 2 * depth
    rows, model = middle.shape
    units = act.shape[2]
    part = model // depth
    buffers, sems = Reduce.scratch(depth, False, (rows, model))
    place = Place(depth)
    r_dh = Reduce(place, False, rows, dh_part, dh_sum, take(len(buffers)), take(len(sems)))
    r_out = Reduce(place, False, rows, out_part, out_sum, take(len(buffers)), take(len(sems)))
    load_sem, wc_send, wc_recv, wy_send, wy_recv, dc_send, dc_recv = take(7)
    sent = []

    def send(src, dst, send_sem, recv_sem, device):
        copy = remote(src, dst, send_sem, recv_sem, device)
        copy.start()
        sent.append(copy)

    def landed(ref, recv_sem):
        remote(ref, ref, wc_send.at[0], recv_sem, place.flip_c()).wait_recv()

    loads = [
        pltpu.make_async_copy(source, target, load_sem.at[number])
        for number, (source, target) in enumerate(
            (
                (hidden_all, tokens_v),
                (wide_all, w_part),
                (cot_all, grads_v),
                (down_all, d_part),
            )
        )
    ]
    for copy in loads:
        copy.start()
    greet(place)
    mine_y, other_y = place.y, 1 - place.y
    wide_rows = w_part.shape[-2]
    half = lax.div(place.z, 2)
    tiles = [3 - 3 * half, 2 - half, 1 + 4 * half - place.z, place.z]
    for copy in loads:
        copy.wait()

    def weights(side, low, high):
        return w_part[side, :, :, :, :, low:high].reshape(model, high - low)

    def forward(zi):
        tokens = tokens_v[zi].reshape(2 * rows, model)
        grads = grads_v[zi].reshape(2 * rows, model)
        out = None
        for low, high in CUTS:
            gate = jnp.dot(tokens, weights(0, low, high), preferred_element_type=F32)
            up = jnp.dot(tokens, weights(1, low, high), preferred_element_type=F32)
            d_act = mul_t(grads, d_part[low:high, :])
            sigma = jax.nn.sigmoid(gate)
            silu = gate * sigma
            act[zi, :, low:high] = (silu * up).astype(BF16)
            d_both[zi, :, low:high] = (
                d_act * up * sigma * (1.0 + gate * (1.0 - sigma))
            ).astype(BF16)
            d_both[zi, :, units + low : units + high] = (d_act * silu).astype(BF16)
        total = mul_t(d_both[zi, :, :units], weights(0, 0, units))
        total = total + mul_t(d_both[zi, :, units:], weights(1, 0, units))
        dh_part[zi] = total.astype(BF16).reshape(2, rows, model)
        out = jnp.dot(act[zi], d_part[...], preferred_element_type=F32)
        out_part[zi] = out.astype(BF16).reshape(2, rows, model)

    def tile(number, carry):
        zi = jnp.where(
            number == 0,
            tiles[0],
            jnp.where(number == 1, tiles[1], jnp.where(number == 2, tiles[2], tiles[3])),
        )
        forward(zi)
        r_dh.cross(zi)
        return carry

    lax.fori_loop(0, depth, tile, 0)
    for zi in tiles:
        r_out.cross(zi)
    r_dh.crossed()
    r_out.crossed()

    def wide_chunk(k, carry):
        lanes = pl.ds(pl.multiple_of(k * part, part), part)
        tokens = tokens_v[:, :, :, lanes].reshape(count * rows, part)
        term = t_mul(tokens, d_both[...].reshape(count * rows, 2 * units))
        for side in range(2):
            w_part[side, pl.ds(2 * k, 2)] = (
                term[:, side * units : (side + 1) * units]
                .astype(BF16)
                .reshape(2, 2, 2, wide_rows, units)
            )
        for step in range(2):
            to = 2 * k + step
            for y in range(2):
                remote(
                    w_part.at[:, to, y, 1 - place.c],
                    w_core.at[y, to],
                    wc_send.at[2 * to + y],
                    wc_recv.at[2 * to + y],
                    place.flip_c(),
                ).start()
        return carry

    def wide_cores(to):
        for y in (other_y, mine_y):
            landed(w_core.at[y, to], wc_recv.at[2 * to + y])
            for side in range(2):
                add_into(
                    w_core.at[y, to, side], w_part.at[side, to, y, place.c], wide_rows
                )
            if y is other_y:
                remote(
                    w_core.at[y, to], w_y.at[to], wy_send.at[to], wy_recv.at[to], place.flip_y()
                ).start()

    def wide_across(to, carry):
        landed(w_y.at[to], wy_recv.at[to])
        for side in range(2):
            add_into(w_y.at[to, side], w_core.at[mine_y, to, side], wide_rows)
        pltpu.make_async_copy(w_y.at[to], wide_out.at[to], load_sem.at[to]).start()
        return carry

    def wide_step(k, carry):
        wide_chunk(k, 0)
        pl.when(k > 0)(lambda: wide_cores(2 * k - 2))
        pl.when(k > 0)(lambda: wide_cores(2 * k - 1))
        return carry

    order = list(range(depth - 1, -1, -1))
    lax.fori_loop(0, depth - 2, wide_step, 0)
    r_dh.along(order[0])
    r_dh.along(order[1])
    lax.fori_loop(depth - 2, depth, wide_step, 0)
    wide_cores(count - 2)
    wide_cores(count - 1)
    r_dh.along(order[2])
    pieces = [
        pltpu.make_async_copy(o_own.at[zi], o_all.at[zi % 2], load_sem.at[zi])
        for zi in range(depth)
    ]
    for copy in pieces[:2]:
        copy.start()

    def down_chunk(k, carry):
        lanes = pl.ds(pl.multiple_of(k * 384, 384), 384)
        chunk = act[:, :, lanes].reshape(count * rows, 384)
        d_part[lanes, :] = t_mul(chunk, grads_v[...].reshape(count * rows, model)).astype(BF16)
        return carry

    lax.fori_loop(0, units // 384, down_chunk, 0)
    down_rows = units // 4

    def down_block(owner):
        return d_part.at[pl.ds(pl.multiple_of(owner * down_rows, down_rows), down_rows)]

    for y in (other_y, mine_y):
        send(
            down_block(2 * y + 1 - place.c),
            d_core.at[y],
            dc_send.at[y],
            dc_recv.at[y],
            place.flip_c(),
        )
    r_dh.along(order[3])
    r_dh.finish()

    after = middle[...]
    inv_two = lax.rsqrt(jnp.mean(after * after, axis=-1, keepdims=True) + EPSILON)
    normed = after * inv_two
    d_hidden = dh_sum[...]
    gain_two[...] = jnp.broadcast_to(
        jnp.sum(d_hidden * normed, axis=0, keepdims=True), gain_two.shape
    )
    scaled = d_hidden * vectors[4:5]
    total = cotangent[...].astype(F32) + inv_two * (
        scaled - normed * jnp.mean(scaled * normed, axis=-1, keepdims=True)
    )
    d_middle[...] = total
    d_branch[...] = total.astype(BF16)
    for zi in range(depth):
        pieces[zi].wait()
        term = mul_t(d_branch[...], o_all[zi % 2].reshape(part, model)).astype(BF16)
        for piece in range(part // HEAD_DIM):
            h = zi * (part // HEAD_DIM) + piece
            at = (h % GROUP) * rows
            d_mixed[h // GROUP, at : at + rows, :] = term[
                :, piece * HEAD_DIM : (piece + 1) * HEAD_DIM
            ]
        if zi + 2 < depth:
            pieces[zi + 2].start()
    for y in (other_y, mine_y):
        landed(d_core.at[y], dc_recv.at[y])
        add_into(d_core.at[y], down_block(2 * y + place.c), down_rows)
    keep = pltpu.make_async_copy(d_core, down_out, load_sem.at[count])
    keep.start()
    for step in range(depth):
        r_out.along(order[step])
        lax.fori_loop(2 * step, 2 * step + 2, wide_across, 0)
    r_out.finish()
    layer_out[...] = (middle[...] + out_sum[...]).astype(BF16)
    keep.wait()

    def end(to, carry):
        pltpu.make_async_copy(w_y.at[to], wide_out.at[to], load_sem.at[to]).wait()
        for y in range(2):
            slot = 2 * to + y
            remote(
                w_core.at[y, to], w_core.at[y, to], wc_send.at[slot], wc_recv.at[slot], place.flip_c()
            ).wait_send()
        remote(
            w_y.at[to], w_y.at[to], wy_send.at[to], wy_recv.at[to], place.flip_y()
        ).wait_send()
        return carry

    lax.fori_loop(0, count, end, 0)
    r_dh.settle()
    r_out.settle()
    for copy in sent:
        copy.wait_send()


def call_middle(depth, collective_id, hbm, vmems):
    hidden, cot, wide, down, o_all = hbm
    count = 2 * depth
    rows, model = vmems[0].shape
    units, wide_rows = wide.shape[-1], wide.shape[-2]
    any_, vmem = pl.BlockSpec(memory_space=pl.ANY), pl.BlockSpec(memory_space=pltpu.VMEM)
    buffers, sems = Reduce.scratch(depth, False, (rows, model))
    scratch = [pltpu.VMEM((depth, 2, rows, model), BF16)] * 2
    scratch += [pltpu.VMEM(wide.shape, BF16), pltpu.VMEM(down.shape, BF16)]
    scratch += [pltpu.VMEM((depth, 2 * rows, width), BF16) for width in (units, 2 * units)]
    scratch += [pltpu.VMEM((depth, 2, rows, model), BF16)] * 2
    scratch += [pltpu.VMEM((rows, model), F32)] * 2
    scratch += [
        pltpu.VMEM((2, count, 2, wide_rows, units), BF16),
        pltpu.VMEM((count, 2, wide_rows, units), BF16),
        pltpu.VMEM((2, units // 4, model), BF16),
        pltpu.VMEM((2,) + o_all.shape[1:], BF16),
    ]
    scratch += buffers + sems + buffers + sems
    scratch += [DMA((count + 1,)), DMA((2 * count,)), DMA((2 * count,))]
    scratch += [DMA((count,)), DMA((count,)), DMA((2,)), DMA((2,))]
    return pl.pallas_call(
        functools.partial(middle_kernel, depth),
        out_shape=[
            jax.ShapeDtypeStruct((rows, model), BF16),
            jax.ShapeDtypeStruct((rows, model), F32),
            jax.ShapeDtypeStruct((KV_HEADS, GROUP * rows, HEAD_DIM), BF16),
            jax.ShapeDtypeStruct((rows, model), BF16),
            jax.ShapeDtypeStruct((8, model), F32),
            jax.ShapeDtypeStruct((2, units // 4, model), BF16),
            jax.ShapeDtypeStruct((count, 2, wide_rows, units), BF16),
        ],
        in_specs=[any_] * 5 + [vmem] * 3,
        out_specs=[vmem] * 5 + [any_] * 2,
        scratch_shapes=scratch,
        compiler_params=pltpu.CompilerParams(
            collective_id=collective_id, has_side_effects=True, vmem_limit_bytes=VMEM_JOINED
        ),
    )(*hbm, *vmems)


LAST_PLAN = (
    ("d7", "d4", "d2", "d3", "down", "delta", "a0", "a1", "out"),
    ("Ck1", "Ck0", "Yk1", "d5", "Co0", "d1", "Co2", "Bo0", "a2"),
    ("Ck2", "Yk0", "a3", "Bo2", "Zk0", "Ck3", "turn", "Yk3", "Yk2"),
    ("Co1", "Zk1", "Co3", "hq", "Bo1", "query", "Zk2", "Bo3", "Cq0"),
    ("Cq2", "Ao0", "Cq1", "Zk3", "key", "Ao1", "Ao2", "d6", "hk"),
    ("kg", "small", "Cs0", "Yq0", "Cs2", "Cs1", "Zo0", "Yq1", "Ys0"),
    ("Cq3", "Ys2", "Yq2", "Zo1", "Cs3", "Zq0", "Ys1", "Ys3", "Zo2"),
    ("Yq3", "Ao3", "input", "Zs0", "Zq1", "Zs1", "Zq2", "Zs2", "Zq3"),
    ("Xq", "Zs3", "Xs", "Zo3"),
)


def follow_last(plan, works, depart, attend_wave, jobs):
    depth = 4
    steps = {"C": "cores", "B": "over_second", "A": "over_first", "Z": "along", "Y": "over"}
    for words in plan:
        for word in words:
            if word in works:
                works[word]()
            elif word[0] == "d":
                depart(int(word[1:]))
            elif word[0] == "a":
                attend_wave(int(word[1:]))
            else:
                getattr(jobs[word[1]], steps[word[0]])(depth - 1 - int(word[2:]))


def last_kernel(depth, *refs):
    (kv_own, pack_own, wide, down) = refs[:4]
    (queries, mixed, lse, d_mixed, angles, begin) = refs[4:10]
    (pair, d_middle, vectors, gain_two, hidden_pair, mixed_low, d_branch) = refs[10:17]
    (input_grad, q_out, kvs_out, o_out, down_out, wide_out) = refs[17:23]
    (kv_all, weights, d_query, delta, d_lin, d_keys, d_kv) = refs[23:30]
    (o_part, q_part, kvs_part) = refs[30:33]
    (d_near, d_far, d_hidden, kv_weights, d_pair, h_send, h_far, lines, pairs) = refs[33:42]
    rest = list(refs[42:])

    def take(number):
        taken = rest[:number]
        del rest[:number]
        return taken

    count = 2 * depth
    devices = 4 * count
    _, rows, model = pair.shape
    part = model // depth
    key_width = KV_HEADS * HEAD_DIM
    group_width = GROUP * HEAD_DIM
    qkv_width = group_width + 2 * HEAD_DIM
    model_rows = model // devices
    share = key_width // devices
    span = 4 * rows
    score_scale = HEAD_DIM ** (-0.5)
    scale = score_scale * LOG2E

    place = Place(depth)
    buffers, sems = Reduce.scratch(depth, True, o_part.shape[-2:])
    r_o = Reduce(
        place, True, model_rows, o_part, o_out, take(len(buffers)), take(len(sems))
    )

    def reduce_of(own, out, causal=False, crossing=True):
        buffers, sems = PairReduce.scratch(depth, own.shape[-2:])
        return PairReduce(
            place, own, out, take(len(buffers)), take(len(sems)), causal, crossing
        )

    r_kv = reduce_of(d_keys, d_kv, True, False)
    r_q = reduce_of(q_part, q_out)
    r_s = reduce_of(kvs_part, kvs_out)
    load_sem, e_send, e_recv, y_send, y_recv, x_send, x_recv = take(7)
    order = list(range(depth - 1, -1, -1))
    sent = []

    def depart(offset):
        to = lax.rem(place.s + offset, count)
        copy = remote(
            wide.at[to], wide_out.at[place.s], e_send.at[offset], e_recv.at[offset], (to, place.f)
        )
        copy.start()
        sent.append(copy)

    kv_load = pltpu.make_async_copy(kv_own, kv_all, load_sem.at[0])
    kv_load.start()
    own_wide = pltpu.make_async_copy(wide.at[place.s], wide_out.at[place.s], load_sem.at[1])
    own_wide.start()
    down_load = pltpu.make_async_copy(down.at[place.y], d_near, load_sem.at[2 + depth])
    down_load.start()
    greet(place, [(lax.rem(place.s + offset, count), place.f) for offset in range(1, count)])
    mixed_copy = remote(
        d_mixed.at[1 - place.x],
        d_pair.at[place.x],
        x_send.at[0],
        x_recv.at[0],
        place.flip_x(),
    )
    mixed_copy.start()
    sent.append(mixed_copy)
    d_pair[place.x] = d_mixed[place.x]
    down_copy = remote(
        down.at[1 - place.y], d_far, y_send.at[0], y_recv.at[0], place.flip_y()
    )
    hidden_copy = remote(h_send, h_far, x_send.at[1], x_recv.at[1], place.flip_x())
    loads = [
        pltpu.make_async_copy(pack_own.at[zi], weights.at[zi % 2], load_sem.at[2 + zi])
        for zi in range(depth)
    ]

    local_rows = lax.broadcasted_iota(jnp.int32, (rows, span), 0)
    offsets = lax.broadcasted_iota(jnp.int32, (rows, span), 1)

    def attend(number, carry):
        keys_at = number * span + offsets
        z, x_at = lax.div(number, 2), lax.rem(number, 2)
        block = kv_all.at[z, x_at]
        key = block[:, :, :, :HEAD_DIM].reshape(span, HEAD_DIM)
        value = block[:, :, :, HEAD_DIM:].reshape(span, HEAD_DIM)
        d_key, d_value = None, None
        for x in range(2):
            places = ((2 * place.z + x) * 4 + place.f) * rows + local_rows
            visible = jnp.logical_and(keys_at >= begin[x], keys_at <= places)
            scores = mul_t(queries[x], key)
            d_probs = mul_t(d_pair[x], value)
            probs = jnp.exp2(scores * scale - lse[x][:, :1])
            probs = jnp.where(
                visible[None], probs.reshape(GROUP, rows, span), 0.0
            ).reshape(GROUP * rows, span)
            d_scores = (probs * (d_probs - delta[x][:, :1])).astype(BF16)
            d_query[x] += jnp.dot(d_scores, key, preferred_element_type=F32)
            key_term = t_mul(d_scores, queries[x])
            value_term = t_mul(probs.astype(BF16), d_pair[x])
            d_key = key_term if x == 0 else d_key + key_term
            d_value = value_term if x == 0 else d_value + value_term
        target = d_keys.at[z, x_at]
        target[:, :, :, :HEAD_DIM] = d_key.astype(BF16).reshape(2, 2, rows, HEAD_DIM)
        target[:, :, :, HEAD_DIM:] = d_value.astype(BF16).reshape(2, 2, rows, HEAD_DIM)
        return carry

    def normed_of(rows_of):
        inputs = rows_of.astype(F32)
        inverse = lax.rsqrt(jnp.mean(inputs * inputs, axis=-1, keepdims=True) + EPSILON)
        return inputs * inverse, inverse

    def out_gradient():
        for copy in loads[:2]:
            copy.start()
        for zi in range(depth):
            lanes = slice(zi * part, (zi + 1) * part)
            term = t_mul(mixed_low[:, lanes], d_branch[...]).astype(BF16)
            o_part[zi] = term.reshape(2, 2, 2, model_rows, model)

    def deltas():
        mixed_copy.wait_recv()
        for x in range(2):
            delta[x] = jnp.broadcast_to(
                jnp.sum(d_pair[x].astype(F32) * mixed[x], axis=-1, keepdims=True),
                delta.shape[1:],
            )
        d_query[...] = jnp.zeros_like(d_query)
        kv_load.wait()

    def attend_wave(step):
        zi = place.z - order[step]
        low = jnp.maximum(2 * zi, 0)
        high = jnp.maximum(2 * zi + 2, 0)
        lax.fori_loop(low, high, attend, 0)

    def query_turn():
        for x in range(2):
            for j in range(GROUP):
                lanes = slice(j * HEAD_DIM, (j + 1) * HEAD_DIM)
                head = d_query[x, j * rows : (j + 1) * rows, :] * score_scale
                d_lin[x * rows : (x + 1) * rows, lanes] = turned(
                    head, angles[x, 0], -angles[x, 1]
                ).astype(BF16)

    def query_gradient():
        for zi in range(depth):
            lanes = slice(zi * part, (zi + 1) * part)
            term = t_mul(hidden_pair[:, lanes], d_lin[:, :group_width]).astype(BF16)
            q_part[zi] = term.reshape(2, 2, 2, model_rows, group_width)

    def key_turn():
        r_kv.finish()
        for x in range(2):
            at = slice(x * rows, (x + 1) * rows)
            head = d_kv[x, :, :HEAD_DIM] * score_scale
            d_lin[at, group_width : group_width + HEAD_DIM] = turned(
                head, angles[x, 0], -angles[x, 1]
            ).astype(BF16)
            d_lin[at, group_width + HEAD_DIM :] = d_kv[x, :, HEAD_DIM:].astype(BF16)

    def hidden_query():
        for zi in range(depth):
            lanes = slice(zi * part, (zi + 1) * part)
            loads[zi].wait()
            block = weights[zi % 2][:, :, :, :, :group_width].reshape(part, group_width)
            term = mul_t(d_lin[:, :group_width], block)
            for x in range(2):
                d_hidden[x, :, lanes] = term[x * rows : (x + 1) * rows]
            block = weights[zi % 2][:, :, :, :, group_width:qkv_width]
            kv_weights[lanes, :] = block.reshape(part, 2 * HEAD_DIM)
            if zi + 2 < depth:
                loads[zi + 2].start()

    def hidden_key():
        for zi in range(depth):
            lanes = slice(zi * part, (zi + 1) * part)
            term = mul_t(d_lin[:, group_width:], kv_weights[lanes, :])
            for x in range(2):
                d_hidden[x, :, lanes] += term[x * rows : (x + 1) * rows]
        h_send[...] = d_hidden[1 - place.x].astype(BF16)
        hidden_copy.start()

    def key_gradient():
        for zi in range(depth):
            lanes = slice(zi * part, (zi + 1) * part)
            term = t_mul(hidden_pair[:, lanes], d_lin[:, group_width:]).astype(BF16)
            kvs_part[zi, :, :, :, :, : 2 * HEAD_DIM] = term.reshape(
                2, 2, 2, model_rows, 2 * HEAD_DIM
            )

    def small_gradients():
        lines[...] = jnp.zeros_like(lines)
        pairs[...] = jnp.zeros_like(pairs)
        bias = jnp.sum(d_lin[...].astype(F32), axis=0, keepdims=True)
        own_head = pl.ds(pl.multiple_of(place.x * HEAD_DIM, HEAD_DIM), HEAD_DIM)
        own_heads = pl.ds(pl.multiple_of(place.x * group_width, group_width), group_width)
        gain_one = jnp.zeros((1, model), F32)
        for x in range(2):
            normed, _ = normed_of(pair[x])
            gain_one = gain_one + jnp.sum(d_hidden[x] * normed, axis=0, keepdims=True)
        lines[0:1, :] = gain_one
        lines[1:2, own_heads] = bias[:, :group_width]
        lines[4:5, :] = gain_two[0:1]
        pairs[0:1, own_head] = bias[:, group_width : group_width + HEAD_DIM]
        pairs[1:2, own_head] = bias[:, group_width + HEAD_DIM :]
        chosen = lax.broadcasted_iota(jnp.int32, (key_width, model), 0)
        chosen = lax.div(chosen, share) * model_rows + lax.rem(chosen, share)
        chosen = (lax.broadcasted_iota(jnp.int32, (key_width, model), 1) == chosen).astype(BF16)
        spread = jnp.dot(pairs[...].astype(BF16), chosen, preferred_element_type=F32)
        lines[2:4, :] = spread[0:2]
        small = jnp.concatenate([lines[...], jnp.zeros((120, model), F32)], axis=0)
        small = small.T.astype(BF16)
        for zi in range(depth):
            kvs_part[zi, :, :, :, :, 2 * HEAD_DIM :] = small[
                zi * part : (zi + 1) * part
            ].reshape(2, 2, 2, model_rows, 128)

    def input_gradient():
        hidden_copy.wait_recv()
        normed, inv_one = normed_of(pair[place.x])
        scaled = (d_hidden[place.x] + h_far[...].astype(F32)) * vectors[0:1]
        input_grad[...] = d_middle[...] + inv_one * (
            scaled - normed * jnp.mean(scaled * normed, axis=-1, keepdims=True)
        )

    works = {
        "out": out_gradient,
        "delta": deltas,
        "turn": query_turn,
        "query": query_gradient,
        "key": key_turn,
        "hq": hidden_query,
        "hk": hidden_key,
        "kg": key_gradient,
        "Xq": r_q.swap,
        "Xs": r_s.swap,
        "small": small_gradients,
        "input": input_gradient,
        "down": down_copy.start,
    }
    jobs = {"o": r_o, "k": r_kv, "q": r_q, "s": r_s}
    follow_last(LAST_PLAN, works, depart, attend_wave, jobs)
    for job in (r_o, r_q, r_s):
        job.finish()
    for offset in range(1, count):
        origin = lax.rem(place.s + count - offset, count)
        block = wide_out.at[origin]
        remote(block, block, e_send.at[0], e_recv.at[offset], place.flip_c()).wait_recv()
    own_wide.wait()
    down_load.wait()
    down_copy.wait()
    down_out[...] = d_near[...].astype(F32) + d_far[...].astype(F32)
    hidden_copy.wait_send()
    for job in (r_kv, r_o, r_q, r_s):
        job.settle()
    for copy in sent:
        copy.wait_send()


def call_last(depth, collective_id, hbm, vmems):
    kv_all, pack_all, wide, down = hbm
    pair = vmems[6]
    count = 2 * depth
    _, rows, model = pair.shape
    model_rows = model // (4 * count)
    key_width, group_width = KV_HEADS * HEAD_DIM, GROUP * HEAD_DIM
    heads = (2, GROUP * rows, HEAD_DIM)
    lead = (depth, 2, 2, 2)
    kv_block, o_block = (rows, 2 * HEAD_DIM), (model_rows, model)
    blocks = [
        (model_rows, group_width),
        (model_rows, 2 * HEAD_DIM + 128),
    ]
    scratch = [
        pltpu.VMEM(kv_all.shape, BF16),
        pltpu.VMEM((2,) + pack_all.shape[1:], BF16),
        pltpu.VMEM(heads, F32),
        pltpu.VMEM(heads, F32),
        pltpu.VMEM((2 * rows, group_width + 2 * HEAD_DIM), BF16),
        pltpu.VMEM(lead + kv_block, BF16),
        pltpu.VMEM((2,) + kv_block, F32),
        pltpu.VMEM(lead + o_block, BF16),
    ]
    scratch += [pltpu.VMEM(lead + block, BF16) for block in blocks]
    scratch += [pltpu.VMEM(down.shape[1:], BF16)] * 2
    scratch += [
        pltpu.VMEM((2, rows, model), F32),
        pltpu.VMEM((model, 2 * HEAD_DIM), BF16),
        pltpu.VMEM(heads, BF16),
        pltpu.VMEM((rows, model), BF16),
        pltpu.VMEM((rows, model), BF16),
        pltpu.VMEM((8, model), F32),
        pltpu.VMEM((8, key_width), F32),
    ]
    buffers, sems = Reduce.scratch(depth, True, o_block)
    scratch += buffers + sems
    for block in [kv_block] + blocks:
        buffers, sems = PairReduce.scratch(depth, block)
        scratch += buffers + sems
    scratch += [DMA((3 + depth,)), DMA((count,)), DMA((count,)), DMA((1,)), DMA((1,))]
    scratch += [DMA((2,)), DMA((2,))]
    any_, vmem = pl.BlockSpec(memory_space=pl.ANY), pl.BlockSpec(memory_space=pltpu.VMEM)
    return pl.pallas_call(
        functools.partial(last_kernel, depth),
        out_shape=[
            jax.ShapeDtypeStruct((rows, model), F32),
            jax.ShapeDtypeStruct((2,) + blocks[0], F32),
            jax.ShapeDtypeStruct((2,) + blocks[1], F32),
            jax.ShapeDtypeStruct(o_block, F32),
            jax.ShapeDtypeStruct(down.shape[1:], F32),
            jax.ShapeDtypeStruct(wide.shape, BF16),
        ],
        in_specs=[any_] * 4 + [vmem] * len(vmems),
        out_specs=[vmem] * 6,
        scratch_shapes=scratch,
        compiler_params=pltpu.CompilerParams(
            collective_id=collective_id, has_side_effects=True, vmem_limit_bytes=VMEM_JOINED
        ),
    )(*hbm, *vmems)


def finish_kernel(few, plain, *refs):
    wide, down, q_in, kvs_in = refs[:4]
    sources = refs[4 : 4 + plain]
    gate_out, up_out, down_out, q_out, k_out, v_out = refs[4 + plain : 10 + plain]
    vectors = refs[10 + plain : 15 + plain]
    targets = refs[15 + plain : 15 + 2 * plain]
    for source, target in zip(sources, targets):
        target[...] = source[...]
    down_out[...] = down[:few, :]
    filled = wide.shape[3] // 4
    for side, out in enumerate((gate_out, up_out)):
        for place in range(wide.shape[0]):
            block = wide[place, side].astype(F32)
            for owner in range(4):
                low = (4 * place + owner) * few
                out[:, low : low + few] = block[:, owner * filled : owner * filled + few]
    for g in range(KV_HEADS):
        width = q_in.shape[2]
        q_out[:, g * width : (g + 1) * width] = q_in[g]
        lanes = slice(g * HEAD_DIM, (g + 1) * HEAD_DIM)
        k_out[:, lanes] = kvs_in[g, :, :HEAD_DIM]
        v_out[:, lanes] = kvs_in[g, :, HEAD_DIM : 2 * HEAD_DIM]
    rows_of = (kvs_in[0, :, 2 * HEAD_DIM :] + kvs_in[1, :, 2 * HEAD_DIM :]).T
    for number, out in enumerate(vectors):
        out[...] = rows_of[number : number + 1, : out.shape[1]]


def call_finish(few, sizes, wide, down, q_grad, kvs_grad, plain):
    seq, _, rows, _ = wide.shape
    key_width = KV_HEADS * HEAD_DIM
    units = seq * 4 * few
    vmem = pl.BlockSpec(memory_space=pltpu.VMEM)
    out_shape = [
        jax.ShapeDtypeStruct((rows, units), F32),
        jax.ShapeDtypeStruct((rows, units), F32),
        jax.ShapeDtypeStruct((few, down.shape[1]), F32),
        jax.ShapeDtypeStruct((rows, HEADS * HEAD_DIM), F32),
        jax.ShapeDtypeStruct((rows, key_width), F32),
        jax.ShapeDtypeStruct((rows, key_width), F32),
        *[jax.ShapeDtypeStruct((1, size), F32) for size in sizes],
    ] + [jax.ShapeDtypeStruct(array.shape, array.dtype) for array in plain]
    return pl.pallas_call(
        functools.partial(finish_kernel, few, len(plain)),
        out_shape=out_shape,
        in_specs=[vmem] * (4 + len(plain)),
        out_specs=[vmem] * len(out_shape),
        compiler_params=pltpu.CompilerParams(vmem_limit_bytes=VMEM_LIMIT),
    )(wide, down, q_grad, kvs_grad, *plain)


def begin_of(positions, lengths):
    ends = jnp.cumsum(lengths)
    starts = ends - lengths
    inside = (positions[:, None] >= starts[None, :]) & (positions[:, None] < ends[None, :])
    return jnp.sum(jnp.where(inside, starts[None, :], 0), axis=1)


def rope_tables(places, head_size):
    half_size = head_size // 2
    frequency = ROPE_BASE ** (-2.0 * jnp.arange(half_size, dtype=F32) / head_size)
    angles = places.astype(F32)[:, None] * frequency[None, :]
    return (jnp.cos(angles), jnp.sin(angles))


def rotate(vector, cosine, sine_table, direction):
    half_size = vector.shape[-1] // 2
    front_half = vector[..., :half_size]
    back_half = vector[..., half_size:]
    cosine = cosine[:, None, :]
    sine_table = direction * sine_table[:, None, :]
    return jnp.concatenate(
        [
            front_half * cosine - back_half * sine_table,
            back_half * cosine + front_half * sine_table,
        ],
        axis=-1,
    )


def norm_back(grad_normed, normed, inverse, gain_row):
    scaled = grad_normed * gain_row
    return inverse * (scaled - normed * jnp.mean(scaled * normed, axis=-1, keepdims=True))


def dot(left, right):
    return jnp.dot(left, right, preferred_element_type=F32)


def dot_t(left, right):
    return lax.dot_general(left, right, (((1,), (1,)), ((), ())), preferred_element_type=F32)


def t_dot(left, right):
    return lax.dot_general(left, right, (((0,), (0,)), ((), ())), preferred_element_type=F32)


def column(vector, rows):
    return jnp.pad(vector, (0, rows - vector.shape[0]))[:, None]


def shards_apart(
    tokens,
    cotangent,
    lengths,
    attn_gain,
    q_weight,
    q_bias,
    k_weight,
    k_bias,
    v_weight,
    v_bias,
    o_weight,
    mlp_gain,
    gate_weight,
    up_weight,
    down_weight,
):
    seq, fsdp = lax.axis_size("seq"), lax.axis_size("fsdp")
    devices = seq * fsdp
    depth = seq // 2
    rows, model = tokens.shape
    total = rows * devices
    key_width = KV_HEADS * HEAD_DIM
    query_width = HEADS * HEAD_DIM
    model_rows = q_weight.shape[0]
    units = gate_weight.shape[1] // seq
    first_row = lax.axis_index(AXES) * rows
    positions = first_row + jnp.arange(rows, dtype=jnp.int32)
    begin = begin_of(positions, lengths)
    cosine, sine_table = rope_tables(positions - begin, HEAD_DIM)
    score_scale = HEAD_DIM ** (-0.5)

    small = jnp.concatenate(
        [column(v, model_rows) for v in (attn_gain, q_bias, k_bias, v_bias, mlp_gain)]
        + [jnp.zeros((model_rows, 123), BF16)],
        axis=1,
    )
    pack = jnp.concatenate([q_weight, k_weight, v_weight, o_weight, small], axis=1)
    wide = jnp.stack([gate_weight, up_weight]).reshape(2, model_rows, seq, units)
    wide = wide.transpose(0, 2, 1, 3)
    pack_all, cot_all, wide_all, down_all = call_start(
        depth, 0, pack, cotangent, wide, down_weight
    )
    pack_all = pack_all.reshape(model, pack.shape[1])
    qkv_width = query_width + 2 * key_width
    w_qkv = pack_all[:, :qkv_width]
    w_out = pack_all[:, qkv_width : qkv_width + query_width]
    smalls = pack_all[:, qkv_width + query_width :].astype(F32)
    gain_one, b_query = smalls[:, 0], smalls[:, 1]
    gain_two = smalls[:, 4]
    kv_share = k_bias.shape[0]
    b_key = smalls[:, 2].reshape(devices, model_rows)[:, :kv_share].reshape(key_width)
    b_value = smalls[:, 3].reshape(devices, model_rows)[:, :kv_share].reshape(key_width)
    cot_all = cot_all.reshape(seq * rows, model)
    w_gate = wide_all[0].reshape(model, units)
    w_up = wide_all[1].reshape(model, units)
    w_down = down_all.reshape(units, model)

    inputs = tokens.astype(F32)
    inv_one = lax.rsqrt(jnp.mean(inputs * inputs, axis=-1, keepdims=True) + EPSILON)
    normed_one = inputs * inv_one
    hidden_one = (normed_one * gain_one).astype(BF16)
    lin = dot(hidden_one, w_qkv) + jnp.concatenate([b_query, b_key, b_value])
    queries = rotate(
        lin[:, :query_width].reshape(rows, HEADS, HEAD_DIM), cosine, sine_table, 1.0
    ).astype(BF16)
    queries = queries.transpose(1, 0, 2).reshape(KV_HEADS, GROUP * rows, HEAD_DIM)
    keys = rotate(
        lin[:, query_width : query_width + key_width].reshape(rows, KV_HEADS, HEAD_DIM),
        cosine,
        sine_table,
        1.0,
    ).reshape(rows, key_width)
    kv = jnp.concatenate([keys, lin[:, query_width + key_width :]], axis=1).astype(BF16)
    (kv_all,) = call_gathers(depth, 1, [True], [kv])
    kv_all = kv_all.reshape(total, 2 * key_width)
    all_keys, all_values = kv_all[:, :key_width], kv_all[:, key_width:]

    span = min(512, total)
    low = begin[0] // span
    high = (first_row + rows - 1) // span + 1
    info = jnp.stack([first_row, low, high]).astype(jnp.int32)
    begin_column = begin[:, None]
    mixed, lse = call_forward(span, info, begin_column, queries, all_keys, all_values)
    mixed_low = (
        mixed.reshape(HEADS, rows, HEAD_DIM)
        .transpose(1, 0, 2)
        .reshape(rows, query_width)
        .astype(BF16)
    )
    middle = inputs + dot(mixed_low, w_out)
    inv_two = lax.rsqrt(jnp.mean(middle * middle, axis=-1, keepdims=True) + EPSILON)
    normed_two = middle * inv_two
    hidden_two = (normed_two * gain_two).astype(BF16)

    (hidden_all,) = call_gathers(depth, 2, [False], [hidden_two])
    hidden_all = hidden_all.reshape(seq * rows, model)
    gate = dot(hidden_all, w_gate)
    up = dot(hidden_all, w_up)
    sigma = jax.nn.sigmoid(gate)
    silu = gate * sigma
    activated = (silu * up).astype(BF16)
    d_act = dot_t(cot_all, w_down)
    d_gate = (d_act * up * sigma * (1.0 + gate * (1.0 - sigma))).astype(BF16)
    d_up = (d_act * silu).astype(BF16)
    d_hidden_part = dot_t(d_gate, w_gate) + dot_t(d_up, w_up)
    out_part = dot(activated, w_down)
    shape = (depth, 2, rows, model)
    d_hidden_two, branch = call_reduces(
        depth,
        3,
        [False, False],
        [d_hidden_part.astype(BF16).reshape(shape), out_part.astype(BF16).reshape(shape)],
    )
    layer_out = (middle + branch).astype(BF16)
    gate_part = t_dot(hidden_all, d_gate).astype(BF16)
    up_part = t_dot(hidden_all, d_up).astype(BF16)
    down_part = t_dot(activated, cot_all).astype(BF16)

    gain_two_grad = jnp.sum(d_hidden_two * normed_two, axis=0)
    d_middle = cotangent.astype(F32) + norm_back(d_hidden_two, normed_two, inv_two, gain_two)

    d_branch = d_middle.astype(BF16)
    d_mixed = dot_t(d_branch, w_out).astype(BF16)
    d_mixed = (
        d_mixed.reshape(rows, HEADS, HEAD_DIM)
        .transpose(1, 0, 2)
        .reshape(KV_HEADS, GROUP * rows, HEAD_DIM)
    )
    d_query, d_kv_part = call_backward(
        span, info, begin_column, queries, all_keys, all_values, mixed, lse, d_mixed
    )
    (d_kv,) = call_reduces(
        depth, 4, [True], [d_kv_part.reshape(depth, 2, 2, 2, rows, 2 * key_width)]
    )
    d_query = d_query.reshape(HEADS, rows, HEAD_DIM).transpose(1, 0, 2)
    d_q = rotate(d_query * score_scale, cosine, sine_table, -1.0).reshape(rows, query_width)
    d_k = rotate(
        d_kv[:, :key_width].reshape(rows, KV_HEADS, HEAD_DIM) * score_scale,
        cosine,
        sine_table,
        -1.0,
    ).reshape(rows, key_width)
    d_lin = jnp.concatenate([d_q, d_k, d_kv[:, key_width:]], axis=1).astype(BF16)
    bias_grad = jnp.sum(d_lin.astype(F32), axis=0)
    d_hidden_one = dot_t(d_lin, w_qkv)
    gain_one_grad = jnp.sum(d_hidden_one * normed_one, axis=0)
    input_grad = d_middle + norm_back(d_hidden_one, normed_one, inv_one, gain_one)

    def spread(vector):
        parts = vector.reshape(devices, -1)
        return jnp.pad(parts, ((0, 0), (0, model_rows - parts.shape[1]))).reshape(model, 1)

    small_part = jnp.concatenate(
        [
            spread(gain_one_grad),
            spread(bias_grad[:query_width]),
            spread(bias_grad[query_width : query_width + key_width]),
            spread(bias_grad[query_width + key_width :]),
            spread(gain_two_grad),
            jnp.zeros((model, 123), F32),
        ],
        axis=1,
    )
    pack_part = jnp.concatenate(
        [
            t_dot(hidden_one, d_lin).astype(BF16),
            t_dot(mixed_low, d_branch).astype(BF16),
            small_part.astype(BF16),
        ],
        axis=1,
    ).reshape(depth, 2, 2, 2, model_rows, pack.shape[1])
    wide_part = jnp.stack([gate_part, up_part]).reshape(2, seq, fsdp, model_rows, units)
    down_part = down_part.reshape(fsdp, units // fsdp, model)
    pack_grad, wide_grad, down_grad = call_end(depth, 5, pack_part, wide_part, down_part)
    wide_grad = wide_grad.transpose(1, 2, 0, 3).reshape(2, model_rows, seq * units).astype(F32)
    small_grad = pack_grad[:, qkv_width + query_width :]
    return (
        layer_out,
        input_grad,
        small_grad[:, 0],
        pack_grad[:, :query_width],
        small_grad[:, 1],
        pack_grad[:, query_width : query_width + key_width],
        small_grad[:kv_share, 2],
        pack_grad[:, query_width + key_width : qkv_width],
        small_grad[:kv_share, 3],
        pack_grad[:, qkv_width : qkv_width + query_width],
        small_grad[:, 4],
        wide_grad[0],
        wide_grad[1],
        down_grad,
    )


def shards_joined(
    tokens,
    cotangent,
    lengths,
    attn_gain,
    q_weight,
    q_bias,
    k_weight,
    k_bias,
    v_weight,
    v_bias,
    o_weight,
    mlp_gain,
    gate_weight,
    up_weight,
    down_weight,
):
    seq, fsdp = lax.axis_size("seq"), lax.axis_size("fsdp")
    devices = seq * fsdp
    depth = seq // 2
    rows, model = tokens.shape
    key_width = KV_HEADS * HEAD_DIM
    model_rows = q_weight.shape[0]
    kv_share = k_bias.shape[0]
    small = jnp.stack(
        [jnp.pad(v, (0, model_rows - v.shape[0])) for v in (attn_gain, q_bias, k_bias, v_bias, mlp_gain)],
        axis=1,
    )
    small = jnp.pad(small, ((0, 0), (0, 123)))
    few = down_weight.shape[0]
    filled = fsdp * (few + -few % 16)
    steps = np.arange(HEAD_DIM) % (HEAD_DIM // 2)
    frequency = jnp.asarray((ROPE_BASE ** (-2.0 * steps / HEAD_DIM)).astype(np.float32)[None, :])
    (
        pack_all,
        o_all,
        kv_all,
        cot_all,
        wide_all,
        down_all,
        hidden_all,
        queries,
        mixed,
        lse,
        middle,
        hidden_pair,
        mixed_low,
        pair,
        angles,
        begin,
        vectors,
    ) = call_head(
        depth,
        6,
        (o_weight,),
        (
            q_weight,
            k_weight,
            v_weight,
            small,
            gate_weight,
            up_weight,
            down_weight,
            tokens,
            cotangent,
            frequency,
        ),
        lengths,
    )
    layer_out, d_middle, d_mixed, d_branch, gain_two_grad, down_part, wide_part = call_middle(
        depth,
        7,
        (
            hidden_all,
            cot_all,
            wide_all.reshape(2, seq, 2, 2, model_rows, filled),
            down_all.reshape(filled, model),
            o_all,
        ),
        (middle, cotangent, vectors),
    )
    input_grad, q_grad, kvs_grad, o_grad, down_grad, wide_grad = call_last(
        depth,
        8,
        (kv_all, pack_all, wide_part, down_part),
        (
            queries,
            mixed,
            lse,
            d_mixed,
            angles,
            begin,
            pair,
            d_middle,
            vectors,
            gain_two_grad,
            hidden_pair,
            mixed_low,
            d_branch,
        ),
    )
    sizes = (model_rows, model_rows, kv_share, kv_share, model_rows)
    gate_grad, up_grad, down_grad, q_grad, k_grad, v_grad, *rest = call_finish(
        few, sizes, wide_grad, down_grad, q_grad, kvs_grad, (layer_out, input_grad, o_grad)
    )
    small_grad = [vector.reshape(-1) for vector in rest[:5]]
    layer_out, input_grad, o_grad = rest[5:]
    return (
        layer_out,
        input_grad,
        small_grad[0],
        q_grad,
        small_grad[1],
        k_grad,
        small_grad[2],
        v_grad,
        small_grad[3],
        o_grad,
        small_grad[4],
        gate_grad,
        up_grad,
        down_grad,
    )


def shards(*arguments):
    model_rows, rows = arguments[4].shape[0], arguments[0].shape[0]
    if model_rows % 16 == 0 and rows % 128 == 0 and lax.axis_size("seq") == 8:
        return shards_joined(*arguments)
    return shards_apart(*arguments)


def solution(mesh):
    matrix, vector = P(AXES, None), P(AXES)
    in_specs = (
        matrix,
        matrix,
        P(),
        vector,
        matrix,
        vector,
        matrix,
        vector,
        matrix,
        vector,
        matrix,
        vector,
        matrix,
        matrix,
        matrix,
    )
    out_specs = (
        matrix,
        matrix,
        vector,
        matrix,
        vector,
        matrix,
        vector,
        matrix,
        vector,
        matrix,
        vector,
        matrix,
        matrix,
        matrix,
    )
    return jax.shard_map(shards, mesh=mesh, in_specs=in_specs, out_specs=out_specs, check_vma=False)
```

```python
import functools

import jax
import jax.numpy as jnp
import numpy as np
from jax import lax
from jax.experimental import pallas as pl
from jax.experimental.pallas import tpu as pltpu
from jax.sharding import PartitionSpec as P

HEADS = 12
KV_HEADS = 2
HEAD_DIM = 128
GROUP = HEADS // KV_HEADS
EPSILON = 1e-06
ROPE_BASE = 10000.0
LOG2E = 1.4426950408889634
AXES = ("seq", "fsdp")
VMEM_LIMIT = 56 << 20
VMEM_JOINED = 60 << 20
F32 = jnp.float32
BF16 = jnp.bfloat16
DMA = pltpu.SemaphoreType.DMA


class Place:
    def __init__(self, depth):
        self.depth = depth
        self.s = lax.axis_index("seq")
        self.f = lax.axis_index("fsdp")
        self.z = lax.div(self.s, 2)
        self.x = lax.rem(self.s, 2)
        self.y = lax.div(self.f, 2)
        self.c = lax.rem(self.f, 2)
        self.up = self.z + 1 < depth
        self.down = self.z > 0

    def flip_x(self):
        return (self.s + 1 - 2 * self.x, self.f)

    def flip_y(self):
        return (self.s, self.f + 2 - 4 * self.y)

    def flip_c(self):
        return (self.s, self.f + 1 - 2 * self.c)

    def z_up(self):
        return (self.s + 2, self.f)

    def z_down(self):
        return (self.s - 2, self.f)

    def first(self):
        return (
            self.s + (1 - self.c) * (1 - 2 * self.x),
            self.f + self.c * (2 - 4 * self.y),
        )

    def second(self):
        return (
            self.s + self.c * (1 - 2 * self.x),
            self.f + (1 - self.c) * (2 - 4 * self.y),
        )

    def corner(self, i, j):
        over_x = i * (1 - self.c) + j * self.c
        over_y = j * (1 - self.c) + i * self.c
        return (self.x + over_x * (1 - 2 * self.x), self.y + over_y * (1 - 2 * self.y))

    def wave(self, k):
        if k == 0:
            return [(self.z, None)]
        return [(self.z - k, self.z - k >= 0), (self.z + k, self.z + k < self.depth)]


def guard(condition, body):
    if condition is None:
        body()
    else:
        pl.when(condition)(body)


def both(one, other):
    return one if other is None else jnp.logical_and(one, other)


def greet(place, others=()):
    barrier = pltpu.get_barrier_semaphore()
    partners = [place.flip_x(), place.flip_y(), place.flip_c(), *others]
    for partner in partners:
        pl.semaphore_signal(barrier, inc=1, device_id=partner, device_id_type=pl.DeviceIdType.MESH)

    def tell_up():
        pl.semaphore_signal(
            barrier, inc=1, device_id=place.z_up(), device_id_type=pl.DeviceIdType.MESH
        )

    def tell_down():
        pl.semaphore_signal(
            barrier, inc=1, device_id=place.z_down(), device_id_type=pl.DeviceIdType.MESH
        )

    pl.when(place.up)(tell_up)
    pl.when(place.down)(tell_down)
    pl.semaphore_wait(
        barrier, len(partners) + place.up.astype(jnp.int32) + place.down.astype(jnp.int32)
    )


def remote(src, dst, send_sem, recv_sem, device):
    return pltpu.make_async_remote_copy(
        src_ref=src,
        dst_ref=dst,
        send_sem=send_sem,
        recv_sem=recv_sem,
        device_id=device,
        device_id_type=pl.DeviceIdType.MESH,
    )


def add_into(target, term, rows):
    step = 16 if rows % 16 == 0 else rows

    def body(number, carry):
        at = pl.ds(pl.multiple_of(number * step, step), step)
        target[at, :] = (target[at, :].astype(F32) + term[at, :].astype(F32)).astype(BF16)
        return carry

    lax.fori_loop(0, rows // step, body, 0)


class Gather:
    def __init__(self, place, wide, own, out, sems, mixed=False):
        self.place, self.wide, self.own, self.out, self.sems = place, wide, own, out, sems
        self.mixed = mixed
        self.sent = []

    @staticmethod
    def semaphores(depth, wide, mixed=False):
        base = [DMA((1,)), DMA((2 * depth,)), DMA((depth,)), DMA((depth,)), DMA((depth,))]
        if mixed:
            base += [DMA((2 * depth,)), DMA((depth,))]
        if wide:
            base += [DMA((2 * depth,)), DMA((2 * depth,)), DMA((4 * depth,)), DMA((4 * depth,))]
        return base

    def at(self, zi, i, j):
        place = self.place
        if self.wide:
            x, y = place.corner(i, j)
            return self.out.at[zi, x, y, place.c]
        return self.out.at[zi, place.x + i * (1 - 2 * place.x)]

    def send(self, src, dst, send_sem, recv_sem, device, condition):
        copy = remote(src, dst, send_sem, recv_sem, device)
        guard(condition, copy.start)
        self.sent.append((copy, condition))

    def local(self):
        copy = pltpu.make_async_copy(
            self.own, self.at(self.place.z, 0, 0), self.sems[0].at[0]
        )
        return copy

    def along(self, k, zi, side, ok, column, z_send, z_recv, source=None):
        place, depth = self.place, self.place.depth
        block = self.at(zi, column, 0)
        source = block if source is None else source
        if k == 0 or side == 0:
            self.send(
                source, block, z_send.at[k], z_recv.at[zi], place.z_up(), both(place.up, ok)
            )
        if k == 0 or side == 1:
            self.send(
                source,
                block,
                z_send.at[depth + k],
                z_recv.at[zi],
                place.z_down(),
                both(place.down, ok),
            )

    def arrive(self, k):
        place = self.place
        z_send, z_recv, a_send, a_recv = self.sems[1:5]
        across = place.first() if self.wide else place.flip_x()
        for side, (zi, ok) in enumerate(place.wave(k)):
            block = self.at(zi, 0, 0)
            source = self.own if k == 0 else block
            if k > 0:
                landed = remote(block, block, z_send.at[0], z_recv.at[zi], place.z_up())
                guard(ok, landed.wait_recv)
            self.along(k, zi, side, ok, 0, z_send, z_recv, source)
            crossing = both(place.c == 0, ok) if self.mixed and k > 0 else ok
            self.send(source, block, a_send.at[zi], a_recv.at[zi], across, crossing)
            if self.wide:
                b_send, b_recv = self.sems[5:7]
                self.send(
                    source, block, b_send.at[2 * zi], b_recv.at[2 * zi], place.second(), ok
                )

    def across(self, k):
        place = self.place
        a_send, a_recv = self.sems[3:5]
        for side, (zi, ok) in enumerate(place.wave(k)):
            block = self.at(zi, 1, 0)
            crossing = both(place.c == 0, ok) if self.mixed and k > 0 else ok
            landed = remote(block, block, a_send.at[0], a_recv.at[zi], place.first())
            guard(crossing, landed.wait_recv)
            if self.mixed:
                z_send, z_recv = self.sems[5:7]
                carried = both(place.c == 1, ok)
                if k > 0:
                    landed = remote(block, block, z_send.at[0], z_recv.at[zi], place.z_up())
                    guard(carried, landed.wait_recv)
                self.along(k, zi, side, carried, 1, z_send, z_recv)
            if self.wide:
                b_send, b_recv = self.sems[5:7]
                self.send(
                    block, block, b_send.at[2 * zi + 1], b_recv.at[2 * zi + 1], place.second(), ok
                )

    def hand(self, k):
        place = self.place
        b_send, b_recv, c_send, c_recv = self.sems[5:9]
        for zi, ok in place.wave(k):
            for i in range(2):
                block = self.at(zi, i, 1)
                landed = remote(block, block, b_send.at[0], b_recv.at[2 * zi + i], place.second())
                guard(ok, landed.wait_recv)
            for x in range(2):
                for y in range(2):
                    block = self.out.at[zi, x, y, place.c]
                    slot = 4 * zi + 2 * x + y
                    self.send(
                        block, block, c_send.at[slot], c_recv.at[slot], place.flip_c(), ok
                    )

    def take(self, k):
        place = self.place
        c_send, c_recv = self.sems[7:9]
        for zi, ok in place.wave(k):
            for x in range(2):
                for y in range(2):
                    block = self.out.at[zi, x, y, 1 - place.c]
                    slot = 4 * zi + 2 * x + y
                    landed = remote(block, block, c_send.at[0], c_recv.at[slot], place.flip_c())
                    guard(ok, landed.wait_recv)

    def settle(self):
        for copy, condition in self.sent:
            guard(condition, copy.wait_send)


def drive_gathers(place, gathers):
    depth = place.depth
    locals_ = [gather.local() for gather in gathers]
    for copy in locals_:
        copy.start()
    for step in range(depth + 3):
        for gather in gathers:
            if step < depth:
                gather.arrive(step)
        if step == 0:
            for copy in locals_:
                copy.wait()
        for gather in gathers:
            if 0 <= step - 1 < depth:
                gather.across(step - 1)
        for gather in gathers:
            if gather.wide and 0 <= step - 2 < depth:
                gather.hand(step - 2)
        for gather in gathers:
            if gather.wide and 0 <= step - 3 < depth:
                gather.take(step - 3)
    for gather in gathers:
        gather.settle()


def gather_shape(depth, wide, own):
    lead = (depth, 2, 2, 2) if wide else (depth, 2)
    return jax.ShapeDtypeStruct(lead + own.shape, own.dtype)


def call_gathers(depth, collective_id, wides, owns):
    def kernel(*refs):
        count = len(owns)
        place = Place(depth)
        greet(place)
        gathers, used = [], 2 * count
        for number, wide in enumerate(wides):
            need = len(Gather.semaphores(depth, wide))
            gathers.append(
                Gather(place, wide, refs[number], refs[count + number], refs[used : used + need])
            )
            used += need
        drive_gathers(place, gathers)

    scratch = []
    for wide in wides:
        scratch += Gather.semaphores(depth, wide)
    return pl.pallas_call(
        kernel,
        out_shape=[gather_shape(depth, wide, own) for wide, own in zip(wides, owns)],
        in_specs=[pl.BlockSpec(memory_space=pl.ANY)] * len(owns),
        out_specs=[pl.BlockSpec(memory_space=pl.ANY)] * len(owns),
        scratch_shapes=scratch,
        compiler_params=pltpu.CompilerParams(
            collective_id=collective_id, has_side_effects=True, vmem_limit_bytes=VMEM_LIMIT
        ),
    )(*owns)


def start_kernel(depth, *refs):
    (pack, cot, wide_in, down_in, pack_out, cot_out, wide_out, down_out), sems = refs[:8], refs[8:]
    place = Place(depth)
    count = 2 * depth
    partners = []
    for offset in range(1, count):
        partners.append((lax.rem(place.s + offset, count), place.f))
    greet(place, partners)
    first = len(Gather.semaphores(depth, True))
    second = first + len(Gather.semaphores(depth, False))
    gathers = [
        Gather(place, True, pack, pack_out, sems[:first]),
        Gather(place, False, cot, cot_out, sems[first:second]),
    ]
    local_sem, e_send, e_recv, y_send, y_recv, c_send, c_recv, d_sem, d_send, d_recv = sems[second:]
    sent = []

    def send(src, dst, send_sem, recv_sem, device):
        copy = remote(src, dst, send_sem, recv_sem, device)
        copy.start()
        sent.append(copy)

    locals_ = [gather.local() for gather in gathers]
    locals_.append(
        pltpu.make_async_copy(
            wide_in.at[:, place.s], wide_out.at[:, place.s, place.f], local_sem.at[0]
        )
    )
    locals_.append(pltpu.make_async_copy(down_in, down_out.at[place.f], d_sem.at[0]))
    for copy in locals_:
        copy.start()

    y_f = place.f + 2 - 4 * place.y
    c_f = place.f + 1 - 2 * place.c
    yc_f = y_f + 1 - 2 * place.c

    def exchange(offset):
        to = lax.rem(place.s + offset, count)
        send(
            wide_in.at[:, to],
            wide_out.at[:, place.s, place.f],
            e_send.at[offset],
            e_recv.at[offset],
            (to, place.f),
        )

    def onward(offset):
        origin = lax.rem(place.s + count - offset, count)
        block = wide_out.at[:, origin, place.f]
        if offset > 0:
            remote(block, block, e_send.at[0], e_recv.at[offset], place.flip_y()).wait_recv()
        send(block, block, y_send.at[offset], y_recv.at[offset], place.flip_y())
        send(block, block, c_send.at[2 * offset], c_recv.at[2 * offset], place.flip_c())

    def sideways(offset):
        origin = lax.rem(place.s + count - offset, count)
        block = wide_out.at[:, origin, y_f]
        remote(block, block, y_send.at[0], y_recv.at[offset], place.flip_y()).wait_recv()
        send(block, block, c_send.at[2 * offset + 1], c_recv.at[2 * offset + 1], place.flip_c())

    def last(offset):
        origin = lax.rem(place.s + count - offset, count)
        for slot, owner in ((2 * offset, c_f), (2 * offset + 1, yc_f)):
            block = wide_out.at[:, origin, owner]
            remote(block, block, c_send.at[0], c_recv.at[slot], place.flip_c()).wait_recv()

    for gather in gathers:
        gather.arrive(0)
    send(down_in, down_out.at[place.f], d_send.at[0], d_recv.at[0], place.flip_y())
    send(down_in, down_out.at[place.f], d_send.at[1], d_recv.at[1], place.flip_c())
    for offset in range(1, count):
        exchange(offset)
    for copy in locals_:
        copy.wait()
    onward(0)
    total = depth + 3
    for step in range(1, total):
        for gather in gathers:
            if step < depth:
                gather.arrive(step)
        for gather in gathers:
            if 0 <= step - 1 < depth:
                gather.across(step - 1)
        for gather in gathers:
            if gather.wide and 0 <= step - 2 < depth:
                gather.hand(step - 2)
        for gather in gathers:
            if gather.wide and 0 <= step - 3 < depth:
                gather.take(step - 3)
    block = down_out.at[y_f]
    remote(block, block, d_send.at[0], d_recv.at[0], place.flip_y()).wait_recv()
    send(block, block, d_send.at[2], d_recv.at[2], place.flip_c())
    for offset in range(1, count):
        onward(offset)
        sideways(offset - 1)
    sideways(count - 1)
    for offset in range(count):
        last(offset)
    for slot, owner in ((1, c_f), (2, yc_f)):
        block = down_out.at[owner]
        remote(block, block, d_send.at[0], d_recv.at[slot], place.flip_c()).wait_recv()
    for gather in gathers:
        gather.settle()
    for copy in sent:
        copy.wait_send()


def call_start(depth, collective_id, pack, cot, wide, down):
    count = 2 * depth
    _, _, rows, columns = wide.shape
    scratch = Gather.semaphores(depth, True) + Gather.semaphores(depth, False)
    scratch += [DMA((1,)), DMA((count,)), DMA((count,)), DMA((count,)), DMA((count,))]
    scratch += [DMA((2 * count,)), DMA((2 * count,)), DMA((1,)), DMA((3,)), DMA((3,))]
    return pl.pallas_call(
        functools.partial(start_kernel, depth),
        out_shape=[
            gather_shape(depth, True, pack),
            gather_shape(depth, False, cot),
            jax.ShapeDtypeStruct((2, count, 4, rows, columns), BF16),
            jax.ShapeDtypeStruct((4,) + down.shape, BF16),
        ],
        in_specs=[pl.BlockSpec(memory_space=pl.ANY)] * 4,
        out_specs=[pl.BlockSpec(memory_space=pl.ANY)] * 4,
        scratch_shapes=scratch,
        compiler_params=pltpu.CompilerParams(
            collective_id=collective_id, has_side_effects=True, vmem_limit_bytes=VMEM_LIMIT
        ),
    )(pack, cot, wide, down)


class Reduce:
    def __init__(self, place, wide, rows, own, out, buffers, sems, near=None, causal=False):
        self.place, self.wide, self.rows = place, wide, rows
        self.own, self.out, self.buffers, self.sems = own, out, buffers, sems
        self.near = near
        self.causal = causal
        self.sent = []

    def wave(self, k):
        waves = self.place.wave(k)
        return waves[:1] if self.causal else waves

    def near_block(self, zi):
        return self.own.at[zi, self.place.x] if self.near is None else self.near.at[zi]

    @staticmethod
    def scratch(depth, wide, block):
        buffers = [
            pltpu.VMEM((depth,) + block, BF16),
            pltpu.VMEM((depth + 1,) + block, BF16),
        ]
        sems = [DMA((depth,)), DMA((depth,)), DMA((2 * depth,)), DMA((2 * depth,))]
        if wide:
            buffers += [
                pltpu.VMEM((depth, 2, 2) + block, BF16),
                pltpu.VMEM((depth, 2) + block, BF16),
            ]
            sems += [DMA((4 * depth,)), DMA((4 * depth,)), DMA((2 * depth,)), DMA((2 * depth,))]
        return buffers, sems

    def send(self, src, dst, send_sem, recv_sem, device, condition):
        copy = remote(src, dst, send_sem, recv_sem, device)
        guard(condition, copy.start)
        self.sent.append((copy, condition))

    def cores(self, k):
        place = self.place
        c_send, c_recv = self.sems[4:6]
        got = self.buffers[2]
        for zi, ok in self.wave(k):
            for x in range(2):
                for y in range(2):
                    slot = 4 * zi + 2 * x + y
                    self.send(
                        self.own.at[zi, x, y, 1 - place.c],
                        got.at[zi, x, y],
                        c_send.at[slot],
                        c_recv.at[slot],
                        place.flip_c(),
                        ok,
                    )

    def over_second(self, k):
        place = self.place
        c_send, c_recv, b_send, b_recv = self.sems[4:8]
        got, next_ = self.buffers[2:4]
        for zi, ok in self.wave(k):

            def body(zi=zi):
                for j in (1, 0):
                    for i in (1, 0):
                        x, y = place.corner(i, j)
                        block = got.at[zi, x, y]
                        slot = 4 * zi + 2 * x + y
                        remote(
                            block, block, c_send.at[0], c_recv.at[slot], place.flip_c()
                        ).wait_recv()
                        add_into(block, self.own.at[zi, x, y, place.c], self.rows)
                        if j == 1:
                            remote(
                                block,
                                next_.at[zi, i],
                                b_send.at[2 * zi + i],
                                b_recv.at[2 * zi + i],
                                place.second(),
                            ).start()

            guard(ok, body)
            for i in (1, 0):
                x, y = place.corner(i, 1)
                copy = remote(
                    got.at[zi, x, y],
                    next_.at[zi, i],
                    b_send.at[2 * zi + i],
                    b_recv.at[2 * zi + i],
                    place.second(),
                )
                self.sent.append((copy, ok))

    def over_first(self, k):
        place = self.place
        a_send, a_recv = self.sems[0:2]
        got = self.buffers[0]
        for zi, ok in self.wave(k):
            if self.wide:
                b_send, b_recv = self.sems[6:8]
                before, held = self.buffers[2:4]

                def body(zi=zi):
                    for i in (1, 0):
                        block = held.at[zi, i]
                        x, y = place.corner(i, 0)
                        remote(
                            block, block, b_send.at[0], b_recv.at[2 * zi + i], place.second()
                        ).wait_recv()
                        add_into(block, before.at[zi, x, y], self.rows)
                        if i == 1:
                            remote(
                                block, got.at[zi], a_send.at[zi], a_recv.at[zi], place.first()
                            ).start()

                guard(ok, body)
                copy = remote(
                    held.at[zi, 1], got.at[zi], a_send.at[zi], a_recv.at[zi], place.first()
                )
                self.sent.append((copy, ok))
            else:
                self.send(
                    self.own.at[zi, 1 - place.x],
                    got.at[zi],
                    a_send.at[zi],
                    a_recv.at[zi],
                    place.flip_x(),
                    ok,
                )

    def cross_copy(self, zi):
        place = self.place
        return remote(
            self.own.at[zi, 1 - place.x],
            self.buffers[0].at[zi],
            self.sems[0].at[zi],
            self.sems[1].at[zi],
            place.flip_x(),
        )

    def cross(self, zi):
        self.cross_copy(zi).start()

    def crossed(self):
        for zi in range(self.place.depth):
            self.sent.append((self.cross_copy(zi), None))

    def along(self, k):
        place, depth = self.place, self.place.depth
        a_send, a_recv, z_send, z_recv = self.sems[0:4]
        held, line = self.buffers[0:2]
        for side, (zi, ok) in enumerate(self.wave(k)):
            block = held.at[zi]

            def body(zi=zi, side=side, block=block):
                remote(block, block, a_send.at[0], a_recv.at[zi], place.first()).wait_recv()
                if self.wide:
                    add_into(block, self.buffers[3].at[zi, 0], self.rows)
                else:
                    add_into(block, self.near_block(zi), self.rows)

                def more(direction):
                    slot = direction * depth + zi
                    term = line.at[depth if k == 0 and direction == 1 else zi]
                    remote(term, term, z_send.at[0], z_recv.at[slot], place.z_up()).wait_recv()
                    add_into(block, term, self.rows)

                def pass_on(direction, to):
                    slot = direction * depth + zi
                    there = line.at[depth if k == 1 and direction == 1 else zi]
                    remote(block, there, z_send.at[slot], z_recv.at[slot], to).start()

                if k == 0:
                    if not self.causal:
                        pl.when(place.down)(functools.partial(more, 0))
                    pl.when(place.up)(functools.partial(more, 1))
                elif side == 0:
                    pl.when(place.up)(functools.partial(more, 1))
                    pass_on(1, place.z_down())
                else:
                    pl.when(place.down)(functools.partial(more, 0))
                    pass_on(0, place.z_up())

            guard(ok, body)
            if k > 0:
                direction = 1 - side
                slot = direction * depth + zi
                to = place.z_up() if side == 1 else place.z_down()
                there = line.at[depth if k == 1 and direction == 1 else zi]
                copy = remote(block, there, z_send.at[slot], z_recv.at[slot], to)
                self.sent.append((copy, ok))

    def finish(self):
        self.out[...] = self.buffers[0][self.place.z].astype(self.out.dtype)

    def settle(self):
        for copy, condition in self.sent:
            guard(condition, copy.wait_send)


def drive_reduces(place, reduces):
    depth = place.depth
    order = list(range(depth - 1, -1, -1))
    for reduce in reduces:
        for k in order:
            reduce.cores(k) if reduce.wide else reduce.over_first(k)
    for step in range(depth + 2):
        for reduce in reduces:
            if not reduce.wide:
                if step < depth:
                    reduce.along(order[step])
                continue
            if step < depth:
                reduce.over_second(order[step])
            if 0 <= step - 1 < depth:
                reduce.over_first(order[step - 1])
            if 0 <= step - 2 < depth:
                reduce.along(order[step - 2])
    for reduce in reduces:
        reduce.finish()
    for reduce in reduces:
        reduce.settle()


def call_reduces(depth, collective_id, wides, owns):
    count = len(owns)
    blocks = [own.shape[-2:] for own in owns]
    parts = [Reduce.scratch(depth, wide, block) for wide, block in zip(wides, blocks)]
    scratch = []
    for buffers, sems in parts:
        scratch += buffers + sems

    def kernel(*refs):
        place = Place(depth)
        greet(place)
        reduces, used = [], 2 * count
        for number, (buffers, sems) in enumerate(parts):
            middle, end = used + len(buffers), used + len(buffers) + len(sems)
            reduces.append(
                Reduce(
                    place,
                    wides[number],
                    blocks[number][0],
                    refs[number],
                    refs[count + number],
                    refs[used:middle],
                    refs[middle:end],
                )
            )
            used = end
        drive_reduces(place, reduces)

    return pl.pallas_call(
        kernel,
        out_shape=[jax.ShapeDtypeStruct(block, F32) for block in blocks],
        in_specs=[pl.BlockSpec(memory_space=pltpu.VMEM)] * count,
        out_specs=[pl.BlockSpec(memory_space=pltpu.VMEM)] * count,
        scratch_shapes=scratch,
        compiler_params=pltpu.CompilerParams(
            collective_id=collective_id, has_side_effects=True, vmem_limit_bytes=VMEM_LIMIT
        ),
    )(*owns)


def end_kernel(depth, shapes, *refs):
    pack, wide, down, pack_out, wide_out, down_out = refs[:6]
    block, wide_block, down_block = shapes
    buffers, sems = Reduce.scratch(depth, True, block)
    used = 6 + len(buffers)
    place = Place(depth)
    count = 2 * depth
    partners = []
    for offset in range(1, count):
        partners.append((lax.rem(place.s + offset, count), place.f))
    greet(place, partners)
    reduce = Reduce(
        place, True, block[0], pack, pack_out, refs[6:used], refs[used : used + len(sems)]
    )
    used += len(sems)
    w_core, w_y, d_core, d_y = refs[used : used + 4]
    wc_send, wc_recv, wy_send, wy_recv, e_send, e_recv, e_sem = refs[used + 4 : used + 11]
    dc_send, dc_recv, dy_send, dy_recv = refs[used + 11 :]
    sent = []
    wide_rows, down_rows = wide_block[1], down_block[0]

    def send(src, dst, send_sem, recv_sem, device):
        copy = remote(src, dst, send_sem, recv_sem, device)
        copy.start()
        sent.append(copy)

    def landed(ref, recv_sem):
        remote(ref, ref, e_send.at[0], recv_sem, place.flip_c()).wait_recv()

    mine_y, other_y = place.y, 1 - place.y
    offsets = list(range(1, count)) + [0]
    for y in range(2):
        side = other_y if y == 0 else mine_y
        send(
            down.at[2 * side + 1 - place.c],
            d_core.at[side],
            dc_send.at[side],
            dc_recv.at[side],
            place.flip_c(),
        )
    for offset in offsets:
        to = lax.rem(place.s + offset, count)
        for y in range(2):
            send(
                wide.at[:, to, 2 * y + 1 - place.c],
                w_core.at[y, offset],
                wc_send.at[2 * offset + y],
                wc_recv.at[2 * offset + y],
                place.flip_c(),
            )
    order = list(range(depth - 1, -1, -1))
    for k in order:
        reduce.cores(k)

    def wide_add(target, term):
        for part in range(2):
            add_into(target.at[part], term.at[part], wide_rows)

    def wide_cores(offset):
        to = lax.rem(place.s + offset, count)
        for side in (other_y, mine_y):
            landed(w_core.at[side, offset], wc_recv.at[2 * offset + side])
            wide_add(w_core.at[side, offset], wide.at[:, to, 2 * side + place.c])
            if side is other_y:
                send(
                    w_core.at[side, offset],
                    w_y.at[offset],
                    wy_send.at[offset],
                    wy_recv.at[offset],
                    place.flip_y(),
                )

    def wide_across(offset):
        landed(w_y.at[offset], wy_recv.at[offset])
        wide_add(w_y.at[offset], w_core.at[mine_y, offset])
        to = lax.rem(place.s + offset, count)
        if offset > 0:
            send(
                w_y.at[offset],
                wide_out.at[place.s],
                e_send.at[offset],
                e_recv.at[offset],
                (to, place.f),
            )
        else:
            pltpu.make_async_copy(w_y.at[0], wide_out.at[place.s], e_sem.at[0]).start()

    for offset in offsets[: count // 2]:
        wide_cores(offset)
    for step in range(depth):
        reduce.over_second(order[step])
        if step >= 1:
            reduce.over_first(order[step - 1])
        if step == 0:
            for offset in offsets[count // 2 :]:
                wide_cores(offset)
            for side in (other_y, mine_y):
                landed(d_core.at[side], dc_recv.at[side])
                add_into(d_core.at[side], down.at[2 * side + place.c], down_rows)
                if side is other_y:
                    send(d_core.at[side], d_y.at[0], dy_send.at[0], dy_recv.at[0], place.flip_y())
        for offset in offsets[step * count // depth : (step + 1) * count // depth]:
            wide_across(offset)
        if step >= 2:
            reduce.along(order[step - 2])
    reduce.over_first(order[depth - 1])
    for step in range(max(depth - 2, 0), depth):
        reduce.along(order[step])
    reduce.finish()
    landed(d_y.at[0], dy_recv.at[0])
    down_out[...] = d_y[0].astype(F32) + d_core[mine_y].astype(F32)
    for offset in range(1, count):
        origin = lax.rem(place.s + count - offset, count)
        landed(wide_out.at[origin], e_recv.at[offset])
    pltpu.make_async_copy(w_y.at[0], wide_out.at[place.s], e_sem.at[0]).wait()
    reduce.settle()
    for copy in sent:
        copy.wait_send()


def call_end(depth, collective_id, pack, wide, down):
    count = 2 * depth
    block = pack.shape[-2:]
    wide_block = (2,) + wide.shape[-2:]
    down_block = down.shape[-2:]
    buffers, sems = Reduce.scratch(depth, True, block)
    scratch = buffers + sems
    scratch += [
        pltpu.VMEM((2, count) + wide_block, BF16),
        pltpu.VMEM((count,) + wide_block, BF16),
        pltpu.VMEM((2,) + down_block, BF16),
        pltpu.VMEM((1,) + down_block, BF16),
    ]
    scratch += [DMA((2 * count,)), DMA((2 * count,)), DMA((count,)), DMA((count,))]
    scratch += [DMA((count,)), DMA((count,)), DMA((1,))]
    scratch += [DMA((2,)), DMA((2,)), DMA((1,)), DMA((1,))]
    vmem = pl.BlockSpec(memory_space=pltpu.VMEM)
    return pl.pallas_call(
        functools.partial(end_kernel, depth, (block, wide_block, down_block)),
        out_shape=[
            jax.ShapeDtypeStruct(block, F32),
            jax.ShapeDtypeStruct((count,) + wide_block, BF16),
            jax.ShapeDtypeStruct(down_block, F32),
        ],
        in_specs=[vmem] * 3,
        out_specs=[vmem, vmem, vmem],
        scratch_shapes=scratch,
        compiler_params=pltpu.CompilerParams(
            collective_id=collective_id, has_side_effects=True, vmem_limit_bytes=VMEM_LIMIT
        ),
    )(pack, wide, down)


def forward_kernel(span, info, begin, query, key, value, mixed, lse, m_acc, l_acc, o_acc):
    rows = begin.shape[0]
    first_row, low, high = info[0], info[1], info[2]
    scale = HEAD_DIM ** (-0.5) * LOG2E
    m_acc[...] = jnp.full_like(m_acc, -1e30)
    l_acc[...] = jnp.zeros_like(l_acc)
    o_acc[...] = jnp.zeros_like(o_acc)
    places = first_row + lax.broadcasted_iota(jnp.int32, (rows, span), 0)
    offsets = lax.broadcasted_iota(jnp.int32, (rows, span), 1)

    def step(number, carry):
        base = pl.multiple_of(number * span, span)
        keys_at = base + offsets
        visible = jnp.logical_and(keys_at >= begin[...], keys_at <= places)
        for g in range(KV_HEADS):
            lanes = slice(g * HEAD_DIM, (g + 1) * HEAD_DIM)
            scores = lax.dot_general(
                query[g],
                key[pl.ds(base, span), lanes],
                (((1,), (1,)), ((), ())),
                preferred_element_type=F32,
            )
            scores = scores.reshape(GROUP, rows, span) * scale
            scores = jnp.where(visible[None], scores, -1e30).reshape(GROUP * rows, span)
            old = m_acc[g]
            new = jnp.maximum(old, jnp.max(scores, axis=-1, keepdims=True))
            weights = jnp.exp2(scores - new[:, :1])
            weights = jnp.where(
                visible[None], weights.reshape(GROUP, rows, span), 0.0
            ).reshape(GROUP * rows, span)
            fade = jnp.exp2(old - new)
            l_acc[g] = l_acc[g] * fade + jnp.sum(weights, axis=-1, keepdims=True)
            o_acc[g] = o_acc[g] * fade + jnp.dot(
                weights.astype(BF16),
                value[pl.ds(base, span), lanes],
                preferred_element_type=F32,
            )
            m_acc[g] = new
        return carry

    lax.fori_loop(low, high, step, 0)
    for g in range(KV_HEADS):
        mixed[g] = o_acc[g] / l_acc[g]
        lse[g] = m_acc[g] + jnp.log2(l_acc[g])


def call_forward(span, info, begin, query, key, value):
    stacked = query.shape[1]
    vmem = pl.BlockSpec(memory_space=pltpu.VMEM)
    return pl.pallas_call(
        functools.partial(forward_kernel, span),
        out_shape=[
            jax.ShapeDtypeStruct((KV_HEADS, stacked, HEAD_DIM), F32),
            jax.ShapeDtypeStruct((KV_HEADS, stacked, HEAD_DIM), F32),
        ],
        in_specs=[pl.BlockSpec(memory_space=pltpu.SMEM)] + [vmem] * 4,
        out_specs=[vmem, vmem],
        scratch_shapes=[pltpu.VMEM((KV_HEADS, stacked, HEAD_DIM), F32)] * 3,
        compiler_params=pltpu.CompilerParams(vmem_limit_bytes=VMEM_LIMIT),
    )(info, begin, query, key, value)


def backward_kernel(
    span, info, begin, query, key, value, mixed, lse, grad, dquery, dkeys, delta
):
    rows = begin.shape[0]
    first_row, low, high = info[0], info[1], info[2]
    scale = HEAD_DIM ** (-0.5) * LOG2E
    dquery[...] = jnp.zeros_like(dquery)
    width = KV_HEADS * HEAD_DIM
    for g in range(KV_HEADS):
        delta[g] = jnp.broadcast_to(
            jnp.sum(grad[g].astype(F32) * mixed[g], axis=-1, keepdims=True), delta.shape[1:]
        )
    places = first_row + lax.broadcasted_iota(jnp.int32, (rows, span), 0)
    offsets = lax.broadcasted_iota(jnp.int32, (rows, span), 1)

    def clear(number, carry):
        base = pl.multiple_of(number * span, span)
        dkeys[pl.ds(base, span), :] = jnp.zeros((span, dkeys.shape[1]), BF16)
        return carry

    lax.fori_loop(0, low, clear, 0)
    lax.fori_loop(high, dkeys.shape[0] // span, clear, 0)

    def step(number, carry):
        base = pl.multiple_of(number * span, span)
        keys_at = base + offsets
        visible = jnp.logical_and(keys_at >= begin[...], keys_at <= places)
        for g in range(KV_HEADS):
            lanes = slice(g * HEAD_DIM, (g + 1) * HEAD_DIM)
            key_rows = key[pl.ds(base, span), lanes]
            value_rows = value[pl.ds(base, span), lanes]
            scores = lax.dot_general(
                query[g], key_rows, (((1,), (1,)), ((), ())), preferred_element_type=F32
            )
            dprobs = lax.dot_general(
                grad[g], value_rows, (((1,), (1,)), ((), ())), preferred_element_type=F32
            )
            probs = jnp.exp2(scores * scale - lse[g][:, :1])
            probs = jnp.where(
                visible[None], probs.reshape(GROUP, rows, span), 0.0
            ).reshape(GROUP * rows, span)
            dscores = (probs * (dprobs - delta[g][:, :1])).astype(BF16)
            dquery[g] += jnp.dot(dscores, key_rows, preferred_element_type=F32)
            dkeys[pl.ds(base, span), lanes] = lax.dot_general(
                dscores, query[g], (((0,), (0,)), ((), ())), preferred_element_type=F32
            ).astype(BF16)
            dkeys[
                pl.ds(base, span), width + g * HEAD_DIM : width + (g + 1) * HEAD_DIM
            ] = lax.dot_general(
                probs.astype(BF16),
                grad[g],
                (((0,), (0,)), ((), ())),
                preferred_element_type=F32,
            ).astype(BF16)
        return carry

    lax.fori_loop(low, high, step, 0)


def call_backward(span, info, begin, query, key, value, mixed, lse, grad):
    stacked = query.shape[1]
    vmem = pl.BlockSpec(memory_space=pltpu.VMEM)
    return pl.pallas_call(
        functools.partial(backward_kernel, span),
        out_shape=[
            jax.ShapeDtypeStruct((KV_HEADS, stacked, HEAD_DIM), F32),
            jax.ShapeDtypeStruct((key.shape[0], 2 * key.shape[1]), BF16),
        ],
        in_specs=[pl.BlockSpec(memory_space=pltpu.SMEM)] + [vmem] * 7,
        out_specs=[vmem, vmem],
        scratch_shapes=[pltpu.VMEM((KV_HEADS, stacked, HEAD_DIM), F32)],
        compiler_params=pltpu.CompilerParams(vmem_limit_bytes=VMEM_LIMIT),
    )(info, begin, query, key, value, mixed, lse, grad)


class PairGather:
    def __init__(self, place, own, out, sems, crossing):
        self.place, self.own, self.out, self.sems = place, own, out, sems
        self.crossing = crossing
        self.parts = [place.x, 1 - place.x] if crossing else [None]
        self.sent = []

    @staticmethod
    def semaphores(depth):
        sizes = (1, 1, 1, 4 * depth, 2 * depth, 2 * depth, 2 * depth, 4 * depth, 4 * depth)
        return [DMA((size,)) for size in sizes]

    def send(self, src, dst, send_sem, recv_sem, device, condition=None):
        copy = remote(src, dst, send_sem, recv_sem, device)
        guard(condition, copy.start)
        self.sent.append((copy, condition))

    def block(self, zi, y, c, part):
        if part is None:
            return self.out.at[zi, :, y, c]
        return self.out.at[zi, part, y, c]

    def slot(self, zi, part):
        return 2 * zi if part is None else 2 * zi + part

    def landed(self, ref, recv_sem, condition=None):
        guard(condition, remote(ref, ref, self.sems[3].at[0], recv_sem, self.place.flip_c()).wait_recv)

    def local(self):
        place = self.place
        source = self.own.at[place.x] if self.crossing else self.own
        return pltpu.make_async_copy(
            source, self.block(place.z, place.y, place.c, self.parts[0]), self.sems[0].at[0]
        )

    def begin(self):
        place = self.place
        self.send(
            self.own.at[1 - place.x],
            self.out.at[place.z, place.x, place.y, place.c],
            self.sems[1].at[0],
            self.sems[2].at[0],
            place.flip_x(),
        )
        self.spread(0, 0, place.z, None, place.x, self.own.at[place.x])

    def spread(self, k, side, zi, ok, part, source):
        place, depth = self.place, self.place.depth
        z_send, z_recv, y_send, y_recv, c_send, c_recv = self.sems[3:9]
        block, slot = self.block(zi, place.y, place.c, part), self.slot(zi, part)
        if k == 0 or side == 0:
            self.send(
                source,
                block,
                z_send.at[self.slot(k, part)],
                z_recv.at[slot],
                place.z_up(),
                both(place.up, ok),
            )
        if k == 0 or side == 1:
            self.send(
                source,
                block,
                z_send.at[2 * depth + self.slot(k, part)],
                z_recv.at[slot],
                place.z_down(),
                both(place.down, ok),
            )
        self.send(source, block, y_send.at[slot], y_recv.at[slot], place.flip_y(), ok)
        self.send(source, block, c_send.at[slot], c_recv.at[slot], place.flip_c(), ok)

    def arrive(self, k):
        place = self.place
        z_recv = self.sems[4]
        for side, (zi, ok) in enumerate(place.wave(k)):
            for number, part in enumerate(self.parts):
                block = self.block(zi, place.y, place.c, part)
                source = block
                if k > 0:
                    self.landed(block, z_recv.at[self.slot(zi, part)], ok)
                elif not self.crossing:
                    source = self.own
                elif number == 0:
                    continue
                else:
                    self.landed(block, self.sems[2].at[0])
                self.spread(k, side, zi, ok, part, source)

    def across(self, k):
        place, depth = self.place, self.place.depth
        y_recv, c_send, c_recv = self.sems[6:9]
        for zi, ok in place.wave(k):
            for part in self.parts:
                block = self.block(zi, 1 - place.y, place.c, part)
                self.landed(block, y_recv.at[self.slot(zi, part)], ok)
                slot = 2 * depth + self.slot(zi, part)
                self.send(block, block, c_send.at[slot], c_recv.at[slot], place.flip_c(), ok)

    def take(self, k):
        place, depth = self.place, self.place.depth
        c_recv = self.sems[8]
        for zi, ok in place.wave(k):
            for part in self.parts:
                slot = self.slot(zi, part)
                self.landed(self.block(zi, place.y, 1 - place.c, part), c_recv.at[slot], ok)
                slot = 2 * depth + slot
                self.landed(self.block(zi, 1 - place.y, 1 - place.c, part), c_recv.at[slot], ok)

    def settle(self):
        for copy, condition in self.sent:
            guard(condition, copy.wait_send)


class PairReduce:
    def __init__(self, place, own, out, buffers, sems, causal=False, crossing=False):
        self.place, self.own, self.out, self.sems = place, own, out, sems
        self.from_core, self.from_y, self.line, self.from_x = buffers
        self.causal, self.crossing = causal, crossing
        self.sent = []

    @staticmethod
    def scratch(depth, block):
        buffers = [
            pltpu.VMEM((depth, 2, 2) + block, BF16),
            pltpu.VMEM((depth, 2) + block, BF16),
            pltpu.VMEM((depth + 1, 2) + block, BF16),
            pltpu.VMEM((1,) + block, BF16),
        ]
        sems = [DMA((2 * depth,)), DMA((2 * depth,)), DMA((depth,)), DMA((depth,))]
        sems += [DMA((2 * depth,)), DMA((2 * depth,)), DMA((1,)), DMA((1,))]
        return buffers, sems

    def wave(self, k):
        waves = self.place.wave(k)
        return waves[:1] if self.causal else waves

    def send(self, src, dst, send_sem, recv_sem, device, condition=None):
        copy = remote(src, dst, send_sem, recv_sem, device)
        guard(condition, copy.start)
        self.sent.append((copy, condition))

    def landed(self, ref, recv_sem):
        remote(ref, ref, self.sems[0].at[0], recv_sem, self.place.flip_c()).wait_recv()

    def add(self, target, term):
        for x in range(2):
            add_into(target.at[x], term.at[x], target.shape[1])

    def cores(self, k):
        place = self.place
        for zi, ok in self.wave(k):
            for y in range(2):
                slot = 2 * zi + y
                self.send(
                    self.own.at[zi, :, y, 1 - place.c],
                    self.from_core.at[zi, y],
                    self.sems[0].at[slot],
                    self.sems[1].at[slot],
                    place.flip_c(),
                    ok,
                )

    def over(self, k):
        place = self.place
        for zi, ok in self.wave(k):

            def body(zi=zi):
                for y in (1 - place.y, place.y):
                    block = self.from_core.at[zi, y]
                    self.landed(block, self.sems[1].at[2 * zi + y])
                    self.add(block, self.own.at[zi, :, y, place.c])
                    if y is not place.y:
                        self.y_copy(zi).start()

            guard(ok, body)
            self.sent.append((self.y_copy(zi), ok))

    def y_copy(self, zi):
        place = self.place
        return remote(
            self.from_core.at[zi, 1 - place.y],
            self.from_y.at[zi],
            self.sems[2].at[zi],
            self.sems[3].at[zi],
            place.flip_y(),
        )

    def z_copy(self, k, side, zi):
        depth = self.place.depth
        direction = 1 - side
        slot = direction * depth + zi
        there = self.line.at[depth if k == 1 and direction == 1 else zi]
        to = self.place.z_up() if side == 1 else self.place.z_down()
        return remote(
            self.from_y.at[zi], there, self.sems[4].at[slot], self.sems[5].at[slot], to
        )

    def along(self, k):
        place, depth = self.place, self.place.depth
        for side, (zi, ok) in enumerate(self.wave(k)):
            block = self.from_y.at[zi]

            def body(zi=zi, side=side, block=block):
                self.landed(block, self.sems[3].at[zi])
                self.add(block, self.from_core.at[zi, place.y])

                def more(direction):
                    term = self.line.at[depth if k == 0 and direction == 1 else zi]
                    self.landed(term, self.sems[5].at[direction * depth + zi])
                    self.add(block, term)

                if k == 0:
                    if not self.causal:
                        pl.when(place.down)(functools.partial(more, 0))
                    pl.when(place.up)(functools.partial(more, 1))
                elif side == 0:
                    pl.when(place.up)(functools.partial(more, 1))
                else:
                    pl.when(place.down)(functools.partial(more, 0))
                if k > 0:
                    self.z_copy(k, side, zi).start()

            guard(ok, body)
            if k > 0:
                self.sent.append((self.z_copy(k, side, zi), ok))

    def swap(self):
        place = self.place
        self.send(
            self.from_y.at[place.z, 1 - place.x],
            self.from_x.at[0],
            self.sems[6].at[0],
            self.sems[7].at[0],
            place.flip_x(),
        )

    def finish(self):
        place = self.place
        if self.crossing:
            self.landed(self.from_x.at[0], self.sems[7].at[0])
            self.out[place.x] = self.from_y[place.z, place.x].astype(self.out.dtype)
            self.out[1 - place.x] = self.from_x[0].astype(self.out.dtype)
        else:
            self.out[...] = self.from_y[place.z].astype(self.out.dtype)

    def settle(self):
        for copy, condition in self.sent:
            guard(condition, copy.wait_send)


class Exchange:
    def __init__(self, place, own, out, sems):
        self.place, self.own, self.out, self.sems = place, own, out, sems
        self.count = 2 * place.depth
        self.sent = []
        self.y_f = place.f + 2 - 4 * place.y
        self.c_f = place.f + 1 - 2 * place.c
        self.yc_f = self.y_f + 1 - 2 * place.c

    @staticmethod
    def semaphores(depth):
        count = 2 * depth
        return [
            DMA((1,)),
            DMA((count,)),
            DMA((count,)),
            DMA((count,)),
            DMA((count,)),
            DMA((2 * count,)),
            DMA((2 * count,)),
        ]

    def send(self, block, send_sem, recv_sem, device, source=None):
        copy = remote(block if source is None else source, block, send_sem, recv_sem, device)
        copy.start()
        self.sent.append(copy)

    def block(self, offset, owner):
        origin = lax.rem(self.place.s + self.count - offset, self.count)
        return self.out.at[:, origin, owner]

    def landed(self, block, recv_sem):
        remote(block, block, self.sems[1].at[0], recv_sem, self.place.flip_c()).wait_recv()

    def local(self):
        return pltpu.make_async_copy(
            self.own.at[:, self.place.s], self.block(0, self.place.f), self.sems[0].at[0]
        )

    def depart(self, offset):
        place = self.place
        to = lax.rem(place.s + offset, self.count)
        self.send(
            self.block(0, place.f),
            self.sems[1].at[offset],
            self.sems[2].at[offset],
            (to, place.f),
            self.own.at[:, to],
        )

    def onward(self, offset):
        place = self.place
        block = self.block(offset, place.f)
        if offset > 0:
            self.landed(block, self.sems[2].at[offset])
        self.send(block, self.sems[3].at[offset], self.sems[4].at[offset], place.flip_y())
        slot = 2 * offset
        self.send(block, self.sems[5].at[slot], self.sems[6].at[slot], place.flip_c())

    def sideways(self, offset):
        block = self.block(offset, self.y_f)
        self.landed(block, self.sems[4].at[offset])
        slot = 2 * offset + 1
        self.send(block, self.sems[5].at[slot], self.sems[6].at[slot], self.place.flip_c())

    def last(self, offset):
        self.landed(self.block(offset, self.c_f), self.sems[6].at[2 * offset])
        self.landed(self.block(offset, self.yc_f), self.sems[6].at[2 * offset + 1])

    def settle(self):
        for copy in self.sent:
            copy.wait_send()


class Quarter:
    def __init__(self, place, own, out, sems):
        self.place, self.own, self.out, self.sems = place, own, out, sems
        self.sent = []

    @staticmethod
    def semaphores():
        return [DMA((1,)), DMA((3,)), DMA((3,))]

    def local(self):
        return pltpu.make_async_copy(self.own, self.out.at[self.place.f], self.sems[0].at[0])

    def send(self, source, block, slot, device):
        copy = remote(source, block, self.sems[1].at[slot], self.sems[2].at[slot], device)
        copy.start()
        self.sent.append(copy)

    def depart(self):
        place = self.place
        self.send(self.own, self.out.at[place.f], 0, place.flip_y())
        self.send(self.own, self.out.at[place.f], 1, place.flip_c())

    def landed(self, owner, slot):
        block = self.out.at[owner]
        remote(block, block, self.sems[1].at[0], self.sems[2].at[slot], self.place.flip_c()).wait_recv()

    def sideways(self):
        place = self.place
        y_f = place.f + 2 - 4 * place.y
        self.landed(y_f, 0)
        self.send(self.out.at[y_f], self.out.at[y_f], 2, place.flip_c())

    def last(self):
        place = self.place
        self.landed(place.f + 1 - 2 * place.c, 1)
        self.landed(place.f + 2 - 4 * place.y + 1 - 2 * place.c, 2)

    def settle(self):
        for copy in self.sent:
            copy.wait_send()


def stage(gather, step):
    depth = gather.place.depth
    if step < depth:
        gather.arrive(step)
    if 0 <= step - 1 < depth:
        gather.across(step - 1)
    if isinstance(gather, PairGather):
        if 0 <= step - 2 < depth:
            gather.take(step - 2)
        return
    if gather.wide and 0 <= step - 2 < depth:
        gather.hand(step - 2)
    if gather.wide and 0 <= step - 3 < depth:
        gather.take(step - 3)


def turned(vector, cosine, sine):
    return vector * cosine + pltpu.roll(vector, HEAD_DIM // 2, 1) * sine


HEAD_PLAN = (
    ("tables", "P0", "wide", "P1", "P2", "d1", "d5", "P3", "o0", "d7", "P4", "P5", "project", "K0", "o1", "c0", "n7"),
    ("K1", "K2", "d2", "K3", "K4", "o2", "d6", "c1", "K5", "n0", "A0", "d4", "A1", "o3", "A2"),
    ("o4", "s0", "n6", "A3", "s7", "o5", "mix", "n1", "n5", "d3", "o6", "D", "after", "h0", "keep", "h1"),
    ("c2", "s1", "n4", "n3", "s6", "s5", "h2", "n2", "c3", "S", "s3", "s4", "s2", "h3", "h4", "c4"),
)
HEAD_INS = 12
HEAD_OUTS = 16


def head_kernel(depth, *refs):
    (o_own, q_own, k_own, v_own, small_own, gate_own, up_own, down_own) = refs[:8]
    (tokens, cot, frequency, lengths) = refs[8:HEAD_INS]
    (
        pack_out,
        o_out,
        kv_out,
        cot_out,
        wide_out,
        down_out,
        hidden_out,
        queries_out,
        mixed_out,
        lse_out,
        middle_out,
        hidden_pair_out,
        mixed_low_out,
        pair_out,
        angles_out,
        begin,
    ) = refs[HEAD_INS : HEAD_INS + HEAD_OUTS]
    vectors = refs[HEAD_INS + HEAD_OUTS]
    rest = refs[HEAD_INS + HEAD_OUTS + 1 :]
    pack_all, o_all, kv_all, kv_own, hidden_two, lin, m_acc, l_acc, o_acc = rest[:9]
    pack, wide, down, mixed_pair, mixed_far, spread = rest[9:15]
    queries, mixed, lse, middle, hidden_pair, mixed_low, pair, angles = rest[15:23]
    sems = list(rest[23:])

    def take(count):
        taken = sems[:count]
        del sems[:count]
        return taken

    wide_need = len(Gather.semaphores(depth, True))
    line_need = len(Gather.semaphores(depth, False))
    count = 2 * depth
    devices = 4 * count
    rows, model = tokens.shape
    key_width = KV_HEADS * HEAD_DIM
    group_width = GROUP * HEAD_DIM
    qkv_width = group_width + 2 * HEAD_DIM

    place = Place(depth)
    for g in range(KV_HEADS):
        at = 0
        for source in (q_own, k_own, v_own):
            width = source.shape[1] // KV_HEADS
            pack[g, :, at : at + width] = source[:, g * width : (g + 1) * width]
            at += width
        pack[g, :, at:] = small_own[...]
    greet(place, [(lax.rem(place.s + offset, count), place.f) for offset in range(1, count)])
    pair_need = len(PairGather.semaphores(depth))
    g_pack = PairGather(place, pack, pack_all, take(pair_need), True)
    g_o = Gather(place, True, o_own, o_all, take(wide_need))
    g_kv = PairGather(place, kv_own, kv_all, take(pair_need), False)
    g_cot = Gather(place, False, cot, cot_out, take(line_need + 2), True)
    g_hidden = Gather(place, False, hidden_two, hidden_out, take(line_need))
    x_wide = Exchange(place, wide, wide_out, take(len(Exchange.semaphores(depth))))
    x_down = Quarter(place, down, down_out, take(len(Quarter.semaphores())))
    out_sem, x_send, x_recv = take(3)

    g_pack.begin()
    token_copy = remote(
        tokens, pair.at[place.x], x_send.at[0], x_recv.at[0], place.flip_x()
    )
    token_copy.start()
    pair[place.x] = tokens[...]
    pack_local = g_pack.local()
    pack_local.start()
    pack_local.wait()
    few = down_own.shape[0]
    filled = down.shape[0]
    locals_ = [job.local() for job in (g_o, g_cot, x_wide, x_down)]
    for copy in locals_[:2]:
        copy.start()
    inputs = tokens[...].astype(F32)

    def pack_wide():
        for side, source in enumerate((gate_own, up_own)):
            for to in range(count):
                parts = []
                for owner in range(4):
                    low = (4 * to + owner) * few
                    parts.append(source[:, low : low + few])
                    parts.append(jnp.zeros((wide.shape[2], filled - few), BF16))
                wide[side, to] = jnp.concatenate(parts, axis=1)
        locals_[2].start()

    def tables():
        down[...] = jnp.concatenate(
            [down_own[...], jnp.zeros((filled - few, model), BF16)], axis=0
        )
        locals_[3].start()
        ahead = lax.broadcasted_iota(jnp.int32, (1, HEAD_DIM), 1) < HEAD_DIM // 2
        for x in range(2):
            first_row = ((2 * place.z + x) * 4 + place.f) * rows
            positions = first_row + lax.broadcasted_iota(jnp.int32, (rows, 1), 0)
            start, found = jnp.int32(0), jnp.zeros((rows, 1), jnp.int32)
            for number in range(lengths.shape[0]):
                found = jnp.where(positions >= start, start, found)
                start = start + lengths[number]
            begin[x] = found
            turns = (positions - found).astype(F32) * frequency[...]
            angles[x, 0] = jnp.cos(turns)
            sine = jnp.sin(turns)
            angles[x, 1] = jnp.where(ahead, -sine, sine)

    part = model // depth
    own_head = pl.ds(pl.multiple_of(place.x * HEAD_DIM, HEAD_DIM), HEAD_DIM)
    own_heads = pl.ds(pl.multiple_of(place.x * group_width, group_width), group_width)
    kv_local = g_kv.local()
    hidden_local = g_hidden.local()
    mixed_copy = remote(
        mixed_pair.at[1 - place.x], mixed_far, x_send.at[1], x_recv.at[1], place.flip_x()
    )

    def project():
        share = key_width // devices
        chosen = lax.broadcasted_iota(jnp.int32, (model, key_width), 1)
        chosen = lax.div(chosen, share) * (model // devices) + lax.rem(chosen, share)
        chosen = lax.broadcasted_iota(jnp.int32, (model, key_width), 0) == chosen
        small = pack_all[:, :, :, :, :, qkv_width:].reshape(model, 128).astype(F32).T
        vectors[...] = small[:8]
        spread[...] = jnp.dot(
            small[:8].astype(BF16), chosen.astype(BF16), preferred_element_type=F32
        )
        for copy in locals_:
            copy.wait()
        token_copy.wait_recv()
        pair_inputs = pair[...].reshape(2 * rows, model).astype(F32)
        inv_pair = lax.rsqrt(jnp.mean(pair_inputs * pair_inputs, axis=-1, keepdims=True) + EPSILON)
        hidden_pair[...] = (pair_inputs * inv_pair * small[0:1]).astype(BF16)
        for zi in range(depth):
            weights = pack_all[zi][:, :, :, :, :qkv_width].reshape(part, qkv_width)
            term = jnp.dot(
                hidden_pair[:, zi * part : (zi + 1) * part], weights, preferred_element_type=F32
            )
            if zi == 0:
                lin[...] = term
            else:
                lin[...] += term
        for x in range(2):
            at = slice(x * rows, (x + 1) * rows)
            head = lin[at, group_width : group_width + HEAD_DIM] + spread[2:3, own_head]
            kv_own[x, :, :HEAD_DIM] = turned(head, angles[x, 0], angles[x, 1]).astype(BF16)
            values = lin[at, group_width + HEAD_DIM :] + spread[3:4, own_head]
            kv_own[x, :, HEAD_DIM:] = values.astype(BF16)
        kv_local.start()

    def queries_of():
        query_bias = vectors[1:2, own_heads]
        for x in range(2):
            for j in range(GROUP):
                lanes = slice(j * HEAD_DIM, (j + 1) * HEAD_DIM)
                head = lin[x * rows : (x + 1) * rows, lanes] + query_bias[:, lanes]
                queries[x, j * rows : (j + 1) * rows, :] = turned(
                    head, angles[x, 0], angles[x, 1]
                ).astype(BF16)
        kv_local.wait()

    span = 4 * rows
    scale = HEAD_DIM ** (-0.5) * LOG2E
    m_acc[...] = jnp.full_like(m_acc, -1e30)
    l_acc[...] = jnp.zeros_like(l_acc)
    o_acc[...] = jnp.zeros_like(o_acc)
    local_rows = lax.broadcasted_iota(jnp.int32, (rows, span), 0)
    offsets = lax.broadcasted_iota(jnp.int32, (rows, span), 1)

    def attend(number, carry):
        keys_at = number * span + offsets
        block = kv_all.at[lax.div(number, 2), lax.rem(number, 2)]
        key = block[:, :, :, :HEAD_DIM].reshape(span, HEAD_DIM)
        value = block[:, :, :, HEAD_DIM:].reshape(span, HEAD_DIM)
        for x in range(2):
            places = ((2 * place.z + x) * 4 + place.f) * rows + local_rows
            visible = jnp.logical_and(keys_at >= begin[x], keys_at <= places)
            scores = mul_t(queries[x], key)
            scores = scores.reshape(GROUP, rows, span) * scale
            scores = jnp.where(visible[None], scores, -1e30).reshape(GROUP * rows, span)
            old = m_acc[x]
            new = jnp.maximum(old, jnp.max(scores, axis=-1, keepdims=True))
            weights = jnp.exp2(scores - new[:, :1])
            fade = jnp.exp2(old - new)
            l_acc[x] = l_acc[x] * fade + jnp.sum(weights, axis=-1, keepdims=True)
            o_acc[x] = o_acc[x] * fade + jnp.dot(
                weights.astype(BF16), value, preferred_element_type=F32
            )
            m_acc[x] = new
        return carry

    def attend_quarter(piece):
        low, high = piece * count // 4, (piece + 1) * count // 4
        reach = 2 * place.z + 2
        lax.fori_loop(jnp.minimum(low, reach), jnp.minimum(high, reach), attend, 0)

    def mix():
        for x in range(2):
            total = o_acc[x] / l_acc[x]
            mixed[x] = total
            lse[x] = m_acc[x] + jnp.log2(l_acc[x])
            mixed_pair[x] = total.astype(BF16)
        mixed_copy.start()

    def after_attention():
        mixed_copy.wait_recv()
        for j in range(GROUP):
            at = slice(j * rows, (j + 1) * rows)
            near = pl.multiple_of((place.x * GROUP + j) * HEAD_DIM, HEAD_DIM)
            far = pl.multiple_of(((1 - place.x) * GROUP + j) * HEAD_DIM, HEAD_DIM)
            mixed_low[:, pl.ds(near, HEAD_DIM)] = mixed_pair[place.x, at, :]
            mixed_low[:, pl.ds(far, HEAD_DIM)] = mixed_far[at, :]
        after = inputs
        for zi in range(depth):
            after = after + jnp.dot(
                mixed_low[:, zi * part : (zi + 1) * part],
                o_all[zi].reshape(part, model),
                preferred_element_type=F32,
            )
        middle[...] = after
        inv_two = lax.rsqrt(jnp.mean(after * after, axis=-1, keepdims=True) + EPSILON)
        hidden_two[...] = (after * inv_two * vectors[4:5]).astype(BF16)
        hidden_local.start()

    keeps = [
        pltpu.make_async_copy(source, target, out_sem.at[number])
        for number, (source, target) in enumerate(
            (
                (pack_all, pack_out),
                (o_all, o_out),
                (kv_all, kv_out),
                (queries, queries_out),
                (mixed, mixed_out),
                (lse, lse_out),
                (middle, middle_out),
                (hidden_pair, hidden_pair_out),
                (mixed_low, mixed_low_out),
                (pair, pair_out),
                (angles, angles_out),
            )
        )
    ]

    def keep():
        for copy in keeps:
            copy.start()

    jobs = {"P": g_pack, "K": g_kv, "o": g_o, "c": g_cot, "h": g_hidden}
    moves = {"d": x_wide.depart, "n": x_wide.onward, "s": x_wide.sideways, "A": attend_quarter}
    works = {
        "wide": pack_wide,
        "tables": tables,
        "project": project,
        "mix": mix,
        "after": after_attention,
        "keep": keep,
        "D": x_down.depart,
        "S": x_down.sideways,
    }
    for words in HEAD_PLAN:
        for word in words:
            if word in works:
                works[word]()
            elif word[0] in moves:
                moves[word[0]](int(word[1:]))
            else:
                stage(jobs[word[0]], int(word[1:]))
                if word == "K0":
                    queries_of()

    hidden_local.wait()
    for offset in range(count):
        x_wide.last(offset)
    x_down.last()
    for copy in keeps:
        copy.wait()
    token_copy.wait_send()
    mixed_copy.wait_send()
    for job in (g_pack, g_o, g_kv, g_cot, g_hidden, x_wide, x_down):
        job.settle()


def call_head(depth, collective_id, hbm, vmems, lengths):
    (o_own,) = hbm
    q_own, k_own, v_own, small_own, gate_own, _, down_own, tokens, cot = vmems[:9]
    count = 2 * depth
    few = down_own.shape[0]
    filled = -(-few // 16) * 16
    qkv_width = (GROUP + 2) * HEAD_DIM
    width = qkv_width + small_own.shape[1]
    pack = jax.ShapeDtypeStruct((q_own.shape[0], width), BF16)
    wide = jax.ShapeDtypeStruct((2, count, gate_own.shape[0], 4 * filled), BF16)
    down = jax.ShapeDtypeStruct((filled, down_own.shape[1]), BF16)
    rows, model = tokens.shape
    key_width = KV_HEADS * HEAD_DIM
    stacked = GROUP * rows
    kv_own = jax.ShapeDtypeStruct((rows, 2 * HEAD_DIM), BF16)
    any_, vmem = pl.BlockSpec(memory_space=pl.ANY), pl.BlockSpec(memory_space=pltpu.VMEM)
    heads = (KV_HEADS, stacked, HEAD_DIM)
    outs = [
        gather_shape(depth, True, pack),
        gather_shape(depth, True, o_own),
        gather_shape(depth, True, kv_own),
        gather_shape(depth, False, cot),
        jax.ShapeDtypeStruct((2, count, 4) + wide.shape[2:], BF16),
        jax.ShapeDtypeStruct((4,) + down.shape, BF16),
        gather_shape(depth, False, tokens),
        jax.ShapeDtypeStruct(heads, BF16),
        jax.ShapeDtypeStruct(heads, F32),
        jax.ShapeDtypeStruct(heads, F32),
        jax.ShapeDtypeStruct((rows, model), F32),
        jax.ShapeDtypeStruct((2 * rows, model), BF16),
        jax.ShapeDtypeStruct((rows, model), BF16),
        jax.ShapeDtypeStruct((2, rows, model), BF16),
        jax.ShapeDtypeStruct((2, 2, rows, HEAD_DIM), F32),
        jax.ShapeDtypeStruct((2, rows, 1), jnp.int32),
        jax.ShapeDtypeStruct((8, model), F32),
    ]
    scratch = [pltpu.VMEM(out.shape, BF16) for out in outs[:3]]
    scratch += [
        pltpu.VMEM((2,) + kv_own.shape, BF16),
        pltpu.VMEM((rows, model), BF16),
        pltpu.VMEM((2 * rows, qkv_width), F32),
        pltpu.VMEM(heads, F32),
        pltpu.VMEM(heads, F32),
        pltpu.VMEM(heads, F32),
        pltpu.VMEM((KV_HEADS,) + pack.shape, BF16),
        pltpu.VMEM(wide.shape, BF16),
        pltpu.VMEM(down.shape, BF16),
        pltpu.VMEM(heads, BF16),
        pltpu.VMEM(heads[1:], BF16),
        pltpu.VMEM((8, key_width), F32),
    ]
    scratch += [pltpu.VMEM(out.shape, out.dtype) for out in outs[7:15]]
    scratch += PairGather.semaphores(depth) + Gather.semaphores(depth, True)
    scratch += PairGather.semaphores(depth)
    scratch += Gather.semaphores(depth, False, True) + Gather.semaphores(depth, False)
    scratch += Exchange.semaphores(depth) + Quarter.semaphores()
    scratch += [DMA((11,)), DMA((2,)), DMA((2,))]
    return pl.pallas_call(
        functools.partial(head_kernel, depth),
        out_shape=outs,
        in_specs=[any_] + [vmem] * len(vmems) + [pl.BlockSpec(memory_space=pltpu.SMEM)],
        out_specs=[any_] * 15 + [vmem] * 2,
        scratch_shapes=scratch,
        compiler_params=pltpu.CompilerParams(
            collective_id=collective_id, has_side_effects=True, vmem_limit_bytes=VMEM_LIMIT
        ),
    )(*hbm, *vmems, lengths)


def t_mul(left, right):
    return lax.dot_general(left, right, (((0,), (0,)), ((), ())), preferred_element_type=F32)


def mul_t(left, right):
    return lax.dot_general(left, right, (((1,), (1,)), ((), ())), preferred_element_type=F32)


CUTS = ((0, 512), (512, 1024), (1024, 1152))


def middle_kernel(depth, *refs):
    (hidden_all, cot_all, wide_all, down_all, o_own) = refs[:5]
    (middle, cotangent, vectors) = refs[5:8]
    (layer_out, d_middle, d_mixed, d_branch, gain_two, down_out, wide_out) = refs[8:15]
    (tokens_v, grads_v, w_part, d_part, act, d_both, dh_part, out_part) = refs[15:23]
    (dh_sum, out_sum, w_core, w_y, d_core, o_all) = refs[23:29]
    rest = list(refs[29:])

    def take(count):
        taken = rest[:count]
        del rest[:count]
        return taken

    count = 2 * depth
    rows, model = middle.shape
    units = act.shape[2]
    part = model // depth
    buffers, sems = Reduce.scratch(depth, False, (rows, model))
    place = Place(depth)
    r_dh = Reduce(place, False, rows, dh_part, dh_sum, take(len(buffers)), take(len(sems)))
    r_out = Reduce(place, False, rows, out_part, out_sum, take(len(buffers)), take(len(sems)))
    load_sem, wc_send, wc_recv, wy_send, wy_recv, dc_send, dc_recv = take(7)
    sent = []

    def send(src, dst, send_sem, recv_sem, device):
        copy = remote(src, dst, send_sem, recv_sem, device)
        copy.start()
        sent.append(copy)

    def landed(ref, recv_sem):
        remote(ref, ref, wc_send.at[0], recv_sem, place.flip_c()).wait_recv()

    loads = [
        pltpu.make_async_copy(source, target, load_sem.at[number])
        for number, (source, target) in enumerate(
            (
                (hidden_all, tokens_v),
                (wide_all, w_part),
                (cot_all, grads_v),
                (down_all, d_part),
            )
        )
    ]
    for copy in loads:
        copy.start()
    greet(place)
    mine_y, other_y = place.y, 1 - place.y
    wide_rows = w_part.shape[-2]
    half = lax.div(place.z, 2)
    tiles = [3 - 3 * half, 2 - half, 1 + 4 * half - place.z, place.z]
    for copy in loads:
        copy.wait()

    def weights(side, low, high):
        return w_part[side, :, :, :, :, low:high].reshape(model, high - low)

    def forward(zi):
        tokens = tokens_v[zi].reshape(2 * rows, model)
        grads = grads_v[zi].reshape(2 * rows, model)
        out = None
        for low, high in CUTS:
            gate = jnp.dot(tokens, weights(0, low, high), preferred_element_type=F32)
            up = jnp.dot(tokens, weights(1, low, high), preferred_element_type=F32)
            d_act = mul_t(grads, d_part[low:high, :])
            sigma = jax.nn.sigmoid(gate)
            silu = gate * sigma
            act[zi, :, low:high] = (silu * up).astype(BF16)
            d_both[zi, :, low:high] = (
                d_act * up * sigma * (1.0 + gate * (1.0 - sigma))
            ).astype(BF16)
            d_both[zi, :, units + low : units + high] = (d_act * silu).astype(BF16)
        total = mul_t(d_both[zi, :, :units], weights(0, 0, units))
        total = total + mul_t(d_both[zi, :, units:], weights(1, 0, units))
        dh_part[zi] = total.astype(BF16).reshape(2, rows, model)
        out = jnp.dot(act[zi], d_part[...], preferred_element_type=F32)
        out_part[zi] = out.astype(BF16).reshape(2, rows, model)

    def tile(number, carry):
        zi = jnp.where(
            number == 0,
            tiles[0],
            jnp.where(number == 1, tiles[1], jnp.where(number == 2, tiles[2], tiles[3])),
        )
        forward(zi)
        r_dh.cross(zi)
        return carry

    lax.fori_loop(0, depth, tile, 0)
    for zi in tiles:
        r_out.cross(zi)
    r_dh.crossed()
    r_out.crossed()

    def wide_chunk(k, carry):
        lanes = pl.ds(pl.multiple_of(k * part, part), part)
        tokens = tokens_v[:, :, :, lanes].reshape(count * rows, part)
        term = t_mul(tokens, d_both[...].reshape(count * rows, 2 * units))
        for side in range(2):
            w_part[side, pl.ds(2 * k, 2)] = (
                term[:, side * units : (side + 1) * units]
                .astype(BF16)
                .reshape(2, 2, 2, wide_rows, units)
            )
        for step in range(2):
            to = 2 * k + step
            for y in range(2):
                remote(
                    w_part.at[:, to, y, 1 - place.c],
                    w_core.at[y, to],
                    wc_send.at[2 * to + y],
                    wc_recv.at[2 * to + y],
                    place.flip_c(),
                ).start()
        return carry

    def wide_cores(to):
        for y in (other_y, mine_y):
            landed(w_core.at[y, to], wc_recv.at[2 * to + y])
            for side in range(2):
                add_into(
                    w_core.at[y, to, side], w_part.at[side, to, y, place.c], wide_rows
                )
            if y is other_y:
                remote(
                    w_core.at[y, to], w_y.at[to], wy_send.at[to], wy_recv.at[to], place.flip_y()
                ).start()

    def wide_across(to, carry):
        landed(w_y.at[to], wy_recv.at[to])
        for side in range(2):
            add_into(w_y.at[to, side], w_core.at[mine_y, to, side], wide_rows)
        pltpu.make_async_copy(w_y.at[to], wide_out.at[to], load_sem.at[to]).start()
        return carry

    def wide_step(k, carry):
        wide_chunk(k, 0)
        pl.when(k > 0)(lambda: wide_cores(2 * k - 2))
        pl.when(k > 0)(lambda: wide_cores(2 * k - 1))
        return carry

    order = list(range(depth - 1, -1, -1))
    lax.fori_loop(0, depth - 2, wide_step, 0)
    r_dh.along(order[0])
    r_dh.along(order[1])
    lax.fori_loop(depth - 2, depth, wide_step, 0)
    wide_cores(count - 2)
    wide_cores(count - 1)
    r_dh.along(order[2])
    pieces = [
        pltpu.make_async_copy(o_own.at[zi], o_all.at[zi % 2], load_sem.at[zi])
        for zi in range(depth)
    ]
    for copy in pieces[:2]:
        copy.start()

    def down_chunk(k, carry):
        lanes = pl.ds(pl.multiple_of(k * 384, 384), 384)
        chunk = act[:, :, lanes].reshape(count * rows, 384)
        d_part[lanes, :] = t_mul(chunk, grads_v[...].reshape(count * rows, model)).astype(BF16)
        return carry

    lax.fori_loop(0, units // 384, down_chunk, 0)
    down_rows = units // 4

    def down_block(owner):
        return d_part.at[pl.ds(pl.multiple_of(owner * down_rows, down_rows), down_rows)]

    for y in (other_y, mine_y):
        send(
            down_block(2 * y + 1 - place.c),
            d_core.at[y],
            dc_send.at[y],
            dc_recv.at[y],
            place.flip_c(),
        )
    r_dh.along(order[3])
    r_dh.finish()

    after = middle[...]
    inv_two = lax.rsqrt(jnp.mean(after * after, axis=-1, keepdims=True) + EPSILON)
    normed = after * inv_two
    d_hidden = dh_sum[...]
    gain_two[...] = jnp.broadcast_to(
        jnp.sum(d_hidden * normed, axis=0, keepdims=True), gain_two.shape
    )
    scaled = d_hidden * vectors[4:5]
    total = cotangent[...].astype(F32) + inv_two * (
        scaled - normed * jnp.mean(scaled * normed, axis=-1, keepdims=True)
    )
    d_middle[...] = total
    d_branch[...] = total.astype(BF16)
    for zi in range(depth):
        pieces[zi].wait()
        term = mul_t(d_branch[...], o_all[zi % 2].reshape(part, model)).astype(BF16)
        for piece in range(part // HEAD_DIM):
            h = zi * (part // HEAD_DIM) + piece
            at = (h % GROUP) * rows
            d_mixed[h // GROUP, at : at + rows, :] = term[
                :, piece * HEAD_DIM : (piece + 1) * HEAD_DIM
            ]
        if zi + 2 < depth:
            pieces[zi + 2].start()
    for y in (other_y, mine_y):
        landed(d_core.at[y], dc_recv.at[y])
        add_into(d_core.at[y], down_block(2 * y + place.c), down_rows)
    keep = pltpu.make_async_copy(d_core, down_out, load_sem.at[count])
    keep.start()
    for step in range(depth):
        r_out.along(order[step])
        lax.fori_loop(2 * step, 2 * step + 2, wide_across, 0)
    r_out.finish()
    layer_out[...] = (middle[...] + out_sum[...]).astype(BF16)
    keep.wait()

    def end(to, carry):
        pltpu.make_async_copy(w_y.at[to], wide_out.at[to], load_sem.at[to]).wait()
        for y in range(2):
            slot = 2 * to + y
            remote(
                w_core.at[y, to], w_core.at[y, to], wc_send.at[slot], wc_recv.at[slot], place.flip_c()
            ).wait_send()
        remote(
            w_y.at[to], w_y.at[to], wy_send.at[to], wy_recv.at[to], place.flip_y()
        ).wait_send()
        return carry

    lax.fori_loop(0, count, end, 0)
    r_dh.settle()
    r_out.settle()
    for copy in sent:
        copy.wait_send()


def call_middle(depth, collective_id, hbm, vmems):
    hidden, cot, wide, down, o_all = hbm
    count = 2 * depth
    rows, model = vmems[0].shape
    units, wide_rows = wide.shape[-1], wide.shape[-2]
    any_, vmem = pl.BlockSpec(memory_space=pl.ANY), pl.BlockSpec(memory_space=pltpu.VMEM)
    buffers, sems = Reduce.scratch(depth, False, (rows, model))
    scratch = [pltpu.VMEM((depth, 2, rows, model), BF16)] * 2
    scratch += [pltpu.VMEM(wide.shape, BF16), pltpu.VMEM(down.shape, BF16)]
    scratch += [pltpu.VMEM((depth, 2 * rows, width), BF16) for width in (units, 2 * units)]
    scratch += [pltpu.VMEM((depth, 2, rows, model), BF16)] * 2
    scratch += [pltpu.VMEM((rows, model), F32)] * 2
    scratch += [
        pltpu.VMEM((2, count, 2, wide_rows, units), BF16),
        pltpu.VMEM((count, 2, wide_rows, units), BF16),
        pltpu.VMEM((2, units // 4, model), BF16),
        pltpu.VMEM((2,) + o_all.shape[1:], BF16),
    ]
    scratch += buffers + sems + buffers + sems
    scratch += [DMA((count + 1,)), DMA((2 * count,)), DMA((2 * count,))]
    scratch += [DMA((count,)), DMA((count,)), DMA((2,)), DMA((2,))]
    return pl.pallas_call(
        functools.partial(middle_kernel, depth),
        out_shape=[
            jax.ShapeDtypeStruct((rows, model), BF16),
            jax.ShapeDtypeStruct((rows, model), F32),
            jax.ShapeDtypeStruct((KV_HEADS, GROUP * rows, HEAD_DIM), BF16),
            jax.ShapeDtypeStruct((rows, model), BF16),
            jax.ShapeDtypeStruct((8, model), F32),
            jax.ShapeDtypeStruct((2, units // 4, model), BF16),
            jax.ShapeDtypeStruct((count, 2, wide_rows, units), BF16),
        ],
        in_specs=[any_] * 5 + [vmem] * 3,
        out_specs=[vmem] * 5 + [any_] * 2,
        scratch_shapes=scratch,
        compiler_params=pltpu.CompilerParams(
            collective_id=collective_id, has_side_effects=True, vmem_limit_bytes=VMEM_JOINED
        ),
    )(*hbm, *vmems)


LAST_PLAN = (
    ("d7", "d4", "d2", "d3", "down", "delta", "a0", "a1", "out"),
    ("Ck1", "Ck0", "Yk1", "d5", "Co0", "d1", "Co2", "Bo0", "a2"),
    ("Ck2", "Yk0", "a3", "Bo2", "Zk0", "Ck3", "turn", "Yk3", "Yk2"),
    ("Co1", "Zk1", "Co3", "hq", "Bo1", "query", "Zk2", "Bo3", "Cq0"),
    ("Cq2", "Ao0", "Cq1", "Zk3", "key", "Ao1", "Ao2", "d6", "hk"),
    ("kg", "small", "Cs0", "Yq0", "Cs2", "Cs1", "Zo0", "Yq1", "Ys0"),
    ("Cq3", "Ys2", "Yq2", "Zo1", "Cs3", "Zq0", "Ys1", "Ys3", "Zo2"),
    ("Yq3", "Ao3", "input", "Zs0", "Zq1", "Zs1", "Zq2", "Zs2", "Zq3"),
    ("Xq", "Zs3", "Xs", "Zo3"),
)


def follow_last(plan, works, depart, attend_wave, jobs):
    depth = 4
    steps = {"C": "cores", "B": "over_second", "A": "over_first", "Z": "along", "Y": "over"}
    for words in plan:
        for word in words:
            if word in works:
                works[word]()
            elif word[0] == "d":
                depart(int(word[1:]))
            elif word[0] == "a":
                attend_wave(int(word[1:]))
            else:
                getattr(jobs[word[1]], steps[word[0]])(depth - 1 - int(word[2:]))


def last_kernel(depth, *refs):
    (kv_own, pack_own, wide, down) = refs[:4]
    (queries, mixed, lse, d_mixed, angles, begin) = refs[4:10]
    (pair, d_middle, vectors, gain_two, hidden_pair, mixed_low, d_branch) = refs[10:17]
    (input_grad, q_out, kvs_out, o_out, down_out, wide_out) = refs[17:23]
    (kv_all, weights, d_query, delta, d_lin, d_keys, d_kv) = refs[23:30]
    (o_part, q_part, kvs_part) = refs[30:33]
    (d_near, d_far, d_hidden, kv_weights, d_pair, h_send, h_far, lines, pairs) = refs[33:42]
    rest = list(refs[42:])

    def take(number):
        taken = rest[:number]
        del rest[:number]
        return taken

    count = 2 * depth
    devices = 4 * count
    _, rows, model = pair.shape
    part = model // depth
    key_width = KV_HEADS * HEAD_DIM
    group_width = GROUP * HEAD_DIM
    qkv_width = group_width + 2 * HEAD_DIM
    model_rows = model // devices
    share = key_width // devices
    span = 4 * rows
    score_scale = HEAD_DIM ** (-0.5)
    scale = score_scale * LOG2E

    place = Place(depth)
    buffers, sems = Reduce.scratch(depth, True, o_part.shape[-2:])
    r_o = Reduce(
        place, True, model_rows, o_part, o_out, take(len(buffers)), take(len(sems))
    )

    def reduce_of(own, out, causal=False, crossing=True):
        buffers, sems = PairReduce.scratch(depth, own.shape[-2:])
        return PairReduce(
            place, own, out, take(len(buffers)), take(len(sems)), causal, crossing
        )

    r_kv = reduce_of(d_keys, d_kv, True, False)
    r_q = reduce_of(q_part, q_out)
    r_s = reduce_of(kvs_part, kvs_out)
    load_sem, e_send, e_recv, y_send, y_recv, x_send, x_recv = take(7)
    order = list(range(depth - 1, -1, -1))
    sent = []

    def depart(offset):
        to = lax.rem(place.s + offset, count)
        copy = remote(
            wide.at[to], wide_out.at[place.s], e_send.at[offset], e_recv.at[offset], (to, place.f)
        )
        copy.start()
        sent.append(copy)

    kv_load = pltpu.make_async_copy(kv_own, kv_all, load_sem.at[0])
    kv_load.start()
    own_wide = pltpu.make_async_copy(wide.at[place.s], wide_out.at[place.s], load_sem.at[1])
    own_wide.start()
    down_load = pltpu.make_async_copy(down.at[place.y], d_near, load_sem.at[2 + depth])
    down_load.start()
    greet(place, [(lax.rem(place.s + offset, count), place.f) for offset in range(1, count)])
    mixed_copy = remote(
        d_mixed.at[1 - place.x],
        d_pair.at[place.x],
        x_send.at[0],
        x_recv.at[0],
        place.flip_x(),
    )
    mixed_copy.start()
    sent.append(mixed_copy)
    d_pair[place.x] = d_mixed[place.x]
    down_copy = remote(
        down.at[1 - place.y], d_far, y_send.at[0], y_recv.at[0], place.flip_y()
    )
    hidden_copy = remote(h_send, h_far, x_send.at[1], x_recv.at[1], place.flip_x())
    loads = [
        pltpu.make_async_copy(pack_own.at[zi], weights.at[zi % 2], load_sem.at[2 + zi])
        for zi in range(depth)
    ]

    local_rows = lax.broadcasted_iota(jnp.int32, (rows, span), 0)
    offsets = lax.broadcasted_iota(jnp.int32, (rows, span), 1)

    def attend(number, carry):
        keys_at = number * span + offsets
        z, x_at = lax.div(number, 2), lax.rem(number, 2)
        block = kv_all.at[z, x_at]
        key = block[:, :, :, :HEAD_DIM].reshape(span, HEAD_DIM)
        value = block[:, :, :, HEAD_DIM:].reshape(span, HEAD_DIM)
        d_key, d_value = None, None
        for x in range(2):
            places = ((2 * place.z + x) * 4 + place.f) * rows + local_rows
            visible = jnp.logical_and(keys_at >= begin[x], keys_at <= places)
            scores = mul_t(queries[x], key)
            d_probs = mul_t(d_pair[x], value)
            probs = jnp.exp2(scores * scale - lse[x][:, :1])
            probs = jnp.where(
                visible[None], probs.reshape(GROUP, rows, span), 0.0
            ).reshape(GROUP * rows, span)
            d_scores = (probs * (d_probs - delta[x][:, :1])).astype(BF16)
            d_query[x] += jnp.dot(d_scores, key, preferred_element_type=F32)
            key_term = t_mul(d_scores, queries[x])
            value_term = t_mul(probs.astype(BF16), d_pair[x])
            d_key = key_term if x == 0 else d_key + key_term
            d_value = value_term if x == 0 else d_value + value_term
        target = d_keys.at[z, x_at]
        target[:, :, :, :HEAD_DIM] = d_key.astype(BF16).reshape(2, 2, rows, HEAD_DIM)
        target[:, :, :, HEAD_DIM:] = d_value.astype(BF16).reshape(2, 2, rows, HEAD_DIM)
        return carry

    def normed_of(rows_of):
        inputs = rows_of.astype(F32)
        inverse = lax.rsqrt(jnp.mean(inputs * inputs, axis=-1, keepdims=True) + EPSILON)
        return inputs * inverse, inverse

    def out_gradient():
        for copy in loads[:2]:
            copy.start()
        for zi in range(depth):
            lanes = slice(zi * part, (zi + 1) * part)
            term = t_mul(mixed_low[:, lanes], d_branch[...]).astype(BF16)
            o_part[zi] = term.reshape(2, 2, 2, model_rows, model)

    def deltas():
        mixed_copy.wait_recv()
        for x in range(2):
            delta[x] = jnp.broadcast_to(
                jnp.sum(d_pair[x].astype(F32) * mixed[x], axis=-1, keepdims=True),
                delta.shape[1:],
            )
        d_query[...] = jnp.zeros_like(d_query)
        kv_load.wait()

    def attend_wave(step):
        zi = place.z - order[step]
        low = jnp.maximum(2 * zi, 0)
        high = jnp.maximum(2 * zi + 2, 0)
        lax.fori_loop(low, high, attend, 0)

    def query_turn():
        for x in range(2):
            for j in range(GROUP):
                lanes = slice(j * HEAD_DIM, (j + 1) * HEAD_DIM)
                head = d_query[x, j * rows : (j + 1) * rows, :] * score_scale
                d_lin[x * rows : (x + 1) * rows, lanes] = turned(
                    head, angles[x, 0], -angles[x, 1]
                ).astype(BF16)

    def query_gradient():
        for zi in range(depth):
            lanes = slice(zi * part, (zi + 1) * part)
            term = t_mul(hidden_pair[:, lanes], d_lin[:, :group_width]).astype(BF16)
            q_part[zi] = term.reshape(2, 2, 2, model_rows, group_width)

    def key_turn():
        r_kv.finish()
        for x in range(2):
            at = slice(x * rows, (x + 1) * rows)
            head = d_kv[x, :, :HEAD_DIM] * score_scale
            d_lin[at, group_width : group_width + HEAD_DIM] = turned(
                head, angles[x, 0], -angles[x, 1]
            ).astype(BF16)
            d_lin[at, group_width + HEAD_DIM :] = d_kv[x, :, HEAD_DIM:].astype(BF16)

    def hidden_query():
        for zi in range(depth):
            lanes = slice(zi * part, (zi + 1) * part)
            loads[zi].wait()
            block = weights[zi % 2][:, :, :, :, :group_width].reshape(part, group_width)
            term = mul_t(d_lin[:, :group_width], block)
            for x in range(2):
                d_hidden[x, :, lanes] = term[x * rows : (x + 1) * rows]
            block = weights[zi % 2][:, :, :, :, group_width:qkv_width]
            kv_weights[lanes, :] = block.reshape(part, 2 * HEAD_DIM)
            if zi + 2 < depth:
                loads[zi + 2].start()

    def hidden_key():
        for zi in range(depth):
            lanes = slice(zi * part, (zi + 1) * part)
            term = mul_t(d_lin[:, group_width:], kv_weights[lanes, :])
            for x in range(2):
                d_hidden[x, :, lanes] += term[x * rows : (x + 1) * rows]
        h_send[...] = d_hidden[1 - place.x].astype(BF16)
        hidden_copy.start()

    def key_gradient():
        for zi in range(depth):
            lanes = slice(zi * part, (zi + 1) * part)
            term = t_mul(hidden_pair[:, lanes], d_lin[:, group_width:]).astype(BF16)
            kvs_part[zi, :, :, :, :, : 2 * HEAD_DIM] = term.reshape(
                2, 2, 2, model_rows, 2 * HEAD_DIM
            )

    def small_gradients():
        lines[...] = jnp.zeros_like(lines)
        pairs[...] = jnp.zeros_like(pairs)
        bias = jnp.sum(d_lin[...].astype(F32), axis=0, keepdims=True)
        own_head = pl.ds(pl.multiple_of(place.x * HEAD_DIM, HEAD_DIM), HEAD_DIM)
        own_heads = pl.ds(pl.multiple_of(place.x * group_width, group_width), group_width)
        gain_one = jnp.zeros((1, model), F32)
        for x in range(2):
            normed, _ = normed_of(pair[x])
            gain_one = gain_one + jnp.sum(d_hidden[x] * normed, axis=0, keepdims=True)
        lines[0:1, :] = gain_one
        lines[1:2, own_heads] = bias[:, :group_width]
        lines[4:5, :] = gain_two[0:1]
        pairs[0:1, own_head] = bias[:, group_width : group_width + HEAD_DIM]
        pairs[1:2, own_head] = bias[:, group_width + HEAD_DIM :]
        chosen = lax.broadcasted_iota(jnp.int32, (key_width, model), 0)
        chosen = lax.div(chosen, share) * model_rows + lax.rem(chosen, share)
        chosen = (lax.broadcasted_iota(jnp.int32, (key_width, model), 1) == chosen).astype(BF16)
        spread = jnp.dot(pairs[...].astype(BF16), chosen, preferred_element_type=F32)
        lines[2:4, :] = spread[0:2]
        small = jnp.concatenate([lines[...], jnp.zeros((120, model), F32)], axis=0)
        small = small.T.astype(BF16)
        for zi in range(depth):
            kvs_part[zi, :, :, :, :, 2 * HEAD_DIM :] = small[
                zi * part : (zi + 1) * part
            ].reshape(2, 2, 2, model_rows, 128)

    def input_gradient():
        hidden_copy.wait_recv()
        normed, inv_one = normed_of(pair[place.x])
        scaled = (d_hidden[place.x] + h_far[...].astype(F32)) * vectors[0:1]
        input_grad[...] = d_middle[...] + inv_one * (
            scaled - normed * jnp.mean(scaled * normed, axis=-1, keepdims=True)
        )

    works = {
        "out": out_gradient,
        "delta": deltas,
        "turn": query_turn,
        "query": query_gradient,
        "key": key_turn,
        "hq": hidden_query,
        "hk": hidden_key,
        "kg": key_gradient,
        "Xq": r_q.swap,
        "Xs": r_s.swap,
        "small": small_gradients,
        "input": input_gradient,
        "down": down_copy.start,
    }
    jobs = {"o": r_o, "k": r_kv, "q": r_q, "s": r_s}
    follow_last(LAST_PLAN, works, depart, attend_wave, jobs)
    for job in (r_o, r_q, r_s):
        job.finish()
    for offset in range(1, count):
        origin = lax.rem(place.s + count - offset, count)
        block = wide_out.at[origin]
        remote(block, block, e_send.at[0], e_recv.at[offset], place.flip_c()).wait_recv()
    own_wide.wait()
    down_load.wait()
    down_copy.wait()
    down_out[...] = d_near[...].astype(F32) + d_far[...].astype(F32)
    hidden_copy.wait_send()
    for job in (r_kv, r_o, r_q, r_s):
        job.settle()
    for copy in sent:
        copy.wait_send()


def call_last(depth, collective_id, hbm, vmems):
    kv_all, pack_all, wide, down = hbm
    pair = vmems[6]
    count = 2 * depth
    _, rows, model = pair.shape
    model_rows = model // (4 * count)
    key_width, group_width = KV_HEADS * HEAD_DIM, GROUP * HEAD_DIM
    heads = (2, GROUP * rows, HEAD_DIM)
    lead = (depth, 2, 2, 2)
    kv_block, o_block = (rows, 2 * HEAD_DIM), (model_rows, model)
    blocks = [
        (model_rows, group_width),
        (model_rows, 2 * HEAD_DIM + 128),
    ]
    scratch = [
        pltpu.VMEM(kv_all.shape, BF16),
        pltpu.VMEM((2,) + pack_all.shape[1:], BF16),
        pltpu.VMEM(heads, F32),
        pltpu.VMEM(heads, F32),
        pltpu.VMEM((2 * rows, group_width + 2 * HEAD_DIM), BF16),
        pltpu.VMEM(lead + kv_block, BF16),
        pltpu.VMEM((2,) + kv_block, F32),
        pltpu.VMEM(lead + o_block, BF16),
    ]
    scratch += [pltpu.VMEM(lead + block, BF16) for block in blocks]
    scratch += [pltpu.VMEM(down.shape[1:], BF16)] * 2
    scratch += [
        pltpu.VMEM((2, rows, model), F32),
        pltpu.VMEM((model, 2 * HEAD_DIM), BF16),
        pltpu.VMEM(heads, BF16),
        pltpu.VMEM((rows, model), BF16),
        pltpu.VMEM((rows, model), BF16),
        pltpu.VMEM((8, model), F32),
        pltpu.VMEM((8, key_width), F32),
    ]
    buffers, sems = Reduce.scratch(depth, True, o_block)
    scratch += buffers + sems
    for block in [kv_block] + blocks:
        buffers, sems = PairReduce.scratch(depth, block)
        scratch += buffers + sems
    scratch += [DMA((3 + depth,)), DMA((count,)), DMA((count,)), DMA((1,)), DMA((1,))]
    scratch += [DMA((2,)), DMA((2,))]
    any_, vmem = pl.BlockSpec(memory_space=pl.ANY), pl.BlockSpec(memory_space=pltpu.VMEM)
    return pl.pallas_call(
        functools.partial(last_kernel, depth),
        out_shape=[
            jax.ShapeDtypeStruct((rows, model), F32),
            jax.ShapeDtypeStruct((2,) + blocks[0], F32),
            jax.ShapeDtypeStruct((2,) + blocks[1], F32),
            jax.ShapeDtypeStruct(o_block, F32),
            jax.ShapeDtypeStruct(down.shape[1:], F32),
            jax.ShapeDtypeStruct(wide.shape, BF16),
        ],
        in_specs=[any_] * 4 + [vmem] * len(vmems),
        out_specs=[vmem] * 6,
        scratch_shapes=scratch,
        compiler_params=pltpu.CompilerParams(
            collective_id=collective_id, has_side_effects=True, vmem_limit_bytes=VMEM_JOINED
        ),
    )(*hbm, *vmems)


def finish_kernel(few, plain, *refs):
    ins, refs = refs[: 4 + plain], refs[4 + plain :]
    outs, vectors, refs = refs[: 6 + plain], refs[6 + plain : 11 + plain], refs[11 + plain :]
    held, refs = refs[: 4 + plain], refs[4 + plain :]
    gate, up, query, key, value, in_sem, out_sem = refs
    loads = [
        pltpu.make_async_copy(source, target, in_sem.at[number])
        for number, (source, target) in enumerate(zip(ins, held))
    ]
    for copy in loads:
        copy.start()
    wide, down, q_in, kvs_in = held[:4]
    filled = wide.shape[3] // 4
    stores = []

    def store(source, number):
        copy = pltpu.make_async_copy(source, outs[number], out_sem.at[number])
        copy.start()
        stores.append(copy)

    loads[0].wait()
    for side, out in enumerate((gate, up)):
        for place in range(wide.shape[0]):
            block = wide[place, side].astype(F32)
            for owner in range(4):
                low = (4 * place + owner) * few
                out[:, low : low + few] = block[:, owner * filled : owner * filled + few]
        store(out, side)
    loads[1].wait()
    store(down.at[pl.ds(0, few)], 2)
    for number in range(plain):
        loads[4 + number].wait()
        store(held[4 + number], 6 + number)
    loads[2].wait()
    loads[3].wait()
    for g in range(KV_HEADS):
        width = q_in.shape[2]
        query[:, g * width : (g + 1) * width] = q_in[g]
        lanes = slice(g * HEAD_DIM, (g + 1) * HEAD_DIM)
        key[:, lanes] = kvs_in[g, :, :HEAD_DIM]
        value[:, lanes] = kvs_in[g, :, HEAD_DIM : 2 * HEAD_DIM]
    for number, source in enumerate((query, key, value)):
        store(source, 3 + number)
    rows_of = (kvs_in[0, :, 2 * HEAD_DIM :] + kvs_in[1, :, 2 * HEAD_DIM :]).T
    for number, out in enumerate(vectors):
        out[...] = rows_of[number : number + 1, : out.shape[1]]
    for copy in stores:
        copy.wait()


def call_finish(few, sizes, wide, down, q_grad, kvs_grad, plain):
    seq, _, rows, _ = wide.shape
    key_width = KV_HEADS * HEAD_DIM
    units = seq * 4 * few
    any_, vmem = pl.BlockSpec(memory_space=pl.ANY), pl.BlockSpec(memory_space=pltpu.VMEM)
    ins = (wide, down, q_grad, kvs_grad, *plain)
    made = [
        jax.ShapeDtypeStruct((rows, units), F32),
        jax.ShapeDtypeStruct((rows, units), F32),
        jax.ShapeDtypeStruct((rows, HEADS * HEAD_DIM), F32),
        jax.ShapeDtypeStruct((rows, key_width), F32),
        jax.ShapeDtypeStruct((rows, key_width), F32),
    ]
    out_shape = made[:2] + [jax.ShapeDtypeStruct((few, down.shape[1]), F32)] + made[2:]
    out_shape += [jax.ShapeDtypeStruct(array.shape, array.dtype) for array in plain]
    out_shape += [jax.ShapeDtypeStruct((1, size), F32) for size in sizes]
    return pl.pallas_call(
        functools.partial(finish_kernel, few, len(plain)),
        out_shape=out_shape,
        in_specs=[any_] * len(ins),
        out_specs=[any_] * (6 + len(plain)) + [vmem] * len(sizes),
        scratch_shapes=[pltpu.VMEM(array.shape, array.dtype) for array in (*ins, *made)]
        + [DMA((len(ins),)), DMA((6 + len(plain),))],
        compiler_params=pltpu.CompilerParams(vmem_limit_bytes=VMEM_LIMIT),
    )(*ins)


def begin_of(positions, lengths):
    ends = jnp.cumsum(lengths)
    starts = ends - lengths
    inside = (positions[:, None] >= starts[None, :]) & (positions[:, None] < ends[None, :])
    return jnp.sum(jnp.where(inside, starts[None, :], 0), axis=1)


def rope_tables(places, head_size):
    half_size = head_size // 2
    frequency = ROPE_BASE ** (-2.0 * jnp.arange(half_size, dtype=F32) / head_size)
    angles = places.astype(F32)[:, None] * frequency[None, :]
    return (jnp.cos(angles), jnp.sin(angles))


def rotate(vector, cosine, sine_table, direction):
    half_size = vector.shape[-1] // 2
    front_half = vector[..., :half_size]
    back_half = vector[..., half_size:]
    cosine = cosine[:, None, :]
    sine_table = direction * sine_table[:, None, :]
    return jnp.concatenate(
        [
            front_half * cosine - back_half * sine_table,
            back_half * cosine + front_half * sine_table,
        ],
        axis=-1,
    )


def norm_back(grad_normed, normed, inverse, gain_row):
    scaled = grad_normed * gain_row
    return inverse * (scaled - normed * jnp.mean(scaled * normed, axis=-1, keepdims=True))


def dot(left, right):
    return jnp.dot(left, right, preferred_element_type=F32)


def dot_t(left, right):
    return lax.dot_general(left, right, (((1,), (1,)), ((), ())), preferred_element_type=F32)


def t_dot(left, right):
    return lax.dot_general(left, right, (((0,), (0,)), ((), ())), preferred_element_type=F32)


def column(vector, rows):
    return jnp.pad(vector, (0, rows - vector.shape[0]))[:, None]


def shards_apart(
    tokens,
    cotangent,
    lengths,
    attn_gain,
    q_weight,
    q_bias,
    k_weight,
    k_bias,
    v_weight,
    v_bias,
    o_weight,
    mlp_gain,
    gate_weight,
    up_weight,
    down_weight,
):
    seq, fsdp = lax.axis_size("seq"), lax.axis_size("fsdp")
    devices = seq * fsdp
    depth = seq // 2
    rows, model = tokens.shape
    total = rows * devices
    key_width = KV_HEADS * HEAD_DIM
    query_width = HEADS * HEAD_DIM
    model_rows = q_weight.shape[0]
    units = gate_weight.shape[1] // seq
    first_row = lax.axis_index(AXES) * rows
    positions = first_row + jnp.arange(rows, dtype=jnp.int32)
    begin = begin_of(positions, lengths)
    cosine, sine_table = rope_tables(positions - begin, HEAD_DIM)
    score_scale = HEAD_DIM ** (-0.5)

    small = jnp.concatenate(
        [column(v, model_rows) for v in (attn_gain, q_bias, k_bias, v_bias, mlp_gain)]
        + [jnp.zeros((model_rows, 123), BF16)],
        axis=1,
    )
    pack = jnp.concatenate([q_weight, k_weight, v_weight, o_weight, small], axis=1)
    wide = jnp.stack([gate_weight, up_weight]).reshape(2, model_rows, seq, units)
    wide = wide.transpose(0, 2, 1, 3)
    pack_all, cot_all, wide_all, down_all = call_start(
        depth, 0, pack, cotangent, wide, down_weight
    )
    pack_all = pack_all.reshape(model, pack.shape[1])
    qkv_width = query_width + 2 * key_width
    w_qkv = pack_all[:, :qkv_width]
    w_out = pack_all[:, qkv_width : qkv_width + query_width]
    smalls = pack_all[:, qkv_width + query_width :].astype(F32)
    gain_one, b_query = smalls[:, 0], smalls[:, 1]
    gain_two = smalls[:, 4]
    kv_share = k_bias.shape[0]
    b_key = smalls[:, 2].reshape(devices, model_rows)[:, :kv_share].reshape(key_width)
    b_value = smalls[:, 3].reshape(devices, model_rows)[:, :kv_share].reshape(key_width)
    cot_all = cot_all.reshape(seq * rows, model)
    w_gate = wide_all[0].reshape(model, units)
    w_up = wide_all[1].reshape(model, units)
    w_down = down_all.reshape(units, model)

    inputs = tokens.astype(F32)
    inv_one = lax.rsqrt(jnp.mean(inputs * inputs, axis=-1, keepdims=True) + EPSILON)
    normed_one = inputs * inv_one
    hidden_one = (normed_one * gain_one).astype(BF16)
    lin = dot(hidden_one, w_qkv) + jnp.concatenate([b_query, b_key, b_value])
    queries = rotate(
        lin[:, :query_width].reshape(rows, HEADS, HEAD_DIM), cosine, sine_table, 1.0
    ).astype(BF16)
    queries = queries.transpose(1, 0, 2).reshape(KV_HEADS, GROUP * rows, HEAD_DIM)
    keys = rotate(
        lin[:, query_width : query_width + key_width].reshape(rows, KV_HEADS, HEAD_DIM),
        cosine,
        sine_table,
        1.0,
    ).reshape(rows, key_width)
    kv = jnp.concatenate([keys, lin[:, query_width + key_width :]], axis=1).astype(BF16)
    (kv_all,) = call_gathers(depth, 1, [True], [kv])
    kv_all = kv_all.reshape(total, 2 * key_width)
    all_keys, all_values = kv_all[:, :key_width], kv_all[:, key_width:]

    span = min(512, total)
    low = begin[0] // span
    high = (first_row + rows - 1) // span + 1
    info = jnp.stack([first_row, low, high]).astype(jnp.int32)
    begin_column = begin[:, None]
    mixed, lse = call_forward(span, info, begin_column, queries, all_keys, all_values)
    mixed_low = (
        mixed.reshape(HEADS, rows, HEAD_DIM)
        .transpose(1, 0, 2)
        .reshape(rows, query_width)
        .astype(BF16)
    )
    middle = inputs + dot(mixed_low, w_out)
    inv_two = lax.rsqrt(jnp.mean(middle * middle, axis=-1, keepdims=True) + EPSILON)
    normed_two = middle * inv_two
    hidden_two = (normed_two * gain_two).astype(BF16)

    (hidden_all,) = call_gathers(depth, 2, [False], [hidden_two])
    hidden_all = hidden_all.reshape(seq * rows, model)
    gate = dot(hidden_all, w_gate)
    up = dot(hidden_all, w_up)
    sigma = jax.nn.sigmoid(gate)
    silu = gate * sigma
    activated = (silu * up).astype(BF16)
    d_act = dot_t(cot_all, w_down)
    d_gate = (d_act * up * sigma * (1.0 + gate * (1.0 - sigma))).astype(BF16)
    d_up = (d_act * silu).astype(BF16)
    d_hidden_part = dot_t(d_gate, w_gate) + dot_t(d_up, w_up)
    out_part = dot(activated, w_down)
    shape = (depth, 2, rows, model)
    d_hidden_two, branch = call_reduces(
        depth,
        3,
        [False, False],
        [d_hidden_part.astype(BF16).reshape(shape), out_part.astype(BF16).reshape(shape)],
    )
    layer_out = (middle + branch).astype(BF16)
    gate_part = t_dot(hidden_all, d_gate).astype(BF16)
    up_part = t_dot(hidden_all, d_up).astype(BF16)
    down_part = t_dot(activated, cot_all).astype(BF16)

    gain_two_grad = jnp.sum(d_hidden_two * normed_two, axis=0)
    d_middle = cotangent.astype(F32) + norm_back(d_hidden_two, normed_two, inv_two, gain_two)

    d_branch = d_middle.astype(BF16)
    d_mixed = dot_t(d_branch, w_out).astype(BF16)
    d_mixed = (
        d_mixed.reshape(rows, HEADS, HEAD_DIM)
        .transpose(1, 0, 2)
        .reshape(KV_HEADS, GROUP * rows, HEAD_DIM)
    )
    d_query, d_kv_part = call_backward(
        span, info, begin_column, queries, all_keys, all_values, mixed, lse, d_mixed
    )
    (d_kv,) = call_reduces(
        depth, 4, [True], [d_kv_part.reshape(depth, 2, 2, 2, rows, 2 * key_width)]
    )
    d_query = d_query.reshape(HEADS, rows, HEAD_DIM).transpose(1, 0, 2)
    d_q = rotate(d_query * score_scale, cosine, sine_table, -1.0).reshape(rows, query_width)
    d_k = rotate(
        d_kv[:, :key_width].reshape(rows, KV_HEADS, HEAD_DIM) * score_scale,
        cosine,
        sine_table,
        -1.0,
    ).reshape(rows, key_width)
    d_lin = jnp.concatenate([d_q, d_k, d_kv[:, key_width:]], axis=1).astype(BF16)
    bias_grad = jnp.sum(d_lin.astype(F32), axis=0)
    d_hidden_one = dot_t(d_lin, w_qkv)
    gain_one_grad = jnp.sum(d_hidden_one * normed_one, axis=0)
    input_grad = d_middle + norm_back(d_hidden_one, normed_one, inv_one, gain_one)

    def spread(vector):
        parts = vector.reshape(devices, -1)
        return jnp.pad(parts, ((0, 0), (0, model_rows - parts.shape[1]))).reshape(model, 1)

    small_part = jnp.concatenate(
        [
            spread(gain_one_grad),
            spread(bias_grad[:query_width]),
            spread(bias_grad[query_width : query_width + key_width]),
            spread(bias_grad[query_width + key_width :]),
            spread(gain_two_grad),
            jnp.zeros((model, 123), F32),
        ],
        axis=1,
    )
    pack_part = jnp.concatenate(
        [
            t_dot(hidden_one, d_lin).astype(BF16),
            t_dot(mixed_low, d_branch).astype(BF16),
            small_part.astype(BF16),
        ],
        axis=1,
    ).reshape(depth, 2, 2, 2, model_rows, pack.shape[1])
    wide_part = jnp.stack([gate_part, up_part]).reshape(2, seq, fsdp, model_rows, units)
    down_part = down_part.reshape(fsdp, units // fsdp, model)
    pack_grad, wide_grad, down_grad = call_end(depth, 5, pack_part, wide_part, down_part)
    wide_grad = wide_grad.transpose(1, 2, 0, 3).reshape(2, model_rows, seq * units).astype(F32)
    small_grad = pack_grad[:, qkv_width + query_width :]
    return (
        layer_out,
        input_grad,
        small_grad[:, 0],
        pack_grad[:, :query_width],
        small_grad[:, 1],
        pack_grad[:, query_width : query_width + key_width],
        small_grad[:kv_share, 2],
        pack_grad[:, query_width + key_width : qkv_width],
        small_grad[:kv_share, 3],
        pack_grad[:, qkv_width : qkv_width + query_width],
        small_grad[:, 4],
        wide_grad[0],
        wide_grad[1],
        down_grad,
    )


def shards_joined(
    tokens,
    cotangent,
    lengths,
    attn_gain,
    q_weight,
    q_bias,
    k_weight,
    k_bias,
    v_weight,
    v_bias,
    o_weight,
    mlp_gain,
    gate_weight,
    up_weight,
    down_weight,
):
    seq, fsdp = lax.axis_size("seq"), lax.axis_size("fsdp")
    devices = seq * fsdp
    depth = seq // 2
    rows, model = tokens.shape
    key_width = KV_HEADS * HEAD_DIM
    model_rows = q_weight.shape[0]
    kv_share = k_bias.shape[0]
    small = jnp.stack(
        [jnp.pad(v, (0, model_rows - v.shape[0])) for v in (attn_gain, q_bias, k_bias, v_bias, mlp_gain)],
        axis=1,
    )
    small = jnp.pad(small, ((0, 0), (0, 123)))
    few = down_weight.shape[0]
    filled = fsdp * (few + -few % 16)
    steps = np.arange(HEAD_DIM) % (HEAD_DIM // 2)
    frequency = jnp.asarray((ROPE_BASE ** (-2.0 * steps / HEAD_DIM)).astype(np.float32)[None, :])
    (
        pack_all,
        o_all,
        kv_all,
        cot_all,
        wide_all,
        down_all,
        hidden_all,
        queries,
        mixed,
        lse,
        middle,
        hidden_pair,
        mixed_low,
        pair,
        angles,
        begin,
        vectors,
    ) = call_head(
        depth,
        6,
        (o_weight,),
        (
            q_weight,
            k_weight,
            v_weight,
            small,
            gate_weight,
            up_weight,
            down_weight,
            tokens,
            cotangent,
            frequency,
        ),
        lengths,
    )
    layer_out, d_middle, d_mixed, d_branch, gain_two_grad, down_part, wide_part = call_middle(
        depth,
        7,
        (
            hidden_all,
            cot_all,
            wide_all.reshape(2, seq, 2, 2, model_rows, filled),
            down_all.reshape(filled, model),
            o_all,
        ),
        (middle, cotangent, vectors),
    )
    input_grad, q_grad, kvs_grad, o_grad, down_grad, wide_grad = call_last(
        depth,
        8,
        (kv_all, pack_all, wide_part, down_part),
        (
            queries,
            mixed,
            lse,
            d_mixed,
            angles,
            begin,
            pair,
            d_middle,
            vectors,
            gain_two_grad,
            hidden_pair,
            mixed_low,
            d_branch,
        ),
    )
    sizes = (model_rows, model_rows, kv_share, kv_share, model_rows)
    gate_grad, up_grad, down_grad, q_grad, k_grad, v_grad, *rest = call_finish(
        few, sizes, wide_grad, down_grad, q_grad, kvs_grad, (layer_out, input_grad, o_grad)
    )
    layer_out, input_grad, o_grad = rest[:3]
    small_grad = [vector.reshape(-1) for vector in rest[3:]]
    return (
        layer_out,
        input_grad,
        small_grad[0],
        q_grad,
        small_grad[1],
        k_grad,
        small_grad[2],
        v_grad,
        small_grad[3],
        o_grad,
        small_grad[4],
        gate_grad,
        up_grad,
        down_grad,
    )


def shards(*arguments):
    model_rows, rows = arguments[4].shape[0], arguments[0].shape[0]
    if model_rows % 16 == 0 and rows % 128 == 0 and lax.axis_size("seq") == 8:
        return shards_joined(*arguments)
    return shards_apart(*arguments)


def solution(mesh):
    matrix, vector = P(AXES, None), P(AXES)
    in_specs = (
        matrix,
        matrix,
        P(),
        vector,
        matrix,
        vector,
        matrix,
        vector,
        matrix,
        vector,
        matrix,
        vector,
        matrix,
        matrix,
        matrix,
    )
    out_specs = (
        matrix,
        matrix,
        vector,
        matrix,
        vector,
        matrix,
        vector,
        matrix,
        vector,
        matrix,
        vector,
        matrix,
        matrix,
        matrix,
    )
    return jax.shard_map(shards, mesh=mesh, in_specs=in_specs, out_specs=out_specs, check_vma=False)
```

```python
import functools

import jax
import jax.numpy as jnp
import numpy as np
from jax import lax
from jax.experimental import pallas as pl
from jax.experimental.pallas import tpu as pltpu
from jax.sharding import PartitionSpec as P

HEADS = 12
KV_HEADS = 2
HEAD_DIM = 128
GROUP = HEADS // KV_HEADS
EPSILON = 1e-06
ROPE_BASE = 10000.0
LOG2E = 1.4426950408889634
AXES = ("seq", "fsdp")
VMEM_LIMIT = 56 << 20
VMEM_JOINED = 60 << 20
F32 = jnp.float32
BF16 = jnp.bfloat16
DMA = pltpu.SemaphoreType.DMA


class Place:
    def __init__(self, depth):
        self.depth = depth
        self.s = lax.axis_index("seq")
        self.f = lax.axis_index("fsdp")
        self.z = lax.div(self.s, 2)
        self.x = lax.rem(self.s, 2)
        self.y = lax.div(self.f, 2)
        self.c = lax.rem(self.f, 2)
        self.up = self.z + 1 < depth
        self.down = self.z > 0

    def flip_x(self):
        return (self.s + 1 - 2 * self.x, self.f)

    def flip_y(self):
        return (self.s, self.f + 2 - 4 * self.y)

    def flip_c(self):
        return (self.s, self.f + 1 - 2 * self.c)

    def z_up(self):
        return (self.s + 2, self.f)

    def z_down(self):
        return (self.s - 2, self.f)

    def first(self):
        return (
            self.s + (1 - self.c) * (1 - 2 * self.x),
            self.f + self.c * (2 - 4 * self.y),
        )

    def second(self):
        return (
            self.s + self.c * (1 - 2 * self.x),
            self.f + (1 - self.c) * (2 - 4 * self.y),
        )

    def corner(self, i, j):
        over_x = i * (1 - self.c) + j * self.c
        over_y = j * (1 - self.c) + i * self.c
        return (self.x + over_x * (1 - 2 * self.x), self.y + over_y * (1 - 2 * self.y))

    def wave(self, k):
        if k == 0:
            return [(self.z, None)]
        return [(self.z - k, self.z - k >= 0), (self.z + k, self.z + k < self.depth)]


def guard(condition, body):
    if condition is None:
        body()
    else:
        pl.when(condition)(body)


def both(one, other):
    return one if other is None else jnp.logical_and(one, other)


def greet(place, others=()):
    barrier = pltpu.get_barrier_semaphore()
    partners = [place.flip_x(), place.flip_y(), place.flip_c(), *others]
    for partner in partners:
        pl.semaphore_signal(barrier, inc=1, device_id=partner, device_id_type=pl.DeviceIdType.MESH)

    def tell_up():
        pl.semaphore_signal(
            barrier, inc=1, device_id=place.z_up(), device_id_type=pl.DeviceIdType.MESH
        )

    def tell_down():
        pl.semaphore_signal(
            barrier, inc=1, device_id=place.z_down(), device_id_type=pl.DeviceIdType.MESH
        )

    pl.when(place.up)(tell_up)
    pl.when(place.down)(tell_down)
    pl.semaphore_wait(
        barrier, len(partners) + place.up.astype(jnp.int32) + place.down.astype(jnp.int32)
    )


def remote(src, dst, send_sem, recv_sem, device):
    return pltpu.make_async_remote_copy(
        src_ref=src,
        dst_ref=dst,
        send_sem=send_sem,
        recv_sem=recv_sem,
        device_id=device,
        device_id_type=pl.DeviceIdType.MESH,
    )


def add_into(target, term, rows):
    step = rows if rows <= 48 else (32 if rows % 32 == 0 else 16)

    def body(number, carry):
        at = pl.ds(pl.multiple_of(number * step, step), step)
        target[at, :] = (target[at, :].astype(F32) + term[at, :].astype(F32)).astype(BF16)
        return carry

    lax.fori_loop(0, rows // step, body, 0)


class Gather:
    def __init__(self, place, wide, own, out, sems, mixed=False):
        self.place, self.wide, self.own, self.out, self.sems = place, wide, own, out, sems
        self.mixed = mixed
        self.sent = []

    @staticmethod
    def semaphores(depth, wide, mixed=False):
        base = [DMA((1,)), DMA((2 * depth,)), DMA((depth,)), DMA((depth,)), DMA((depth,))]
        if mixed:
            base += [DMA((2 * depth,)), DMA((depth,))]
        if wide:
            base += [DMA((2 * depth,)), DMA((2 * depth,)), DMA((4 * depth,)), DMA((4 * depth,))]
        return base

    def at(self, zi, i, j):
        place = self.place
        if self.wide:
            x, y = place.corner(i, j)
            return self.out.at[zi, x, y, place.c]
        return self.out.at[zi, place.x + i * (1 - 2 * place.x)]

    def send(self, src, dst, send_sem, recv_sem, device, condition):
        copy = remote(src, dst, send_sem, recv_sem, device)
        guard(condition, copy.start)
        self.sent.append((copy, condition))

    def local(self):
        copy = pltpu.make_async_copy(
            self.own, self.at(self.place.z, 0, 0), self.sems[0].at[0]
        )
        return copy

    def along(self, k, zi, side, ok, column, z_send, z_recv, source=None):
        place, depth = self.place, self.place.depth
        block = self.at(zi, column, 0)
        source = block if source is None else source
        if k == 0 or side == 0:
            self.send(
                source, block, z_send.at[k], z_recv.at[zi], place.z_up(), both(place.up, ok)
            )
        if k == 0 or side == 1:
            self.send(
                source,
                block,
                z_send.at[depth + k],
                z_recv.at[zi],
                place.z_down(),
                both(place.down, ok),
            )

    def arrive(self, k):
        place = self.place
        z_send, z_recv, a_send, a_recv = self.sems[1:5]
        across = place.first() if self.wide else place.flip_x()
        for side, (zi, ok) in enumerate(place.wave(k)):
            block = self.at(zi, 0, 0)
            source = self.own if k == 0 else block
            if k > 0:
                landed = remote(block, block, z_send.at[0], z_recv.at[zi], place.z_up())
                guard(ok, landed.wait_recv)
            self.along(k, zi, side, ok, 0, z_send, z_recv, source)
            crossing = both(place.c == 0, ok) if self.mixed and k > 0 else ok
            self.send(source, block, a_send.at[zi], a_recv.at[zi], across, crossing)
            if self.wide:
                b_send, b_recv = self.sems[5:7]
                self.send(
                    source, block, b_send.at[2 * zi], b_recv.at[2 * zi], place.second(), ok
                )

    def across(self, k):
        place = self.place
        a_send, a_recv = self.sems[3:5]
        for side, (zi, ok) in enumerate(place.wave(k)):
            block = self.at(zi, 1, 0)
            crossing = both(place.c == 0, ok) if self.mixed and k > 0 else ok
            landed = remote(block, block, a_send.at[0], a_recv.at[zi], place.first())
            guard(crossing, landed.wait_recv)
            if self.mixed:
                z_send, z_recv = self.sems[5:7]
                carried = both(place.c == 1, ok)
                if k > 0:
                    landed = remote(block, block, z_send.at[0], z_recv.at[zi], place.z_up())
                    guard(carried, landed.wait_recv)
                self.along(k, zi, side, carried, 1, z_send, z_recv)
            if self.wide:
                b_send, b_recv = self.sems[5:7]
                self.send(
                    block, block, b_send.at[2 * zi + 1], b_recv.at[2 * zi + 1], place.second(), ok
                )

    def hand(self, k):
        place = self.place
        b_send, b_recv, c_send, c_recv = self.sems[5:9]
        for zi, ok in place.wave(k):
            for i in range(2):
                block = self.at(zi, i, 1)
                landed = remote(block, block, b_send.at[0], b_recv.at[2 * zi + i], place.second())
                guard(ok, landed.wait_recv)
            for x in range(2):
                for y in range(2):
                    block = self.out.at[zi, x, y, place.c]
                    slot = 4 * zi + 2 * x + y
                    self.send(
                        block, block, c_send.at[slot], c_recv.at[slot], place.flip_c(), ok
                    )

    def take(self, k):
        place = self.place
        c_send, c_recv = self.sems[7:9]
        for zi, ok in place.wave(k):
            for x in range(2):
                for y in range(2):
                    block = self.out.at[zi, x, y, 1 - place.c]
                    slot = 4 * zi + 2 * x + y
                    landed = remote(block, block, c_send.at[0], c_recv.at[slot], place.flip_c())
                    guard(ok, landed.wait_recv)

    def settle(self):
        for copy, condition in self.sent:
            guard(condition, copy.wait_send)


def drive_gathers(place, gathers):
    depth = place.depth
    locals_ = [gather.local() for gather in gathers]
    for copy in locals_:
        copy.start()
    for step in range(depth + 3):
        for gather in gathers:
            if step < depth:
                gather.arrive(step)
        if step == 0:
            for copy in locals_:
                copy.wait()
        for gather in gathers:
            if 0 <= step - 1 < depth:
                gather.across(step - 1)
        for gather in gathers:
            if gather.wide and 0 <= step - 2 < depth:
                gather.hand(step - 2)
        for gather in gathers:
            if gather.wide and 0 <= step - 3 < depth:
                gather.take(step - 3)
    for gather in gathers:
        gather.settle()


def gather_shape(depth, wide, own):
    lead = (depth, 2, 2, 2) if wide else (depth, 2)
    return jax.ShapeDtypeStruct(lead + own.shape, own.dtype)


def call_gathers(depth, collective_id, wides, owns):
    def kernel(*refs):
        count = len(owns)
        place = Place(depth)
        greet(place)
        gathers, used = [], 2 * count
        for number, wide in enumerate(wides):
            need = len(Gather.semaphores(depth, wide))
            gathers.append(
                Gather(place, wide, refs[number], refs[count + number], refs[used : used + need])
            )
            used += need
        drive_gathers(place, gathers)

    scratch = []
    for wide in wides:
        scratch += Gather.semaphores(depth, wide)
    return pl.pallas_call(
        kernel,
        out_shape=[gather_shape(depth, wide, own) for wide, own in zip(wides, owns)],
        in_specs=[pl.BlockSpec(memory_space=pl.ANY)] * len(owns),
        out_specs=[pl.BlockSpec(memory_space=pl.ANY)] * len(owns),
        scratch_shapes=scratch,
        compiler_params=pltpu.CompilerParams(
            collective_id=collective_id, has_side_effects=True, vmem_limit_bytes=VMEM_LIMIT
        ),
    )(*owns)


def start_kernel(depth, *refs):
    (pack, cot, wide_in, down_in, pack_out, cot_out, wide_out, down_out), sems = refs[:8], refs[8:]
    place = Place(depth)
    count = 2 * depth
    partners = []
    for offset in range(1, count):
        partners.append((lax.rem(place.s + offset, count), place.f))
    greet(place, partners)
    first = len(Gather.semaphores(depth, True))
    second = first + len(Gather.semaphores(depth, False))
    gathers = [
        Gather(place, True, pack, pack_out, sems[:first]),
        Gather(place, False, cot, cot_out, sems[first:second]),
    ]
    local_sem, e_send, e_recv, y_send, y_recv, c_send, c_recv, d_sem, d_send, d_recv = sems[second:]
    sent = []

    def send(src, dst, send_sem, recv_sem, device):
        copy = remote(src, dst, send_sem, recv_sem, device)
        copy.start()
        sent.append(copy)

    locals_ = [gather.local() for gather in gathers]
    locals_.append(
        pltpu.make_async_copy(
            wide_in.at[:, place.s], wide_out.at[:, place.s, place.f], local_sem.at[0]
        )
    )
    locals_.append(pltpu.make_async_copy(down_in, down_out.at[place.f], d_sem.at[0]))
    for copy in locals_:
        copy.start()

    y_f = place.f + 2 - 4 * place.y
    c_f = place.f + 1 - 2 * place.c
    yc_f = y_f + 1 - 2 * place.c

    def exchange(offset):
        to = lax.rem(place.s + offset, count)
        send(
            wide_in.at[:, to],
            wide_out.at[:, place.s, place.f],
            e_send.at[offset],
            e_recv.at[offset],
            (to, place.f),
        )

    def onward(offset):
        origin = lax.rem(place.s + count - offset, count)
        block = wide_out.at[:, origin, place.f]
        if offset > 0:
            remote(block, block, e_send.at[0], e_recv.at[offset], place.flip_y()).wait_recv()
        send(block, block, y_send.at[offset], y_recv.at[offset], place.flip_y())
        send(block, block, c_send.at[2 * offset], c_recv.at[2 * offset], place.flip_c())

    def sideways(offset):
        origin = lax.rem(place.s + count - offset, count)
        block = wide_out.at[:, origin, y_f]
        remote(block, block, y_send.at[0], y_recv.at[offset], place.flip_y()).wait_recv()
        send(block, block, c_send.at[2 * offset + 1], c_recv.at[2 * offset + 1], place.flip_c())

    def last(offset):
        origin = lax.rem(place.s + count - offset, count)
        for slot, owner in ((2 * offset, c_f), (2 * offset + 1, yc_f)):
            block = wide_out.at[:, origin, owner]
            remote(block, block, c_send.at[0], c_recv.at[slot], place.flip_c()).wait_recv()

    for gather in gathers:
        gather.arrive(0)
    send(down_in, down_out.at[place.f], d_send.at[0], d_recv.at[0], place.flip_y())
    send(down_in, down_out.at[place.f], d_send.at[1], d_recv.at[1], place.flip_c())
    for offset in range(1, count):
        exchange(offset)
    for copy in locals_:
        copy.wait()
    onward(0)
    total = depth + 3
    for step in range(1, total):
        for gather in gathers:
            if step < depth:
                gather.arrive(step)
        for gather in gathers:
            if 0 <= step - 1 < depth:
                gather.across(step - 1)
        for gather in gathers:
            if gather.wide and 0 <= step - 2 < depth:
                gather.hand(step - 2)
        for gather in gathers:
            if gather.wide and 0 <= step - 3 < depth:
                gather.take(step - 3)
    block = down_out.at[y_f]
    remote(block, block, d_send.at[0], d_recv.at[0], place.flip_y()).wait_recv()
    send(block, block, d_send.at[2], d_recv.at[2], place.flip_c())
    for offset in range(1, count):
        onward(offset)
        sideways(offset - 1)
    sideways(count - 1)
    for offset in range(count):
        last(offset)
    for slot, owner in ((1, c_f), (2, yc_f)):
        block = down_out.at[owner]
        remote(block, block, d_send.at[0], d_recv.at[slot], place.flip_c()).wait_recv()
    for gather in gathers:
        gather.settle()
    for copy in sent:
        copy.wait_send()


def call_start(depth, collective_id, pack, cot, wide, down):
    count = 2 * depth
    _, _, rows, columns = wide.shape
    scratch = Gather.semaphores(depth, True) + Gather.semaphores(depth, False)
    scratch += [DMA((1,)), DMA((count,)), DMA((count,)), DMA((count,)), DMA((count,))]
    scratch += [DMA((2 * count,)), DMA((2 * count,)), DMA((1,)), DMA((3,)), DMA((3,))]
    return pl.pallas_call(
        functools.partial(start_kernel, depth),
        out_shape=[
            gather_shape(depth, True, pack),
            gather_shape(depth, False, cot),
            jax.ShapeDtypeStruct((2, count, 4, rows, columns), BF16),
            jax.ShapeDtypeStruct((4,) + down.shape, BF16),
        ],
        in_specs=[pl.BlockSpec(memory_space=pl.ANY)] * 4,
        out_specs=[pl.BlockSpec(memory_space=pl.ANY)] * 4,
        scratch_shapes=scratch,
        compiler_params=pltpu.CompilerParams(
            collective_id=collective_id, has_side_effects=True, vmem_limit_bytes=VMEM_LIMIT
        ),
    )(pack, cot, wide, down)


class Reduce:
    def __init__(self, place, wide, rows, own, out, buffers, sems, near=None, causal=False):
        self.place, self.wide, self.rows = place, wide, rows
        self.own, self.out, self.buffers, self.sems = own, out, buffers, sems
        self.near = near
        self.causal = causal
        self.sent = []

    def wave(self, k):
        waves = self.place.wave(k)
        return waves[:1] if self.causal else waves

    def near_block(self, zi):
        return self.own.at[zi, self.place.x] if self.near is None else self.near.at[zi]

    @staticmethod
    def scratch(depth, wide, block):
        buffers = [
            pltpu.VMEM((depth,) + block, BF16),
            pltpu.VMEM((depth + 1,) + block, BF16),
        ]
        sems = [DMA((depth,)), DMA((depth,)), DMA((2 * depth,)), DMA((2 * depth,))]
        if wide:
            buffers += [
                pltpu.VMEM((depth, 2, 2) + block, BF16),
                pltpu.VMEM((depth, 2) + block, BF16),
            ]
            sems += [DMA((4 * depth,)), DMA((4 * depth,)), DMA((2 * depth,)), DMA((2 * depth,))]
        return buffers, sems

    def send(self, src, dst, send_sem, recv_sem, device, condition):
        copy = remote(src, dst, send_sem, recv_sem, device)
        guard(condition, copy.start)
        self.sent.append((copy, condition))

    def cores(self, k):
        place = self.place
        c_send, c_recv = self.sems[4:6]
        got = self.buffers[2]
        for zi, ok in self.wave(k):
            for x in range(2):
                for y in range(2):
                    slot = 4 * zi + 2 * x + y
                    self.send(
                        self.own.at[zi, x, y, 1 - place.c],
                        got.at[zi, x, y],
                        c_send.at[slot],
                        c_recv.at[slot],
                        place.flip_c(),
                        ok,
                    )

    def over_second(self, k):
        place = self.place
        c_send, c_recv, b_send, b_recv = self.sems[4:8]
        got, next_ = self.buffers[2:4]
        for zi, ok in self.wave(k):

            def body(zi=zi):
                for j in (1, 0):
                    for i in (1, 0):
                        x, y = place.corner(i, j)
                        block = got.at[zi, x, y]
                        slot = 4 * zi + 2 * x + y
                        remote(
                            block, block, c_send.at[0], c_recv.at[slot], place.flip_c()
                        ).wait_recv()
                        add_into(block, self.own.at[zi, x, y, place.c], self.rows)
                        if j == 1:
                            remote(
                                block,
                                next_.at[zi, i],
                                b_send.at[2 * zi + i],
                                b_recv.at[2 * zi + i],
                                place.second(),
                            ).start()

            guard(ok, body)
            for i in (1, 0):
                x, y = place.corner(i, 1)
                copy = remote(
                    got.at[zi, x, y],
                    next_.at[zi, i],
                    b_send.at[2 * zi + i],
                    b_recv.at[2 * zi + i],
                    place.second(),
                )
                self.sent.append((copy, ok))

    def over_first(self, k):
        place = self.place
        a_send, a_recv = self.sems[0:2]
        got = self.buffers[0]
        for zi, ok in self.wave(k):
            if self.wide:
                b_send, b_recv = self.sems[6:8]
                before, held = self.buffers[2:4]

                def body(zi=zi):
                    for i in (1, 0):
                        block = held.at[zi, i]
                        x, y = place.corner(i, 0)
                        remote(
                            block, block, b_send.at[0], b_recv.at[2 * zi + i], place.second()
                        ).wait_recv()
                        add_into(block, before.at[zi, x, y], self.rows)
                        if i == 1:
                            remote(
                                block, got.at[zi], a_send.at[zi], a_recv.at[zi], place.first()
                            ).start()

                guard(ok, body)
                copy = remote(
                    held.at[zi, 1], got.at[zi], a_send.at[zi], a_recv.at[zi], place.first()
                )
                self.sent.append((copy, ok))
            else:
                self.send(
                    self.own.at[zi, 1 - place.x],
                    got.at[zi],
                    a_send.at[zi],
                    a_recv.at[zi],
                    place.flip_x(),
                    ok,
                )

    def cross_copy(self, zi):
        place = self.place
        return remote(
            self.own.at[zi, 1 - place.x],
            self.buffers[0].at[zi],
            self.sems[0].at[zi],
            self.sems[1].at[zi],
            place.flip_x(),
        )

    def cross(self, zi):
        self.cross_copy(zi).start()

    def crossed(self):
        for zi in range(self.place.depth):
            self.sent.append((self.cross_copy(zi), None))

    def along(self, k):
        place, depth = self.place, self.place.depth
        a_send, a_recv, z_send, z_recv = self.sems[0:4]
        held, line = self.buffers[0:2]
        for side, (zi, ok) in enumerate(self.wave(k)):
            block = held.at[zi]

            def body(zi=zi, side=side, block=block):
                remote(block, block, a_send.at[0], a_recv.at[zi], place.first()).wait_recv()
                if self.wide:
                    add_into(block, self.buffers[3].at[zi, 0], self.rows)
                else:
                    add_into(block, self.near_block(zi), self.rows)

                def more(direction):
                    slot = direction * depth + zi
                    term = line.at[depth if k == 0 and direction == 1 else zi]
                    remote(term, term, z_send.at[0], z_recv.at[slot], place.z_up()).wait_recv()
                    add_into(block, term, self.rows)

                def pass_on(direction, to):
                    slot = direction * depth + zi
                    there = line.at[depth if k == 1 and direction == 1 else zi]
                    remote(block, there, z_send.at[slot], z_recv.at[slot], to).start()

                if k == 0:
                    if not self.causal:
                        pl.when(place.down)(functools.partial(more, 0))
                    pl.when(place.up)(functools.partial(more, 1))
                elif side == 0:
                    pl.when(place.up)(functools.partial(more, 1))
                    pass_on(1, place.z_down())
                else:
                    pl.when(place.down)(functools.partial(more, 0))
                    pass_on(0, place.z_up())

            guard(ok, body)
            if k > 0:
                direction = 1 - side
                slot = direction * depth + zi
                to = place.z_up() if side == 1 else place.z_down()
                there = line.at[depth if k == 1 and direction == 1 else zi]
                copy = remote(block, there, z_send.at[slot], z_recv.at[slot], to)
                self.sent.append((copy, ok))

    def finish(self):
        self.out[...] = self.buffers[0][self.place.z].astype(self.out.dtype)

    def settle(self):
        for copy, condition in self.sent:
            guard(condition, copy.wait_send)


def drive_reduces(place, reduces):
    depth = place.depth
    order = list(range(depth - 1, -1, -1))
    for reduce in reduces:
        for k in order:
            reduce.cores(k) if reduce.wide else reduce.over_first(k)
    for step in range(depth + 2):
        for reduce in reduces:
            if not reduce.wide:
                if step < depth:
                    reduce.along(order[step])
                continue
            if step < depth:
                reduce.over_second(order[step])
            if 0 <= step - 1 < depth:
                reduce.over_first(order[step - 1])
            if 0 <= step - 2 < depth:
                reduce.along(order[step - 2])
    for reduce in reduces:
        reduce.finish()
    for reduce in reduces:
        reduce.settle()


def call_reduces(depth, collective_id, wides, owns):
    count = len(owns)
    blocks = [own.shape[-2:] for own in owns]
    parts = [Reduce.scratch(depth, wide, block) for wide, block in zip(wides, blocks)]
    scratch = []
    for buffers, sems in parts:
        scratch += buffers + sems

    def kernel(*refs):
        place = Place(depth)
        greet(place)
        reduces, used = [], 2 * count
        for number, (buffers, sems) in enumerate(parts):
            middle, end = used + len(buffers), used + len(buffers) + len(sems)
            reduces.append(
                Reduce(
                    place,
                    wides[number],
                    blocks[number][0],
                    refs[number],
                    refs[count + number],
                    refs[used:middle],
                    refs[middle:end],
                )
            )
            used = end
        drive_reduces(place, reduces)

    return pl.pallas_call(
        kernel,
        out_shape=[jax.ShapeDtypeStruct(block, F32) for block in blocks],
        in_specs=[pl.BlockSpec(memory_space=pltpu.VMEM)] * count,
        out_specs=[pl.BlockSpec(memory_space=pltpu.VMEM)] * count,
        scratch_shapes=scratch,
        compiler_params=pltpu.CompilerParams(
            collective_id=collective_id, has_side_effects=True, vmem_limit_bytes=VMEM_LIMIT
        ),
    )(*owns)


def end_kernel(depth, shapes, *refs):
    pack, wide, down, pack_out, wide_out, down_out = refs[:6]
    block, wide_block, down_block = shapes
    buffers, sems = Reduce.scratch(depth, True, block)
    used = 6 + len(buffers)
    place = Place(depth)
    count = 2 * depth
    partners = []
    for offset in range(1, count):
        partners.append((lax.rem(place.s + offset, count), place.f))
    greet(place, partners)
    reduce = Reduce(
        place, True, block[0], pack, pack_out, refs[6:used], refs[used : used + len(sems)]
    )
    used += len(sems)
    w_core, w_y, d_core, d_y = refs[used : used + 4]
    wc_send, wc_recv, wy_send, wy_recv, e_send, e_recv, e_sem = refs[used + 4 : used + 11]
    dc_send, dc_recv, dy_send, dy_recv = refs[used + 11 :]
    sent = []
    wide_rows, down_rows = wide_block[1], down_block[0]

    def send(src, dst, send_sem, recv_sem, device):
        copy = remote(src, dst, send_sem, recv_sem, device)
        copy.start()
        sent.append(copy)

    def landed(ref, recv_sem):
        remote(ref, ref, e_send.at[0], recv_sem, place.flip_c()).wait_recv()

    mine_y, other_y = place.y, 1 - place.y
    offsets = list(range(1, count)) + [0]
    for y in range(2):
        side = other_y if y == 0 else mine_y
        send(
            down.at[2 * side + 1 - place.c],
            d_core.at[side],
            dc_send.at[side],
            dc_recv.at[side],
            place.flip_c(),
        )
    for offset in offsets:
        to = lax.rem(place.s + offset, count)
        for y in range(2):
            send(
                wide.at[:, to, 2 * y + 1 - place.c],
                w_core.at[y, offset],
                wc_send.at[2 * offset + y],
                wc_recv.at[2 * offset + y],
                place.flip_c(),
            )
    order = list(range(depth - 1, -1, -1))
    for k in order:
        reduce.cores(k)

    def wide_add(target, term):
        for part in range(2):
            add_into(target.at[part], term.at[part], wide_rows)

    def wide_cores(offset):
        to = lax.rem(place.s + offset, count)
        for side in (other_y, mine_y):
            landed(w_core.at[side, offset], wc_recv.at[2 * offset + side])
            wide_add(w_core.at[side, offset], wide.at[:, to, 2 * side + place.c])
            if side is other_y:
                send(
                    w_core.at[side, offset],
                    w_y.at[offset],
                    wy_send.at[offset],
                    wy_recv.at[offset],
                    place.flip_y(),
                )

    def wide_across(offset):
        landed(w_y.at[offset], wy_recv.at[offset])
        wide_add(w_y.at[offset], w_core.at[mine_y, offset])
        to = lax.rem(place.s + offset, count)
        if offset > 0:
            send(
                w_y.at[offset],
                wide_out.at[place.s],
                e_send.at[offset],
                e_recv.at[offset],
                (to, place.f),
            )
        else:
            pltpu.make_async_copy(w_y.at[0], wide_out.at[place.s], e_sem.at[0]).start()

    for offset in offsets[: count // 2]:
        wide_cores(offset)
    for step in range(depth):
        reduce.over_second(order[step])
        if step >= 1:
            reduce.over_first(order[step - 1])
        if step == 0:
            for offset in offsets[count // 2 :]:
                wide_cores(offset)
            for side in (other_y, mine_y):
                landed(d_core.at[side], dc_recv.at[side])
                add_into(d_core.at[side], down.at[2 * side + place.c], down_rows)
                if side is other_y:
                    send(d_core.at[side], d_y.at[0], dy_send.at[0], dy_recv.at[0], place.flip_y())
        for offset in offsets[step * count // depth : (step + 1) * count // depth]:
            wide_across(offset)
        if step >= 2:
            reduce.along(order[step - 2])
    reduce.over_first(order[depth - 1])
    for step in range(max(depth - 2, 0), depth):
        reduce.along(order[step])
    reduce.finish()
    landed(d_y.at[0], dy_recv.at[0])
    down_out[...] = d_y[0].astype(F32) + d_core[mine_y].astype(F32)
    for offset in range(1, count):
        origin = lax.rem(place.s + count - offset, count)
        landed(wide_out.at[origin], e_recv.at[offset])
    pltpu.make_async_copy(w_y.at[0], wide_out.at[place.s], e_sem.at[0]).wait()
    reduce.settle()
    for copy in sent:
        copy.wait_send()


def call_end(depth, collective_id, pack, wide, down):
    count = 2 * depth
    block = pack.shape[-2:]
    wide_block = (2,) + wide.shape[-2:]
    down_block = down.shape[-2:]
    buffers, sems = Reduce.scratch(depth, True, block)
    scratch = buffers + sems
    scratch += [
        pltpu.VMEM((2, count) + wide_block, BF16),
        pltpu.VMEM((count,) + wide_block, BF16),
        pltpu.VMEM((2,) + down_block, BF16),
        pltpu.VMEM((1,) + down_block, BF16),
    ]
    scratch += [DMA((2 * count,)), DMA((2 * count,)), DMA((count,)), DMA((count,))]
    scratch += [DMA((count,)), DMA((count,)), DMA((1,))]
    scratch += [DMA((2,)), DMA((2,)), DMA((1,)), DMA((1,))]
    vmem = pl.BlockSpec(memory_space=pltpu.VMEM)
    return pl.pallas_call(
        functools.partial(end_kernel, depth, (block, wide_block, down_block)),
        out_shape=[
            jax.ShapeDtypeStruct(block, F32),
            jax.ShapeDtypeStruct((count,) + wide_block, BF16),
            jax.ShapeDtypeStruct(down_block, F32),
        ],
        in_specs=[vmem] * 3,
        out_specs=[vmem, vmem, vmem],
        scratch_shapes=scratch,
        compiler_params=pltpu.CompilerParams(
            collective_id=collective_id, has_side_effects=True, vmem_limit_bytes=VMEM_LIMIT
        ),
    )(pack, wide, down)


def forward_kernel(span, info, begin, query, key, value, mixed, lse, m_acc, l_acc, o_acc):
    rows = begin.shape[0]
    first_row, low, high = info[0], info[1], info[2]
    scale = HEAD_DIM ** (-0.5) * LOG2E
    m_acc[...] = jnp.full_like(m_acc, -1e30)
    l_acc[...] = jnp.zeros_like(l_acc)
    o_acc[...] = jnp.zeros_like(o_acc)
    places = first_row + lax.broadcasted_iota(jnp.int32, (rows, span), 0)
    offsets = lax.broadcasted_iota(jnp.int32, (rows, span), 1)

    def step(number, carry):
        base = pl.multiple_of(number * span, span)
        keys_at = base + offsets
        visible = jnp.logical_and(keys_at >= begin[...], keys_at <= places)
        for g in range(KV_HEADS):
            lanes = slice(g * HEAD_DIM, (g + 1) * HEAD_DIM)
            scores = lax.dot_general(
                query[g],
                key[pl.ds(base, span), lanes],
                (((1,), (1,)), ((), ())),
                preferred_element_type=F32,
            )
            scores = scores.reshape(GROUP, rows, span) * scale
            scores = jnp.where(visible[None], scores, -1e30).reshape(GROUP * rows, span)
            old = m_acc[g]
            new = jnp.maximum(old, jnp.max(scores, axis=-1, keepdims=True))
            weights = jnp.exp2(scores - new[:, :1])
            weights = jnp.where(
                visible[None], weights.reshape(GROUP, rows, span), 0.0
            ).reshape(GROUP * rows, span)
            fade = jnp.exp2(old - new)
            l_acc[g] = l_acc[g] * fade + jnp.sum(weights, axis=-1, keepdims=True)
            o_acc[g] = o_acc[g] * fade + jnp.dot(
                weights.astype(BF16),
                value[pl.ds(base, span), lanes],
                preferred_element_type=F32,
            )
            m_acc[g] = new
        return carry

    lax.fori_loop(low, high, step, 0)
    for g in range(KV_HEADS):
        mixed[g] = o_acc[g] / l_acc[g]
        lse[g] = m_acc[g] + jnp.log2(l_acc[g])


def call_forward(span, info, begin, query, key, value):
    stacked = query.shape[1]
    vmem = pl.BlockSpec(memory_space=pltpu.VMEM)
    return pl.pallas_call(
        functools.partial(forward_kernel, span),
        out_shape=[
            jax.ShapeDtypeStruct((KV_HEADS, stacked, HEAD_DIM), F32),
            jax.ShapeDtypeStruct((KV_HEADS, stacked, HEAD_DIM), F32),
        ],
        in_specs=[pl.BlockSpec(memory_space=pltpu.SMEM)] + [vmem] * 4,
        out_specs=[vmem, vmem],
        scratch_shapes=[pltpu.VMEM((KV_HEADS, stacked, HEAD_DIM), F32)] * 3,
        compiler_params=pltpu.CompilerParams(vmem_limit_bytes=VMEM_LIMIT),
    )(info, begin, query, key, value)


def backward_kernel(
    span, info, begin, query, key, value, mixed, lse, grad, dquery, dkeys, delta
):
    rows = begin.shape[0]
    first_row, low, high = info[0], info[1], info[2]
    scale = HEAD_DIM ** (-0.5) * LOG2E
    dquery[...] = jnp.zeros_like(dquery)
    width = KV_HEADS * HEAD_DIM
    for g in range(KV_HEADS):
        delta[g] = jnp.broadcast_to(
            jnp.sum(grad[g].astype(F32) * mixed[g], axis=-1, keepdims=True), delta.shape[1:]
        )
    places = first_row + lax.broadcasted_iota(jnp.int32, (rows, span), 0)
    offsets = lax.broadcasted_iota(jnp.int32, (rows, span), 1)

    def clear(number, carry):
        base = pl.multiple_of(number * span, span)
        dkeys[pl.ds(base, span), :] = jnp.zeros((span, dkeys.shape[1]), BF16)
        return carry

    lax.fori_loop(0, low, clear, 0)
    lax.fori_loop(high, dkeys.shape[0] // span, clear, 0)

    def step(number, carry):
        base = pl.multiple_of(number * span, span)
        keys_at = base + offsets
        visible = jnp.logical_and(keys_at >= begin[...], keys_at <= places)
        for g in range(KV_HEADS):
            lanes = slice(g * HEAD_DIM, (g + 1) * HEAD_DIM)
            key_rows = key[pl.ds(base, span), lanes]
            value_rows = value[pl.ds(base, span), lanes]
            scores = lax.dot_general(
                query[g], key_rows, (((1,), (1,)), ((), ())), preferred_element_type=F32
            )
            dprobs = lax.dot_general(
                grad[g], value_rows, (((1,), (1,)), ((), ())), preferred_element_type=F32
            )
            probs = jnp.exp2(scores * scale - lse[g][:, :1])
            probs = jnp.where(
                visible[None], probs.reshape(GROUP, rows, span), 0.0
            ).reshape(GROUP * rows, span)
            dscores = (probs * (dprobs - delta[g][:, :1])).astype(BF16)
            dquery[g] += jnp.dot(dscores, key_rows, preferred_element_type=F32)
            dkeys[pl.ds(base, span), lanes] = lax.dot_general(
                dscores, query[g], (((0,), (0,)), ((), ())), preferred_element_type=F32
            ).astype(BF16)
            dkeys[
                pl.ds(base, span), width + g * HEAD_DIM : width + (g + 1) * HEAD_DIM
            ] = lax.dot_general(
                probs.astype(BF16),
                grad[g],
                (((0,), (0,)), ((), ())),
                preferred_element_type=F32,
            ).astype(BF16)
        return carry

    lax.fori_loop(low, high, step, 0)


def call_backward(span, info, begin, query, key, value, mixed, lse, grad):
    stacked = query.shape[1]
    vmem = pl.BlockSpec(memory_space=pltpu.VMEM)
    return pl.pallas_call(
        functools.partial(backward_kernel, span),
        out_shape=[
            jax.ShapeDtypeStruct((KV_HEADS, stacked, HEAD_DIM), F32),
            jax.ShapeDtypeStruct((key.shape[0], 2 * key.shape[1]), BF16),
        ],
        in_specs=[pl.BlockSpec(memory_space=pltpu.SMEM)] + [vmem] * 7,
        out_specs=[vmem, vmem],
        scratch_shapes=[pltpu.VMEM((KV_HEADS, stacked, HEAD_DIM), F32)],
        compiler_params=pltpu.CompilerParams(vmem_limit_bytes=VMEM_LIMIT),
    )(info, begin, query, key, value, mixed, lse, grad)


class PairGather:
    def __init__(self, place, own, out, sems, crossing):
        self.place, self.own, self.out, self.sems = place, own, out, sems
        self.crossing = crossing
        self.parts = [place.x, 1 - place.x] if crossing else [None]
        self.sent = []

    @staticmethod
    def semaphores(depth):
        sizes = (1, 1, 1, 4 * depth, 2 * depth, 2 * depth, 2 * depth, 4 * depth, 4 * depth)
        return [DMA((size,)) for size in sizes]

    def send(self, src, dst, send_sem, recv_sem, device, condition=None):
        copy = remote(src, dst, send_sem, recv_sem, device)
        guard(condition, copy.start)
        self.sent.append((copy, condition))

    def block(self, zi, y, c, part):
        if part is None:
            return self.out.at[zi, :, y, c]
        return self.out.at[zi, part, y, c]

    def slot(self, zi, part):
        return 2 * zi if part is None else 2 * zi + part

    def landed(self, ref, recv_sem, condition=None):
        guard(condition, remote(ref, ref, self.sems[3].at[0], recv_sem, self.place.flip_c()).wait_recv)

    def local(self):
        place = self.place
        source = self.own.at[place.x] if self.crossing else self.own
        return pltpu.make_async_copy(
            source, self.block(place.z, place.y, place.c, self.parts[0]), self.sems[0].at[0]
        )

    def begin(self):
        place = self.place
        self.send(
            self.own.at[1 - place.x],
            self.out.at[place.z, place.x, place.y, place.c],
            self.sems[1].at[0],
            self.sems[2].at[0],
            place.flip_x(),
        )
        self.spread(0, 0, place.z, None, place.x, self.own.at[place.x])

    def spread(self, k, side, zi, ok, part, source):
        place, depth = self.place, self.place.depth
        z_send, z_recv, y_send, y_recv, c_send, c_recv = self.sems[3:9]
        block, slot = self.block(zi, place.y, place.c, part), self.slot(zi, part)
        if k == 0 or side == 0:
            self.send(
                source,
                block,
                z_send.at[self.slot(k, part)],
                z_recv.at[slot],
                place.z_up(),
                both(place.up, ok),
            )
        if k == 0 or side == 1:
            self.send(
                source,
                block,
                z_send.at[2 * depth + self.slot(k, part)],
                z_recv.at[slot],
                place.z_down(),
                both(place.down, ok),
            )
        self.send(source, block, y_send.at[slot], y_recv.at[slot], place.flip_y(), ok)
        self.send(source, block, c_send.at[slot], c_recv.at[slot], place.flip_c(), ok)

    def arrive(self, k):
        place = self.place
        z_recv = self.sems[4]
        for side, (zi, ok) in enumerate(place.wave(k)):
            for number, part in enumerate(self.parts):
                block = self.block(zi, place.y, place.c, part)
                source = block
                if k > 0:
                    self.landed(block, z_recv.at[self.slot(zi, part)], ok)
                elif not self.crossing:
                    source = self.own
                elif number == 0:
                    continue
                else:
                    self.landed(block, self.sems[2].at[0])
                self.spread(k, side, zi, ok, part, source)

    def across(self, k):
        place, depth = self.place, self.place.depth
        y_recv, c_send, c_recv = self.sems[6:9]
        for zi, ok in place.wave(k):
            for part in self.parts:
                block = self.block(zi, 1 - place.y, place.c, part)
                self.landed(block, y_recv.at[self.slot(zi, part)], ok)
                slot = 2 * depth + self.slot(zi, part)
                self.send(block, block, c_send.at[slot], c_recv.at[slot], place.flip_c(), ok)

    def take(self, k):
        place, depth = self.place, self.place.depth
        c_recv = self.sems[8]
        for zi, ok in place.wave(k):
            for part in self.parts:
                slot = self.slot(zi, part)
                self.landed(self.block(zi, place.y, 1 - place.c, part), c_recv.at[slot], ok)
                slot = 2 * depth + slot
                self.landed(self.block(zi, 1 - place.y, 1 - place.c, part), c_recv.at[slot], ok)

    def settle(self):
        for copy, condition in self.sent:
            guard(condition, copy.wait_send)


class PairReduce:
    def __init__(self, place, own, out, buffers, sems, causal=False, crossing=False):
        self.place, self.own, self.out, self.sems = place, own, out, sems
        self.from_core, self.from_y, self.line, self.from_x = buffers
        self.causal, self.crossing = causal, crossing
        self.sent = []

    @staticmethod
    def scratch(depth, block):
        buffers = [
            pltpu.VMEM((depth, 2, 2) + block, BF16),
            pltpu.VMEM((depth, 2) + block, BF16),
            pltpu.VMEM((depth + 1, 2) + block, BF16),
            pltpu.VMEM((1,) + block, BF16),
        ]
        sems = [DMA((2 * depth,)), DMA((2 * depth,)), DMA((depth,)), DMA((depth,))]
        sems += [DMA((2 * depth,)), DMA((2 * depth,)), DMA((1,)), DMA((1,))]
        return buffers, sems

    def wave(self, k):
        waves = self.place.wave(k)
        return waves[:1] if self.causal else waves

    def send(self, src, dst, send_sem, recv_sem, device, condition=None):
        copy = remote(src, dst, send_sem, recv_sem, device)
        guard(condition, copy.start)
        self.sent.append((copy, condition))

    def landed(self, ref, recv_sem):
        remote(ref, ref, self.sems[0].at[0], recv_sem, self.place.flip_c()).wait_recv()

    def add(self, target, term):
        for x in range(2):
            add_into(target.at[x], term.at[x], target.shape[1])

    def cores(self, k):
        place = self.place
        for zi, ok in self.wave(k):
            for y in range(2):
                slot = 2 * zi + y
                self.send(
                    self.own.at[zi, :, y, 1 - place.c],
                    self.from_core.at[zi, y],
                    self.sems[0].at[slot],
                    self.sems[1].at[slot],
                    place.flip_c(),
                    ok,
                )

    def over(self, k):
        place = self.place
        for zi, ok in self.wave(k):

            def body(zi=zi):
                for y in (1 - place.y, place.y):
                    block = self.from_core.at[zi, y]
                    self.landed(block, self.sems[1].at[2 * zi + y])
                    self.add(block, self.own.at[zi, :, y, place.c])
                    if y is not place.y:
                        self.y_copy(zi).start()

            guard(ok, body)
            self.sent.append((self.y_copy(zi), ok))

    def y_copy(self, zi):
        place = self.place
        return remote(
            self.from_core.at[zi, 1 - place.y],
            self.from_y.at[zi],
            self.sems[2].at[zi],
            self.sems[3].at[zi],
            place.flip_y(),
        )

    def z_copy(self, k, side, zi):
        depth = self.place.depth
        direction = 1 - side
        slot = direction * depth + zi
        there = self.line.at[depth if k == 1 and direction == 1 else zi]
        to = self.place.z_up() if side == 1 else self.place.z_down()
        return remote(
            self.from_y.at[zi], there, self.sems[4].at[slot], self.sems[5].at[slot], to
        )

    def along(self, k):
        place, depth = self.place, self.place.depth
        for side, (zi, ok) in enumerate(self.wave(k)):
            block = self.from_y.at[zi]

            def body(zi=zi, side=side, block=block):
                self.landed(block, self.sems[3].at[zi])
                self.add(block, self.from_core.at[zi, place.y])

                def more(direction):
                    term = self.line.at[depth if k == 0 and direction == 1 else zi]
                    self.landed(term, self.sems[5].at[direction * depth + zi])
                    self.add(block, term)

                if k == 0:
                    if not self.causal:
                        pl.when(place.down)(functools.partial(more, 0))
                    pl.when(place.up)(functools.partial(more, 1))
                elif side == 0:
                    pl.when(place.up)(functools.partial(more, 1))
                else:
                    pl.when(place.down)(functools.partial(more, 0))
                if k > 0:
                    self.z_copy(k, side, zi).start()

            guard(ok, body)
            if k > 0:
                self.sent.append((self.z_copy(k, side, zi), ok))

    def swap(self):
        place = self.place
        self.send(
            self.from_y.at[place.z, 1 - place.x],
            self.from_x.at[0],
            self.sems[6].at[0],
            self.sems[7].at[0],
            place.flip_x(),
        )

    def finish(self):
        place = self.place
        if self.crossing:
            self.landed(self.from_x.at[0], self.sems[7].at[0])
            self.out[place.x] = self.from_y[place.z, place.x].astype(self.out.dtype)
            self.out[1 - place.x] = self.from_x[0].astype(self.out.dtype)
        else:
            self.out[...] = self.from_y[place.z].astype(self.out.dtype)

    def settle(self):
        for copy, condition in self.sent:
            guard(condition, copy.wait_send)


class Exchange:
    def __init__(self, place, own, out, sems):
        self.place, self.own, self.out, self.sems = place, own, out, sems
        self.count = 2 * place.depth
        self.sent = []
        self.y_f = place.f + 2 - 4 * place.y
        self.c_f = place.f + 1 - 2 * place.c
        self.yc_f = self.y_f + 1 - 2 * place.c

    @staticmethod
    def semaphores(depth):
        count = 2 * depth
        return [
            DMA((1,)),
            DMA((count,)),
            DMA((count,)),
            DMA((count,)),
            DMA((count,)),
            DMA((2 * count,)),
            DMA((2 * count,)),
        ]

    def send(self, block, send_sem, recv_sem, device, source=None):
        copy = remote(block if source is None else source, block, send_sem, recv_sem, device)
        copy.start()
        self.sent.append(copy)

    def block(self, offset, owner):
        origin = lax.rem(self.place.s + self.count - offset, self.count)
        return self.out.at[:, origin, owner]

    def landed(self, block, recv_sem):
        remote(block, block, self.sems[1].at[0], recv_sem, self.place.flip_c()).wait_recv()

    def local(self):
        return pltpu.make_async_copy(
            self.own.at[:, self.place.s], self.block(0, self.place.f), self.sems[0].at[0]
        )

    def depart(self, offset):
        place = self.place
        to = lax.rem(place.s + offset, self.count)
        self.send(
            self.block(0, place.f),
            self.sems[1].at[offset],
            self.sems[2].at[offset],
            (to, place.f),
            self.own.at[:, to],
        )

    def onward(self, offset):
        place = self.place
        block = self.block(offset, place.f)
        if offset > 0:
            self.landed(block, self.sems[2].at[offset])
        self.send(block, self.sems[3].at[offset], self.sems[4].at[offset], place.flip_y())
        slot = 2 * offset
        self.send(block, self.sems[5].at[slot], self.sems[6].at[slot], place.flip_c())

    def sideways(self, offset):
        block = self.block(offset, self.y_f)
        self.landed(block, self.sems[4].at[offset])
        slot = 2 * offset + 1
        self.send(block, self.sems[5].at[slot], self.sems[6].at[slot], self.place.flip_c())

    def last(self, offset):
        self.landed(self.block(offset, self.c_f), self.sems[6].at[2 * offset])
        self.landed(self.block(offset, self.yc_f), self.sems[6].at[2 * offset + 1])

    def settle(self):
        for copy in self.sent:
            copy.wait_send()


class Quarter:
    def __init__(self, place, own, out, sems):
        self.place, self.own, self.out, self.sems = place, own, out, sems
        self.sent = []

    @staticmethod
    def semaphores():
        return [DMA((1,)), DMA((3,)), DMA((3,))]

    def local(self):
        return pltpu.make_async_copy(self.own, self.out.at[self.place.f], self.sems[0].at[0])

    def send(self, source, block, slot, device):
        copy = remote(source, block, self.sems[1].at[slot], self.sems[2].at[slot], device)
        copy.start()
        self.sent.append(copy)

    def depart(self):
        place = self.place
        self.send(self.own, self.out.at[place.f], 0, place.flip_y())
        self.send(self.own, self.out.at[place.f], 1, place.flip_c())

    def landed(self, owner, slot):
        block = self.out.at[owner]
        remote(block, block, self.sems[1].at[0], self.sems[2].at[slot], self.place.flip_c()).wait_recv()

    def sideways(self):
        place = self.place
        y_f = place.f + 2 - 4 * place.y
        self.landed(y_f, 0)
        self.send(self.out.at[y_f], self.out.at[y_f], 2, place.flip_c())

    def last(self):
        place = self.place
        self.landed(place.f + 1 - 2 * place.c, 1)
        self.landed(place.f + 2 - 4 * place.y + 1 - 2 * place.c, 2)

    def settle(self):
        for copy in self.sent:
            copy.wait_send()


def stage(gather, step):
    depth = gather.place.depth
    if step < depth:
        gather.arrive(step)
    if 0 <= step - 1 < depth:
        gather.across(step - 1)
    if isinstance(gather, PairGather):
        if 0 <= step - 2 < depth:
            gather.take(step - 2)
        return
    if gather.wide and 0 <= step - 2 < depth:
        gather.hand(step - 2)
    if gather.wide and 0 <= step - 3 < depth:
        gather.take(step - 3)


def turned(vector, cosine, sine):
    return vector * cosine + pltpu.roll(vector, HEAD_DIM // 2, 1) * sine


HEAD_PLAN = (
    ("tables", "P0", "wide", "P1", "P2", "d1", "d5", "P3", "o0", "d7", "P4", "P5", "project", "K0", "o1", "c0", "n7"),
    ("K1", "K2", "d2", "K3", "K4", "o2", "d6", "c1", "K5", "n0", "A0", "d4", "A1", "o3", "A2"),
    ("o4", "s0", "n6", "A3", "s7", "o5", "mix", "n1", "n5", "d3", "o6", "D", "after", "h0", "keep", "h1"),
    ("c2", "s1", "n4", "n3", "s6", "s5", "h2", "n2", "c3", "S", "s3", "s4", "s2", "h3", "h4", "c4"),
)
HEAD_INS = 12
HEAD_OUTS = 16


def head_kernel(depth, *refs):
    (o_own, q_own, k_own, v_own, small_own, gate_own, up_own, down_own) = refs[:8]
    (tokens, cot, frequency, lengths) = refs[8:HEAD_INS]
    (
        pack_out,
        o_out,
        kv_out,
        cot_out,
        wide_out,
        down_out,
        hidden_out,
        queries_out,
        mixed_out,
        lse_out,
        middle_out,
        hidden_pair_out,
        mixed_low_out,
        pair_out,
        angles_out,
        begin,
    ) = refs[HEAD_INS : HEAD_INS + HEAD_OUTS]
    vectors = refs[HEAD_INS + HEAD_OUTS]
    rest = refs[HEAD_INS + HEAD_OUTS + 1 :]
    pack_all, o_all, kv_all, kv_own, hidden_two, lin, m_acc, l_acc, o_acc = rest[:9]
    pack, wide, down, mixed_pair, mixed_far, spread = rest[9:15]
    queries, mixed, lse, middle, hidden_pair, mixed_low, pair, angles = rest[15:23]
    sems = list(rest[23:])

    def take(count):
        taken = sems[:count]
        del sems[:count]
        return taken

    wide_need = len(Gather.semaphores(depth, True))
    line_need = len(Gather.semaphores(depth, False))
    count = 2 * depth
    devices = 4 * count
    rows, model = tokens.shape
    key_width = KV_HEADS * HEAD_DIM
    group_width = GROUP * HEAD_DIM
    qkv_width = group_width + 2 * HEAD_DIM

    place = Place(depth)
    for g in range(KV_HEADS):
        at = 0
        for source in (q_own, k_own, v_own):
            width = source.shape[1] // KV_HEADS
            pack[g, :, at : at + width] = source[:, g * width : (g + 1) * width]
            at += width
        pack[g, :, at:] = small_own[...]
    greet(place, [(lax.rem(place.s + offset, count), place.f) for offset in range(1, count)])
    pair_need = len(PairGather.semaphores(depth))
    g_pack = PairGather(place, pack, pack_all, take(pair_need), True)
    g_o = Gather(place, True, o_own, o_all, take(wide_need))
    g_kv = PairGather(place, kv_own, kv_all, take(pair_need), False)
    g_cot = Gather(place, False, cot, cot_out, take(line_need + 2), True)
    g_hidden = Gather(place, False, hidden_two, hidden_out, take(line_need))
    x_wide = Exchange(place, wide, wide_out, take(len(Exchange.semaphores(depth))))
    x_down = Quarter(place, down, down_out, take(len(Quarter.semaphores())))
    out_sem, x_send, x_recv = take(3)

    g_pack.begin()
    token_copy = remote(
        tokens, pair.at[place.x], x_send.at[0], x_recv.at[0], place.flip_x()
    )
    token_copy.start()
    pair[place.x] = tokens[...]
    pack_local = g_pack.local()
    pack_local.start()
    pack_local.wait()
    few = down_own.shape[0]
    filled = down.shape[0]
    locals_ = [job.local() for job in (g_o, g_cot, x_wide, x_down)]
    for copy in locals_[:2]:
        copy.start()
    inputs = tokens[...].astype(F32)

    def pack_wide():
        for side, source in enumerate((gate_own, up_own)):
            for to in range(count):
                parts = []
                for owner in range(4):
                    low = (4 * to + owner) * few
                    parts.append(source[:, low : low + few])
                    parts.append(jnp.zeros((wide.shape[2], filled - few), BF16))
                wide[side, to] = jnp.concatenate(parts, axis=1)
        locals_[2].start()

    def tables():
        down[...] = jnp.concatenate(
            [down_own[...], jnp.zeros((filled - few, model), BF16)], axis=0
        )
        locals_[3].start()
        ahead = lax.broadcasted_iota(jnp.int32, (1, HEAD_DIM), 1) < HEAD_DIM // 2
        for x in range(2):
            first_row = ((2 * place.z + x) * 4 + place.f) * rows
            positions = first_row + lax.broadcasted_iota(jnp.int32, (rows, 1), 0)
            start, found = jnp.int32(0), jnp.zeros((rows, 1), jnp.int32)
            for number in range(lengths.shape[0]):
                found = jnp.where(positions >= start, start, found)
                start = start + lengths[number]
            begin[x] = found
            turns = (positions - found).astype(F32) * frequency[...]
            angles[x, 0] = jnp.cos(turns)
            sine = jnp.sin(turns)
            angles[x, 1] = jnp.where(ahead, -sine, sine)

    part = model // depth
    own_head = pl.ds(pl.multiple_of(place.x * HEAD_DIM, HEAD_DIM), HEAD_DIM)
    own_heads = pl.ds(pl.multiple_of(place.x * group_width, group_width), group_width)
    kv_local = g_kv.local()
    hidden_local = g_hidden.local()
    mixed_copy = remote(
        mixed_pair.at[1 - place.x], mixed_far, x_send.at[1], x_recv.at[1], place.flip_x()
    )

    def project():
        share = key_width // devices
        chosen = lax.broadcasted_iota(jnp.int32, (model, key_width), 1)
        chosen = lax.div(chosen, share) * (model // devices) + lax.rem(chosen, share)
        chosen = lax.broadcasted_iota(jnp.int32, (model, key_width), 0) == chosen
        small = pack_all[:, :, :, :, :, qkv_width:].reshape(model, 128).astype(F32).T
        vectors[...] = small[:8]
        spread[...] = jnp.dot(
            small[:8].astype(BF16), chosen.astype(BF16), preferred_element_type=F32
        )
        for copy in locals_:
            copy.wait()
        token_copy.wait_recv()
        pair_inputs = pair[...].reshape(2 * rows, model).astype(F32)
        inv_pair = lax.rsqrt(jnp.mean(pair_inputs * pair_inputs, axis=-1, keepdims=True) + EPSILON)
        hidden_pair[...] = (pair_inputs * inv_pair * small[0:1]).astype(BF16)
        for zi in range(depth):
            weights = pack_all[zi][:, :, :, :, :qkv_width].reshape(part, qkv_width)
            term = jnp.dot(
                hidden_pair[:, zi * part : (zi + 1) * part], weights, preferred_element_type=F32
            )
            if zi == 0:
                lin[...] = term
            else:
                lin[...] += term
        for x in range(2):
            at = slice(x * rows, (x + 1) * rows)
            head = lin[at, group_width : group_width + HEAD_DIM] + spread[2:3, own_head]
            kv_own[x, :, :HEAD_DIM] = turned(head, angles[x, 0], angles[x, 1]).astype(BF16)
            values = lin[at, group_width + HEAD_DIM :] + spread[3:4, own_head]
            kv_own[x, :, HEAD_DIM:] = values.astype(BF16)
        kv_local.start()

    def queries_of():
        query_bias = vectors[1:2, own_heads]
        for x in range(2):
            for j in range(GROUP):
                lanes = slice(j * HEAD_DIM, (j + 1) * HEAD_DIM)
                head = lin[x * rows : (x + 1) * rows, lanes] + query_bias[:, lanes]
                queries[x, j * rows : (j + 1) * rows, :] = turned(
                    head, angles[x, 0], angles[x, 1]
                ).astype(BF16)
        kv_local.wait()

    span = 4 * rows
    scale = HEAD_DIM ** (-0.5) * LOG2E
    m_acc[...] = jnp.full_like(m_acc, -1e30)
    l_acc[...] = jnp.zeros_like(l_acc)
    o_acc[...] = jnp.zeros_like(o_acc)
    local_rows = lax.broadcasted_iota(jnp.int32, (rows, span), 0)
    offsets = lax.broadcasted_iota(jnp.int32, (rows, span), 1)

    def attend(number, carry):
        keys_at = number * span + offsets
        block = kv_all.at[lax.div(number, 2), lax.rem(number, 2)]
        key = block[:, :, :, :HEAD_DIM].reshape(span, HEAD_DIM)
        value = block[:, :, :, HEAD_DIM:].reshape(span, HEAD_DIM)
        for x in range(2):
            places = ((2 * place.z + x) * 4 + place.f) * rows + local_rows
            visible = jnp.logical_and(keys_at >= begin[x], keys_at <= places)
            scores = mul_t(queries[x], key)
            scores = scores.reshape(GROUP, rows, span) * scale
            scores = jnp.where(visible[None], scores, -1e30).reshape(GROUP * rows, span)
            old = m_acc[x]
            new = jnp.maximum(old, jnp.max(scores, axis=-1, keepdims=True))
            weights = jnp.exp2(scores - new[:, :1])
            fade = jnp.exp2(old - new)
            l_acc[x] = l_acc[x] * fade + jnp.sum(weights, axis=-1, keepdims=True)
            o_acc[x] = o_acc[x] * fade + jnp.dot(
                weights.astype(BF16), value, preferred_element_type=F32
            )
            m_acc[x] = new
        return carry

    def attend_quarter(piece):
        low, high = piece * count // 4, (piece + 1) * count // 4
        reach = 2 * place.z + 2
        lax.fori_loop(jnp.minimum(low, reach), jnp.minimum(high, reach), attend, 0)

    def mix():
        for x in range(2):
            total = o_acc[x] / l_acc[x]
            mixed[x] = total
            lse[x] = m_acc[x] + jnp.log2(l_acc[x])
            mixed_pair[x] = total.astype(BF16)
        mixed_copy.start()

    def after_attention():
        mixed_copy.wait_recv()
        for j in range(GROUP):
            at = slice(j * rows, (j + 1) * rows)
            near = pl.multiple_of((place.x * GROUP + j) * HEAD_DIM, HEAD_DIM)
            far = pl.multiple_of(((1 - place.x) * GROUP + j) * HEAD_DIM, HEAD_DIM)
            mixed_low[:, pl.ds(near, HEAD_DIM)] = mixed_pair[place.x, at, :]
            mixed_low[:, pl.ds(far, HEAD_DIM)] = mixed_far[at, :]
        after = inputs
        for zi in range(depth):
            after = after + jnp.dot(
                mixed_low[:, zi * part : (zi + 1) * part],
                o_all[zi].reshape(part, model),
                preferred_element_type=F32,
            )
        middle[...] = after
        inv_two = lax.rsqrt(jnp.mean(after * after, axis=-1, keepdims=True) + EPSILON)
        hidden_two[...] = (after * inv_two * vectors[4:5]).astype(BF16)
        hidden_local.start()

    keeps = [
        pltpu.make_async_copy(source, target, out_sem.at[number])
        for number, (source, target) in enumerate(
            (
                (pack_all, pack_out),
                (o_all, o_out),
                (kv_all, kv_out),
                (queries, queries_out),
                (mixed, mixed_out),
                (lse, lse_out),
                (middle, middle_out),
                (hidden_pair, hidden_pair_out),
                (mixed_low, mixed_low_out),
                (pair, pair_out),
                (angles, angles_out),
            )
        )
    ]

    def keep():
        for copy in keeps:
            copy.start()

    jobs = {"P": g_pack, "K": g_kv, "o": g_o, "c": g_cot, "h": g_hidden}
    moves = {"d": x_wide.depart, "n": x_wide.onward, "s": x_wide.sideways, "A": attend_quarter}
    works = {
        "wide": pack_wide,
        "tables": tables,
        "project": project,
        "mix": mix,
        "after": after_attention,
        "keep": keep,
        "D": x_down.depart,
        "S": x_down.sideways,
    }
    for words in HEAD_PLAN:
        for word in words:
            if word in works:
                works[word]()
            elif word[0] in moves:
                moves[word[0]](int(word[1:]))
            else:
                stage(jobs[word[0]], int(word[1:]))
                if word == "K0":
                    queries_of()

    hidden_local.wait()
    for offset in range(count):
        x_wide.last(offset)
    x_down.last()
    for copy in keeps:
        copy.wait()
    token_copy.wait_send()
    mixed_copy.wait_send()
    for job in (g_pack, g_o, g_kv, g_cot, g_hidden, x_wide, x_down):
        job.settle()


def call_head(depth, collective_id, hbm, vmems, lengths):
    (o_own,) = hbm
    q_own, k_own, v_own, small_own, gate_own, _, down_own, tokens, cot = vmems[:9]
    count = 2 * depth
    few = down_own.shape[0]
    filled = -(-few // 16) * 16
    qkv_width = (GROUP + 2) * HEAD_DIM
    width = qkv_width + small_own.shape[1]
    pack = jax.ShapeDtypeStruct((q_own.shape[0], width), BF16)
    wide = jax.ShapeDtypeStruct((2, count, gate_own.shape[0], 4 * filled), BF16)
    down = jax.ShapeDtypeStruct((filled, down_own.shape[1]), BF16)
    rows, model = tokens.shape
    key_width = KV_HEADS * HEAD_DIM
    stacked = GROUP * rows
    kv_own = jax.ShapeDtypeStruct((rows, 2 * HEAD_DIM), BF16)
    any_, vmem = pl.BlockSpec(memory_space=pl.ANY), pl.BlockSpec(memory_space=pltpu.VMEM)
    heads = (KV_HEADS, stacked, HEAD_DIM)
    outs = [
        gather_shape(depth, True, pack),
        gather_shape(depth, True, o_own),
        gather_shape(depth, True, kv_own),
        gather_shape(depth, False, cot),
        jax.ShapeDtypeStruct((2, count, 4) + wide.shape[2:], BF16),
        jax.ShapeDtypeStruct((4,) + down.shape, BF16),
        gather_shape(depth, False, tokens),
        jax.ShapeDtypeStruct(heads, BF16),
        jax.ShapeDtypeStruct(heads, F32),
        jax.ShapeDtypeStruct(heads, F32),
        jax.ShapeDtypeStruct((rows, model), F32),
        jax.ShapeDtypeStruct((2 * rows, model), BF16),
        jax.ShapeDtypeStruct((rows, model), BF16),
        jax.ShapeDtypeStruct((2, rows, model), BF16),
        jax.ShapeDtypeStruct((2, 2, rows, HEAD_DIM), F32),
        jax.ShapeDtypeStruct((2, rows, 1), jnp.int32),
        jax.ShapeDtypeStruct((8, model), F32),
    ]
    scratch = [pltpu.VMEM(out.shape, BF16) for out in outs[:3]]
    scratch += [
        pltpu.VMEM((2,) + kv_own.shape, BF16),
        pltpu.VMEM((rows, model), BF16),
        pltpu.VMEM((2 * rows, qkv_width), F32),
        pltpu.VMEM(heads, F32),
        pltpu.VMEM(heads, F32),
        pltpu.VMEM(heads, F32),
        pltpu.VMEM((KV_HEADS,) + pack.shape, BF16),
        pltpu.VMEM(wide.shape, BF16),
        pltpu.VMEM(down.shape, BF16),
        pltpu.VMEM(heads, BF16),
        pltpu.VMEM(heads[1:], BF16),
        pltpu.VMEM((8, key_width), F32),
    ]
    scratch += [pltpu.VMEM(out.shape, out.dtype) for out in outs[7:15]]
    scratch += PairGather.semaphores(depth) + Gather.semaphores(depth, True)
    scratch += PairGather.semaphores(depth)
    scratch += Gather.semaphores(depth, False, True) + Gather.semaphores(depth, False)
    scratch += Exchange.semaphores(depth) + Quarter.semaphores()
    scratch += [DMA((11,)), DMA((2,)), DMA((2,))]
    return pl.pallas_call(
        functools.partial(head_kernel, depth),
        out_shape=outs,
        in_specs=[any_] + [vmem] * len(vmems) + [pl.BlockSpec(memory_space=pltpu.SMEM)],
        out_specs=[any_] * 15 + [vmem] * 2,
        scratch_shapes=scratch,
        compiler_params=pltpu.CompilerParams(
            collective_id=collective_id, has_side_effects=True, vmem_limit_bytes=VMEM_LIMIT
        ),
    )(*hbm, *vmems, lengths)


def t_mul(left, right):
    return lax.dot_general(left, right, (((0,), (0,)), ((), ())), preferred_element_type=F32)


def mul_t(left, right):
    return lax.dot_general(left, right, (((1,), (1,)), ((), ())), preferred_element_type=F32)


CUTS = ((0, 512), (512, 1024), (1024, 1152))


def middle_kernel(depth, *refs):
    (hidden_all, cot_all, wide_all, down_all, o_own) = refs[:5]
    (middle, cotangent, vectors) = refs[5:8]
    (layer_out, d_middle, d_mixed, d_branch, gain_two, down_out, wide_out) = refs[8:15]
    (tokens_v, grads_v, w_part, d_part, act, d_both, dh_part, out_part) = refs[15:23]
    (dh_sum, out_sum, w_core, w_y, d_core, o_all) = refs[23:29]
    rest = list(refs[29:])

    def take(count):
        taken = rest[:count]
        del rest[:count]
        return taken

    count = 2 * depth
    rows, model = middle.shape
    units = act.shape[2]
    part = model // depth
    buffers, sems = Reduce.scratch(depth, False, (rows, model))
    place = Place(depth)
    r_dh = Reduce(place, False, rows, dh_part, dh_sum, take(len(buffers)), take(len(sems)))
    r_out = Reduce(place, False, rows, out_part, out_sum, take(len(buffers)), take(len(sems)))
    load_sem, wc_send, wc_recv, wy_send, wy_recv, dc_send, dc_recv = take(7)
    sent = []

    def send(src, dst, send_sem, recv_sem, device):
        copy = remote(src, dst, send_sem, recv_sem, device)
        copy.start()
        sent.append(copy)

    def landed(ref, recv_sem):
        remote(ref, ref, wc_send.at[0], recv_sem, place.flip_c()).wait_recv()

    loads = [
        pltpu.make_async_copy(source, target, load_sem.at[number])
        for number, (source, target) in enumerate(
            (
                (hidden_all, tokens_v),
                (wide_all, w_part),
                (cot_all, grads_v),
                (down_all, d_part),
            )
        )
    ]
    for copy in loads:
        copy.start()
    greet(place)
    mine_y, other_y = place.y, 1 - place.y
    wide_rows = w_part.shape[-2]
    half = lax.div(place.z, 2)
    tiles = [3 - 3 * half, 2 - half, 1 + 4 * half - place.z, place.z]
    for copy in loads:
        copy.wait()

    def weights(side, low, high):
        return w_part[side, :, :, :, :, low:high].reshape(model, high - low)

    def forward(zi):
        tokens = tokens_v[zi].reshape(2 * rows, model)
        grads = grads_v[zi].reshape(2 * rows, model)
        out = None
        for low, high in CUTS:
            gate = jnp.dot(tokens, weights(0, low, high), preferred_element_type=F32)
            up = jnp.dot(tokens, weights(1, low, high), preferred_element_type=F32)
            d_act = mul_t(grads, d_part[low:high, :])
            sigma = jax.nn.sigmoid(gate)
            silu = gate * sigma
            act[zi, :, low:high] = (silu * up).astype(BF16)
            d_both[zi, :, low:high] = (
                d_act * up * sigma * (1.0 + gate * (1.0 - sigma))
            ).astype(BF16)
            d_both[zi, :, units + low : units + high] = (d_act * silu).astype(BF16)
        total = mul_t(d_both[zi, :, :units], weights(0, 0, units))
        total = total + mul_t(d_both[zi, :, units:], weights(1, 0, units))
        dh_part[zi] = total.astype(BF16).reshape(2, rows, model)
        out = jnp.dot(act[zi], d_part[...], preferred_element_type=F32)
        out_part[zi] = out.astype(BF16).reshape(2, rows, model)

    def tile(number, carry):
        zi = jnp.where(
            number == 0,
            tiles[0],
            jnp.where(number == 1, tiles[1], jnp.where(number == 2, tiles[2], tiles[3])),
        )
        forward(zi)
        r_dh.cross(zi)
        return carry

    lax.fori_loop(0, depth, tile, 0)
    for zi in tiles:
        r_out.cross(zi)
    r_dh.crossed()
    r_out.crossed()

    def wide_chunk(k, carry):
        lanes = pl.ds(pl.multiple_of(k * part, part), part)
        tokens = tokens_v[:, :, :, lanes].reshape(count * rows, part)
        term = t_mul(tokens, d_both[...].reshape(count * rows, 2 * units))
        for side in range(2):
            w_part[side, pl.ds(2 * k, 2)] = (
                term[:, side * units : (side + 1) * units]
                .astype(BF16)
                .reshape(2, 2, 2, wide_rows, units)
            )
        for step in range(2):
            to = 2 * k + step
            for y in range(2):
                remote(
                    w_part.at[:, to, y, 1 - place.c],
                    w_core.at[y, to],
                    wc_send.at[2 * to + y],
                    wc_recv.at[2 * to + y],
                    place.flip_c(),
                ).start()
        return carry

    def wide_cores(to):
        for y in (other_y, mine_y):
            landed(w_core.at[y, to], wc_recv.at[2 * to + y])
            for side in range(2):
                add_into(
                    w_core.at[y, to, side], w_part.at[side, to, y, place.c], wide_rows
                )
            if y is other_y:
                remote(
                    w_core.at[y, to], w_y.at[to], wy_send.at[to], wy_recv.at[to], place.flip_y()
                ).start()

    def wide_across(to, carry):
        landed(w_y.at[to], wy_recv.at[to])
        for side in range(2):
            add_into(w_y.at[to, side], w_core.at[mine_y, to, side], wide_rows)
        pltpu.make_async_copy(w_y.at[to], wide_out.at[to], load_sem.at[to]).start()
        return carry

    def wide_step(k, carry):
        wide_chunk(k, 0)
        pl.when(k > 0)(lambda: wide_cores(2 * k - 2))
        pl.when(k > 0)(lambda: wide_cores(2 * k - 1))
        return carry

    order = list(range(depth - 1, -1, -1))
    lax.fori_loop(0, depth - 2, wide_step, 0)
    r_dh.along(order[0])
    r_dh.along(order[1])
    lax.fori_loop(depth - 2, depth, wide_step, 0)
    wide_cores(count - 2)
    wide_cores(count - 1)
    r_dh.along(order[2])
    pieces = [
        pltpu.make_async_copy(o_own.at[zi], o_all.at[zi % 2], load_sem.at[zi])
        for zi in range(depth)
    ]
    for copy in pieces[:2]:
        copy.start()

    def down_chunk(k, carry):
        lanes = pl.ds(pl.multiple_of(k * 384, 384), 384)
        chunk = act[:, :, lanes].reshape(count * rows, 384)
        d_part[lanes, :] = t_mul(chunk, grads_v[...].reshape(count * rows, model)).astype(BF16)
        return carry

    lax.fori_loop(0, units // 384, down_chunk, 0)
    down_rows = units // 4

    def down_block(owner):
        return d_part.at[pl.ds(pl.multiple_of(owner * down_rows, down_rows), down_rows)]

    for y in (other_y, mine_y):
        send(
            down_block(2 * y + 1 - place.c),
            d_core.at[y],
            dc_send.at[y],
            dc_recv.at[y],
            place.flip_c(),
        )
    r_dh.along(order[3])
    r_dh.finish()

    after = middle[...]
    inv_two = lax.rsqrt(jnp.mean(after * after, axis=-1, keepdims=True) + EPSILON)
    normed = after * inv_two
    d_hidden = dh_sum[...]
    gain_two[...] = jnp.broadcast_to(
        jnp.sum(d_hidden * normed, axis=0, keepdims=True), gain_two.shape
    )
    scaled = d_hidden * vectors[4:5]
    total = cotangent[...].astype(F32) + inv_two * (
        scaled - normed * jnp.mean(scaled * normed, axis=-1, keepdims=True)
    )
    d_middle[...] = total
    d_branch[...] = total.astype(BF16)
    for zi in range(depth):
        pieces[zi].wait()
        term = mul_t(d_branch[...], o_all[zi % 2].reshape(part, model)).astype(BF16)
        for piece in range(part // HEAD_DIM):
            h = zi * (part // HEAD_DIM) + piece
            at = (h % GROUP) * rows
            d_mixed[h // GROUP, at : at + rows, :] = term[
                :, piece * HEAD_DIM : (piece + 1) * HEAD_DIM
            ]
        if zi + 2 < depth:
            pieces[zi + 2].start()
    for y in (other_y, mine_y):
        landed(d_core.at[y], dc_recv.at[y])
        add_into(d_core.at[y], down_block(2 * y + place.c), down_rows)
    keep = pltpu.make_async_copy(d_core, down_out, load_sem.at[count])
    keep.start()
    for step in range(depth):
        r_out.along(order[step])
        lax.fori_loop(2 * step, 2 * step + 2, wide_across, 0)
    r_out.finish()
    layer_out[...] = (middle[...] + out_sum[...]).astype(BF16)
    keep.wait()

    def end(to, carry):
        pltpu.make_async_copy(w_y.at[to], wide_out.at[to], load_sem.at[to]).wait()
        for y in range(2):
            slot = 2 * to + y
            remote(
                w_core.at[y, to], w_core.at[y, to], wc_send.at[slot], wc_recv.at[slot], place.flip_c()
            ).wait_send()
        remote(
            w_y.at[to], w_y.at[to], wy_send.at[to], wy_recv.at[to], place.flip_y()
        ).wait_send()
        return carry

    lax.fori_loop(0, count, end, 0)
    r_dh.settle()
    r_out.settle()
    for copy in sent:
        copy.wait_send()


def call_middle(depth, collective_id, hbm, vmems):
    hidden, cot, wide, down, o_all = hbm
    count = 2 * depth
    rows, model = vmems[0].shape
    units, wide_rows = wide.shape[-1], wide.shape[-2]
    any_, vmem = pl.BlockSpec(memory_space=pl.ANY), pl.BlockSpec(memory_space=pltpu.VMEM)
    buffers, sems = Reduce.scratch(depth, False, (rows, model))
    scratch = [pltpu.VMEM((depth, 2, rows, model), BF16)] * 2
    scratch += [pltpu.VMEM(wide.shape, BF16), pltpu.VMEM(down.shape, BF16)]
    scratch += [pltpu.VMEM((depth, 2 * rows, width), BF16) for width in (units, 2 * units)]
    scratch += [pltpu.VMEM((depth, 2, rows, model), BF16)] * 2
    scratch += [pltpu.VMEM((rows, model), F32)] * 2
    scratch += [
        pltpu.VMEM((2, count, 2, wide_rows, units), BF16),
        pltpu.VMEM((count, 2, wide_rows, units), BF16),
        pltpu.VMEM((2, units // 4, model), BF16),
        pltpu.VMEM((2,) + o_all.shape[1:], BF16),
    ]
    scratch += buffers + sems + buffers + sems
    scratch += [DMA((count + 1,)), DMA((2 * count,)), DMA((2 * count,))]
    scratch += [DMA((count,)), DMA((count,)), DMA((2,)), DMA((2,))]
    return pl.pallas_call(
        functools.partial(middle_kernel, depth),
        out_shape=[
            jax.ShapeDtypeStruct((rows, model), BF16),
            jax.ShapeDtypeStruct((rows, model), F32),
            jax.ShapeDtypeStruct((KV_HEADS, GROUP * rows, HEAD_DIM), BF16),
            jax.ShapeDtypeStruct((rows, model), BF16),
            jax.ShapeDtypeStruct((8, model), F32),
            jax.ShapeDtypeStruct((2, units // 4, model), BF16),
            jax.ShapeDtypeStruct((count, 2, wide_rows, units), BF16),
        ],
        in_specs=[any_] * 5 + [vmem] * 3,
        out_specs=[vmem] * 5 + [any_] * 2,
        scratch_shapes=scratch,
        compiler_params=pltpu.CompilerParams(
            collective_id=collective_id, has_side_effects=True, vmem_limit_bytes=VMEM_JOINED
        ),
    )(*hbm, *vmems)


LAST_PLAN = (
    ("d7", "d4", "d2", "d3", "down", "delta", "a0", "a1", "out"),
    ("Ck1", "Ck0", "Yk1", "d5", "Co0", "d1", "Co2", "Bo0", "a2"),
    ("Ck2", "Yk0", "a3", "Bo2", "Zk0", "Ck3", "turn", "Yk3", "Yk2"),
    ("Co1", "Zk1", "Co3", "hq", "Bo1", "query", "Zk2", "Bo3", "Cq0"),
    ("Cq2", "Ao0", "Cq1", "Zk3", "key", "Ao1", "Ao2", "d6", "hk"),
    ("kg", "small", "Cs0", "Yq0", "Cs2", "Cs1", "Zo0", "Yq1", "Ys0"),
    ("Cq3", "Ys2", "Yq2", "Zo1", "Cs3", "Zq0", "Ys1", "Ys3", "Zo2"),
    ("Yq3", "Ao3", "input", "Zs0", "Zq1", "Zs1", "Zq2", "Zs2", "Zq3"),
    ("Xq", "Zs3", "Xs", "Zo3"),
)


def follow_last(plan, works, depart, attend_wave, jobs):
    depth = 4
    steps = {"C": "cores", "B": "over_second", "A": "over_first", "Z": "along", "Y": "over"}
    for words in plan:
        for word in words:
            if word in works:
                works[word]()
            elif word[0] == "d":
                depart(int(word[1:]))
            elif word[0] == "a":
                attend_wave(int(word[1:]))
            else:
                getattr(jobs[word[1]], steps[word[0]])(depth - 1 - int(word[2:]))


def last_kernel(depth, *refs):
    (kv_own, pack_own, wide, down) = refs[:4]
    (d_mixed, angles, begin, vectors, gain_two) = refs[4:9]
    late_own = refs[9:17]
    (input_grad, q_out, kvs_out, o_out, down_out, wide_out) = refs[17:23]
    (kv_all, weights, d_query, delta, d_lin, d_keys, d_kv) = refs[23:30]
    (o_part, q_part, kvs_part) = refs[30:33]
    (d_near, d_far, d_hidden, kv_weights, d_pair, h_send, h_far, lines, pairs) = refs[33:42]
    late = refs[42:50]
    queries, mixed, lse, mixed_low, d_branch, hidden_pair, pair, d_middle = late
    rest = list(refs[50:])

    def take(number):
        taken = rest[:number]
        del rest[:number]
        return taken

    count = 2 * depth
    devices = 4 * count
    _, rows, model = pair.shape
    part = model // depth
    key_width = KV_HEADS * HEAD_DIM
    group_width = GROUP * HEAD_DIM
    qkv_width = group_width + 2 * HEAD_DIM
    model_rows = model // devices
    share = key_width // devices
    span = 4 * rows
    score_scale = HEAD_DIM ** (-0.5)
    scale = score_scale * LOG2E

    place = Place(depth)
    buffers, sems = Reduce.scratch(depth, True, o_part.shape[-2:])
    r_o = Reduce(
        place, True, model_rows, o_part, o_out, take(len(buffers)), take(len(sems))
    )

    def reduce_of(own, out, causal=False, crossing=True):
        buffers, sems = PairReduce.scratch(depth, own.shape[-2:])
        return PairReduce(
            place, own, out, take(len(buffers)), take(len(sems)), causal, crossing
        )

    r_kv = reduce_of(d_keys, d_kv, True, False)
    r_q = reduce_of(q_part, q_out)
    r_s = reduce_of(kvs_part, kvs_out)
    load_sem, e_send, e_recv, y_send, y_recv, x_send, x_recv, late_sem = take(8)
    order = list(range(depth - 1, -1, -1))
    sent = []

    def depart(offset):
        to = lax.rem(place.s + offset, count)
        copy = remote(
            wide.at[to], wide_out.at[place.s], e_send.at[offset], e_recv.at[offset], (to, place.f)
        )
        copy.start()
        sent.append(copy)

    kv_load = pltpu.make_async_copy(kv_own, kv_all, load_sem.at[0])
    kv_load.start()
    late_loads = [
        pltpu.make_async_copy(source, target, late_sem.at[number])
        for number, (source, target) in enumerate(zip(late_own, late))
    ]
    for copy in late_loads:
        copy.start()
    own_wide = pltpu.make_async_copy(wide.at[place.s], wide_out.at[place.s], load_sem.at[1])
    own_wide.start()
    down_load = pltpu.make_async_copy(down.at[place.y], d_near, load_sem.at[2 + depth])
    down_load.start()
    greet(place, [(lax.rem(place.s + offset, count), place.f) for offset in range(1, count)])
    mixed_copy = remote(
        d_mixed.at[1 - place.x],
        d_pair.at[place.x],
        x_send.at[0],
        x_recv.at[0],
        place.flip_x(),
    )
    mixed_copy.start()
    sent.append(mixed_copy)
    d_pair[place.x] = d_mixed[place.x]
    down_copy = remote(
        down.at[1 - place.y], d_far, y_send.at[0], y_recv.at[0], place.flip_y()
    )
    hidden_copy = remote(h_send, h_far, x_send.at[1], x_recv.at[1], place.flip_x())
    loads = [
        pltpu.make_async_copy(pack_own.at[zi], weights.at[zi % 2], load_sem.at[2 + zi])
        for zi in range(depth)
    ]

    local_rows = lax.broadcasted_iota(jnp.int32, (rows, span), 0)
    offsets = lax.broadcasted_iota(jnp.int32, (rows, span), 1)

    def attend(number, carry):
        keys_at = number * span + offsets
        z, x_at = lax.div(number, 2), lax.rem(number, 2)
        block = kv_all.at[z, x_at]
        key = block[:, :, :, :HEAD_DIM].reshape(span, HEAD_DIM)
        value = block[:, :, :, HEAD_DIM:].reshape(span, HEAD_DIM)
        d_key, d_value = None, None
        for x in range(2):
            places = ((2 * place.z + x) * 4 + place.f) * rows + local_rows
            visible = jnp.logical_and(keys_at >= begin[x], keys_at <= places)
            scores = mul_t(queries[x], key)
            d_probs = mul_t(d_pair[x], value)
            probs = jnp.exp2(scores * scale - lse[x][:, :1])
            probs = jnp.where(
                visible[None], probs.reshape(GROUP, rows, span), 0.0
            ).reshape(GROUP * rows, span)
            d_scores = (probs * (d_probs - delta[x][:, :1])).astype(BF16)
            d_query[x] += jnp.dot(d_scores, key, preferred_element_type=F32)
            key_term = t_mul(d_scores, queries[x])
            value_term = t_mul(probs.astype(BF16), d_pair[x])
            d_key = key_term if x == 0 else d_key + key_term
            d_value = value_term if x == 0 else d_value + value_term
        target = d_keys.at[z, x_at]
        target[:, :, :, :HEAD_DIM] = d_key.astype(BF16).reshape(2, 2, rows, HEAD_DIM)
        target[:, :, :, HEAD_DIM:] = d_value.astype(BF16).reshape(2, 2, rows, HEAD_DIM)
        return carry

    def normed_of(rows_of):
        inputs = rows_of.astype(F32)
        inverse = lax.rsqrt(jnp.mean(inputs * inputs, axis=-1, keepdims=True) + EPSILON)
        return inputs * inverse, inverse

    def out_gradient():
        for copy in late_loads[3:5]:
            copy.wait()
        for copy in loads[:2]:
            copy.start()
        for zi in range(depth):
            lanes = slice(zi * part, (zi + 1) * part)
            term = t_mul(mixed_low[:, lanes], d_branch[...]).astype(BF16)
            o_part[zi] = term.reshape(2, 2, 2, model_rows, model)

    def deltas():
        mixed_copy.wait_recv()
        for copy in late_loads[:3]:
            copy.wait()
        for x in range(2):
            delta[x] = jnp.broadcast_to(
                jnp.sum(d_pair[x].astype(F32) * mixed[x], axis=-1, keepdims=True),
                delta.shape[1:],
            )
        d_query[...] = jnp.zeros_like(d_query)
        kv_load.wait()

    def attend_wave(step):
        zi = place.z - order[step]
        low = jnp.maximum(2 * zi, 0)
        high = jnp.maximum(2 * zi + 2, 0)
        lax.fori_loop(low, high, attend, 0)

    def query_turn():
        for x in range(2):
            for j in range(GROUP):
                lanes = slice(j * HEAD_DIM, (j + 1) * HEAD_DIM)
                head = d_query[x, j * rows : (j + 1) * rows, :] * score_scale
                d_lin[x * rows : (x + 1) * rows, lanes] = turned(
                    head, angles[x, 0], -angles[x, 1]
                ).astype(BF16)

    def query_gradient():
        late_loads[5].wait()
        for zi in range(depth):
            lanes = slice(zi * part, (zi + 1) * part)
            term = t_mul(hidden_pair[:, lanes], d_lin[:, :group_width]).astype(BF16)
            q_part[zi] = term.reshape(2, 2, 2, model_rows, group_width)

    def key_turn():
        r_kv.finish()
        for x in range(2):
            at = slice(x * rows, (x + 1) * rows)
            head = d_kv[x, :, :HEAD_DIM] * score_scale
            d_lin[at, group_width : group_width + HEAD_DIM] = turned(
                head, angles[x, 0], -angles[x, 1]
            ).astype(BF16)
            d_lin[at, group_width + HEAD_DIM :] = d_kv[x, :, HEAD_DIM:].astype(BF16)

    def hidden_query():
        for zi in range(depth):
            lanes = slice(zi * part, (zi + 1) * part)
            loads[zi].wait()
            block = weights[zi % 2][:, :, :, :, :group_width].reshape(part, group_width)
            term = mul_t(d_lin[:, :group_width], block)
            for x in range(2):
                d_hidden[x, :, lanes] = term[x * rows : (x + 1) * rows]
            block = weights[zi % 2][:, :, :, :, group_width:qkv_width]
            kv_weights[lanes, :] = block.reshape(part, 2 * HEAD_DIM)
            if zi + 2 < depth:
                loads[zi + 2].start()

    def hidden_key():
        for zi in range(depth):
            lanes = slice(zi * part, (zi + 1) * part)
            term = mul_t(d_lin[:, group_width:], kv_weights[lanes, :])
            for x in range(2):
                d_hidden[x, :, lanes] += term[x * rows : (x + 1) * rows]
        h_send[...] = d_hidden[1 - place.x].astype(BF16)
        hidden_copy.start()

    def key_gradient():
        for zi in range(depth):
            lanes = slice(zi * part, (zi + 1) * part)
            term = t_mul(hidden_pair[:, lanes], d_lin[:, group_width:]).astype(BF16)
            kvs_part[zi, :, :, :, :, : 2 * HEAD_DIM] = term.reshape(
                2, 2, 2, model_rows, 2 * HEAD_DIM
            )

    def small_gradients():
        for copy in late_loads[6:]:
            copy.wait()
        lines[...] = jnp.zeros_like(lines)
        pairs[...] = jnp.zeros_like(pairs)
        bias = jnp.sum(d_lin[...].astype(F32), axis=0, keepdims=True)
        own_head = pl.ds(pl.multiple_of(place.x * HEAD_DIM, HEAD_DIM), HEAD_DIM)
        own_heads = pl.ds(pl.multiple_of(place.x * group_width, group_width), group_width)
        gain_one = jnp.zeros((1, model), F32)
        for x in range(2):
            normed, _ = normed_of(pair[x])
            gain_one = gain_one + jnp.sum(d_hidden[x] * normed, axis=0, keepdims=True)
        lines[0:1, :] = gain_one
        lines[1:2, own_heads] = bias[:, :group_width]
        lines[4:5, :] = gain_two[0:1]
        pairs[0:1, own_head] = bias[:, group_width : group_width + HEAD_DIM]
        pairs[1:2, own_head] = bias[:, group_width + HEAD_DIM :]
        chosen = lax.broadcasted_iota(jnp.int32, (key_width, model), 0)
        chosen = lax.div(chosen, share) * model_rows + lax.rem(chosen, share)
        chosen = (lax.broadcasted_iota(jnp.int32, (key_width, model), 1) == chosen).astype(BF16)
        spread = jnp.dot(pairs[...].astype(BF16), chosen, preferred_element_type=F32)
        lines[2:4, :] = spread[0:2]
        small = jnp.concatenate([lines[...], jnp.zeros((120, model), F32)], axis=0)
        small = small.T.astype(BF16)
        for zi in range(depth):
            kvs_part[zi, :, :, :, :, 2 * HEAD_DIM :] = small[
                zi * part : (zi + 1) * part
            ].reshape(2, 2, 2, model_rows, 128)

    def input_gradient():
        hidden_copy.wait_recv()
        normed, inv_one = normed_of(pair[place.x])
        scaled = (d_hidden[place.x] + h_far[...].astype(F32)) * vectors[0:1]
        input_grad[...] = d_middle[...] + inv_one * (
            scaled - normed * jnp.mean(scaled * normed, axis=-1, keepdims=True)
        )

    works = {
        "out": out_gradient,
        "delta": deltas,
        "turn": query_turn,
        "query": query_gradient,
        "key": key_turn,
        "hq": hidden_query,
        "hk": hidden_key,
        "kg": key_gradient,
        "Xq": r_q.swap,
        "Xs": r_s.swap,
        "small": small_gradients,
        "input": input_gradient,
        "down": down_copy.start,
    }
    jobs = {"o": r_o, "k": r_kv, "q": r_q, "s": r_s}
    follow_last(LAST_PLAN, works, depart, attend_wave, jobs)
    for job in (r_o, r_q, r_s):
        job.finish()
    for offset in range(1, count):
        origin = lax.rem(place.s + count - offset, count)
        block = wide_out.at[origin]
        remote(block, block, e_send.at[0], e_recv.at[offset], place.flip_c()).wait_recv()
    own_wide.wait()
    down_load.wait()
    down_copy.wait()
    down_out[...] = d_near[...].astype(F32) + d_far[...].astype(F32)
    hidden_copy.wait_send()
    for job in (r_kv, r_o, r_q, r_s):
        job.settle()
    for copy in sent:
        copy.wait_send()


def call_last(depth, collective_id, hbm, vmems, late):
    kv_all, pack_all, wide, down = hbm
    pair = late[6]
    count = 2 * depth
    _, rows, model = pair.shape
    model_rows = model // (4 * count)
    key_width, group_width = KV_HEADS * HEAD_DIM, GROUP * HEAD_DIM
    heads = (2, GROUP * rows, HEAD_DIM)
    lead = (depth, 2, 2, 2)
    kv_block, o_block = (rows, 2 * HEAD_DIM), (model_rows, model)
    blocks = [
        (model_rows, group_width),
        (model_rows, 2 * HEAD_DIM + 128),
    ]
    scratch = [
        pltpu.VMEM(kv_all.shape, BF16),
        pltpu.VMEM((2,) + pack_all.shape[1:], BF16),
        pltpu.VMEM(heads, F32),
        pltpu.VMEM(heads, F32),
        pltpu.VMEM((2 * rows, group_width + 2 * HEAD_DIM), BF16),
        pltpu.VMEM(lead + kv_block, BF16),
        pltpu.VMEM((2,) + kv_block, F32),
        pltpu.VMEM(lead + o_block, BF16),
    ]
    scratch += [pltpu.VMEM(lead + block, BF16) for block in blocks]
    scratch += [pltpu.VMEM(down.shape[1:], BF16)] * 2
    scratch += [
        pltpu.VMEM((2, rows, model), F32),
        pltpu.VMEM((model, 2 * HEAD_DIM), BF16),
        pltpu.VMEM(heads, BF16),
        pltpu.VMEM((rows, model), BF16),
        pltpu.VMEM((rows, model), BF16),
        pltpu.VMEM((8, model), F32),
        pltpu.VMEM((8, key_width), F32),
    ]
    scratch += [pltpu.VMEM(array.shape, array.dtype) for array in late]
    buffers, sems = Reduce.scratch(depth, True, o_block)
    scratch += buffers + sems
    for block in [kv_block] + blocks:
        buffers, sems = PairReduce.scratch(depth, block)
        scratch += buffers + sems
    scratch += [DMA((3 + depth,)), DMA((count,)), DMA((count,)), DMA((1,)), DMA((1,))]
    scratch += [DMA((2,)), DMA((2,)), DMA((len(late),))]
    any_, vmem = pl.BlockSpec(memory_space=pl.ANY), pl.BlockSpec(memory_space=pltpu.VMEM)
    return pl.pallas_call(
        functools.partial(last_kernel, depth),
        out_shape=[
            jax.ShapeDtypeStruct((rows, model), F32),
            jax.ShapeDtypeStruct((2,) + blocks[0], F32),
            jax.ShapeDtypeStruct((2,) + blocks[1], F32),
            jax.ShapeDtypeStruct(o_block, F32),
            jax.ShapeDtypeStruct(down.shape[1:], F32),
            jax.ShapeDtypeStruct(wide.shape, BF16),
        ],
        in_specs=[any_] * 4 + [vmem] * len(vmems) + [any_] * len(late),
        out_specs=[vmem] * 6,
        scratch_shapes=scratch,
        compiler_params=pltpu.CompilerParams(
            collective_id=collective_id, has_side_effects=True, vmem_limit_bytes=VMEM_JOINED
        ),
    )(*hbm, *vmems, *late)


def finish_kernel(few, plain, *refs):
    ins, refs = refs[: 4 + plain], refs[4 + plain :]
    outs, vectors, refs = refs[: 6 + plain], refs[6 + plain : 11 + plain], refs[11 + plain :]
    held, refs = refs[: 4 + plain], refs[4 + plain :]
    gate, up, query, key, value, in_sem, out_sem = refs
    loads = [
        pltpu.make_async_copy(source, target, in_sem.at[number])
        for number, (source, target) in enumerate(zip(ins, held))
    ]
    for copy in loads:
        copy.start()
    wide, down, q_in, kvs_in = held[:4]
    filled = wide.shape[3] // 4
    stores = []

    def store(source, number):
        copy = pltpu.make_async_copy(source, outs[number], out_sem.at[number])
        copy.start()
        stores.append(copy)

    loads[0].wait()
    for side, out in enumerate((gate, up)):
        for place in range(wide.shape[0]):
            block = wide[place, side].astype(F32)
            for owner in range(4):
                low = (4 * place + owner) * few
                out[:, low : low + few] = block[:, owner * filled : owner * filled + few]
        store(out, side)
    loads[1].wait()
    store(down.at[pl.ds(0, few)], 2)
    for number in range(plain):
        loads[4 + number].wait()
        store(held[4 + number], 6 + number)
    loads[2].wait()
    loads[3].wait()
    for g in range(KV_HEADS):
        width = q_in.shape[2]
        query[:, g * width : (g + 1) * width] = q_in[g]
        lanes = slice(g * HEAD_DIM, (g + 1) * HEAD_DIM)
        key[:, lanes] = kvs_in[g, :, :HEAD_DIM]
        value[:, lanes] = kvs_in[g, :, HEAD_DIM : 2 * HEAD_DIM]
    for number, source in enumerate((query, key, value)):
        store(source, 3 + number)
    rows_of = (kvs_in[0, :, 2 * HEAD_DIM :] + kvs_in[1, :, 2 * HEAD_DIM :]).T
    for number, out in enumerate(vectors):
        out[...] = rows_of[number : number + 1, : out.shape[1]]
    for copy in stores:
        copy.wait()


def call_finish(few, sizes, wide, down, q_grad, kvs_grad, plain):
    seq, _, rows, _ = wide.shape
    key_width = KV_HEADS * HEAD_DIM
    units = seq * 4 * few
    any_, vmem = pl.BlockSpec(memory_space=pl.ANY), pl.BlockSpec(memory_space=pltpu.VMEM)
    ins = (wide, down, q_grad, kvs_grad, *plain)
    made = [
        jax.ShapeDtypeStruct((rows, units), F32),
        jax.ShapeDtypeStruct((rows, units), F32),
        jax.ShapeDtypeStruct((rows, HEADS * HEAD_DIM), F32),
        jax.ShapeDtypeStruct((rows, key_width), F32),
        jax.ShapeDtypeStruct((rows, key_width), F32),
    ]
    out_shape = made[:2] + [jax.ShapeDtypeStruct((few, down.shape[1]), F32)] + made[2:]
    out_shape += [jax.ShapeDtypeStruct(array.shape, array.dtype) for array in plain]
    out_shape += [jax.ShapeDtypeStruct((1, size), F32) for size in sizes]
    return pl.pallas_call(
        functools.partial(finish_kernel, few, len(plain)),
        out_shape=out_shape,
        in_specs=[any_] * len(ins),
        out_specs=[any_] * (6 + len(plain)) + [vmem] * len(sizes),
        scratch_shapes=[pltpu.VMEM(array.shape, array.dtype) for array in (*ins, *made)]
        + [DMA((len(ins),)), DMA((6 + len(plain),))],
        compiler_params=pltpu.CompilerParams(vmem_limit_bytes=VMEM_LIMIT),
    )(*ins)


def begin_of(positions, lengths):
    ends = jnp.cumsum(lengths)
    starts = ends - lengths
    inside = (positions[:, None] >= starts[None, :]) & (positions[:, None] < ends[None, :])
    return jnp.sum(jnp.where(inside, starts[None, :], 0), axis=1)


def rope_tables(places, head_size):
    half_size = head_size // 2
    frequency = ROPE_BASE ** (-2.0 * jnp.arange(half_size, dtype=F32) / head_size)
    angles = places.astype(F32)[:, None] * frequency[None, :]
    return (jnp.cos(angles), jnp.sin(angles))


def rotate(vector, cosine, sine_table, direction):
    half_size = vector.shape[-1] // 2
    front_half = vector[..., :half_size]
    back_half = vector[..., half_size:]
    cosine = cosine[:, None, :]
    sine_table = direction * sine_table[:, None, :]
    return jnp.concatenate(
        [
            front_half * cosine - back_half * sine_table,
            back_half * cosine + front_half * sine_table,
        ],
        axis=-1,
    )


def norm_back(grad_normed, normed, inverse, gain_row):
    scaled = grad_normed * gain_row
    return inverse * (scaled - normed * jnp.mean(scaled * normed, axis=-1, keepdims=True))


def dot(left, right):
    return jnp.dot(left, right, preferred_element_type=F32)


def dot_t(left, right):
    return lax.dot_general(left, right, (((1,), (1,)), ((), ())), preferred_element_type=F32)


def t_dot(left, right):
    return lax.dot_general(left, right, (((0,), (0,)), ((), ())), preferred_element_type=F32)


def column(vector, rows):
    return jnp.pad(vector, (0, rows - vector.shape[0]))[:, None]


def shards_apart(
    tokens,
    cotangent,
    lengths,
    attn_gain,
    q_weight,
    q_bias,
    k_weight,
    k_bias,
    v_weight,
    v_bias,
    o_weight,
    mlp_gain,
    gate_weight,
    up_weight,
    down_weight,
):
    seq, fsdp = lax.axis_size("seq"), lax.axis_size("fsdp")
    devices = seq * fsdp
    depth = seq // 2
    rows, model = tokens.shape
    total = rows * devices
    key_width = KV_HEADS * HEAD_DIM
    query_width = HEADS * HEAD_DIM
    model_rows = q_weight.shape[0]
    units = gate_weight.shape[1] // seq
    first_row = lax.axis_index(AXES) * rows
    positions = first_row + jnp.arange(rows, dtype=jnp.int32)
    begin = begin_of(positions, lengths)
    cosine, sine_table = rope_tables(positions - begin, HEAD_DIM)
    score_scale = HEAD_DIM ** (-0.5)

    small = jnp.concatenate(
        [column(v, model_rows) for v in (attn_gain, q_bias, k_bias, v_bias, mlp_gain)]
        + [jnp.zeros((model_rows, 123), BF16)],
        axis=1,
    )
    pack = jnp.concatenate([q_weight, k_weight, v_weight, o_weight, small], axis=1)
    wide = jnp.stack([gate_weight, up_weight]).reshape(2, model_rows, seq, units)
    wide = wide.transpose(0, 2, 1, 3)
    pack_all, cot_all, wide_all, down_all = call_start(
        depth, 0, pack, cotangent, wide, down_weight
    )
    pack_all = pack_all.reshape(model, pack.shape[1])
    qkv_width = query_width + 2 * key_width
    w_qkv = pack_all[:, :qkv_width]
    w_out = pack_all[:, qkv_width : qkv_width + query_width]
    smalls = pack_all[:, qkv_width + query_width :].astype(F32)
    gain_one, b_query = smalls[:, 0], smalls[:, 1]
    gain_two = smalls[:, 4]
    kv_share = k_bias.shape[0]
    b_key = smalls[:, 2].reshape(devices, model_rows)[:, :kv_share].reshape(key_width)
    b_value = smalls[:, 3].reshape(devices, model_rows)[:, :kv_share].reshape(key_width)
    cot_all = cot_all.reshape(seq * rows, model)
    w_gate = wide_all[0].reshape(model, units)
    w_up = wide_all[1].reshape(model, units)
    w_down = down_all.reshape(units, model)

    inputs = tokens.astype(F32)
    inv_one = lax.rsqrt(jnp.mean(inputs * inputs, axis=-1, keepdims=True) + EPSILON)
    normed_one = inputs * inv_one
    hidden_one = (normed_one * gain_one).astype(BF16)
    lin = dot(hidden_one, w_qkv) + jnp.concatenate([b_query, b_key, b_value])
    queries = rotate(
        lin[:, :query_width].reshape(rows, HEADS, HEAD_DIM), cosine, sine_table, 1.0
    ).astype(BF16)
    queries = queries.transpose(1, 0, 2).reshape(KV_HEADS, GROUP * rows, HEAD_DIM)
    keys = rotate(
        lin[:, query_width : query_width + key_width].reshape(rows, KV_HEADS, HEAD_DIM),
        cosine,
        sine_table,
        1.0,
    ).reshape(rows, key_width)
    kv = jnp.concatenate([keys, lin[:, query_width + key_width :]], axis=1).astype(BF16)
    (kv_all,) = call_gathers(depth, 1, [True], [kv])
    kv_all = kv_all.reshape(total, 2 * key_width)
    all_keys, all_values = kv_all[:, :key_width], kv_all[:, key_width:]

    span = min(512, total)
    low = begin[0] // span
    high = (first_row + rows - 1) // span + 1
    info = jnp.stack([first_row, low, high]).astype(jnp.int32)
    begin_column = begin[:, None]
    mixed, lse = call_forward(span, info, begin_column, queries, all_keys, all_values)
    mixed_low = (
        mixed.reshape(HEADS, rows, HEAD_DIM)
        .transpose(1, 0, 2)
        .reshape(rows, query_width)
        .astype(BF16)
    )
    middle = inputs + dot(mixed_low, w_out)
    inv_two = lax.rsqrt(jnp.mean(middle * middle, axis=-1, keepdims=True) + EPSILON)
    normed_two = middle * inv_two
    hidden_two = (normed_two * gain_two).astype(BF16)

    (hidden_all,) = call_gathers(depth, 2, [False], [hidden_two])
    hidden_all = hidden_all.reshape(seq * rows, model)
    gate = dot(hidden_all, w_gate)
    up = dot(hidden_all, w_up)
    sigma = jax.nn.sigmoid(gate)
    silu = gate * sigma
    activated = (silu * up).astype(BF16)
    d_act = dot_t(cot_all, w_down)
    d_gate = (d_act * up * sigma * (1.0 + gate * (1.0 - sigma))).astype(BF16)
    d_up = (d_act * silu).astype(BF16)
    d_hidden_part = dot_t(d_gate, w_gate) + dot_t(d_up, w_up)
    out_part = dot(activated, w_down)
    shape = (depth, 2, rows, model)
    d_hidden_two, branch = call_reduces(
        depth,
        3,
        [False, False],
        [d_hidden_part.astype(BF16).reshape(shape), out_part.astype(BF16).reshape(shape)],
    )
    layer_out = (middle + branch).astype(BF16)
    gate_part = t_dot(hidden_all, d_gate).astype(BF16)
    up_part = t_dot(hidden_all, d_up).astype(BF16)
    down_part = t_dot(activated, cot_all).astype(BF16)

    gain_two_grad = jnp.sum(d_hidden_two * normed_two, axis=0)
    d_middle = cotangent.astype(F32) + norm_back(d_hidden_two, normed_two, inv_two, gain_two)

    d_branch = d_middle.astype(BF16)
    d_mixed = dot_t(d_branch, w_out).astype(BF16)
    d_mixed = (
        d_mixed.reshape(rows, HEADS, HEAD_DIM)
        .transpose(1, 0, 2)
        .reshape(KV_HEADS, GROUP * rows, HEAD_DIM)
    )
    d_query, d_kv_part = call_backward(
        span, info, begin_column, queries, all_keys, all_values, mixed, lse, d_mixed
    )
    (d_kv,) = call_reduces(
        depth, 4, [True], [d_kv_part.reshape(depth, 2, 2, 2, rows, 2 * key_width)]
    )
    d_query = d_query.reshape(HEADS, rows, HEAD_DIM).transpose(1, 0, 2)
    d_q = rotate(d_query * score_scale, cosine, sine_table, -1.0).reshape(rows, query_width)
    d_k = rotate(
        d_kv[:, :key_width].reshape(rows, KV_HEADS, HEAD_DIM) * score_scale,
        cosine,
        sine_table,
        -1.0,
    ).reshape(rows, key_width)
    d_lin = jnp.concatenate([d_q, d_k, d_kv[:, key_width:]], axis=1).astype(BF16)
    bias_grad = jnp.sum(d_lin.astype(F32), axis=0)
    d_hidden_one = dot_t(d_lin, w_qkv)
    gain_one_grad = jnp.sum(d_hidden_one * normed_one, axis=0)
    input_grad = d_middle + norm_back(d_hidden_one, normed_one, inv_one, gain_one)

    def spread(vector):
        parts = vector.reshape(devices, -1)
        return jnp.pad(parts, ((0, 0), (0, model_rows - parts.shape[1]))).reshape(model, 1)

    small_part = jnp.concatenate(
        [
            spread(gain_one_grad),
            spread(bias_grad[:query_width]),
            spread(bias_grad[query_width : query_width + key_width]),
            spread(bias_grad[query_width + key_width :]),
            spread(gain_two_grad),
            jnp.zeros((model, 123), F32),
        ],
        axis=1,
    )
    pack_part = jnp.concatenate(
        [
            t_dot(hidden_one, d_lin).astype(BF16),
            t_dot(mixed_low, d_branch).astype(BF16),
            small_part.astype(BF16),
        ],
        axis=1,
    ).reshape(depth, 2, 2, 2, model_rows, pack.shape[1])
    wide_part = jnp.stack([gate_part, up_part]).reshape(2, seq, fsdp, model_rows, units)
    down_part = down_part.reshape(fsdp, units // fsdp, model)
    pack_grad, wide_grad, down_grad = call_end(depth, 5, pack_part, wide_part, down_part)
    wide_grad = wide_grad.transpose(1, 2, 0, 3).reshape(2, model_rows, seq * units).astype(F32)
    small_grad = pack_grad[:, qkv_width + query_width :]
    return (
        layer_out,
        input_grad,
        small_grad[:, 0],
        pack_grad[:, :query_width],
        small_grad[:, 1],
        pack_grad[:, query_width : query_width + key_width],
        small_grad[:kv_share, 2],
        pack_grad[:, query_width + key_width : qkv_width],
        small_grad[:kv_share, 3],
        pack_grad[:, qkv_width : qkv_width + query_width],
        small_grad[:, 4],
        wide_grad[0],
        wide_grad[1],
        down_grad,
    )


def shards_joined(
    tokens,
    cotangent,
    lengths,
    attn_gain,
    q_weight,
    q_bias,
    k_weight,
    k_bias,
    v_weight,
    v_bias,
    o_weight,
    mlp_gain,
    gate_weight,
    up_weight,
    down_weight,
):
    seq, fsdp = lax.axis_size("seq"), lax.axis_size("fsdp")
    devices = seq * fsdp
    depth = seq // 2
    rows, model = tokens.shape
    key_width = KV_HEADS * HEAD_DIM
    model_rows = q_weight.shape[0]
    kv_share = k_bias.shape[0]
    small = jnp.stack(
        [jnp.pad(v, (0, model_rows - v.shape[0])) for v in (attn_gain, q_bias, k_bias, v_bias, mlp_gain)],
        axis=1,
    )
    small = jnp.pad(small, ((0, 0), (0, 123)))
    few = down_weight.shape[0]
    filled = fsdp * (few + -few % 16)
    steps = np.arange(HEAD_DIM) % (HEAD_DIM // 2)
    frequency = jnp.asarray((ROPE_BASE ** (-2.0 * steps / HEAD_DIM)).astype(np.float32)[None, :])
    (
        pack_all,
        o_all,
        kv_all,
        cot_all,
        wide_all,
        down_all,
        hidden_all,
        queries,
        mixed,
        lse,
        middle,
        hidden_pair,
        mixed_low,
        pair,
        angles,
        begin,
        vectors,
    ) = call_head(
        depth,
        6,
        (o_weight,),
        (
            q_weight,
            k_weight,
            v_weight,
            small,
            gate_weight,
            up_weight,
            down_weight,
            tokens,
            cotangent,
            frequency,
        ),
        lengths,
    )
    layer_out, d_middle, d_mixed, d_branch, gain_two_grad, down_part, wide_part = call_middle(
        depth,
        7,
        (
            hidden_all,
            cot_all,
            wide_all.reshape(2, seq, 2, 2, model_rows, filled),
            down_all.reshape(filled, model),
            o_all,
        ),
        (middle, cotangent, vectors),
    )
    input_grad, q_grad, kvs_grad, o_grad, down_grad, wide_grad = call_last(
        depth,
        8,
        (kv_all, pack_all, wide_part, down_part),
        (d_mixed, angles, begin, vectors, gain_two_grad),
        (queries, mixed, lse, mixed_low, d_branch, hidden_pair, pair, d_middle),
    )
    sizes = (model_rows, model_rows, kv_share, kv_share, model_rows)
    gate_grad, up_grad, down_grad, q_grad, k_grad, v_grad, *rest = call_finish(
        few, sizes, wide_grad, down_grad, q_grad, kvs_grad, (layer_out, input_grad, o_grad)
    )
    layer_out, input_grad, o_grad = rest[:3]
    small_grad = [vector.reshape(-1) for vector in rest[3:]]
    return (
        layer_out,
        input_grad,
        small_grad[0],
        q_grad,
        small_grad[1],
        k_grad,
        small_grad[2],
        v_grad,
        small_grad[3],
        o_grad,
        small_grad[4],
        gate_grad,
        up_grad,
        down_grad,
    )


def shards(*arguments):
    model_rows, rows = arguments[4].shape[0], arguments[0].shape[0]
    if model_rows % 16 == 0 and rows % 128 == 0 and lax.axis_size("seq") == 8:
        return shards_joined(*arguments)
    return shards_apart(*arguments)


def solution(mesh):
    matrix, vector = P(AXES, None), P(AXES)
    in_specs = (
        matrix,
        matrix,
        P(),
        vector,
        matrix,
        vector,
        matrix,
        vector,
        matrix,
        vector,
        matrix,
        vector,
        matrix,
        matrix,
        matrix,
    )
    out_specs = (
        matrix,
        matrix,
        vector,
        matrix,
        vector,
        matrix,
        vector,
        matrix,
        vector,
        matrix,
        vector,
        matrix,
        matrix,
        matrix,
    )
    return jax.shard_map(shards, mesh=mesh, in_specs=in_specs, out_specs=out_specs, check_vma=False)
```

```python
import functools

import jax
import jax.numpy as jnp
import numpy as np
from jax import lax
from jax.experimental import pallas as pl
from jax.experimental.pallas import tpu as pltpu
from jax.sharding import PartitionSpec as P

HEADS = 12
KV_HEADS = 2
HEAD_DIM = 128
GROUP = HEADS // KV_HEADS
EPSILON = 1e-06
ROPE_BASE = 10000.0
LOG2E = 1.4426950408889634
AXES = ("seq", "fsdp")
VMEM_LIMIT = 56 << 20
VMEM_JOINED = 60 << 20
F32 = jnp.float32
BF16 = jnp.bfloat16
DMA = pltpu.SemaphoreType.DMA


class Place:
    def __init__(self, depth):
        self.depth = depth
        self.s = lax.axis_index("seq")
        self.f = lax.axis_index("fsdp")
        self.z = lax.div(self.s, 2)
        self.x = lax.rem(self.s, 2)
        self.y = lax.div(self.f, 2)
        self.c = lax.rem(self.f, 2)
        self.up = self.z + 1 < depth
        self.down = self.z > 0

    def flip_x(self):
        return (self.s + 1 - 2 * self.x, self.f)

    def flip_y(self):
        return (self.s, self.f + 2 - 4 * self.y)

    def flip_c(self):
        return (self.s, self.f + 1 - 2 * self.c)

    def z_up(self):
        return (self.s + 2, self.f)

    def z_down(self):
        return (self.s - 2, self.f)

    def first(self):
        return (
            self.s + (1 - self.c) * (1 - 2 * self.x),
            self.f + self.c * (2 - 4 * self.y),
        )

    def second(self):
        return (
            self.s + self.c * (1 - 2 * self.x),
            self.f + (1 - self.c) * (2 - 4 * self.y),
        )

    def corner(self, i, j):
        over_x = i * (1 - self.c) + j * self.c
        over_y = j * (1 - self.c) + i * self.c
        return (self.x + over_x * (1 - 2 * self.x), self.y + over_y * (1 - 2 * self.y))

    def wave(self, k):
        if k == 0:
            return [(self.z, None)]
        return [(self.z - k, self.z - k >= 0), (self.z + k, self.z + k < self.depth)]


def guard(condition, body):
    if condition is None:
        body()
    else:
        pl.when(condition)(body)


def both(one, other):
    return one if other is None else jnp.logical_and(one, other)


def greet(place, others=()):
    barrier = pltpu.get_barrier_semaphore()
    partners = [place.flip_x(), place.flip_y(), place.flip_c(), *others]
    for partner in partners:
        pl.semaphore_signal(barrier, inc=1, device_id=partner, device_id_type=pl.DeviceIdType.MESH)

    def tell_up():
        pl.semaphore_signal(
            barrier, inc=1, device_id=place.z_up(), device_id_type=pl.DeviceIdType.MESH
        )

    def tell_down():
        pl.semaphore_signal(
            barrier, inc=1, device_id=place.z_down(), device_id_type=pl.DeviceIdType.MESH
        )

    pl.when(place.up)(tell_up)
    pl.when(place.down)(tell_down)
    pl.semaphore_wait(
        barrier, len(partners) + place.up.astype(jnp.int32) + place.down.astype(jnp.int32)
    )


def remote(src, dst, send_sem, recv_sem, device):
    return pltpu.make_async_remote_copy(
        src_ref=src,
        dst_ref=dst,
        send_sem=send_sem,
        recv_sem=recv_sem,
        device_id=device,
        device_id_type=pl.DeviceIdType.MESH,
    )


def add_into(target, term, rows):
    step = rows if rows <= 48 else (32 if rows % 32 == 0 else 16)

    def body(number, carry):
        at = pl.ds(pl.multiple_of(number * step, step), step)
        target[at, :] = (target[at, :].astype(F32) + term[at, :].astype(F32)).astype(BF16)
        return carry

    lax.fori_loop(0, rows // step, body, 0)


class Gather:
    def __init__(self, place, wide, own, out, sems, mixed=False):
        self.place, self.wide, self.own, self.out, self.sems = place, wide, own, out, sems
        self.mixed = mixed
        self.sent = []

    @staticmethod
    def semaphores(depth, wide, mixed=False):
        base = [DMA((1,)), DMA((2 * depth,)), DMA((depth,)), DMA((depth,)), DMA((depth,))]
        if mixed:
            base += [DMA((2 * depth,)), DMA((depth,))]
        if wide:
            base += [DMA((2 * depth,)), DMA((2 * depth,)), DMA((4 * depth,)), DMA((4 * depth,))]
        return base

    def at(self, zi, i, j):
        place = self.place
        if self.wide:
            x, y = place.corner(i, j)
            return self.out.at[zi, x, y, place.c]
        return self.out.at[zi, place.x + i * (1 - 2 * place.x)]

    def send(self, src, dst, send_sem, recv_sem, device, condition):
        copy = remote(src, dst, send_sem, recv_sem, device)
        guard(condition, copy.start)
        self.sent.append((copy, condition))

    def local(self):
        copy = pltpu.make_async_copy(
            self.own, self.at(self.place.z, 0, 0), self.sems[0].at[0]
        )
        return copy

    def along(self, k, zi, side, ok, column, z_send, z_recv, source=None):
        place, depth = self.place, self.place.depth
        block = self.at(zi, column, 0)
        source = block if source is None else source
        if k == 0 or side == 0:
            self.send(
                source, block, z_send.at[k], z_recv.at[zi], place.z_up(), both(place.up, ok)
            )
        if k == 0 or side == 1:
            self.send(
                source,
                block,
                z_send.at[depth + k],
                z_recv.at[zi],
                place.z_down(),
                both(place.down, ok),
            )

    def arrive(self, k):
        place = self.place
        z_send, z_recv, a_send, a_recv = self.sems[1:5]
        across = place.first() if self.wide else place.flip_x()
        for side, (zi, ok) in enumerate(place.wave(k)):
            block = self.at(zi, 0, 0)
            source = self.own if k == 0 else block
            if k > 0:
                landed = remote(block, block, z_send.at[0], z_recv.at[zi], place.z_up())
                guard(ok, landed.wait_recv)
            self.along(k, zi, side, ok, 0, z_send, z_recv, source)
            crossing = both(place.c == 0, ok) if self.mixed and k > 0 else ok
            self.send(source, block, a_send.at[zi], a_recv.at[zi], across, crossing)
            if self.wide:
                b_send, b_recv = self.sems[5:7]
                self.send(
                    source, block, b_send.at[2 * zi], b_recv.at[2 * zi], place.second(), ok
                )

    def across(self, k):
        place = self.place
        a_send, a_recv = self.sems[3:5]
        for side, (zi, ok) in enumerate(place.wave(k)):
            block = self.at(zi, 1, 0)
            crossing = both(place.c == 0, ok) if self.mixed and k > 0 else ok
            landed = remote(block, block, a_send.at[0], a_recv.at[zi], place.first())
            guard(crossing, landed.wait_recv)
            if self.mixed:
                z_send, z_recv = self.sems[5:7]
                carried = both(place.c == 1, ok)
                if k > 0:
                    landed = remote(block, block, z_send.at[0], z_recv.at[zi], place.z_up())
                    guard(carried, landed.wait_recv)
                self.along(k, zi, side, carried, 1, z_send, z_recv)
            if self.wide:
                b_send, b_recv = self.sems[5:7]
                self.send(
                    block, block, b_send.at[2 * zi + 1], b_recv.at[2 * zi + 1], place.second(), ok
                )

    def hand(self, k):
        place = self.place
        b_send, b_recv, c_send, c_recv = self.sems[5:9]
        for zi, ok in place.wave(k):
            for i in range(2):
                block = self.at(zi, i, 1)
                landed = remote(block, block, b_send.at[0], b_recv.at[2 * zi + i], place.second())
                guard(ok, landed.wait_recv)
            for x in range(2):
                for y in range(2):
                    block = self.out.at[zi, x, y, place.c]
                    slot = 4 * zi + 2 * x + y
                    self.send(
                        block, block, c_send.at[slot], c_recv.at[slot], place.flip_c(), ok
                    )

    def take(self, k):
        place = self.place
        c_send, c_recv = self.sems[7:9]
        for zi, ok in place.wave(k):
            for x in range(2):
                for y in range(2):
                    block = self.out.at[zi, x, y, 1 - place.c]
                    slot = 4 * zi + 2 * x + y
                    landed = remote(block, block, c_send.at[0], c_recv.at[slot], place.flip_c())
                    guard(ok, landed.wait_recv)

    def settle(self):
        for copy, condition in self.sent:
            guard(condition, copy.wait_send)


def drive_gathers(place, gathers):
    depth = place.depth
    locals_ = [gather.local() for gather in gathers]
    for copy in locals_:
        copy.start()
    for step in range(depth + 3):
        for gather in gathers:
            if step < depth:
                gather.arrive(step)
        if step == 0:
            for copy in locals_:
                copy.wait()
        for gather in gathers:
            if 0 <= step - 1 < depth:
                gather.across(step - 1)
        for gather in gathers:
            if gather.wide and 0 <= step - 2 < depth:
                gather.hand(step - 2)
        for gather in gathers:
            if gather.wide and 0 <= step - 3 < depth:
                gather.take(step - 3)
    for gather in gathers:
        gather.settle()


def gather_shape(depth, wide, own):
    lead = (depth, 2, 2, 2) if wide else (depth, 2)
    return jax.ShapeDtypeStruct(lead + own.shape, own.dtype)


def call_gathers(depth, collective_id, wides, owns):
    def kernel(*refs):
        count = len(owns)
        place = Place(depth)
        greet(place)
        gathers, used = [], 2 * count
        for number, wide in enumerate(wides):
            need = len(Gather.semaphores(depth, wide))
            gathers.append(
                Gather(place, wide, refs[number], refs[count + number], refs[used : used + need])
            )
            used += need
        drive_gathers(place, gathers)

    scratch = []
    for wide in wides:
        scratch += Gather.semaphores(depth, wide)
    return pl.pallas_call(
        kernel,
        out_shape=[gather_shape(depth, wide, own) for wide, own in zip(wides, owns)],
        in_specs=[pl.BlockSpec(memory_space=pl.ANY)] * len(owns),
        out_specs=[pl.BlockSpec(memory_space=pl.ANY)] * len(owns),
        scratch_shapes=scratch,
        compiler_params=pltpu.CompilerParams(
            collective_id=collective_id, has_side_effects=True, vmem_limit_bytes=VMEM_LIMIT
        ),
    )(*owns)


def start_kernel(depth, *refs):
    (pack, cot, wide_in, down_in, pack_out, cot_out, wide_out, down_out), sems = refs[:8], refs[8:]
    place = Place(depth)
    count = 2 * depth
    partners = []
    for offset in range(1, count):
        partners.append((lax.rem(place.s + offset, count), place.f))
    greet(place, partners)
    first = len(Gather.semaphores(depth, True))
    second = first + len(Gather.semaphores(depth, False))
    gathers = [
        Gather(place, True, pack, pack_out, sems[:first]),
        Gather(place, False, cot, cot_out, sems[first:second]),
    ]
    local_sem, e_send, e_recv, y_send, y_recv, c_send, c_recv, d_sem, d_send, d_recv = sems[second:]
    sent = []

    def send(src, dst, send_sem, recv_sem, device):
        copy = remote(src, dst, send_sem, recv_sem, device)
        copy.start()
        sent.append(copy)

    locals_ = [gather.local() for gather in gathers]
    locals_.append(
        pltpu.make_async_copy(
            wide_in.at[:, place.s], wide_out.at[:, place.s, place.f], local_sem.at[0]
        )
    )
    locals_.append(pltpu.make_async_copy(down_in, down_out.at[place.f], d_sem.at[0]))
    for copy in locals_:
        copy.start()

    y_f = place.f + 2 - 4 * place.y
    c_f = place.f + 1 - 2 * place.c
    yc_f = y_f + 1 - 2 * place.c

    def exchange(offset):
        to = lax.rem(place.s + offset, count)
        send(
            wide_in.at[:, to],
            wide_out.at[:, place.s, place.f],
            e_send.at[offset],
            e_recv.at[offset],
            (to, place.f),
        )

    def onward(offset):
        origin = lax.rem(place.s + count - offset, count)
        block = wide_out.at[:, origin, place.f]
        if offset > 0:
            remote(block, block, e_send.at[0], e_recv.at[offset], place.flip_y()).wait_recv()
        send(block, block, y_send.at[offset], y_recv.at[offset], place.flip_y())
        send(block, block, c_send.at[2 * offset], c_recv.at[2 * offset], place.flip_c())

    def sideways(offset):
        origin = lax.rem(place.s + count - offset, count)
        block = wide_out.at[:, origin, y_f]
        remote(block, block, y_send.at[0], y_recv.at[offset], place.flip_y()).wait_recv()
        send(block, block, c_send.at[2 * offset + 1], c_recv.at[2 * offset + 1], place.flip_c())

    def last(offset):
        origin = lax.rem(place.s + count - offset, count)
        for slot, owner in ((2 * offset, c_f), (2 * offset + 1, yc_f)):
            block = wide_out.at[:, origin, owner]
            remote(block, block, c_send.at[0], c_recv.at[slot], place.flip_c()).wait_recv()

    for gather in gathers:
        gather.arrive(0)
    send(down_in, down_out.at[place.f], d_send.at[0], d_recv.at[0], place.flip_y())
    send(down_in, down_out.at[place.f], d_send.at[1], d_recv.at[1], place.flip_c())
    for offset in range(1, count):
        exchange(offset)
    for copy in locals_:
        copy.wait()
    onward(0)
    total = depth + 3
    for step in range(1, total):
        for gather in gathers:
            if step < depth:
                gather.arrive(step)
        for gather in gathers:
            if 0 <= step - 1 < depth:
                gather.across(step - 1)
        for gather in gathers:
            if gather.wide and 0 <= step - 2 < depth:
                gather.hand(step - 2)
        for gather in gathers:
            if gather.wide and 0 <= step - 3 < depth:
                gather.take(step - 3)
    block = down_out.at[y_f]
    remote(block, block, d_send.at[0], d_recv.at[0], place.flip_y()).wait_recv()
    send(block, block, d_send.at[2], d_recv.at[2], place.flip_c())
    for offset in range(1, count):
        onward(offset)
        sideways(offset - 1)
    sideways(count - 1)
    for offset in range(count):
        last(offset)
    for slot, owner in ((1, c_f), (2, yc_f)):
        block = down_out.at[owner]
        remote(block, block, d_send.at[0], d_recv.at[slot], place.flip_c()).wait_recv()
    for gather in gathers:
        gather.settle()
    for copy in sent:
        copy.wait_send()


def call_start(depth, collective_id, pack, cot, wide, down):
    count = 2 * depth
    _, _, rows, columns = wide.shape
    scratch = Gather.semaphores(depth, True) + Gather.semaphores(depth, False)
    scratch += [DMA((1,)), DMA((count,)), DMA((count,)), DMA((count,)), DMA((count,))]
    scratch += [DMA((2 * count,)), DMA((2 * count,)), DMA((1,)), DMA((3,)), DMA((3,))]
    return pl.pallas_call(
        functools.partial(start_kernel, depth),
        out_shape=[
            gather_shape(depth, True, pack),
            gather_shape(depth, False, cot),
            jax.ShapeDtypeStruct((2, count, 4, rows, columns), BF16),
            jax.ShapeDtypeStruct((4,) + down.shape, BF16),
        ],
        in_specs=[pl.BlockSpec(memory_space=pl.ANY)] * 4,
        out_specs=[pl.BlockSpec(memory_space=pl.ANY)] * 4,
        scratch_shapes=scratch,
        compiler_params=pltpu.CompilerParams(
            collective_id=collective_id, has_side_effects=True, vmem_limit_bytes=VMEM_LIMIT
        ),
    )(pack, cot, wide, down)


class Reduce:
    def __init__(self, place, wide, rows, own, out, buffers, sems, near=None, causal=False):
        self.place, self.wide, self.rows = place, wide, rows
        self.own, self.out, self.buffers, self.sems = own, out, buffers, sems
        self.near = near
        self.causal = causal
        self.sent = []

    def wave(self, k):
        waves = self.place.wave(k)
        return waves[:1] if self.causal else waves

    def near_block(self, zi):
        return self.own.at[zi, self.place.x] if self.near is None else self.near.at[zi]

    @staticmethod
    def scratch(depth, wide, block):
        buffers = [
            pltpu.VMEM((depth,) + block, BF16),
            pltpu.VMEM((depth + 1,) + block, BF16),
        ]
        sems = [DMA((depth,)), DMA((depth,)), DMA((2 * depth,)), DMA((2 * depth,))]
        if wide:
            buffers += [
                pltpu.VMEM((depth, 2, 2) + block, BF16),
                pltpu.VMEM((depth, 2) + block, BF16),
            ]
            sems += [DMA((4 * depth,)), DMA((4 * depth,)), DMA((2 * depth,)), DMA((2 * depth,))]
        return buffers, sems

    def send(self, src, dst, send_sem, recv_sem, device, condition):
        copy = remote(src, dst, send_sem, recv_sem, device)
        guard(condition, copy.start)
        self.sent.append((copy, condition))

    def cores(self, k):
        place = self.place
        c_send, c_recv = self.sems[4:6]
        got = self.buffers[2]
        for zi, ok in self.wave(k):
            for x in range(2):
                for y in range(2):
                    slot = 4 * zi + 2 * x + y
                    self.send(
                        self.own.at[zi, x, y, 1 - place.c],
                        got.at[zi, x, y],
                        c_send.at[slot],
                        c_recv.at[slot],
                        place.flip_c(),
                        ok,
                    )

    def over_second(self, k):
        place = self.place
        c_send, c_recv, b_send, b_recv = self.sems[4:8]
        got, next_ = self.buffers[2:4]
        for zi, ok in self.wave(k):

            def body(zi=zi):
                for j in (1, 0):
                    for i in (1, 0):
                        x, y = place.corner(i, j)
                        block = got.at[zi, x, y]
                        slot = 4 * zi + 2 * x + y
                        remote(
                            block, block, c_send.at[0], c_recv.at[slot], place.flip_c()
                        ).wait_recv()
                        add_into(block, self.own.at[zi, x, y, place.c], self.rows)
                        if j == 1:
                            remote(
                                block,
                                next_.at[zi, i],
                                b_send.at[2 * zi + i],
                                b_recv.at[2 * zi + i],
                                place.second(),
                            ).start()

            guard(ok, body)
            for i in (1, 0):
                x, y = place.corner(i, 1)
                copy = remote(
                    got.at[zi, x, y],
                    next_.at[zi, i],
                    b_send.at[2 * zi + i],
                    b_recv.at[2 * zi + i],
                    place.second(),
                )
                self.sent.append((copy, ok))

    def over_first(self, k):
        place = self.place
        a_send, a_recv = self.sems[0:2]
        got = self.buffers[0]
        for zi, ok in self.wave(k):
            if self.wide:
                b_send, b_recv = self.sems[6:8]
                before, held = self.buffers[2:4]

                def body(zi=zi):
                    for i in (1, 0):
                        block = held.at[zi, i]
                        x, y = place.corner(i, 0)
                        remote(
                            block, block, b_send.at[0], b_recv.at[2 * zi + i], place.second()
                        ).wait_recv()
                        add_into(block, before.at[zi, x, y], self.rows)
                        if i == 1:
                            remote(
                                block, got.at[zi], a_send.at[zi], a_recv.at[zi], place.first()
                            ).start()

                guard(ok, body)
                copy = remote(
                    held.at[zi, 1], got.at[zi], a_send.at[zi], a_recv.at[zi], place.first()
                )
                self.sent.append((copy, ok))
            else:
                self.send(
                    self.own.at[zi, 1 - place.x],
                    got.at[zi],
                    a_send.at[zi],
                    a_recv.at[zi],
                    place.flip_x(),
                    ok,
                )

    def cross_copy(self, zi):
        place = self.place
        return remote(
            self.own.at[zi, 1 - place.x],
            self.buffers[0].at[zi],
            self.sems[0].at[zi],
            self.sems[1].at[zi],
            place.flip_x(),
        )

    def cross(self, zi):
        self.cross_copy(zi).start()

    def crossed(self):
        for zi in range(self.place.depth):
            self.sent.append((self.cross_copy(zi), None))

    def along(self, k):
        place, depth = self.place, self.place.depth
        a_send, a_recv, z_send, z_recv = self.sems[0:4]
        held, line = self.buffers[0:2]
        for side, (zi, ok) in enumerate(self.wave(k)):
            block = held.at[zi]

            def body(zi=zi, side=side, block=block):
                remote(block, block, a_send.at[0], a_recv.at[zi], place.first()).wait_recv()
                if self.wide:
                    add_into(block, self.buffers[3].at[zi, 0], self.rows)
                else:
                    add_into(block, self.near_block(zi), self.rows)

                def more(direction):
                    slot = direction * depth + zi
                    term = line.at[depth if k == 0 and direction == 1 else zi]
                    remote(term, term, z_send.at[0], z_recv.at[slot], place.z_up()).wait_recv()
                    add_into(block, term, self.rows)

                def pass_on(direction, to):
                    slot = direction * depth + zi
                    there = line.at[depth if k == 1 and direction == 1 else zi]
                    remote(block, there, z_send.at[slot], z_recv.at[slot], to).start()

                if k == 0:
                    if not self.causal:
                        pl.when(place.down)(functools.partial(more, 0))
                    pl.when(place.up)(functools.partial(more, 1))
                elif side == 0:
                    pl.when(place.up)(functools.partial(more, 1))
                    pass_on(1, place.z_down())
                else:
                    pl.when(place.down)(functools.partial(more, 0))
                    pass_on(0, place.z_up())

            guard(ok, body)
            if k > 0:
                direction = 1 - side
                slot = direction * depth + zi
                to = place.z_up() if side == 1 else place.z_down()
                there = line.at[depth if k == 1 and direction == 1 else zi]
                copy = remote(block, there, z_send.at[slot], z_recv.at[slot], to)
                self.sent.append((copy, ok))

    def finish(self):
        self.out[...] = self.buffers[0][self.place.z].astype(self.out.dtype)

    def settle(self):
        for copy, condition in self.sent:
            guard(condition, copy.wait_send)


def drive_reduces(place, reduces):
    depth = place.depth
    order = list(range(depth - 1, -1, -1))
    for reduce in reduces:
        for k in order:
            reduce.cores(k) if reduce.wide else reduce.over_first(k)
    for step in range(depth + 2):
        for reduce in reduces:
            if not reduce.wide:
                if step < depth:
                    reduce.along(order[step])
                continue
            if step < depth:
                reduce.over_second(order[step])
            if 0 <= step - 1 < depth:
                reduce.over_first(order[step - 1])
            if 0 <= step - 2 < depth:
                reduce.along(order[step - 2])
    for reduce in reduces:
        reduce.finish()
    for reduce in reduces:
        reduce.settle()


def call_reduces(depth, collective_id, wides, owns):
    count = len(owns)
    blocks = [own.shape[-2:] for own in owns]
    parts = [Reduce.scratch(depth, wide, block) for wide, block in zip(wides, blocks)]
    scratch = []
    for buffers, sems in parts:
        scratch += buffers + sems

    def kernel(*refs):
        place = Place(depth)
        greet(place)
        reduces, used = [], 2 * count
        for number, (buffers, sems) in enumerate(parts):
            middle, end = used + len(buffers), used + len(buffers) + len(sems)
            reduces.append(
                Reduce(
                    place,
                    wides[number],
                    blocks[number][0],
                    refs[number],
                    refs[count + number],
                    refs[used:middle],
                    refs[middle:end],
                )
            )
            used = end
        drive_reduces(place, reduces)

    return pl.pallas_call(
        kernel,
        out_shape=[jax.ShapeDtypeStruct(block, F32) for block in blocks],
        in_specs=[pl.BlockSpec(memory_space=pltpu.VMEM)] * count,
        out_specs=[pl.BlockSpec(memory_space=pltpu.VMEM)] * count,
        scratch_shapes=scratch,
        compiler_params=pltpu.CompilerParams(
            collective_id=collective_id, has_side_effects=True, vmem_limit_bytes=VMEM_LIMIT
        ),
    )(*owns)


def end_kernel(depth, shapes, *refs):
    pack, wide, down, pack_out, wide_out, down_out = refs[:6]
    block, wide_block, down_block = shapes
    buffers, sems = Reduce.scratch(depth, True, block)
    used = 6 + len(buffers)
    place = Place(depth)
    count = 2 * depth
    partners = []
    for offset in range(1, count):
        partners.append((lax.rem(place.s + offset, count), place.f))
    greet(place, partners)
    reduce = Reduce(
        place, True, block[0], pack, pack_out, refs[6:used], refs[used : used + len(sems)]
    )
    used += len(sems)
    w_core, w_y, d_core, d_y = refs[used : used + 4]
    wc_send, wc_recv, wy_send, wy_recv, e_send, e_recv, e_sem = refs[used + 4 : used + 11]
    dc_send, dc_recv, dy_send, dy_recv = refs[used + 11 :]
    sent = []
    wide_rows, down_rows = wide_block[1], down_block[0]

    def send(src, dst, send_sem, recv_sem, device):
        copy = remote(src, dst, send_sem, recv_sem, device)
        copy.start()
        sent.append(copy)

    def landed(ref, recv_sem):
        remote(ref, ref, e_send.at[0], recv_sem, place.flip_c()).wait_recv()

    mine_y, other_y = place.y, 1 - place.y
    offsets = list(range(1, count)) + [0]
    for y in range(2):
        side = other_y if y == 0 else mine_y
        send(
            down.at[2 * side + 1 - place.c],
            d_core.at[side],
            dc_send.at[side],
            dc_recv.at[side],
            place.flip_c(),
        )
    for offset in offsets:
        to = lax.rem(place.s + offset, count)
        for y in range(2):
            send(
                wide.at[:, to, 2 * y + 1 - place.c],
                w_core.at[y, offset],
                wc_send.at[2 * offset + y],
                wc_recv.at[2 * offset + y],
                place.flip_c(),
            )
    order = list(range(depth - 1, -1, -1))
    for k in order:
        reduce.cores(k)

    def wide_add(target, term):
        for part in range(2):
            add_into(target.at[part], term.at[part], wide_rows)

    def wide_cores(offset):
        to = lax.rem(place.s + offset, count)
        for side in (other_y, mine_y):
            landed(w_core.at[side, offset], wc_recv.at[2 * offset + side])
            wide_add(w_core.at[side, offset], wide.at[:, to, 2 * side + place.c])
            if side is other_y:
                send(
                    w_core.at[side, offset],
                    w_y.at[offset],
                    wy_send.at[offset],
                    wy_recv.at[offset],
                    place.flip_y(),
                )

    def wide_across(offset):
        landed(w_y.at[offset], wy_recv.at[offset])
        wide_add(w_y.at[offset], w_core.at[mine_y, offset])
        to = lax.rem(place.s + offset, count)
        if offset > 0:
            send(
                w_y.at[offset],
                wide_out.at[place.s],
                e_send.at[offset],
                e_recv.at[offset],
                (to, place.f),
            )
        else:
            pltpu.make_async_copy(w_y.at[0], wide_out.at[place.s], e_sem.at[0]).start()

    for offset in offsets[: count // 2]:
        wide_cores(offset)
    for step in range(depth):
        reduce.over_second(order[step])
        if step >= 1:
            reduce.over_first(order[step - 1])
        if step == 0:
            for offset in offsets[count // 2 :]:
                wide_cores(offset)
            for side in (other_y, mine_y):
                landed(d_core.at[side], dc_recv.at[side])
                add_into(d_core.at[side], down.at[2 * side + place.c], down_rows)
                if side is other_y:
                    send(d_core.at[side], d_y.at[0], dy_send.at[0], dy_recv.at[0], place.flip_y())
        for offset in offsets[step * count // depth : (step + 1) * count // depth]:
            wide_across(offset)
        if step >= 2:
            reduce.along(order[step - 2])
    reduce.over_first(order[depth - 1])
    for step in range(max(depth - 2, 0), depth):
        reduce.along(order[step])
    reduce.finish()
    landed(d_y.at[0], dy_recv.at[0])
    down_out[...] = d_y[0].astype(F32) + d_core[mine_y].astype(F32)
    for offset in range(1, count):
        origin = lax.rem(place.s + count - offset, count)
        landed(wide_out.at[origin], e_recv.at[offset])
    pltpu.make_async_copy(w_y.at[0], wide_out.at[place.s], e_sem.at[0]).wait()
    reduce.settle()
    for copy in sent:
        copy.wait_send()


def call_end(depth, collective_id, pack, wide, down):
    count = 2 * depth
    block = pack.shape[-2:]
    wide_block = (2,) + wide.shape[-2:]
    down_block = down.shape[-2:]
    buffers, sems = Reduce.scratch(depth, True, block)
    scratch = buffers + sems
    scratch += [
        pltpu.VMEM((2, count) + wide_block, BF16),
        pltpu.VMEM((count,) + wide_block, BF16),
        pltpu.VMEM((2,) + down_block, BF16),
        pltpu.VMEM((1,) + down_block, BF16),
    ]
    scratch += [DMA((2 * count,)), DMA((2 * count,)), DMA((count,)), DMA((count,))]
    scratch += [DMA((count,)), DMA((count,)), DMA((1,))]
    scratch += [DMA((2,)), DMA((2,)), DMA((1,)), DMA((1,))]
    vmem = pl.BlockSpec(memory_space=pltpu.VMEM)
    return pl.pallas_call(
        functools.partial(end_kernel, depth, (block, wide_block, down_block)),
        out_shape=[
            jax.ShapeDtypeStruct(block, F32),
            jax.ShapeDtypeStruct((count,) + wide_block, BF16),
            jax.ShapeDtypeStruct(down_block, F32),
        ],
        in_specs=[vmem] * 3,
        out_specs=[vmem, vmem, vmem],
        scratch_shapes=scratch,
        compiler_params=pltpu.CompilerParams(
            collective_id=collective_id, has_side_effects=True, vmem_limit_bytes=VMEM_LIMIT
        ),
    )(pack, wide, down)


def forward_kernel(span, info, begin, query, key, value, mixed, lse, m_acc, l_acc, o_acc):
    rows = begin.shape[0]
    first_row, low, high = info[0], info[1], info[2]
    scale = HEAD_DIM ** (-0.5) * LOG2E
    m_acc[...] = jnp.full_like(m_acc, -1e30)
    l_acc[...] = jnp.zeros_like(l_acc)
    o_acc[...] = jnp.zeros_like(o_acc)
    places = first_row + lax.broadcasted_iota(jnp.int32, (rows, span), 0)
    offsets = lax.broadcasted_iota(jnp.int32, (rows, span), 1)

    def step(number, carry):
        base = pl.multiple_of(number * span, span)
        keys_at = base + offsets
        visible = jnp.logical_and(keys_at >= begin[...], keys_at <= places)
        for g in range(KV_HEADS):
            lanes = slice(g * HEAD_DIM, (g + 1) * HEAD_DIM)
            scores = lax.dot_general(
                query[g],
                key[pl.ds(base, span), lanes],
                (((1,), (1,)), ((), ())),
                preferred_element_type=F32,
            )
            scores = scores.reshape(GROUP, rows, span) * scale
            scores = jnp.where(visible[None], scores, -1e30).reshape(GROUP * rows, span)
            old = m_acc[g]
            new = jnp.maximum(old, jnp.max(scores, axis=-1, keepdims=True))
            weights = jnp.exp2(scores - new[:, :1])
            weights = jnp.where(
                visible[None], weights.reshape(GROUP, rows, span), 0.0
            ).reshape(GROUP * rows, span)
            fade = jnp.exp2(old - new)
            l_acc[g] = l_acc[g] * fade + jnp.sum(weights, axis=-1, keepdims=True)
            o_acc[g] = o_acc[g] * fade + jnp.dot(
                weights.astype(BF16),
                value[pl.ds(base, span), lanes],
                preferred_element_type=F32,
            )
            m_acc[g] = new
        return carry

    lax.fori_loop(low, high, step, 0)
    for g in range(KV_HEADS):
        mixed[g] = o_acc[g] / l_acc[g]
        lse[g] = m_acc[g] + jnp.log2(l_acc[g])


def call_forward(span, info, begin, query, key, value):
    stacked = query.shape[1]
    vmem = pl.BlockSpec(memory_space=pltpu.VMEM)
    return pl.pallas_call(
        functools.partial(forward_kernel, span),
        out_shape=[
            jax.ShapeDtypeStruct((KV_HEADS, stacked, HEAD_DIM), F32),
            jax.ShapeDtypeStruct((KV_HEADS, stacked, HEAD_DIM), F32),
        ],
        in_specs=[pl.BlockSpec(memory_space=pltpu.SMEM)] + [vmem] * 4,
        out_specs=[vmem, vmem],
        scratch_shapes=[pltpu.VMEM((KV_HEADS, stacked, HEAD_DIM), F32)] * 3,
        compiler_params=pltpu.CompilerParams(vmem_limit_bytes=VMEM_LIMIT),
    )(info, begin, query, key, value)


def backward_kernel(
    span, info, begin, query, key, value, mixed, lse, grad, dquery, dkeys, delta
):
    rows = begin.shape[0]
    first_row, low, high = info[0], info[1], info[2]
    scale = HEAD_DIM ** (-0.5) * LOG2E
    dquery[...] = jnp.zeros_like(dquery)
    width = KV_HEADS * HEAD_DIM
    for g in range(KV_HEADS):
        delta[g] = jnp.broadcast_to(
            jnp.sum(grad[g].astype(F32) * mixed[g], axis=-1, keepdims=True), delta.shape[1:]
        )
    places = first_row + lax.broadcasted_iota(jnp.int32, (rows, span), 0)
    offsets = lax.broadcasted_iota(jnp.int32, (rows, span), 1)

    def clear(number, carry):
        base = pl.multiple_of(number * span, span)
        dkeys[pl.ds(base, span), :] = jnp.zeros((span, dkeys.shape[1]), BF16)
        return carry

    lax.fori_loop(0, low, clear, 0)
    lax.fori_loop(high, dkeys.shape[0] // span, clear, 0)

    def step(number, carry):
        base = pl.multiple_of(number * span, span)
        keys_at = base + offsets
        visible = jnp.logical_and(keys_at >= begin[...], keys_at <= places)
        for g in range(KV_HEADS):
            lanes = slice(g * HEAD_DIM, (g + 1) * HEAD_DIM)
            key_rows = key[pl.ds(base, span), lanes]
            value_rows = value[pl.ds(base, span), lanes]
            scores = lax.dot_general(
                query[g], key_rows, (((1,), (1,)), ((), ())), preferred_element_type=F32
            )
            dprobs = lax.dot_general(
                grad[g], value_rows, (((1,), (1,)), ((), ())), preferred_element_type=F32
            )
            probs = jnp.exp2(scores * scale - lse[g][:, :1])
            probs = jnp.where(
                visible[None], probs.reshape(GROUP, rows, span), 0.0
            ).reshape(GROUP * rows, span)
            dscores = (probs * (dprobs - delta[g][:, :1])).astype(BF16)
            dquery[g] += jnp.dot(dscores, key_rows, preferred_element_type=F32)
            dkeys[pl.ds(base, span), lanes] = lax.dot_general(
                dscores, query[g], (((0,), (0,)), ((), ())), preferred_element_type=F32
            ).astype(BF16)
            dkeys[
                pl.ds(base, span), width + g * HEAD_DIM : width + (g + 1) * HEAD_DIM
            ] = lax.dot_general(
                probs.astype(BF16),
                grad[g],
                (((0,), (0,)), ((), ())),
                preferred_element_type=F32,
            ).astype(BF16)
        return carry

    lax.fori_loop(low, high, step, 0)


def call_backward(span, info, begin, query, key, value, mixed, lse, grad):
    stacked = query.shape[1]
    vmem = pl.BlockSpec(memory_space=pltpu.VMEM)
    return pl.pallas_call(
        functools.partial(backward_kernel, span),
        out_shape=[
            jax.ShapeDtypeStruct((KV_HEADS, stacked, HEAD_DIM), F32),
            jax.ShapeDtypeStruct((key.shape[0], 2 * key.shape[1]), BF16),
        ],
        in_specs=[pl.BlockSpec(memory_space=pltpu.SMEM)] + [vmem] * 7,
        out_specs=[vmem, vmem],
        scratch_shapes=[pltpu.VMEM((KV_HEADS, stacked, HEAD_DIM), F32)],
        compiler_params=pltpu.CompilerParams(vmem_limit_bytes=VMEM_LIMIT),
    )(info, begin, query, key, value, mixed, lse, grad)


class PairGather:
    def __init__(self, place, own, out, sems, crossing):
        self.place, self.own, self.out, self.sems = place, own, out, sems
        self.crossing = crossing
        self.parts = [place.x, 1 - place.x] if crossing else [None]
        self.sent = []

    @staticmethod
    def semaphores(depth):
        sizes = (1, 1, 1, 4 * depth, 2 * depth, 2 * depth, 2 * depth, 4 * depth, 4 * depth)
        return [DMA((size,)) for size in sizes]

    def send(self, src, dst, send_sem, recv_sem, device, condition=None):
        copy = remote(src, dst, send_sem, recv_sem, device)
        guard(condition, copy.start)
        self.sent.append((copy, condition))

    def block(self, zi, y, c, part):
        if part is None:
            return self.out.at[zi, :, y, c]
        return self.out.at[zi, part, y, c]

    def slot(self, zi, part):
        return 2 * zi if part is None else 2 * zi + part

    def landed(self, ref, recv_sem, condition=None):
        guard(condition, remote(ref, ref, self.sems[3].at[0], recv_sem, self.place.flip_c()).wait_recv)

    def local(self):
        place = self.place
        source = self.own.at[place.x] if self.crossing else self.own
        return pltpu.make_async_copy(
            source, self.block(place.z, place.y, place.c, self.parts[0]), self.sems[0].at[0]
        )

    def begin(self):
        place = self.place
        self.send(
            self.own.at[1 - place.x],
            self.out.at[place.z, place.x, place.y, place.c],
            self.sems[1].at[0],
            self.sems[2].at[0],
            place.flip_x(),
        )
        self.spread(0, 0, place.z, None, place.x, self.own.at[place.x])

    def spread(self, k, side, zi, ok, part, source):
        place, depth = self.place, self.place.depth
        z_send, z_recv, y_send, y_recv, c_send, c_recv = self.sems[3:9]
        block, slot = self.block(zi, place.y, place.c, part), self.slot(zi, part)
        if k == 0 or side == 0:
            self.send(
                source,
                block,
                z_send.at[self.slot(k, part)],
                z_recv.at[slot],
                place.z_up(),
                both(place.up, ok),
            )
        if k == 0 or side == 1:
            self.send(
                source,
                block,
                z_send.at[2 * depth + self.slot(k, part)],
                z_recv.at[slot],
                place.z_down(),
                both(place.down, ok),
            )
        self.send(source, block, y_send.at[slot], y_recv.at[slot], place.flip_y(), ok)
        self.send(source, block, c_send.at[slot], c_recv.at[slot], place.flip_c(), ok)

    def arrive(self, k):
        place = self.place
        z_recv = self.sems[4]
        for side, (zi, ok) in enumerate(place.wave(k)):
            for number, part in enumerate(self.parts):
                block = self.block(zi, place.y, place.c, part)
                source = block
                if k > 0:
                    self.landed(block, z_recv.at[self.slot(zi, part)], ok)
                elif not self.crossing:
                    source = self.own
                elif number == 0:
                    continue
                else:
                    self.landed(block, self.sems[2].at[0])
                self.spread(k, side, zi, ok, part, source)

    def across(self, k):
        place, depth = self.place, self.place.depth
        y_recv, c_send, c_recv = self.sems[6:9]
        for zi, ok in place.wave(k):
            for part in self.parts:
                block = self.block(zi, 1 - place.y, place.c, part)
                self.landed(block, y_recv.at[self.slot(zi, part)], ok)
                slot = 2 * depth + self.slot(zi, part)
                self.send(block, block, c_send.at[slot], c_recv.at[slot], place.flip_c(), ok)

    def take(self, k):
        place, depth = self.place, self.place.depth
        c_recv = self.sems[8]
        for zi, ok in place.wave(k):
            for part in self.parts:
                slot = self.slot(zi, part)
                self.landed(self.block(zi, place.y, 1 - place.c, part), c_recv.at[slot], ok)
                slot = 2 * depth + slot
                self.landed(self.block(zi, 1 - place.y, 1 - place.c, part), c_recv.at[slot], ok)

    def settle(self):
        for copy, condition in self.sent:
            guard(condition, copy.wait_send)


class PairReduce:
    def __init__(self, place, own, out, buffers, sems, causal=False, crossing=False):
        self.place, self.own, self.out, self.sems = place, own, out, sems
        self.from_core, self.from_y, self.line, self.from_x = buffers
        self.causal, self.crossing = causal, crossing
        self.sent = []

    @staticmethod
    def scratch(depth, block):
        buffers = [
            pltpu.VMEM((depth, 2, 2) + block, BF16),
            pltpu.VMEM((depth, 2) + block, BF16),
            pltpu.VMEM((depth + 1, 2) + block, BF16),
            pltpu.VMEM((1,) + block, BF16),
        ]
        sems = [DMA((2 * depth,)), DMA((2 * depth,)), DMA((depth,)), DMA((depth,))]
        sems += [DMA((2 * depth,)), DMA((2 * depth,)), DMA((1,)), DMA((1,))]
        return buffers, sems

    def wave(self, k):
        waves = self.place.wave(k)
        return waves[:1] if self.causal else waves

    def send(self, src, dst, send_sem, recv_sem, device, condition=None):
        copy = remote(src, dst, send_sem, recv_sem, device)
        guard(condition, copy.start)
        self.sent.append((copy, condition))

    def landed(self, ref, recv_sem):
        remote(ref, ref, self.sems[0].at[0], recv_sem, self.place.flip_c()).wait_recv()

    def add(self, target, term):
        for x in range(2):
            add_into(target.at[x], term.at[x], target.shape[1])

    def cores(self, k):
        place = self.place
        for zi, ok in self.wave(k):
            for y in range(2):
                slot = 2 * zi + y
                self.send(
                    self.own.at[zi, :, y, 1 - place.c],
                    self.from_core.at[zi, y],
                    self.sems[0].at[slot],
                    self.sems[1].at[slot],
                    place.flip_c(),
                    ok,
                )

    def over(self, k):
        place = self.place
        for zi, ok in self.wave(k):

            def body(zi=zi):
                for y in (1 - place.y, place.y):
                    block = self.from_core.at[zi, y]
                    self.landed(block, self.sems[1].at[2 * zi + y])
                    self.add(block, self.own.at[zi, :, y, place.c])
                    if y is not place.y:
                        self.y_copy(zi).start()

            guard(ok, body)
            self.sent.append((self.y_copy(zi), ok))

    def y_copy(self, zi):
        place = self.place
        return remote(
            self.from_core.at[zi, 1 - place.y],
            self.from_y.at[zi],
            self.sems[2].at[zi],
            self.sems[3].at[zi],
            place.flip_y(),
        )

    def z_copy(self, k, side, zi):
        depth = self.place.depth
        direction = 1 - side
        slot = direction * depth + zi
        there = self.line.at[depth if k == 1 and direction == 1 else zi]
        to = self.place.z_up() if side == 1 else self.place.z_down()
        return remote(
            self.from_y.at[zi], there, self.sems[4].at[slot], self.sems[5].at[slot], to
        )

    def along(self, k):
        place, depth = self.place, self.place.depth
        for side, (zi, ok) in enumerate(self.wave(k)):
            block = self.from_y.at[zi]

            def body(zi=zi, side=side, block=block):
                self.landed(block, self.sems[3].at[zi])
                self.add(block, self.from_core.at[zi, place.y])

                def more(direction):
                    term = self.line.at[depth if k == 0 and direction == 1 else zi]
                    self.landed(term, self.sems[5].at[direction * depth + zi])
                    self.add(block, term)

                if k == 0:
                    if not self.causal:
                        pl.when(place.down)(functools.partial(more, 0))
                    pl.when(place.up)(functools.partial(more, 1))
                elif side == 0:
                    pl.when(place.up)(functools.partial(more, 1))
                else:
                    pl.when(place.down)(functools.partial(more, 0))
                if k > 0:
                    self.z_copy(k, side, zi).start()

            guard(ok, body)
            if k > 0:
                self.sent.append((self.z_copy(k, side, zi), ok))

    def swap(self):
        place = self.place
        self.send(
            self.from_y.at[place.z, 1 - place.x],
            self.from_x.at[0],
            self.sems[6].at[0],
            self.sems[7].at[0],
            place.flip_x(),
        )

    def finish(self):
        place = self.place
        if self.crossing:
            self.landed(self.from_x.at[0], self.sems[7].at[0])
            self.out[place.x] = self.from_y[place.z, place.x].astype(self.out.dtype)
            self.out[1 - place.x] = self.from_x[0].astype(self.out.dtype)
        else:
            self.out[...] = self.from_y[place.z].astype(self.out.dtype)

    def settle(self):
        for copy, condition in self.sent:
            guard(condition, copy.wait_send)


class Exchange:
    def __init__(self, place, own, out, sems):
        self.place, self.own, self.out, self.sems = place, own, out, sems
        self.count = 2 * place.depth
        self.sent = []
        self.y_f = place.f + 2 - 4 * place.y
        self.c_f = place.f + 1 - 2 * place.c
        self.yc_f = self.y_f + 1 - 2 * place.c

    @staticmethod
    def semaphores(depth):
        count = 2 * depth
        return [
            DMA((1,)),
            DMA((count,)),
            DMA((count,)),
            DMA((count,)),
            DMA((count,)),
            DMA((2 * count,)),
            DMA((2 * count,)),
        ]

    def send(self, block, send_sem, recv_sem, device, source=None):
        copy = remote(block if source is None else source, block, send_sem, recv_sem, device)
        copy.start()
        self.sent.append(copy)

    def block(self, offset, owner):
        origin = lax.rem(self.place.s + self.count - offset, self.count)
        return self.out.at[:, origin, owner]

    def landed(self, block, recv_sem):
        remote(block, block, self.sems[1].at[0], recv_sem, self.place.flip_c()).wait_recv()

    def local(self):
        return pltpu.make_async_copy(
            self.own.at[:, self.place.s], self.block(0, self.place.f), self.sems[0].at[0]
        )

    def depart(self, offset):
        place = self.place
        to = lax.rem(place.s + offset, self.count)
        self.send(
            self.block(0, place.f),
            self.sems[1].at[offset],
            self.sems[2].at[offset],
            (to, place.f),
            self.own.at[:, to],
        )

    def onward(self, offset):
        place = self.place
        block = self.block(offset, place.f)
        if offset > 0:
            self.landed(block, self.sems[2].at[offset])
        self.send(block, self.sems[3].at[offset], self.sems[4].at[offset], place.flip_y())
        slot = 2 * offset
        self.send(block, self.sems[5].at[slot], self.sems[6].at[slot], place.flip_c())

    def sideways(self, offset):
        block = self.block(offset, self.y_f)
        self.landed(block, self.sems[4].at[offset])
        slot = 2 * offset + 1
        self.send(block, self.sems[5].at[slot], self.sems[6].at[slot], self.place.flip_c())

    def last(self, offset):
        self.landed(self.block(offset, self.c_f), self.sems[6].at[2 * offset])
        self.landed(self.block(offset, self.yc_f), self.sems[6].at[2 * offset + 1])

    def settle(self):
        for copy in self.sent:
            copy.wait_send()


class Quarter:
    def __init__(self, place, own, out, sems):
        self.place, self.own, self.out, self.sems = place, own, out, sems
        self.sent = []

    @staticmethod
    def semaphores():
        return [DMA((1,)), DMA((3,)), DMA((3,))]

    def local(self):
        return pltpu.make_async_copy(self.own, self.out.at[self.place.f], self.sems[0].at[0])

    def send(self, source, block, slot, device):
        copy = remote(source, block, self.sems[1].at[slot], self.sems[2].at[slot], device)
        copy.start()
        self.sent.append(copy)

    def depart(self):
        place = self.place
        self.send(self.own, self.out.at[place.f], 0, place.flip_y())
        self.send(self.own, self.out.at[place.f], 1, place.flip_c())

    def landed(self, owner, slot):
        block = self.out.at[owner]
        remote(block, block, self.sems[1].at[0], self.sems[2].at[slot], self.place.flip_c()).wait_recv()

    def sideways(self):
        place = self.place
        y_f = place.f + 2 - 4 * place.y
        self.landed(y_f, 0)
        self.send(self.out.at[y_f], self.out.at[y_f], 2, place.flip_c())

    def last(self):
        place = self.place
        self.landed(place.f + 1 - 2 * place.c, 1)
        self.landed(place.f + 2 - 4 * place.y + 1 - 2 * place.c, 2)

    def settle(self):
        for copy in self.sent:
            copy.wait_send()


def stage(gather, step):
    depth = gather.place.depth
    if step < depth:
        gather.arrive(step)
    if 0 <= step - 1 < depth:
        gather.across(step - 1)
    if isinstance(gather, PairGather):
        if 0 <= step - 2 < depth:
            gather.take(step - 2)
        return
    if gather.wide and 0 <= step - 2 < depth:
        gather.hand(step - 2)
    if gather.wide and 0 <= step - 3 < depth:
        gather.take(step - 3)


def turned(vector, cosine, sine):
    return vector * cosine + pltpu.roll(vector, HEAD_DIM // 2, 1) * sine


HEAD_PLAN = (
    ("tables", "P0", "wide", "P1", "P2", "d1", "d5", "P3", "o0", "d7", "P4", "P5", "project", "K0", "o1", "c0", "n7"),
    ("K1", "K2", "d2", "K3", "K4", "o2", "d6", "c1", "K5", "n0", "A0", "d4", "A1", "o3", "A2"),
    ("o4", "s0", "n6", "A3", "s7", "o5", "mix", "n1", "n5", "d3", "o6", "D", "after", "h0", "keep", "h1"),
    ("c2", "s1", "n4", "n3", "s6", "s5", "h2", "n2", "c3", "S", "s3", "s4", "s2", "h3", "h4", "c4"),
)
HEAD_INS = 12
HEAD_OUTS = 16


def head_kernel(depth, *refs):
    (o_own, gate_far, up_far, down_far, q_own, k_own, v_own, small_own) = refs[:8]
    (tokens, cot, frequency, lengths) = refs[8:HEAD_INS]
    (
        pack_out,
        o_out,
        kv_out,
        cot_out,
        wide_out,
        down_out,
        hidden_out,
        queries_out,
        mixed_out,
        lse_out,
        middle_out,
        hidden_pair_out,
        mixed_low_out,
        pair_out,
        angles_out,
        begin,
    ) = refs[HEAD_INS : HEAD_INS + HEAD_OUTS]
    vectors = refs[HEAD_INS + HEAD_OUTS]
    rest = refs[HEAD_INS + HEAD_OUTS + 1 :]
    pack_all, o_all, kv_all, kv_own, hidden_two, lin, m_acc, l_acc, o_acc = rest[:9]
    pack, wide, down, mixed_pair, mixed_far, spread = rest[9:15]
    queries, mixed, lse, middle, hidden_pair, mixed_low, pair, angles = rest[15:23]
    gate_own, up_own, down_own = rest[23:26]
    sems = list(rest[26:])

    def take(count):
        taken = sems[:count]
        del sems[:count]
        return taken

    wide_need = len(Gather.semaphores(depth, True))
    line_need = len(Gather.semaphores(depth, False))
    count = 2 * depth
    devices = 4 * count
    rows, model = tokens.shape
    key_width = KV_HEADS * HEAD_DIM
    group_width = GROUP * HEAD_DIM
    qkv_width = group_width + 2 * HEAD_DIM

    place = Place(depth)
    for g in range(KV_HEADS):
        at = 0
        for source in (q_own, k_own, v_own):
            width = source.shape[1] // KV_HEADS
            pack[g, :, at : at + width] = source[:, g * width : (g + 1) * width]
            at += width
        pack[g, :, at:] = small_own[...]
    greet(place, [(lax.rem(place.s + offset, count), place.f) for offset in range(1, count)])
    pair_need = len(PairGather.semaphores(depth))
    g_pack = PairGather(place, pack, pack_all, take(pair_need), True)
    g_o = Gather(place, True, o_own, o_all, take(wide_need))
    g_kv = PairGather(place, kv_own, kv_all, take(pair_need), False)
    g_cot = Gather(place, False, cot, cot_out, take(line_need + 2), True)
    g_hidden = Gather(place, False, hidden_two, hidden_out, take(line_need))
    x_wide = Exchange(place, wide, wide_out, take(len(Exchange.semaphores(depth))))
    x_down = Quarter(place, down, down_out, take(len(Quarter.semaphores())))
    out_sem, x_send, x_recv, far_sem = take(4)
    far_loads = [
        pltpu.make_async_copy(source, target, far_sem.at[number])
        for number, (source, target) in enumerate(
            ((gate_far, gate_own), (up_far, up_own), (down_far, down_own))
        )
    ]
    for copy in far_loads:
        copy.start()

    g_pack.begin()
    token_copy = remote(
        tokens, pair.at[place.x], x_send.at[0], x_recv.at[0], place.flip_x()
    )
    token_copy.start()
    pair[place.x] = tokens[...]
    pack_local = g_pack.local()
    pack_local.start()
    pack_local.wait()
    few = down_own.shape[0]
    filled = down.shape[0]
    locals_ = [job.local() for job in (g_o, g_cot, x_wide, x_down)]
    for copy in locals_[:2]:
        copy.start()
    inputs = tokens[...].astype(F32)

    def pack_wide():
        for copy in far_loads[:2]:
            copy.wait()
        for side, source in enumerate((gate_own, up_own)):
            for to in range(count):
                parts = []
                for owner in range(4):
                    low = (4 * to + owner) * few
                    parts.append(source[:, low : low + few])
                    parts.append(jnp.zeros((wide.shape[2], filled - few), BF16))
                wide[side, to] = jnp.concatenate(parts, axis=1)
        locals_[2].start()

    def tables():
        far_loads[2].wait()
        down[...] = jnp.concatenate(
            [down_own[...], jnp.zeros((filled - few, model), BF16)], axis=0
        )
        locals_[3].start()
        ahead = lax.broadcasted_iota(jnp.int32, (1, HEAD_DIM), 1) < HEAD_DIM // 2
        for x in range(2):
            first_row = ((2 * place.z + x) * 4 + place.f) * rows
            positions = first_row + lax.broadcasted_iota(jnp.int32, (rows, 1), 0)
            start, found = jnp.int32(0), jnp.zeros((rows, 1), jnp.int32)
            for number in range(lengths.shape[0]):
                found = jnp.where(positions >= start, start, found)
                start = start + lengths[number]
            begin[x] = found
            turns = (positions - found).astype(F32) * frequency[...]
            angles[x, 0] = jnp.cos(turns)
            sine = jnp.sin(turns)
            angles[x, 1] = jnp.where(ahead, -sine, sine)

    part = model // depth
    own_head = pl.ds(pl.multiple_of(place.x * HEAD_DIM, HEAD_DIM), HEAD_DIM)
    own_heads = pl.ds(pl.multiple_of(place.x * group_width, group_width), group_width)
    kv_local = g_kv.local()
    hidden_local = g_hidden.local()
    mixed_copy = remote(
        mixed_pair.at[1 - place.x], mixed_far, x_send.at[1], x_recv.at[1], place.flip_x()
    )

    def project():
        share = key_width // devices
        chosen = lax.broadcasted_iota(jnp.int32, (model, key_width), 1)
        chosen = lax.div(chosen, share) * (model // devices) + lax.rem(chosen, share)
        chosen = lax.broadcasted_iota(jnp.int32, (model, key_width), 0) == chosen
        small = pack_all[:, :, :, :, :, qkv_width:].reshape(model, 128).astype(F32).T
        vectors[...] = small[:8]
        spread[...] = jnp.dot(
            small[:8].astype(BF16), chosen.astype(BF16), preferred_element_type=F32
        )
        for copy in locals_:
            copy.wait()
        token_copy.wait_recv()
        pair_inputs = pair[...].reshape(2 * rows, model).astype(F32)
        inv_pair = lax.rsqrt(jnp.mean(pair_inputs * pair_inputs, axis=-1, keepdims=True) + EPSILON)
        hidden_pair[...] = (pair_inputs * inv_pair * small[0:1]).astype(BF16)
        for zi in range(depth):
            weights = pack_all[zi][:, :, :, :, :qkv_width].reshape(part, qkv_width)
            term = jnp.dot(
                hidden_pair[:, zi * part : (zi + 1) * part], weights, preferred_element_type=F32
            )
            if zi == 0:
                lin[...] = term
            else:
                lin[...] += term
        for x in range(2):
            at = slice(x * rows, (x + 1) * rows)
            head = lin[at, group_width : group_width + HEAD_DIM] + spread[2:3, own_head]
            kv_own[x, :, :HEAD_DIM] = turned(head, angles[x, 0], angles[x, 1]).astype(BF16)
            values = lin[at, group_width + HEAD_DIM :] + spread[3:4, own_head]
            kv_own[x, :, HEAD_DIM:] = values.astype(BF16)
        kv_local.start()

    def queries_of():
        query_bias = vectors[1:2, own_heads]
        for x in range(2):
            for j in range(GROUP):
                lanes = slice(j * HEAD_DIM, (j + 1) * HEAD_DIM)
                head = lin[x * rows : (x + 1) * rows, lanes] + query_bias[:, lanes]
                queries[x, j * rows : (j + 1) * rows, :] = turned(
                    head, angles[x, 0], angles[x, 1]
                ).astype(BF16)
        kv_local.wait()

    span = 4 * rows
    scale = HEAD_DIM ** (-0.5) * LOG2E
    m_acc[...] = jnp.full_like(m_acc, -1e30)
    l_acc[...] = jnp.zeros_like(l_acc)
    o_acc[...] = jnp.zeros_like(o_acc)
    local_rows = lax.broadcasted_iota(jnp.int32, (rows, span), 0)
    offsets = lax.broadcasted_iota(jnp.int32, (rows, span), 1)

    def attend(number, carry):
        keys_at = number * span + offsets
        block = kv_all.at[lax.div(number, 2), lax.rem(number, 2)]
        key = block[:, :, :, :HEAD_DIM].reshape(span, HEAD_DIM)
        value = block[:, :, :, HEAD_DIM:].reshape(span, HEAD_DIM)
        for x in range(2):
            places = ((2 * place.z + x) * 4 + place.f) * rows + local_rows
            visible = jnp.logical_and(keys_at >= begin[x], keys_at <= places)
            scores = mul_t(queries[x], key)
            scores = scores.reshape(GROUP, rows, span) * scale
            scores = jnp.where(visible[None], scores, -1e30).reshape(GROUP * rows, span)
            old = m_acc[x]
            new = jnp.maximum(old, jnp.max(scores, axis=-1, keepdims=True))
            weights = jnp.exp2(scores - new[:, :1])
            fade = jnp.exp2(old - new)
            l_acc[x] = l_acc[x] * fade + jnp.sum(weights, axis=-1, keepdims=True)
            o_acc[x] = o_acc[x] * fade + jnp.dot(
                weights.astype(BF16), value, preferred_element_type=F32
            )
            m_acc[x] = new
        return carry

    def attend_quarter(piece):
        low, high = piece * count // 4, (piece + 1) * count // 4
        reach = 2 * place.z + 2
        lax.fori_loop(jnp.minimum(low, reach), jnp.minimum(high, reach), attend, 0)

    def mix():
        for x in range(2):
            total = o_acc[x] / l_acc[x]
            mixed[x] = total
            lse[x] = m_acc[x] + jnp.log2(l_acc[x])
            mixed_pair[x] = total.astype(BF16)
        mixed_copy.start()

    def after_attention():
        mixed_copy.wait_recv()
        for j in range(GROUP):
            at = slice(j * rows, (j + 1) * rows)
            near = pl.multiple_of((place.x * GROUP + j) * HEAD_DIM, HEAD_DIM)
            far = pl.multiple_of(((1 - place.x) * GROUP + j) * HEAD_DIM, HEAD_DIM)
            mixed_low[:, pl.ds(near, HEAD_DIM)] = mixed_pair[place.x, at, :]
            mixed_low[:, pl.ds(far, HEAD_DIM)] = mixed_far[at, :]
        after = inputs
        for zi in range(depth):
            after = after + jnp.dot(
                mixed_low[:, zi * part : (zi + 1) * part],
                o_all[zi].reshape(part, model),
                preferred_element_type=F32,
            )
        middle[...] = after
        inv_two = lax.rsqrt(jnp.mean(after * after, axis=-1, keepdims=True) + EPSILON)
        hidden_two[...] = (after * inv_two * vectors[4:5]).astype(BF16)
        hidden_local.start()

    keeps = [
        pltpu.make_async_copy(source, target, out_sem.at[number])
        for number, (source, target) in enumerate(
            (
                (pack_all, pack_out),
                (o_all, o_out),
                (kv_all, kv_out),
                (queries, queries_out),
                (mixed, mixed_out),
                (lse, lse_out),
                (middle, middle_out),
                (hidden_pair, hidden_pair_out),
                (mixed_low, mixed_low_out),
                (pair, pair_out),
                (angles, angles_out),
            )
        )
    ]

    def keep():
        for copy in keeps:
            copy.start()

    jobs = {"P": g_pack, "K": g_kv, "o": g_o, "c": g_cot, "h": g_hidden}
    moves = {"d": x_wide.depart, "n": x_wide.onward, "s": x_wide.sideways, "A": attend_quarter}
    works = {
        "wide": pack_wide,
        "tables": tables,
        "project": project,
        "mix": mix,
        "after": after_attention,
        "keep": keep,
        "D": x_down.depart,
        "S": x_down.sideways,
    }
    for words in HEAD_PLAN:
        for word in words:
            if word in works:
                works[word]()
            elif word[0] in moves:
                moves[word[0]](int(word[1:]))
            else:
                stage(jobs[word[0]], int(word[1:]))
                if word == "K0":
                    queries_of()

    hidden_local.wait()
    for offset in range(count):
        x_wide.last(offset)
    x_down.last()
    for copy in keeps:
        copy.wait()
    token_copy.wait_send()
    mixed_copy.wait_send()
    for job in (g_pack, g_o, g_kv, g_cot, g_hidden, x_wide, x_down):
        job.settle()


def call_head(depth, collective_id, hbm, vmems, lengths):
    o_own, gate_own, _, down_own = hbm
    q_own, k_own, v_own, small_own, tokens, cot = vmems[:6]
    count = 2 * depth
    few = down_own.shape[0]
    filled = -(-few // 16) * 16
    qkv_width = (GROUP + 2) * HEAD_DIM
    width = qkv_width + small_own.shape[1]
    pack = jax.ShapeDtypeStruct((q_own.shape[0], width), BF16)
    wide = jax.ShapeDtypeStruct((2, count, gate_own.shape[0], 4 * filled), BF16)
    down = jax.ShapeDtypeStruct((filled, down_own.shape[1]), BF16)
    rows, model = tokens.shape
    key_width = KV_HEADS * HEAD_DIM
    stacked = GROUP * rows
    kv_own = jax.ShapeDtypeStruct((rows, 2 * HEAD_DIM), BF16)
    any_, vmem = pl.BlockSpec(memory_space=pl.ANY), pl.BlockSpec(memory_space=pltpu.VMEM)
    heads = (KV_HEADS, stacked, HEAD_DIM)
    outs = [
        gather_shape(depth, True, pack),
        gather_shape(depth, True, o_own),
        gather_shape(depth, True, kv_own),
        gather_shape(depth, False, cot),
        jax.ShapeDtypeStruct((2, count, 4) + wide.shape[2:], BF16),
        jax.ShapeDtypeStruct((4,) + down.shape, BF16),
        gather_shape(depth, False, tokens),
        jax.ShapeDtypeStruct(heads, BF16),
        jax.ShapeDtypeStruct(heads, F32),
        jax.ShapeDtypeStruct(heads, F32),
        jax.ShapeDtypeStruct((rows, model), F32),
        jax.ShapeDtypeStruct((2 * rows, model), BF16),
        jax.ShapeDtypeStruct((rows, model), BF16),
        jax.ShapeDtypeStruct((2, rows, model), BF16),
        jax.ShapeDtypeStruct((2, 2, rows, HEAD_DIM), F32),
        jax.ShapeDtypeStruct((2, rows, 1), jnp.int32),
        jax.ShapeDtypeStruct((8, model), F32),
    ]
    scratch = [pltpu.VMEM(out.shape, BF16) for out in outs[:3]]
    scratch += [
        pltpu.VMEM((2,) + kv_own.shape, BF16),
        pltpu.VMEM((rows, model), BF16),
        pltpu.VMEM((2 * rows, qkv_width), F32),
        pltpu.VMEM(heads, F32),
        pltpu.VMEM(heads, F32),
        pltpu.VMEM(heads, F32),
        pltpu.VMEM((KV_HEADS,) + pack.shape, BF16),
        pltpu.VMEM(wide.shape, BF16),
        pltpu.VMEM(down.shape, BF16),
        pltpu.VMEM(heads, BF16),
        pltpu.VMEM(heads[1:], BF16),
        pltpu.VMEM((8, key_width), F32),
    ]
    scratch += [pltpu.VMEM(out.shape, out.dtype) for out in outs[7:15]]
    scratch += [pltpu.VMEM(array.shape, BF16) for array in hbm[1:]]
    scratch += PairGather.semaphores(depth) + Gather.semaphores(depth, True)
    scratch += PairGather.semaphores(depth)
    scratch += Gather.semaphores(depth, False, True) + Gather.semaphores(depth, False)
    scratch += Exchange.semaphores(depth) + Quarter.semaphores()
    scratch += [DMA((11,)), DMA((2,)), DMA((2,)), DMA((3,))]
    return pl.pallas_call(
        functools.partial(head_kernel, depth),
        out_shape=outs,
        in_specs=[any_] * len(hbm) + [vmem] * len(vmems) + [pl.BlockSpec(memory_space=pltpu.SMEM)],
        out_specs=[any_] * 15 + [vmem] * 2,
        scratch_shapes=scratch,
        compiler_params=pltpu.CompilerParams(
            collective_id=collective_id, has_side_effects=True, vmem_limit_bytes=VMEM_LIMIT
        ),
    )(*hbm, *vmems, lengths)


def t_mul(left, right):
    return lax.dot_general(left, right, (((0,), (0,)), ((), ())), preferred_element_type=F32)


def mul_t(left, right):
    return lax.dot_general(left, right, (((1,), (1,)), ((), ())), preferred_element_type=F32)


CUTS = ((0, 512), (512, 1024), (1024, 1152))


def middle_kernel(depth, *refs):
    (hidden_all, cot_all, wide_all, down_all, o_own) = refs[:5]
    (middle, cotangent, vectors) = refs[5:8]
    (layer_out, d_middle, d_mixed, d_branch, gain_two, down_out, wide_out) = refs[8:15]
    (tokens_v, grads_v, w_part, d_part, act, d_both, dh_part, out_part) = refs[15:23]
    (dh_sum, out_sum, w_core, w_y, d_core, o_all) = refs[23:29]
    rest = list(refs[29:])

    def take(count):
        taken = rest[:count]
        del rest[:count]
        return taken

    count = 2 * depth
    rows, model = middle.shape
    units = act.shape[2]
    part = model // depth
    buffers, sems = Reduce.scratch(depth, False, (rows, model))
    place = Place(depth)
    r_dh = Reduce(place, False, rows, dh_part, dh_sum, take(len(buffers)), take(len(sems)))
    r_out = Reduce(place, False, rows, out_part, out_sum, take(len(buffers)), take(len(sems)))
    load_sem, wc_send, wc_recv, wy_send, wy_recv, dc_send, dc_recv = take(7)
    sent = []

    def send(src, dst, send_sem, recv_sem, device):
        copy = remote(src, dst, send_sem, recv_sem, device)
        copy.start()
        sent.append(copy)

    def landed(ref, recv_sem):
        remote(ref, ref, wc_send.at[0], recv_sem, place.flip_c()).wait_recv()

    loads = [
        pltpu.make_async_copy(source, target, load_sem.at[number])
        for number, (source, target) in enumerate(
            (
                (hidden_all, tokens_v),
                (wide_all, w_part),
                (cot_all, grads_v),
                (down_all, d_part),
            )
        )
    ]
    for copy in loads:
        copy.start()
    greet(place)
    mine_y, other_y = place.y, 1 - place.y
    wide_rows = w_part.shape[-2]
    half = lax.div(place.z, 2)
    tiles = [3 - 3 * half, 2 - half, 1 + 4 * half - place.z, place.z]
    for copy in loads:
        copy.wait()

    def weights(side, low, high):
        return w_part[side, :, :, :, :, low:high].reshape(model, high - low)

    def forward(zi):
        tokens = tokens_v[zi].reshape(2 * rows, model)
        grads = grads_v[zi].reshape(2 * rows, model)
        out = None
        for low, high in CUTS:
            gate = jnp.dot(tokens, weights(0, low, high), preferred_element_type=F32)
            up = jnp.dot(tokens, weights(1, low, high), preferred_element_type=F32)
            d_act = mul_t(grads, d_part[low:high, :])
            sigma = jax.nn.sigmoid(gate)
            silu = gate * sigma
            act[zi, :, low:high] = (silu * up).astype(BF16)
            d_both[zi, :, low:high] = (
                d_act * up * sigma * (1.0 + gate * (1.0 - sigma))
            ).astype(BF16)
            d_both[zi, :, units + low : units + high] = (d_act * silu).astype(BF16)
        total = mul_t(d_both[zi, :, :units], weights(0, 0, units))
        total = total + mul_t(d_both[zi, :, units:], weights(1, 0, units))
        dh_part[zi] = total.astype(BF16).reshape(2, rows, model)
        out = jnp.dot(act[zi], d_part[...], preferred_element_type=F32)
        out_part[zi] = out.astype(BF16).reshape(2, rows, model)

    def tile(number, carry):
        zi = jnp.where(
            number == 0,
            tiles[0],
            jnp.where(number == 1, tiles[1], jnp.where(number == 2, tiles[2], tiles[3])),
        )
        forward(zi)
        r_dh.cross(zi)
        return carry

    lax.fori_loop(0, depth, tile, 0)
    for zi in tiles:
        r_out.cross(zi)
    r_dh.crossed()
    r_out.crossed()

    def wide_chunk(k, carry):
        lanes = pl.ds(pl.multiple_of(k * part, part), part)
        tokens = tokens_v[:, :, :, lanes].reshape(count * rows, part)
        term = t_mul(tokens, d_both[...].reshape(count * rows, 2 * units))
        for side in range(2):
            w_part[side, pl.ds(2 * k, 2)] = (
                term[:, side * units : (side + 1) * units]
                .astype(BF16)
                .reshape(2, 2, 2, wide_rows, units)
            )
        for step in range(2):
            to = 2 * k + step
            for y in range(2):
                remote(
                    w_part.at[:, to, y, 1 - place.c],
                    w_core.at[y, to],
                    wc_send.at[2 * to + y],
                    wc_recv.at[2 * to + y],
                    place.flip_c(),
                ).start()
        return carry

    def wide_cores(to):
        for y in (other_y, mine_y):
            landed(w_core.at[y, to], wc_recv.at[2 * to + y])
            for side in range(2):
                add_into(
                    w_core.at[y, to, side], w_part.at[side, to, y, place.c], wide_rows
                )
            if y is other_y:
                remote(
                    w_core.at[y, to], w_y.at[to], wy_send.at[to], wy_recv.at[to], place.flip_y()
                ).start()

    def wide_across(to, carry):
        landed(w_y.at[to], wy_recv.at[to])
        for side in range(2):
            add_into(w_y.at[to, side], w_core.at[mine_y, to, side], wide_rows)
        pltpu.make_async_copy(w_y.at[to], wide_out.at[to], load_sem.at[to]).start()
        return carry

    def wide_step(k, carry):
        wide_chunk(k, 0)
        pl.when(k > 0)(lambda: wide_cores(2 * k - 2))
        pl.when(k > 0)(lambda: wide_cores(2 * k - 1))
        return carry

    order = list(range(depth - 1, -1, -1))
    lax.fori_loop(0, depth - 2, wide_step, 0)
    r_dh.along(order[0])
    r_dh.along(order[1])
    lax.fori_loop(depth - 2, depth, wide_step, 0)
    wide_cores(count - 2)
    wide_cores(count - 1)
    r_dh.along(order[2])
    pieces = [
        pltpu.make_async_copy(o_own.at[zi], o_all.at[zi % 2], load_sem.at[zi])
        for zi in range(depth)
    ]
    for copy in pieces[:2]:
        copy.start()

    def down_chunk(k, carry):
        lanes = pl.ds(pl.multiple_of(k * 384, 384), 384)
        chunk = act[:, :, lanes].reshape(count * rows, 384)
        d_part[lanes, :] = t_mul(chunk, grads_v[...].reshape(count * rows, model)).astype(BF16)
        return carry

    lax.fori_loop(0, units // 384, down_chunk, 0)
    down_rows = units // 4

    def down_block(owner):
        return d_part.at[pl.ds(pl.multiple_of(owner * down_rows, down_rows), down_rows)]

    for y in (other_y, mine_y):
        send(
            down_block(2 * y + 1 - place.c),
            d_core.at[y],
            dc_send.at[y],
            dc_recv.at[y],
            place.flip_c(),
        )
    r_dh.along(order[3])
    r_dh.finish()

    after = middle[...]
    inv_two = lax.rsqrt(jnp.mean(after * after, axis=-1, keepdims=True) + EPSILON)
    normed = after * inv_two
    d_hidden = dh_sum[...]
    gain_two[...] = jnp.broadcast_to(
        jnp.sum(d_hidden * normed, axis=0, keepdims=True), gain_two.shape
    )
    scaled = d_hidden * vectors[4:5]
    total = cotangent[...].astype(F32) + inv_two * (
        scaled - normed * jnp.mean(scaled * normed, axis=-1, keepdims=True)
    )
    d_middle[...] = total
    d_branch[...] = total.astype(BF16)
    for zi in range(depth):
        pieces[zi].wait()
        term = mul_t(d_branch[...], o_all[zi % 2].reshape(part, model)).astype(BF16)
        for piece in range(part // HEAD_DIM):
            h = zi * (part // HEAD_DIM) + piece
            at = (h % GROUP) * rows
            d_mixed[h // GROUP, at : at + rows, :] = term[
                :, piece * HEAD_DIM : (piece + 1) * HEAD_DIM
            ]
        if zi + 2 < depth:
            pieces[zi + 2].start()
    for y in (other_y, mine_y):
        landed(d_core.at[y], dc_recv.at[y])
        add_into(d_core.at[y], down_block(2 * y + place.c), down_rows)
    keep = pltpu.make_async_copy(d_core, down_out, load_sem.at[count])
    keep.start()
    for step in range(depth):
        r_out.along(order[step])
        lax.fori_loop(2 * step, 2 * step + 2, wide_across, 0)
    r_out.finish()
    layer_out[...] = (middle[...] + out_sum[...]).astype(BF16)
    keep.wait()

    def end(to, carry):
        pltpu.make_async_copy(w_y.at[to], wide_out.at[to], load_sem.at[to]).wait()
        for y in range(2):
            slot = 2 * to + y
            remote(
                w_core.at[y, to], w_core.at[y, to], wc_send.at[slot], wc_recv.at[slot], place.flip_c()
            ).wait_send()
        remote(
            w_y.at[to], w_y.at[to], wy_send.at[to], wy_recv.at[to], place.flip_y()
        ).wait_send()
        return carry

    lax.fori_loop(0, count, end, 0)
    r_dh.settle()
    r_out.settle()
    for copy in sent:
        copy.wait_send()


def call_middle(depth, collective_id, hbm, vmems):
    hidden, cot, wide, down, o_all = hbm
    count = 2 * depth
    rows, model = vmems[0].shape
    units, wide_rows = wide.shape[-1], wide.shape[-2]
    any_, vmem = pl.BlockSpec(memory_space=pl.ANY), pl.BlockSpec(memory_space=pltpu.VMEM)
    buffers, sems = Reduce.scratch(depth, False, (rows, model))
    scratch = [pltpu.VMEM((depth, 2, rows, model), BF16)] * 2
    scratch += [pltpu.VMEM(wide.shape, BF16), pltpu.VMEM(down.shape, BF16)]
    scratch += [pltpu.VMEM((depth, 2 * rows, width), BF16) for width in (units, 2 * units)]
    scratch += [pltpu.VMEM((depth, 2, rows, model), BF16)] * 2
    scratch += [pltpu.VMEM((rows, model), F32)] * 2
    scratch += [
        pltpu.VMEM((2, count, 2, wide_rows, units), BF16),
        pltpu.VMEM((count, 2, wide_rows, units), BF16),
        pltpu.VMEM((2, units // 4, model), BF16),
        pltpu.VMEM((2,) + o_all.shape[1:], BF16),
    ]
    scratch += buffers + sems + buffers + sems
    scratch += [DMA((count + 1,)), DMA((2 * count,)), DMA((2 * count,))]
    scratch += [DMA((count,)), DMA((count,)), DMA((2,)), DMA((2,))]
    return pl.pallas_call(
        functools.partial(middle_kernel, depth),
        out_shape=[
            jax.ShapeDtypeStruct((rows, model), BF16),
            jax.ShapeDtypeStruct((rows, model), F32),
            jax.ShapeDtypeStruct((KV_HEADS, GROUP * rows, HEAD_DIM), BF16),
            jax.ShapeDtypeStruct((rows, model), BF16),
            jax.ShapeDtypeStruct((8, model), F32),
            jax.ShapeDtypeStruct((2, units // 4, model), BF16),
            jax.ShapeDtypeStruct((count, 2, wide_rows, units), BF16),
        ],
        in_specs=[any_] * 5 + [vmem] * 3,
        out_specs=[vmem] * 5 + [any_] * 2,
        scratch_shapes=scratch,
        compiler_params=pltpu.CompilerParams(
            collective_id=collective_id, has_side_effects=True, vmem_limit_bytes=VMEM_JOINED
        ),
    )(*hbm, *vmems)


LAST_PLAN = (
    ("d7", "d4", "d2", "d3", "down", "delta", "a0", "a1", "out"),
    ("Ck1", "Ck0", "Yk1", "d5", "Co0", "d1", "Co2", "Bo0", "a2"),
    ("Ck2", "Yk0", "a3", "Bo2", "Zk0", "Ck3", "turn", "Yk3", "Yk2"),
    ("Co1", "Zk1", "Co3", "hq", "Bo1", "query", "Zk2", "Bo3", "Cq0"),
    ("Cq2", "Ao0", "Cq1", "Zk3", "key", "Ao1", "Ao2", "d6", "hk"),
    ("kg", "small", "Cs0", "Yq0", "Cs2", "Cs1", "Zo0", "Yq1", "Ys0"),
    ("Cq3", "Ys2", "Yq2", "Zo1", "Cs3", "Zq0", "Ys1", "Ys3", "Zo2"),
    ("Yq3", "Ao3", "input", "Zs0", "Zq1", "Zs1", "Zq2", "Zs2", "Zq3"),
    ("Xq", "Zs3", "Xs", "Zo3"),
)


def follow_last(plan, works, depart, attend_wave, jobs):
    depth = 4
    steps = {"C": "cores", "B": "over_second", "A": "over_first", "Z": "along", "Y": "over"}
    for words in plan:
        for word in words:
            if word in works:
                works[word]()
            elif word[0] == "d":
                depart(int(word[1:]))
            elif word[0] == "a":
                attend_wave(int(word[1:]))
            else:
                getattr(jobs[word[1]], steps[word[0]])(depth - 1 - int(word[2:]))


def last_kernel(depth, *refs):
    (kv_own, pack_own, wide, down) = refs[:4]
    (d_mixed, angles, begin, vectors, gain_two) = refs[4:9]
    late_own = refs[9:17]
    (input_grad, q_out, kvs_out, o_out, down_out, wide_out) = refs[17:23]
    (kv_all, weights, d_query, delta, d_lin, d_keys, d_kv) = refs[23:30]
    (o_part, q_part, kvs_part) = refs[30:33]
    (d_near, d_far, d_hidden, kv_weights, d_pair, h_send, h_far, lines, pairs) = refs[33:42]
    late = refs[42:50]
    queries, mixed, lse, mixed_low, d_branch, hidden_pair, pair, d_middle = late
    rest = list(refs[50:])

    def take(number):
        taken = rest[:number]
        del rest[:number]
        return taken

    count = 2 * depth
    devices = 4 * count
    _, rows, model = pair.shape
    part = model // depth
    key_width = KV_HEADS * HEAD_DIM
    group_width = GROUP * HEAD_DIM
    qkv_width = group_width + 2 * HEAD_DIM
    model_rows = model // devices
    share = key_width // devices
    span = 4 * rows
    score_scale = HEAD_DIM ** (-0.5)
    scale = score_scale * LOG2E

    place = Place(depth)
    buffers, sems = Reduce.scratch(depth, True, o_part.shape[-2:])
    r_o = Reduce(
        place, True, model_rows, o_part, o_out, take(len(buffers)), take(len(sems))
    )

    def reduce_of(own, out, causal=False, crossing=True):
        buffers, sems = PairReduce.scratch(depth, own.shape[-2:])
        return PairReduce(
            place, own, out, take(len(buffers)), take(len(sems)), causal, crossing
        )

    r_kv = reduce_of(d_keys, d_kv, True, False)
    r_q = reduce_of(q_part, q_out)
    r_s = reduce_of(kvs_part, kvs_out)
    load_sem, e_send, e_recv, y_send, y_recv, x_send, x_recv, late_sem = take(8)
    order = list(range(depth - 1, -1, -1))
    sent = []

    def depart(offset):
        to = lax.rem(place.s + offset, count)
        copy = remote(
            wide.at[to], wide_out.at[place.s], e_send.at[offset], e_recv.at[offset], (to, place.f)
        )
        copy.start()
        sent.append(copy)

    kv_load = pltpu.make_async_copy(kv_own, kv_all, load_sem.at[0])
    kv_load.start()
    late_loads = [
        pltpu.make_async_copy(source, target, late_sem.at[number])
        for number, (source, target) in enumerate(zip(late_own, late))
    ]
    for copy in late_loads:
        copy.start()
    own_wide = pltpu.make_async_copy(wide.at[place.s], wide_out.at[place.s], load_sem.at[1])
    own_wide.start()
    down_load = pltpu.make_async_copy(down.at[place.y], d_near, load_sem.at[2 + depth])
    down_load.start()
    greet(place, [(lax.rem(place.s + offset, count), place.f) for offset in range(1, count)])
    mixed_copy = remote(
        d_mixed.at[1 - place.x],
        d_pair.at[place.x],
        x_send.at[0],
        x_recv.at[0],
        place.flip_x(),
    )
    mixed_copy.start()
    sent.append(mixed_copy)
    d_pair[place.x] = d_mixed[place.x]
    down_copy = remote(
        down.at[1 - place.y], d_far, y_send.at[0], y_recv.at[0], place.flip_y()
    )
    hidden_copy = remote(h_send, h_far, x_send.at[1], x_recv.at[1], place.flip_x())
    loads = [
        pltpu.make_async_copy(pack_own.at[zi], weights.at[zi % 2], load_sem.at[2 + zi])
        for zi in range(depth)
    ]

    local_rows = lax.broadcasted_iota(jnp.int32, (rows, span), 0)
    offsets = lax.broadcasted_iota(jnp.int32, (rows, span), 1)

    def attend(number, carry):
        keys_at = number * span + offsets
        z, x_at = lax.div(number, 2), lax.rem(number, 2)
        block = kv_all.at[z, x_at]
        key = block[:, :, :, :HEAD_DIM].reshape(span, HEAD_DIM)
        value = block[:, :, :, HEAD_DIM:].reshape(span, HEAD_DIM)
        d_key, d_value = None, None
        for x in range(2):
            places = ((2 * place.z + x) * 4 + place.f) * rows + local_rows
            visible = jnp.logical_and(keys_at >= begin[x], keys_at <= places)
            scores = mul_t(queries[x], key)
            d_probs = mul_t(d_pair[x], value)
            probs = jnp.exp2(scores * scale - lse[x][:, :1])
            probs = jnp.where(
                visible[None], probs.reshape(GROUP, rows, span), 0.0
            ).reshape(GROUP * rows, span)
            d_scores = (probs * (d_probs - delta[x][:, :1])).astype(BF16)
            d_query[x] += jnp.dot(d_scores, key, preferred_element_type=F32)
            key_term = t_mul(d_scores, queries[x])
            value_term = t_mul(probs.astype(BF16), d_pair[x])
            d_key = key_term if x == 0 else d_key + key_term
            d_value = value_term if x == 0 else d_value + value_term
        target = d_keys.at[z, x_at]
        target[:, :, :, :HEAD_DIM] = d_key.astype(BF16).reshape(2, 2, rows, HEAD_DIM)
        target[:, :, :, HEAD_DIM:] = d_value.astype(BF16).reshape(2, 2, rows, HEAD_DIM)
        return carry

    def normed_of(rows_of):
        inputs = rows_of.astype(F32)
        inverse = lax.rsqrt(jnp.mean(inputs * inputs, axis=-1, keepdims=True) + EPSILON)
        return inputs * inverse, inverse

    def out_gradient():
        for copy in late_loads[3:5]:
            copy.wait()
        for copy in loads[:2]:
            copy.start()
        for zi in range(depth):
            lanes = slice(zi * part, (zi + 1) * part)
            term = t_mul(mixed_low[:, lanes], d_branch[...]).astype(BF16)
            o_part[zi] = term.reshape(2, 2, 2, model_rows, model)

    def deltas():
        mixed_copy.wait_recv()
        for copy in late_loads[:3]:
            copy.wait()
        for x in range(2):
            delta[x] = jnp.broadcast_to(
                jnp.sum(d_pair[x].astype(F32) * mixed[x], axis=-1, keepdims=True),
                delta.shape[1:],
            )
        d_query[...] = jnp.zeros_like(d_query)
        kv_load.wait()

    def attend_wave(step):
        zi = place.z - order[step]
        low = jnp.maximum(2 * zi, 0)
        high = jnp.maximum(2 * zi + 2, 0)
        lax.fori_loop(low, high, attend, 0)

    def query_turn():
        for x in range(2):
            for j in range(GROUP):
                lanes = slice(j * HEAD_DIM, (j + 1) * HEAD_DIM)
                head = d_query[x, j * rows : (j + 1) * rows, :] * score_scale
                d_lin[x * rows : (x + 1) * rows, lanes] = turned(
                    head, angles[x, 0], -angles[x, 1]
                ).astype(BF16)

    def query_gradient():
        late_loads[5].wait()
        for zi in range(depth):
            lanes = slice(zi * part, (zi + 1) * part)
            term = t_mul(hidden_pair[:, lanes], d_lin[:, :group_width]).astype(BF16)
            q_part[zi] = term.reshape(2, 2, 2, model_rows, group_width)

    def key_turn():
        r_kv.finish()
        for x in range(2):
            at = slice(x * rows, (x + 1) * rows)
            head = d_kv[x, :, :HEAD_DIM] * score_scale
            d_lin[at, group_width : group_width + HEAD_DIM] = turned(
                head, angles[x, 0], -angles[x, 1]
            ).astype(BF16)
            d_lin[at, group_width + HEAD_DIM :] = d_kv[x, :, HEAD_DIM:].astype(BF16)

    def hidden_query():
        for zi in range(depth):
            lanes = slice(zi * part, (zi + 1) * part)
            loads[zi].wait()
            block = weights[zi % 2][:, :, :, :, :group_width].reshape(part, group_width)
            term = mul_t(d_lin[:, :group_width], block)
            for x in range(2):
                d_hidden[x, :, lanes] = term[x * rows : (x + 1) * rows]
            block = weights[zi % 2][:, :, :, :, group_width:qkv_width]
            kv_weights[lanes, :] = block.reshape(part, 2 * HEAD_DIM)
            if zi + 2 < depth:
                loads[zi + 2].start()

    def hidden_key():
        for zi in range(depth):
            lanes = slice(zi * part, (zi + 1) * part)
            term = mul_t(d_lin[:, group_width:], kv_weights[lanes, :])
            for x in range(2):
                d_hidden[x, :, lanes] += term[x * rows : (x + 1) * rows]
        h_send[...] = d_hidden[1 - place.x].astype(BF16)
        hidden_copy.start()

    def key_gradient():
        for zi in range(depth):
            lanes = slice(zi * part, (zi + 1) * part)
            term = t_mul(hidden_pair[:, lanes], d_lin[:, group_width:]).astype(BF16)
            kvs_part[zi, :, :, :, :, : 2 * HEAD_DIM] = term.reshape(
                2, 2, 2, model_rows, 2 * HEAD_DIM
            )

    def small_gradients():
        for copy in late_loads[6:]:
            copy.wait()
        lines[...] = jnp.zeros_like(lines)
        pairs[...] = jnp.zeros_like(pairs)
        bias = jnp.sum(d_lin[...].astype(F32), axis=0, keepdims=True)
        own_head = pl.ds(pl.multiple_of(place.x * HEAD_DIM, HEAD_DIM), HEAD_DIM)
        own_heads = pl.ds(pl.multiple_of(place.x * group_width, group_width), group_width)
        gain_one = jnp.zeros((1, model), F32)
        for x in range(2):
            normed, _ = normed_of(pair[x])
            gain_one = gain_one + jnp.sum(d_hidden[x] * normed, axis=0, keepdims=True)
        lines[0:1, :] = gain_one
        lines[1:2, own_heads] = bias[:, :group_width]
        lines[4:5, :] = gain_two[0:1]
        pairs[0:1, own_head] = bias[:, group_width : group_width + HEAD_DIM]
        pairs[1:2, own_head] = bias[:, group_width + HEAD_DIM :]
        chosen = lax.broadcasted_iota(jnp.int32, (key_width, model), 0)
        chosen = lax.div(chosen, share) * model_rows + lax.rem(chosen, share)
        chosen = (lax.broadcasted_iota(jnp.int32, (key_width, model), 1) == chosen).astype(BF16)
        spread = jnp.dot(pairs[...].astype(BF16), chosen, preferred_element_type=F32)
        lines[2:4, :] = spread[0:2]
        small = jnp.concatenate([lines[...], jnp.zeros((120, model), F32)], axis=0)
        small = small.T.astype(BF16)
        for zi in range(depth):
            kvs_part[zi, :, :, :, :, 2 * HEAD_DIM :] = small[
                zi * part : (zi + 1) * part
            ].reshape(2, 2, 2, model_rows, 128)

    def input_gradient():
        hidden_copy.wait_recv()
        normed, inv_one = normed_of(pair[place.x])
        scaled = (d_hidden[place.x] + h_far[...].astype(F32)) * vectors[0:1]
        input_grad[...] = d_middle[...] + inv_one * (
            scaled - normed * jnp.mean(scaled * normed, axis=-1, keepdims=True)
        )

    works = {
        "out": out_gradient,
        "delta": deltas,
        "turn": query_turn,
        "query": query_gradient,
        "key": key_turn,
        "hq": hidden_query,
        "hk": hidden_key,
        "kg": key_gradient,
        "Xq": r_q.swap,
        "Xs": r_s.swap,
        "small": small_gradients,
        "input": input_gradient,
        "down": down_copy.start,
    }
    jobs = {"o": r_o, "k": r_kv, "q": r_q, "s": r_s}
    follow_last(LAST_PLAN, works, depart, attend_wave, jobs)
    for job in (r_o, r_q, r_s):
        job.finish()
    for offset in range(1, count):
        origin = lax.rem(place.s + count - offset, count)
        block = wide_out.at[origin]
        remote(block, block, e_send.at[0], e_recv.at[offset], place.flip_c()).wait_recv()
    own_wide.wait()
    down_load.wait()
    down_copy.wait()
    down_out[...] = d_near[...].astype(F32) + d_far[...].astype(F32)
    hidden_copy.wait_send()
    for job in (r_kv, r_o, r_q, r_s):
        job.settle()
    for copy in sent:
        copy.wait_send()


def call_last(depth, collective_id, hbm, vmems, late):
    kv_all, pack_all, wide, down = hbm
    pair = late[6]
    count = 2 * depth
    _, rows, model = pair.shape
    model_rows = model // (4 * count)
    key_width, group_width = KV_HEADS * HEAD_DIM, GROUP * HEAD_DIM
    heads = (2, GROUP * rows, HEAD_DIM)
    lead = (depth, 2, 2, 2)
    kv_block, o_block = (rows, 2 * HEAD_DIM), (model_rows, model)
    blocks = [
        (model_rows, group_width),
        (model_rows, 2 * HEAD_DIM + 128),
    ]
    scratch = [
        pltpu.VMEM(kv_all.shape, BF16),
        pltpu.VMEM((2,) + pack_all.shape[1:], BF16),
        pltpu.VMEM(heads, F32),
        pltpu.VMEM(heads, F32),
        pltpu.VMEM((2 * rows, group_width + 2 * HEAD_DIM), BF16),
        pltpu.VMEM(lead + kv_block, BF16),
        pltpu.VMEM((2,) + kv_block, F32),
        pltpu.VMEM(lead + o_block, BF16),
    ]
    scratch += [pltpu.VMEM(lead + block, BF16) for block in blocks]
    scratch += [pltpu.VMEM(down.shape[1:], BF16)] * 2
    scratch += [
        pltpu.VMEM((2, rows, model), F32),
        pltpu.VMEM((model, 2 * HEAD_DIM), BF16),
        pltpu.VMEM(heads, BF16),
        pltpu.VMEM((rows, model), BF16),
        pltpu.VMEM((rows, model), BF16),
        pltpu.VMEM((8, model), F32),
        pltpu.VMEM((8, key_width), F32),
    ]
    scratch += [pltpu.VMEM(array.shape, array.dtype) for array in late]
    buffers, sems = Reduce.scratch(depth, True, o_block)
    scratch += buffers + sems
    for block in [kv_block] + blocks:
        buffers, sems = PairReduce.scratch(depth, block)
        scratch += buffers + sems
    scratch += [DMA((3 + depth,)), DMA((count,)), DMA((count,)), DMA((1,)), DMA((1,))]
    scratch += [DMA((2,)), DMA((2,)), DMA((len(late),))]
    any_, vmem = pl.BlockSpec(memory_space=pl.ANY), pl.BlockSpec(memory_space=pltpu.VMEM)
    return pl.pallas_call(
        functools.partial(last_kernel, depth),
        out_shape=[
            jax.ShapeDtypeStruct((rows, model), F32),
            jax.ShapeDtypeStruct((2,) + blocks[0], F32),
            jax.ShapeDtypeStruct((2,) + blocks[1], F32),
            jax.ShapeDtypeStruct(o_block, F32),
            jax.ShapeDtypeStruct(down.shape[1:], F32),
            jax.ShapeDtypeStruct(wide.shape, BF16),
        ],
        in_specs=[any_] * 4 + [vmem] * len(vmems) + [any_] * len(late),
        out_specs=[vmem] * 6,
        scratch_shapes=scratch,
        compiler_params=pltpu.CompilerParams(
            collective_id=collective_id, has_side_effects=True, vmem_limit_bytes=VMEM_JOINED
        ),
    )(*hbm, *vmems, *late)


def finish_kernel(few, plain, *refs):
    ins, refs = refs[: 4 + plain], refs[4 + plain :]
    outs, vectors, refs = refs[: 6 + plain], refs[6 + plain : 11 + plain], refs[11 + plain :]
    held, refs = refs[: 4 + plain], refs[4 + plain :]
    gate, up, query, key, value, in_sem, out_sem = refs
    loads = [
        pltpu.make_async_copy(source, target, in_sem.at[number])
        for number, (source, target) in enumerate(zip(ins, held))
    ]
    for copy in loads:
        copy.start()
    wide, down, q_in, kvs_in = held[:4]
    filled = wide.shape[3] // 4
    stores = []

    def store(source, number):
        copy = pltpu.make_async_copy(source, outs[number], out_sem.at[number])
        copy.start()
        stores.append(copy)

    loads[0].wait()
    for side, out in enumerate((gate, up)):
        for place in range(wide.shape[0]):
            block = wide[place, side].astype(F32)
            for owner in range(4):
                low = (4 * place + owner) * few
                out[:, low : low + few] = block[:, owner * filled : owner * filled + few]
        store(out, side)
    loads[1].wait()
    store(down.at[pl.ds(0, few)], 2)
    for number in range(plain):
        loads[4 + number].wait()
        store(held[4 + number], 6 + number)
    loads[2].wait()
    loads[3].wait()
    for g in range(KV_HEADS):
        width = q_in.shape[2]
        query[:, g * width : (g + 1) * width] = q_in[g]
        lanes = slice(g * HEAD_DIM, (g + 1) * HEAD_DIM)
        key[:, lanes] = kvs_in[g, :, :HEAD_DIM]
        value[:, lanes] = kvs_in[g, :, HEAD_DIM : 2 * HEAD_DIM]
    for number, source in enumerate((query, key, value)):
        store(source, 3 + number)
    rows_of = (kvs_in[0, :, 2 * HEAD_DIM :] + kvs_in[1, :, 2 * HEAD_DIM :]).T
    for number, out in enumerate(vectors):
        out[...] = rows_of[number : number + 1, : out.shape[1]]
    for copy in stores:
        copy.wait()


def call_finish(few, sizes, wide, down, q_grad, kvs_grad, plain):
    seq, _, rows, _ = wide.shape
    key_width = KV_HEADS * HEAD_DIM
    units = seq * 4 * few
    any_, vmem = pl.BlockSpec(memory_space=pl.ANY), pl.BlockSpec(memory_space=pltpu.VMEM)
    ins = (wide, down, q_grad, kvs_grad, *plain)
    made = [
        jax.ShapeDtypeStruct((rows, units), F32),
        jax.ShapeDtypeStruct((rows, units), F32),
        jax.ShapeDtypeStruct((rows, HEADS * HEAD_DIM), F32),
        jax.ShapeDtypeStruct((rows, key_width), F32),
        jax.ShapeDtypeStruct((rows, key_width), F32),
    ]
    out_shape = made[:2] + [jax.ShapeDtypeStruct((few, down.shape[1]), F32)] + made[2:]
    out_shape += [jax.ShapeDtypeStruct(array.shape, array.dtype) for array in plain]
    out_shape += [jax.ShapeDtypeStruct((1, size), F32) for size in sizes]
    return pl.pallas_call(
        functools.partial(finish_kernel, few, len(plain)),
        out_shape=out_shape,
        in_specs=[any_] * len(ins),
        out_specs=[any_] * (6 + len(plain)) + [vmem] * len(sizes),
        scratch_shapes=[pltpu.VMEM(array.shape, array.dtype) for array in (*ins, *made)]
        + [DMA((len(ins),)), DMA((6 + len(plain),))],
        compiler_params=pltpu.CompilerParams(vmem_limit_bytes=VMEM_LIMIT),
    )(*ins)


def begin_of(positions, lengths):
    ends = jnp.cumsum(lengths)
    starts = ends - lengths
    inside = (positions[:, None] >= starts[None, :]) & (positions[:, None] < ends[None, :])
    return jnp.sum(jnp.where(inside, starts[None, :], 0), axis=1)


def rope_tables(places, head_size):
    half_size = head_size // 2
    frequency = ROPE_BASE ** (-2.0 * jnp.arange(half_size, dtype=F32) / head_size)
    angles = places.astype(F32)[:, None] * frequency[None, :]
    return (jnp.cos(angles), jnp.sin(angles))


def rotate(vector, cosine, sine_table, direction):
    half_size = vector.shape[-1] // 2
    front_half = vector[..., :half_size]
    back_half = vector[..., half_size:]
    cosine = cosine[:, None, :]
    sine_table = direction * sine_table[:, None, :]
    return jnp.concatenate(
        [
            front_half * cosine - back_half * sine_table,
            back_half * cosine + front_half * sine_table,
        ],
        axis=-1,
    )


def norm_back(grad_normed, normed, inverse, gain_row):
    scaled = grad_normed * gain_row
    return inverse * (scaled - normed * jnp.mean(scaled * normed, axis=-1, keepdims=True))


def dot(left, right):
    return jnp.dot(left, right, preferred_element_type=F32)


def dot_t(left, right):
    return lax.dot_general(left, right, (((1,), (1,)), ((), ())), preferred_element_type=F32)


def t_dot(left, right):
    return lax.dot_general(left, right, (((0,), (0,)), ((), ())), preferred_element_type=F32)


def column(vector, rows):
    return jnp.pad(vector, (0, rows - vector.shape[0]))[:, None]


def shards_apart(
    tokens,
    cotangent,
    lengths,
    attn_gain,
    q_weight,
    q_bias,
    k_weight,
    k_bias,
    v_weight,
    v_bias,
    o_weight,
    mlp_gain,
    gate_weight,
    up_weight,
    down_weight,
):
    seq, fsdp = lax.axis_size("seq"), lax.axis_size("fsdp")
    devices = seq * fsdp
    depth = seq // 2
    rows, model = tokens.shape
    total = rows * devices
    key_width = KV_HEADS * HEAD_DIM
    query_width = HEADS * HEAD_DIM
    model_rows = q_weight.shape[0]
    units = gate_weight.shape[1] // seq
    first_row = lax.axis_index(AXES) * rows
    positions = first_row + jnp.arange(rows, dtype=jnp.int32)
    begin = begin_of(positions, lengths)
    cosine, sine_table = rope_tables(positions - begin, HEAD_DIM)
    score_scale = HEAD_DIM ** (-0.5)

    small = jnp.concatenate(
        [column(v, model_rows) for v in (attn_gain, q_bias, k_bias, v_bias, mlp_gain)]
        + [jnp.zeros((model_rows, 123), BF16)],
        axis=1,
    )
    pack = jnp.concatenate([q_weight, k_weight, v_weight, o_weight, small], axis=1)
    wide = jnp.stack([gate_weight, up_weight]).reshape(2, model_rows, seq, units)
    wide = wide.transpose(0, 2, 1, 3)
    pack_all, cot_all, wide_all, down_all = call_start(
        depth, 0, pack, cotangent, wide, down_weight
    )
    pack_all = pack_all.reshape(model, pack.shape[1])
    qkv_width = query_width + 2 * key_width
    w_qkv = pack_all[:, :qkv_width]
    w_out = pack_all[:, qkv_width : qkv_width + query_width]
    smalls = pack_all[:, qkv_width + query_width :].astype(F32)
    gain_one, b_query = smalls[:, 0], smalls[:, 1]
    gain_two = smalls[:, 4]
    kv_share = k_bias.shape[0]
    b_key = smalls[:, 2].reshape(devices, model_rows)[:, :kv_share].reshape(key_width)
    b_value = smalls[:, 3].reshape(devices, model_rows)[:, :kv_share].reshape(key_width)
    cot_all = cot_all.reshape(seq * rows, model)
    w_gate = wide_all[0].reshape(model, units)
    w_up = wide_all[1].reshape(model, units)
    w_down = down_all.reshape(units, model)

    inputs = tokens.astype(F32)
    inv_one = lax.rsqrt(jnp.mean(inputs * inputs, axis=-1, keepdims=True) + EPSILON)
    normed_one = inputs * inv_one
    hidden_one = (normed_one * gain_one).astype(BF16)
    lin = dot(hidden_one, w_qkv) + jnp.concatenate([b_query, b_key, b_value])
    queries = rotate(
        lin[:, :query_width].reshape(rows, HEADS, HEAD_DIM), cosine, sine_table, 1.0
    ).astype(BF16)
    queries = queries.transpose(1, 0, 2).reshape(KV_HEADS, GROUP * rows, HEAD_DIM)
    keys = rotate(
        lin[:, query_width : query_width + key_width].reshape(rows, KV_HEADS, HEAD_DIM),
        cosine,
        sine_table,
        1.0,
    ).reshape(rows, key_width)
    kv = jnp.concatenate([keys, lin[:, query_width + key_width :]], axis=1).astype(BF16)
    (kv_all,) = call_gathers(depth, 1, [True], [kv])
    kv_all = kv_all.reshape(total, 2 * key_width)
    all_keys, all_values = kv_all[:, :key_width], kv_all[:, key_width:]

    span = min(512, total)
    low = begin[0] // span
    high = (first_row + rows - 1) // span + 1
    info = jnp.stack([first_row, low, high]).astype(jnp.int32)
    begin_column = begin[:, None]
    mixed, lse = call_forward(span, info, begin_column, queries, all_keys, all_values)
    mixed_low = (
        mixed.reshape(HEADS, rows, HEAD_DIM)
        .transpose(1, 0, 2)
        .reshape(rows, query_width)
        .astype(BF16)
    )
    middle = inputs + dot(mixed_low, w_out)
    inv_two = lax.rsqrt(jnp.mean(middle * middle, axis=-1, keepdims=True) + EPSILON)
    normed_two = middle * inv_two
    hidden_two = (normed_two * gain_two).astype(BF16)

    (hidden_all,) = call_gathers(depth, 2, [False], [hidden_two])
    hidden_all = hidden_all.reshape(seq * rows, model)
    gate = dot(hidden_all, w_gate)
    up = dot(hidden_all, w_up)
    sigma = jax.nn.sigmoid(gate)
    silu = gate * sigma
    activated = (silu * up).astype(BF16)
    d_act = dot_t(cot_all, w_down)
    d_gate = (d_act * up * sigma * (1.0 + gate * (1.0 - sigma))).astype(BF16)
    d_up = (d_act * silu).astype(BF16)
    d_hidden_part = dot_t(d_gate, w_gate) + dot_t(d_up, w_up)
    out_part = dot(activated, w_down)
    shape = (depth, 2, rows, model)
    d_hidden_two, branch = call_reduces(
        depth,
        3,
        [False, False],
        [d_hidden_part.astype(BF16).reshape(shape), out_part.astype(BF16).reshape(shape)],
    )
    layer_out = (middle + branch).astype(BF16)
    gate_part = t_dot(hidden_all, d_gate).astype(BF16)
    up_part = t_dot(hidden_all, d_up).astype(BF16)
    down_part = t_dot(activated, cot_all).astype(BF16)

    gain_two_grad = jnp.sum(d_hidden_two * normed_two, axis=0)
    d_middle = cotangent.astype(F32) + norm_back(d_hidden_two, normed_two, inv_two, gain_two)

    d_branch = d_middle.astype(BF16)
    d_mixed = dot_t(d_branch, w_out).astype(BF16)
    d_mixed = (
        d_mixed.reshape(rows, HEADS, HEAD_DIM)
        .transpose(1, 0, 2)
        .reshape(KV_HEADS, GROUP * rows, HEAD_DIM)
    )
    d_query, d_kv_part = call_backward(
        span, info, begin_column, queries, all_keys, all_values, mixed, lse, d_mixed
    )
    (d_kv,) = call_reduces(
        depth, 4, [True], [d_kv_part.reshape(depth, 2, 2, 2, rows, 2 * key_width)]
    )
    d_query = d_query.reshape(HEADS, rows, HEAD_DIM).transpose(1, 0, 2)
    d_q = rotate(d_query * score_scale, cosine, sine_table, -1.0).reshape(rows, query_width)
    d_k = rotate(
        d_kv[:, :key_width].reshape(rows, KV_HEADS, HEAD_DIM) * score_scale,
        cosine,
        sine_table,
        -1.0,
    ).reshape(rows, key_width)
    d_lin = jnp.concatenate([d_q, d_k, d_kv[:, key_width:]], axis=1).astype(BF16)
    bias_grad = jnp.sum(d_lin.astype(F32), axis=0)
    d_hidden_one = dot_t(d_lin, w_qkv)
    gain_one_grad = jnp.sum(d_hidden_one * normed_one, axis=0)
    input_grad = d_middle + norm_back(d_hidden_one, normed_one, inv_one, gain_one)

    def spread(vector):
        parts = vector.reshape(devices, -1)
        return jnp.pad(parts, ((0, 0), (0, model_rows - parts.shape[1]))).reshape(model, 1)

    small_part = jnp.concatenate(
        [
            spread(gain_one_grad),
            spread(bias_grad[:query_width]),
            spread(bias_grad[query_width : query_width + key_width]),
            spread(bias_grad[query_width + key_width :]),
            spread(gain_two_grad),
            jnp.zeros((model, 123), F32),
        ],
        axis=1,
    )
    pack_part = jnp.concatenate(
        [
            t_dot(hidden_one, d_lin).astype(BF16),
            t_dot(mixed_low, d_branch).astype(BF16),
            small_part.astype(BF16),
        ],
        axis=1,
    ).reshape(depth, 2, 2, 2, model_rows, pack.shape[1])
    wide_part = jnp.stack([gate_part, up_part]).reshape(2, seq, fsdp, model_rows, units)
    down_part = down_part.reshape(fsdp, units // fsdp, model)
    pack_grad, wide_grad, down_grad = call_end(depth, 5, pack_part, wide_part, down_part)
    wide_grad = wide_grad.transpose(1, 2, 0, 3).reshape(2, model_rows, seq * units).astype(F32)
    small_grad = pack_grad[:, qkv_width + query_width :]
    return (
        layer_out,
        input_grad,
        small_grad[:, 0],
        pack_grad[:, :query_width],
        small_grad[:, 1],
        pack_grad[:, query_width : query_width + key_width],
        small_grad[:kv_share, 2],
        pack_grad[:, query_width + key_width : qkv_width],
        small_grad[:kv_share, 3],
        pack_grad[:, qkv_width : qkv_width + query_width],
        small_grad[:, 4],
        wide_grad[0],
        wide_grad[1],
        down_grad,
    )


def shards_joined(
    tokens,
    cotangent,
    lengths,
    attn_gain,
    q_weight,
    q_bias,
    k_weight,
    k_bias,
    v_weight,
    v_bias,
    o_weight,
    mlp_gain,
    gate_weight,
    up_weight,
    down_weight,
):
    seq, fsdp = lax.axis_size("seq"), lax.axis_size("fsdp")
    devices = seq * fsdp
    depth = seq // 2
    rows, model = tokens.shape
    key_width = KV_HEADS * HEAD_DIM
    model_rows = q_weight.shape[0]
    kv_share = k_bias.shape[0]
    small = jnp.stack(
        [jnp.pad(v, (0, model_rows - v.shape[0])) for v in (attn_gain, q_bias, k_bias, v_bias, mlp_gain)],
        axis=1,
    )
    small = jnp.pad(small, ((0, 0), (0, 123)))
    few = down_weight.shape[0]
    filled = fsdp * (few + -few % 16)
    steps = np.arange(HEAD_DIM) % (HEAD_DIM // 2)
    frequency = jnp.asarray((ROPE_BASE ** (-2.0 * steps / HEAD_DIM)).astype(np.float32)[None, :])
    (
        pack_all,
        o_all,
        kv_all,
        cot_all,
        wide_all,
        down_all,
        hidden_all,
        queries,
        mixed,
        lse,
        middle,
        hidden_pair,
        mixed_low,
        pair,
        angles,
        begin,
        vectors,
    ) = call_head(
        depth,
        6,
        (o_weight, gate_weight, up_weight, down_weight),
        (
            q_weight,
            k_weight,
            v_weight,
            small,
            tokens,
            cotangent,
            frequency,
        ),
        lengths,
    )
    layer_out, d_middle, d_mixed, d_branch, gain_two_grad, down_part, wide_part = call_middle(
        depth,
        7,
        (
            hidden_all,
            cot_all,
            wide_all.reshape(2, seq, 2, 2, model_rows, filled),
            down_all.reshape(filled, model),
            o_all,
        ),
        (middle, cotangent, vectors),
    )
    input_grad, q_grad, kvs_grad, o_grad, down_grad, wide_grad = call_last(
        depth,
        8,
        (kv_all, pack_all, wide_part, down_part),
        (d_mixed, angles, begin, vectors, gain_two_grad),
        (queries, mixed, lse, mixed_low, d_branch, hidden_pair, pair, d_middle),
    )
    sizes = (model_rows, model_rows, kv_share, kv_share, model_rows)
    gate_grad, up_grad, down_grad, q_grad, k_grad, v_grad, *rest = call_finish(
        few, sizes, wide_grad, down_grad, q_grad, kvs_grad, (layer_out, input_grad, o_grad)
    )
    layer_out, input_grad, o_grad = rest[:3]
    small_grad = [vector.reshape(-1) for vector in rest[3:]]
    return (
        layer_out,
        input_grad,
        small_grad[0],
        q_grad,
        small_grad[1],
        k_grad,
        small_grad[2],
        v_grad,
        small_grad[3],
        o_grad,
        small_grad[4],
        gate_grad,
        up_grad,
        down_grad,
    )


def shards(*arguments):
    model_rows, rows = arguments[4].shape[0], arguments[0].shape[0]
    if model_rows % 16 == 0 and rows % 128 == 0 and lax.axis_size("seq") == 8:
        return shards_joined(*arguments)
    return shards_apart(*arguments)


def solution(mesh):
    matrix, vector = P(AXES, None), P(AXES)
    in_specs = (
        matrix,
        matrix,
        P(),
        vector,
        matrix,
        vector,
        matrix,
        vector,
        matrix,
        vector,
        matrix,
        vector,
        matrix,
        matrix,
        matrix,
    )
    out_specs = (
        matrix,
        matrix,
        vector,
        matrix,
        vector,
        matrix,
        vector,
        matrix,
        vector,
        matrix,
        vector,
        matrix,
        matrix,
        matrix,
    )
    return jax.shard_map(shards, mesh=mesh, in_specs=in_specs, out_specs=out_specs, check_vma=False)
```
